32 devices in a mesh: ctx: 8 (over z, x), zero: 4 (over y, core).
Axes of the slice: x: 2, y: 2, z: 4, core: 2. Of those that a mesh axis runs over, the one named last changes fastest.
Arguments:
- activations: bfloat16 [4096, 4096], P('ctx', 'zero'), may hold values from -1200 to 1200
- norm_gain: bfloat16 [4096], replicated, may hold values from 0.099609375 to 1.8984375
- query_weight: bfloat16 [4096, 1024], P('ctx', 'zero'), may hold values from -24 to 24
- kv_weight: bfloat16 [4096, 4, 128], P('ctx', 'zero'), may hold values from -1 to 1
- out_weight: bfloat16 [1024, 4096], P('zero', 'ctx'), may hold values from -0.1875 to 0.1875
- tile_mask: int32 [8, 4, 4], P('ctx'), may hold values from 0 to 1, as said below
- anchor_mask: int32 [8, 4, 4], P('ctx'), may hold values 0 or 1
- anchor_index: int32 [1], replicated, may hold values from 0 to 7
Outputs:
- mixed: bfloat16 [4096, 4096], P(('ctx', 'zero'))
The draws below stay inside these ranges and needn't reach their ends.
Inputs may be any that keep to these rules, and one draw needn't show every extreme that they name: `tile_mask`: entries of every block's table above the diagonal are 0 and diagonal entries are 1.
All inputs are finite; a program needn't handle non-finite values. No bound on the sum of `anchor_mask` on one device may be relied on, other than what follows from the above.
Results may differ from the reference program's by a relative error of at most 0.02.
Values may be sent and summed in bfloat16 or wider, within the bound.
No kernel may reach another device: no remote copies, remote signals or barrier semaphores. Data moves between devices by JAX's collectives and lax.ppermute only.
A program may use at most 64 MiB of HBM per device.

```python
import math
import jax
import jax.numpy as jnp
from jax import lax

D = 4096
HD = 128
QH_DEV = 2
TILE = 128
BLOCK = 512
HQ = 8
KVH = 2
BLOCKS = 8
TOKENS = 4096
NT = 4


def key_base(key):
    return jnp.clip(jax.random.normal(jax.random.fold_in(key, 11), (D, KVH, HD), jnp.float32), -6.0, 6.0) * D ** (-0.5)


def draw_activations(key, part):
    first, second, third = jax.random.split(key, 3)
    row_scale = jnp.exp(jax.random.uniform(second, (TOKENS, 1), jnp.float32) * math.log(10.0))
    column_scale = jnp.exp(jax.random.uniform(third, (1, D), jnp.float32) * math.log(10.0))
    base = jnp.clip(jax.random.normal(first, (TOKENS, D), jnp.float32), -6.0, 6.0)
    return (base * row_scale * column_scale).astype(jnp.bfloat16)


def draw_query_weight(key, part):
    drawn = jnp.clip(jax.random.normal(jax.random.fold_in(key, 12), (D, HQ, HD), jnp.float32), -6.0, 6.0) * D ** (-0.5)
    return drawn.reshape(D, HQ * HD).astype(jnp.bfloat16)


def draw_kv_weight(key, part):
    key_part = key_base(key)
    value_part = jnp.clip(jax.random.normal(jax.random.fold_in(key, 14), (D, KVH, HD), jnp.float32), -6.0, 6.0) * D ** (-0.5)
    return jnp.stack([key_part, value_part], axis=2).reshape(D, 2 * KVH, HD).astype(jnp.bfloat16)


def draw_tile_mask(key, part):
    coins = jax.random.randint(key, (BLOCKS, NT, NT), 0, 2, jnp.int32)
    lower = jnp.tril(coins, -1)
    return lower + jnp.eye(NT, dtype=jnp.int32)[None]


def with_ends(array, rng, smallest, high):
    longest = array.shape.index(max(array.shape))
    spots = []
    for shift in (0, 1):
        where = [jax.random.randint(jax.random.fold_in(rng, axis), (), 0, length) for axis, length in enumerate(array.shape)]
        where[longest] = (where[longest] + shift) % array.shape[longest]
        spots.append(tuple(where))
    return array.at[spots[0]].set(smallest).at[spots[1]].set(high)


def shard_levels(stream_key, shape, cuts, least, high):
    loudness, own = 1.0, jax.random.fold_in(stream_key, 6)
    for position, parts in cuts:
        draws = jnp.exp(jax.random.uniform(jax.random.fold_in(own, position), (parts,), jnp.float32, least / len(cuts), high / len(cuts)))
        loudness = loudness * jnp.repeat(draws, shape[position] // parts).reshape([-1 if axis == position else 1 for axis in range(len(shape))])
    return loudness


def noise(stream_key, shape, spread, bound, shards=(), held_as=jnp.bfloat16):
    drawn = jax.random.normal(stream_key, shape, jnp.float32) * spread
    if len(shards) > 0:
        drawn = shard_levels(stream_key, shape, shards, -0.22, 0.18) * drawn
    return jnp.clip(drawn, min=-bound, max=bound).astype(held_as)


def setup_inputs(seed: int = 0) -> dict:
    seeds = jax.random.split(jax.random.key(seed), 9)
    activations = draw_activations(jax.random.fold_in(seeds[8], 71), 0)
    norm_gain = jnp.clip(1.0 + 0.18 * jax.random.normal(seeds[1], (D,), jnp.float32), 0.099609375, 1.8984375).astype(jnp.bfloat16)
    query_weight = draw_query_weight(jax.random.fold_in(seeds[8], 71), 0)
    kv_weight = draw_kv_weight(jax.random.fold_in(seeds[8], 71), 0)
    out_weight = noise(seeds[4], (HQ * HD, D), (HQ * HD) ** -0.5, 0.1875, ((0, 4), (1, 8)))
    tile_mask = draw_tile_mask(jax.random.fold_in(seeds[8], 71), 0)
    anchor_mask = with_ends((jax.random.randint(seeds[6], (BLOCKS, NT, NT), 0, 4) < 3).astype(jnp.int32), jax.random.fold_in(seeds[6], 1), 0, 1)
    anchor_index = jax.random.randint(seeds[7], (1,), 0, BLOCKS).astype(jnp.int32)
    return dict(activations=activations, norm_gain=norm_gain, query_weight=query_weight, kv_weight=kv_weight, out_weight=out_weight, tile_mask=tile_mask, anchor_mask=anchor_mask, anchor_index=anchor_index)


def rotate(vectors, positions):
    half_size = vectors.shape[-1] // 2
    frequency = jnp.power(jnp.float32(500000.0), -(jnp.arange(half_size, dtype=jnp.float32) * 2.0 / vectors.shape[-1]))
    angles = positions.astype(jnp.float32)[:, None] * frequency[None, :]
    cosine_table = jnp.cos(angles)[:, None, :]
    sine_table = jnp.sin(angles)[:, None, :]
    first = vectors[..., :half_size]
    second = vectors[..., half_size:]
    return jnp.concatenate([first * cosine_table - second * sine_table, second * cosine_table + first * sine_table], -1)

def expand_tiles(table):
    tiles = table.shape[0]
    return jnp.broadcast_to(table[:, None, :, None], (tiles, TILE, tiles, TILE)).reshape(tiles * TILE, tiles * TILE)

def reference(activations, norm_gain, query_weight, kv_weight, out_weight, tile_mask, anchor_mask, anchor_index):
    x_float = activations.astype(jnp.float32)
    mean_square = lax.optimization_barrier(jnp.mean(x_float * x_float, -1, keepdims=True))
    normed = (x_float * lax.rsqrt(mean_square + 1e-05) * norm_gain.astype(jnp.float32)).astype(jnp.bfloat16)
    positions = jnp.arange(TOKENS, dtype=jnp.int32)
    queries = (rotate(jnp.dot(normed, query_weight, preferred_element_type=jnp.float32).reshape(TOKENS, HQ, HD), positions) * HD ** (-0.5)).astype(jnp.bfloat16)
    key_weight = kv_weight[:, 0::2, :].reshape(D, KVH * HD)
    value_weight = kv_weight[:, 1::2, :].reshape(D, KVH * HD)
    keys = rotate(jnp.dot(normed, key_weight, preferred_element_type=jnp.float32).reshape(TOKENS, KVH, HD), positions).astype(jnp.bfloat16)
    values = jnp.dot(normed, value_weight, preferred_element_type=jnp.float32).astype(jnp.bfloat16).reshape(TOKENS, KVH, HD)
    anchor_block = anchor_index[0]
    group_size = HQ // KVH
    row_offsets = jnp.arange(BLOCK, dtype=jnp.int32)

    def host(host_index):
        host_queries = lax.dynamic_slice_in_dim(queries, host_index * BLOCK, BLOCK, 0).astype(jnp.float32)
        all_keys = jnp.concatenate([lax.dynamic_slice_in_dim(keys, anchor_block * BLOCK, BLOCK, 0), lax.dynamic_slice_in_dim(keys, host_index * BLOCK, BLOCK, 0)], 0)
        all_values = jnp.concatenate([lax.dynamic_slice_in_dim(values, anchor_block * BLOCK, BLOCK, 0), lax.dynamic_slice_in_dim(values, host_index * BLOCK, BLOCK, 0)], 0)
        all_keys = jnp.repeat(all_keys.astype(jnp.float32), group_size, axis=1)
        all_values = jnp.repeat(all_values.astype(jnp.float32), group_size, axis=1)
        scores = jnp.einsum('thd,khd->htk', host_queries, all_keys)
        far_visible = (expand_tiles(anchor_mask[host_index]) == 1) & (host_index != anchor_block)
        near_visible = (expand_tiles(tile_mask[host_index]) == 1) & (row_offsets[None, :] <= row_offsets[:, None])
        visible = jnp.concatenate([far_visible, near_visible], 1)[None]
        scores = jnp.where(visible, scores, jnp.float32(-1e+30))
        largest = lax.optimization_barrier(jnp.max(scores, -1, keepdims=True))
        weights = jnp.where(visible, jnp.exp(scores - largest), jnp.float32(0.0))
        row_total = lax.optimization_barrier(jnp.sum(weights, -1))
        rounded = lax.optimization_barrier(weights.astype(jnp.bfloat16)).astype(jnp.float32)
        attended = jnp.einsum('htk,khd->thd', rounded, all_values) / jnp.transpose(row_total)[:, :, None]
        return attended.astype(jnp.bfloat16).reshape(BLOCK, HQ * HD)
    attended = lax.map(host, jnp.arange(BLOCKS, dtype=jnp.int32)).reshape(TOKENS, HQ * HD)
    group_width = QH_DEV * HD

    def add_group(running, group_index):
        columns = lax.dynamic_slice_in_dim(attended, group_index * group_width, group_width, 1)
        weight_rows = lax.dynamic_slice_in_dim(out_weight, group_index * group_width, group_width, 0)
        group_term = jnp.dot(columns, weight_rows, preferred_element_type=jnp.float32)
        group_term = lax.optimization_barrier(group_term.astype(jnp.bfloat16)).astype(jnp.float32)
        return (running + group_term, None)
    running = lax.scan(add_group, jnp.zeros((TOKENS, D), jnp.float32), jnp.arange(HQ // QH_DEV, dtype=jnp.int32))[0]
    return running.astype(jnp.bfloat16)
```

```python
import functools
import math

import jax
import jax.numpy as jnp
from jax import lax
from jax.experimental import pallas as pl
from jax.experimental.pallas import tpu as pltpu
from jax.sharding import PartitionSpec as P

ANY = pl.BlockSpec(memory_space=pl.ANY)
VMEM = pl.BlockSpec(memory_space=pltpu.VMEM)
SMEM = pl.BlockSpec(memory_space=pltpu.SMEM)
VMEM_LIMIT = 48 * 1024 * 1024
ROPE_BASE = 500000.0
CHUNKS = 4


def swap(value, axis, stride):
    pairs = [(source, source ^ stride) for source in range(lax.axis_size(axis))]
    return lax.ppermute(value, axis, pairs)


def cycle(size):
    return list(range(0, size, 2)) + list(range(1, size, 2))[::-1]


def ring_gather(shard):
    size = lax.axis_size("ctx")
    order = cycle(size)
    ahead = [(order[i], order[(i + 1) % size]) for i in range(size)]
    back = [(target, source) for source, target in ahead]
    rows = shard.shape[0]
    held = {0: [(0, shard)]}
    fwd = bwd = shard
    for step in range(1, size // 2):
        fwd = lax.ppermute(fwd, "ctx", ahead)
        bwd = lax.ppermute(bwd, "ctx", back)
        held[size - step] = [(0, fwd)]
        held[step] = [(0, bwd)]
    half = rows // 2
    held[size // 2] = [
        (0, lax.ppermute(fwd[:half], "ctx", ahead)),
        (half, lax.ppermute(bwd[half:], "ctx", back)),
    ]
    return held


def cube_gather(piece):
    size = lax.axis_size("zero")
    held = [piece] + [None] * (size - 1)
    stride = size // 2
    while stride:
        for known in range(0, size, 2 * stride):
            held[known + stride] = swap(held[known], "zero", stride)
        stride //= 2
    return held


def project_kernel(layout, pieces, order_ref, scale_ref, cos_ref, sin_ref, *refs):
    (out_ref, x_buf, w_buf, x_sem, w_sem) = refs[-5:]
    x_refs = refs[:pieces]
    w_refs = refs[pieces:-5]
    shard_rows = w_buf.shape[0] // len({offset for offset, _ in layout})
    copies = []
    for at, (ref, (offset, first)) in enumerate(zip(w_refs, layout)):
        start = order_ref[offset] * shard_rows + first
        copies.append(
            pltpu.make_async_copy(
                ref, w_buf.at[pl.ds(pl.multiple_of(start, 16), ref.shape[0])], w_sem.at[at]
            )
        )
    for at, ref in enumerate(x_refs):
        place = jnp.bitwise_xor(order_ref[order_ref.shape[0] - 1], at)
        copies.append(pltpu.make_async_copy(ref, x_buf.at[place], x_sem.at[at]))
    for copy in copies:
        copy.start()
    for copy in copies:
        copy.wait()
    depth = x_buf.shape[2]
    total = jnp.zeros(out_ref.shape, jnp.float32)
    for at in range(pieces):
        total += jnp.dot(
            x_buf[at], w_buf[at * depth : (at + 1) * depth, :], preferred_element_type=jnp.float32
        )
    total = total * scale_ref[...]
    head = cos_ref.shape[1]
    for first in range(0, out_ref.shape[1], head):
        part = total[:, first : first + head]
        turned = part * cos_ref[...] + pltpu.roll(part, head // 2, 1) * sin_ref[...]
        out_ref[:, first : first + head] = turned.astype(out_ref.dtype)


def project(order, scale, cos, sin, x_pieces, held):
    layout = [(offset, first) for offset in held for first, _ in held[offset]]
    shards = [piece for offset in held for _, piece in held[offset]]
    tokens, depth = x_pieces[0].shape
    width = shards[0].shape[1]
    full = depth * len(x_pieces)
    return pl.pallas_call(
        functools.partial(project_kernel, layout, len(x_pieces)),
        out_shape=jax.ShapeDtypeStruct((tokens, width), jnp.bfloat16),
        in_specs=[SMEM, VMEM, VMEM, VMEM] + [ANY] * (len(x_pieces) + len(shards)),
        out_specs=VMEM,
        scratch_shapes=[
            pltpu.VMEM((len(x_pieces), tokens, depth), jnp.bfloat16),
            pltpu.VMEM((full, width), jnp.bfloat16),
            pltpu.SemaphoreType.DMA((len(x_pieces),)),
            pltpu.SemaphoreType.DMA((len(shards),)),
        ],
        compiler_params=pltpu.CompilerParams(vmem_limit_bytes=VMEM_LIMIT),
        cost_estimate=pl.CostEstimate(
            flops=2 * tokens * full * width,
            bytes_accessed=2 * full * (tokens + width),
            transcendentals=0,
        ),
    )(order, scale, cos, sin, *x_pieces, *shards)


def attend_kernel(own_ref, far_ref, q_ref, kf_ref, vf_ref, kn_ref, vn_ref, out_ref):
    tokens, head = kn_ref.shape
    tiles = own_ref.shape[0]
    tile = tokens // tiles
    heads = q_ref.shape[1] // head
    rows = heads * tile
    column = lax.broadcasted_iota(jnp.int32, (rows, tile), 1)
    row = lax.rem(lax.broadcasted_iota(jnp.int32, (rows, tile), 0), tile)
    hidden = jnp.float32(-1e30)
    nt = (((1,), (1,)), ((), ()))
    for i in range(tiles):
        across = slice(i * tile, (i + 1) * tile)
        q = jnp.concatenate(
            [q_ref[across, h * head : (h + 1) * head] for h in range(heads)], axis=0
        )
        seen = (i + 1) * tile
        far = lax.dot_general(q, kf_ref[...], nt, preferred_element_type=jnp.float32)
        near = lax.dot_general(q, kn_ref[:seen, :], nt, preferred_element_type=jnp.float32)
        parts = []
        for j in range(tiles):
            block = far[:, j * tile : (j + 1) * tile]
            parts.append(jnp.where(far_ref[i, j] == 1, block, hidden))
        for j in range(i + 1):
            block = near[:, j * tile : (j + 1) * tile]
            block = jnp.where(own_ref[i, j] == 1, block, hidden)
            if j == i:
                block = jnp.where(column <= row, block, hidden)
            parts.append(block)
        scores = jnp.concatenate(parts, axis=1)
        largest = jnp.max(scores, axis=1, keepdims=True)
        weights = jnp.exp(scores - largest)
        total = jnp.sum(weights, axis=1, keepdims=True)
        rounded = weights.astype(jnp.bfloat16)
        mixed = jnp.dot(rounded[:, :tokens], vf_ref[...], preferred_element_type=jnp.float32)
        mixed += jnp.dot(
            rounded[:, tokens:], vn_ref[:seen, :], preferred_element_type=jnp.float32
        )
        mixed = (mixed / total).astype(out_ref.dtype)
        for h in range(heads):
            out_ref[across, h * head : (h + 1) * head] = mixed[h * tile : (h + 1) * tile, :]


def attend(own_mask, far_mask, queries, far_keys, far_values, keys, values):
    tokens, head = keys.shape
    heads = queries.shape[1] // head
    return pl.pallas_call(
        attend_kernel,
        out_shape=jax.ShapeDtypeStruct(queries.shape, jnp.bfloat16),
        in_specs=[SMEM, SMEM] + [VMEM] * 5,
        out_specs=VMEM,
        compiler_params=pltpu.CompilerParams(vmem_limit_bytes=VMEM_LIMIT),
        cost_estimate=pl.CostEstimate(
            flops=8 * heads * tokens * tokens * head,
            bytes_accessed=4 * tokens * head * (heads + 2),
            transcendentals=2 * heads * tokens * tokens,
        ),
    )(own_mask, far_mask, queries, far_keys, far_values, keys, values)


def terms_kernel(layout, pick_ref, a_ref, *refs):
    keep_ref, send_ref, w_buf, sem = refs[-4:]
    half = keep_ref.shape[0]
    width = w_buf.shape[2]
    copies = []
    for at, (ref, (slot, first)) in enumerate(zip(refs[:-4], layout)):
        copies.append(
            pltpu.make_async_copy(ref, w_buf.at[slot, pl.ds(first, ref.shape[0])], sem.at[at])
        )
    for copy in copies:
        copy.start()
    for copy in copies:
        copy.wait()
    pick = pick_ref[0]
    mine = a_ref[pl.ds(pl.multiple_of(pick * half, 16), half), :]
    other = a_ref[pl.ds(pl.multiple_of((1 - pick) * half, 16), half), :]
    both = jnp.concatenate([other, mine], axis=0)
    for slot in range(w_buf.shape[0]):
        out = jnp.dot(both, w_buf[slot], preferred_element_type=jnp.float32)
        columns = slice(slot * width, (slot + 1) * width)
        send_ref[:, columns] = out[:half].astype(send_ref.dtype)
        keep_ref[:, columns] = out[half:]


def terms(pick, both_heads, own, partner):
    pair_rows = own[0][0][1].shape[0]
    if len(own[0]) > 1:
        pair_rows = sum(piece.shape[0] for _, piece in own[0])
    layout, shards = [], []
    for slot, (mine, theirs) in enumerate(zip(own, partner)):
        for base, pieces in ((0, mine), (pair_rows, theirs)):
            for first, piece in pieces:
                layout.append((slot, base + first))
                shards.append(piece)
    width = own[0][0][1].shape[1]
    rows, depth = both_heads.shape
    columns = width * len(own)
    return pl.pallas_call(
        functools.partial(terms_kernel, layout),
        out_shape=(
            jax.ShapeDtypeStruct((rows // 2, columns), jnp.float32),
            jax.ShapeDtypeStruct((rows // 2, columns), jnp.bfloat16),
        ),
        in_specs=[SMEM, VMEM] + [ANY] * len(shards),
        out_specs=(VMEM, VMEM),
        scratch_shapes=[
            pltpu.VMEM((len(own), depth, width), jnp.bfloat16),
            pltpu.SemaphoreType.DMA((len(shards),)),
        ],
        compiler_params=pltpu.CompilerParams(vmem_limit_bytes=VMEM_LIMIT),
        cost_estimate=pl.CostEstimate(
            flops=2 * rows * depth * columns,
            bytes_accessed=2 * (rows + columns) * depth + 3 * rows * columns,
            transcendentals=0,
        ),
    )(pick, both_heads, *shards)


def join_kernel(groups, order_ref, *refs):
    out_ref = refs[-1]
    count = len(groups)
    width = out_ref.shape[1] // sum(len(group) for group in groups)
    for group, keep_ref, got_ref in zip(groups, refs[:count], refs[count:-1]):
        for slot, offset in enumerate(group):
            columns = slice(slot * width, (slot + 1) * width)
            start = pl.multiple_of(order_ref[offset] * width, 128)
            total = keep_ref[:, columns] + got_ref[:, columns].astype(jnp.float32)
            out_ref[:, pl.ds(start, width)] = total.astype(out_ref.dtype)


def join(order, groups, keeps, gots):
    rows = keeps[0].shape[0]
    columns = sum(keep.shape[1] for keep in keeps)
    return pl.pallas_call(
        functools.partial(join_kernel, groups),
        out_shape=jax.ShapeDtypeStruct((rows, columns), jnp.bfloat16),
        in_specs=[SMEM] + [VMEM] * (2 * len(keeps)),
        out_specs=VMEM,
        compiler_params=pltpu.CompilerParams(vmem_limit_bytes=VMEM_LIMIT),
        cost_estimate=pl.CostEstimate(
            flops=rows * columns, bytes_accessed=8 * rows * columns, transcendentals=0
        ),
    )(order, *keeps, *gots)


def broadcast_from(value, root):
    me = lax.axis_index("ctx")
    for bit in range(int(math.log2(lax.axis_size("ctx")))):
        other = swap(value, "ctx", 1 << bit)
        same = ((me >> bit) & 1) == ((root >> bit) & 1)
        value = jnp.where(same, value, other)
    return value


def local(
    activations,
    norm_gain,
    query_weight,
    kv_weight,
    out_weight,
    tile_mask,
    anchor_mask,
    anchor_index,
):
    tokens, depth = activations.shape
    head = kv_weight.shape[2]
    ctx_size, zero_size = lax.axis_size("ctx"), lax.axis_size("zero")
    ctx_rank, zero_rank = lax.axis_index("ctx"), lax.axis_index("zero")
    order = jnp.array(cycle(ctx_size), jnp.int32)
    where = jnp.array([cycle(ctx_size).index(i) for i in range(ctx_size)], jnp.int32)[ctx_rank]
    source = order[(where + jnp.arange(ctx_size, dtype=jnp.int32)) % ctx_size]
    source = jnp.concatenate([source, zero_rank[None].astype(jnp.int32)])

    shard_rows = kv_weight.shape[0]
    gain = lax.dynamic_slice_in_dim(norm_gain, ctx_rank * shard_rows, shard_rows)
    gain = gain.astype(jnp.float32)[:, None]
    kv_shard = (kv_weight[:, 0, :].astype(jnp.float32) * gain).astype(jnp.bfloat16)
    query_shard = (query_weight.astype(jnp.float32) * gain).astype(jnp.bfloat16)

    x_pieces = cube_gather(activations)
    kv_held = ring_gather(kv_shard)
    query_held = ring_gather(query_shard)
    out_held = ring_gather(out_weight)
    out_swapped = {
        offset: [(first, swap(piece, "zero", 1)) for first, piece in pieces]
        for offset, pieces in out_held.items()
    }

    x_float = activations.astype(jnp.float32)
    squares = jnp.sum(x_float * x_float, -1)
    stride = 1
    while stride < zero_size:
        squares = squares + swap(squares, "zero", stride)
        stride *= 2
    scale = lax.rsqrt(squares / (depth * zero_size) + 1e-05)[:, None]

    half = head // 2
    frequency = jnp.power(
        jnp.float32(ROPE_BASE), -(jnp.arange(half, dtype=jnp.float32) * 2.0 / head)
    )
    positions = ctx_rank * tokens + jnp.arange(tokens, dtype=jnp.int32)
    angles = positions.astype(jnp.float32)[:, None] * frequency[None, :]
    cos_half, sin_half = jnp.cos(angles), jnp.sin(angles)
    cos = jnp.concatenate([cos_half, cos_half], -1)
    sin = jnp.concatenate([-sin_half, sin_half], -1)
    is_key = zero_rank % 2 == 0
    shrink = head ** (-0.5)

    own_half = project(
        source, scale, jnp.where(is_key, cos, 1.0), jnp.where(is_key, sin, 0.0), x_pieces, kv_held
    )
    anchor = anchor_index[0]
    far_half = broadcast_from(own_half, anchor)
    own_other = swap(own_half, "zero", 1)
    far_other = swap(far_half, "zero", 1)
    keys = jnp.where(is_key, own_half, own_other)
    values = jnp.where(is_key, own_other, own_half)
    far_keys = jnp.where(is_key, far_half, far_other)
    far_values = jnp.where(is_key, far_other, far_half)

    queries = project(source, scale, cos * shrink, sin * shrink, x_pieces, query_held)
    far_mask = jnp.where(ctx_rank != anchor, anchor_mask[0], 0)
    attended = attend(tile_mask[0], far_mask, queries, far_keys, far_values, keys, values)

    core = zero_rank % 2
    by_core = attended.reshape(zero_size // 2, 2, tokens // zero_size, attended.shape[1])
    mine = lax.dynamic_index_in_dim(by_core, core, 1, keepdims=False)
    theirs = lax.dynamic_index_in_dim(by_core, 1 - core, 1, keepdims=False)
    both_heads = jnp.concatenate([mine, swap(theirs, "zero", 1)], -1)
    both_heads = both_heads.reshape(-1, both_heads.shape[-1])

    arrival = sorted(range(ctx_size), key=lambda o: min(o, ctx_size - o))
    per = max(1, ctx_size // CHUNKS)
    groups = [arrival[at : at + per] for at in range(0, ctx_size, per)]
    top = zero_size // 2
    pick = ((zero_rank // top) % 2).astype(jnp.int32)[None]
    keeps, gots = [], []
    for group in groups:
        keep, send = terms(
            pick, both_heads, [out_held[o] for o in group], [out_swapped[o] for o in group]
        )
        got = swap(send, "zero", top)
        stride = top // 2
        while stride > 1:
            both = keep + got.astype(jnp.float32)
            rows = both.shape[0] // 2
            bit = (zero_rank // stride) % 2
            keep = lax.dynamic_slice_in_dim(both, bit * rows, rows, 0)
            send = lax.dynamic_slice_in_dim(both, (1 - bit) * rows, rows, 0)
            got = swap(send.astype(jnp.bfloat16), "zero", stride)
            stride //= 2
        keeps.append(keep)
        gots.append(got)
    return join(source, groups, keeps, gots)


def solution(mesh):
    placed = (
        P("ctx", "zero"),
        P(),
        P("ctx", "zero"),
        P("ctx", "zero", None),
        P("zero", "ctx"),
        P("ctx", None, None),
        P("ctx", None, None),
        P(),
    )
    return jax.shard_map(
        local, mesh=mesh, in_specs=placed, out_specs=P(("ctx", "zero"), None), check_vma=False
    )
```

```python
import functools
import math

import jax
import jax.numpy as jnp
from jax import lax
from jax.experimental import pallas as pl
from jax.experimental.pallas import tpu as pltpu
from jax.sharding import PartitionSpec as P

HBM = pl.BlockSpec(memory_space=pltpu.HBM)
VMEM = pl.BlockSpec(memory_space=pltpu.VMEM)
SMEM = pl.BlockSpec(memory_space=pltpu.SMEM)
VMEM_LIMIT = 48 * 1024 * 1024
ROPE_BASE = 500000.0
CHUNKS = 4


def swap(value, axis, stride):
    pairs = [(source, source ^ stride) for source in range(lax.axis_size(axis))]
    return lax.ppermute(value, axis, pairs)


def cycle(size):
    return list(range(0, size, 2)) + list(range(1, size, 2))[::-1]


def ring_step(value):
    ctx_size, zero_size = lax.axis_size("ctx"), lax.axis_size("zero")
    order = cycle(ctx_size)
    pairs = []
    for at in range(ctx_size):
        for zero in range(zero_size):
            to = order[(at + (1 if zero % 2 == 0 else -1)) % ctx_size]
            pairs.append((order[at] * zero_size + zero, to * zero_size + zero))
    return lax.ppermute(value, ("ctx", "zero"), pairs)


def ring_gather(shard, core):
    size = lax.axis_size("ctx")
    held = [(0, None, shard)]
    moving = shard
    half = shard.shape[0] // 2
    for step in range(1, size // 2 + 1):
        last = step == size // 2
        if last:
            moving = lax.dynamic_slice_in_dim(moving, core * half, half, 0)
        moving = ring_step(moving)
        held.append((-step, 0 if last else None, moving))
        held.append((step, 1 if last else None, swap(moving, "zero", 1)))
    return held


def source_of(steps):
    size = lax.axis_size("ctx")
    ctx, core = lax.axis_index("ctx"), lax.axis_index("zero") % 2
    place = jnp.where(ctx % 2 == 0, ctx // 2, size - 1 - ctx // 2)
    place = lax.rem(place + steps * (1 - 2 * core) + size, size)
    return jnp.where(place < size // 2, 2 * place, 2 * (size - 1 - place) + 1)


def share_of(share):
    core = lax.axis_index("zero") % 2
    return core if share == 0 else 1 - core


def project_kernel(layout, pieces, first_call, *refs):
    (x_buf, w_buf, x_sem, w_sem) = refs[-4:]
    scale_ref, cos_ref, sin_ref = refs[:3]
    x_refs = refs[3 : 3 + pieces]
    w_refs = refs[3 + pieces : 3 + pieces + len(layout)]
    out_ref = refs[3 + pieces + len(layout)]
    zero = lax.axis_index("zero")
    shard_rows = w_refs[0].shape[0]
    x_copies, w_copies = [], []
    for at, ref in enumerate(x_refs):
        place = jnp.bitwise_xor(zero, at)
        x_copies.append(pltpu.make_async_copy(ref, x_buf.at[place], x_sem.at[at]))
    for at, (ref, (steps, share)) in enumerate(zip(w_refs, layout)):
        start = source_of(steps) * shard_rows
        if share is not None:
            start = start + share_of(share) * ref.shape[0]
        rows = pl.ds(pl.multiple_of(start, 16), ref.shape[0])
        w_copies.append(pltpu.make_async_copy(ref, w_buf.at[rows], w_sem.at[at]))
    for copy in x_copies + w_copies:
        copy.start()
    for copy in x_copies:
        copy.wait()
    depth = x_buf.shape[2]
    if first_call:
        squares = jnp.zeros((x_buf.shape[1], 128), jnp.float32)
        for at in range(pieces):
            for first in range(0, depth, 128):
                x_float = x_buf[at, :, first : first + 128].astype(jnp.float32)
                squares += x_float * x_float
        mean = jnp.sum(squares, axis=1, keepdims=True) / (depth * pieces)
        scale = jnp.broadcast_to(lax.rsqrt(mean + 1e-05), squares.shape)
        scale_out = refs[4 + pieces + len(layout)]
        scale_out[...] = scale
    else:
        scale = scale_ref[...]
    for copy in w_copies:
        copy.wait()
    total = jnp.zeros(out_ref.shape, jnp.float32)
    for at in range(pieces):
        total += jnp.dot(
            x_buf[at], w_buf[at * depth : (at + 1) * depth, :], preferred_element_type=jnp.float32
        )
    head = cos_ref.shape[1]
    for first in range(0, out_ref.shape[1], head):
        part = total[:, first : first + head] * scale
        if not first_call or first == 0:
            part = part * cos_ref[...] + pltpu.roll(part, head // 2, 1) * sin_ref[...]
        out_ref[:, first : first + head] = part.astype(out_ref.dtype)


def project(scale, cos, sin, x_pieces, held, first_call):
    layout = [(steps, share) for steps, share, _ in held]
    shards = [piece for _, _, piece in held]
    tokens, depth = x_pieces[0].shape
    width = shards[0].shape[1]
    full = depth * len(x_pieces)
    out = [jax.ShapeDtypeStruct((tokens, width), jnp.bfloat16)]
    if first_call:
        out.append(jax.ShapeDtypeStruct((tokens, 128), jnp.float32))
    return pl.pallas_call(
        functools.partial(project_kernel, layout, len(x_pieces), first_call),
        out_shape=out,
        in_specs=[VMEM, VMEM, VMEM] + [HBM] * (len(x_pieces) + len(shards)),
        out_specs=[VMEM] * len(out),
        scratch_shapes=[
            pltpu.VMEM((len(x_pieces), tokens, depth), jnp.bfloat16),
            pltpu.VMEM((full, width), jnp.bfloat16),
            pltpu.SemaphoreType.DMA((len(x_pieces),)),
            pltpu.SemaphoreType.DMA((len(shards),)),
        ],
        compiler_params=pltpu.CompilerParams(vmem_limit_bytes=VMEM_LIMIT),
        cost_estimate=pl.CostEstimate(
            flops=2 * tokens * full * width,
            bytes_accessed=2 * full * (tokens + width),
            transcendentals=0,
        ),
    )(scale, cos, sin, *x_pieces, *shards)


def attend_kernel(groups, own_ref, far_ref, q_ref, near0, near1, far0, far1, out_ref):
    tokens, pair = near0.shape
    head = pair // 2
    size = tokens // groups
    tiles = own_ref.shape[0]
    tile = 2 * tokens // tiles
    heads = q_ref.shape[1] // head
    rows = heads * size
    core = lax.axis_index("zero") % 2
    column = lax.broadcasted_iota(jnp.int32, (1, tokens), 1)
    column_group = column // size
    within = lax.rem(lax.broadcasted_iota(jnp.int32, (rows, 1), 0), size)
    hidden = jnp.float32(-1e30)
    nt = (((1,), (1,)), ((), ()))
    for h in range(groups):
        across = slice(h * size, (h + 1) * size)
        q = jnp.concatenate(
            [q_ref[across, g * head : (g + 1) * head] for g in range(heads)], axis=0
        )
        first = (2 * h + core) * size
        own_tile = first // tile
        seen = min(tokens, -(-(h + 1) * size // 128) * 128)
        parts, blocks = [], []
        for ref, mask_ref, width, parity, causal in (
            (far0, far_ref, tokens, core, False),
            (far1, far_ref, tokens, 1 - core, False),
            (near0, own_ref, seen, core, True),
            (near1, own_ref, seen, 1 - core, True),
        ):
            visible = jnp.zeros((1, width), jnp.int32)
            for g in range(-(-width // size)):
                at = mask_ref[own_tile, (2 * g + parity) * size // tile]
                visible = jnp.where(column_group[:, :width] == g, at, visible)
            visible = visible == 1
            if causal:
                group = column_group[:, :width]
                offset = (2 * group + parity) * size + column[:, :width] - group * size
                visible = visible & (offset <= first + within)
            scores = lax.dot_general(
                q, ref[:width, :head], nt, preferred_element_type=jnp.float32
            )
            parts.append(jnp.where(visible, scores, hidden))
            blocks.append((ref, width))
        scores = jnp.concatenate(parts, axis=1)
        largest = jnp.max(scores, axis=1, keepdims=True)
        weights = jnp.exp(scores - largest)
        total = jnp.sum(weights, axis=1, keepdims=True)
        rounded = weights.astype(jnp.bfloat16)
        mixed = jnp.zeros((rows, head), jnp.float32)
        start = 0
        for ref, width in blocks:
            mixed += jnp.dot(
                rounded[:, start : start + width],
                ref[:width, head:],
                preferred_element_type=jnp.float32,
            )
            start += width
        mixed = (mixed / total).astype(out_ref.dtype)
        for g in range(heads):
            out_ref[across, g * head : (g + 1) * head] = mixed[g * size : (g + 1) * size, :]


def attend(groups, own_mask, far_mask, queries, near, near_other, far, far_other):
    tokens, width = queries.shape
    return pl.pallas_call(
        functools.partial(attend_kernel, groups),
        out_shape=jax.ShapeDtypeStruct(queries.shape, jnp.bfloat16),
        in_specs=[SMEM, SMEM] + [VMEM] * 5,
        out_specs=VMEM,
        compiler_params=pltpu.CompilerParams(vmem_limit_bytes=VMEM_LIMIT),
        cost_estimate=pl.CostEstimate(
            flops=16 * tokens * tokens * width,
            bytes_accessed=8 * tokens * width,
            transcendentals=16 * tokens * tokens,
        ),
    )(own_mask, far_mask, queries, near, near_other, far, far_other)


def terms_kernel(layout, split, a_ref, *refs):
    keep_ref, send_ref, w_buf, sem = refs[-4:]
    half = keep_ref.shape[0]
    width = w_buf.shape[2]
    copies = []
    for at, (ref, (slot, share)) in enumerate(zip(refs[:-4], layout)):
        target = w_buf.at[slot]
        if share is not None:
            rows = ref.shape[0]
            target = w_buf.at[slot, pl.ds(pl.multiple_of(share_of(share) * rows, 16), rows)]
        copies.append(pltpu.make_async_copy(ref, target, sem.at[at]))
    for copy in copies:
        copy.start()
    pick = lax.axis_index("zero") // split % 2
    mine = a_ref[pl.ds(pl.multiple_of(pick * half, 16), half), :]
    other = a_ref[pl.ds(pl.multiple_of((1 - pick) * half, 16), half), :]
    both = jnp.concatenate([other, mine], axis=0)
    for copy in copies:
        copy.wait()
    for slot in range(w_buf.shape[0]):
        out = jnp.dot(both, w_buf[slot], preferred_element_type=jnp.float32)
        columns = slice(slot * width, (slot + 1) * width)
        send_ref[:, columns] = out[:half].astype(send_ref.dtype)
        keep_ref[:, columns] = out[half:]


def terms(split, attended, slots):
    layout = [(slot, share) for slot, pieces in enumerate(slots) for share, _ in pieces]
    shards = [piece for pieces in slots for _, piece in pieces]
    width = shards[0].shape[1]
    rows, depth = attended.shape
    columns = width * len(slots)
    return pl.pallas_call(
        functools.partial(terms_kernel, layout, split),
        out_shape=(
            jax.ShapeDtypeStruct((rows // 2, columns), jnp.float32),
            jax.ShapeDtypeStruct((rows // 2, columns), jnp.bfloat16),
        ),
        in_specs=[VMEM] + [HBM] * len(shards),
        out_specs=(VMEM, VMEM),
        scratch_shapes=[
            pltpu.VMEM((len(slots), depth, width), jnp.bfloat16),
            pltpu.SemaphoreType.DMA((len(shards),)),
        ],
        compiler_params=pltpu.CompilerParams(vmem_limit_bytes=VMEM_LIMIT),
        cost_estimate=pl.CostEstimate(
            flops=2 * rows * depth * columns,
            bytes_accessed=2 * (rows + columns) * depth + 3 * rows * columns,
            transcendentals=0,
        ),
    )(attended, *shards)


def join_kernel(groups, *refs):
    out_ref = refs[-1]
    count = len(groups)
    width = out_ref.shape[1] // sum(len(group) for group in groups)
    for group, keep_ref, got_ref in zip(groups, refs[:count], refs[count:-1]):
        for slot, steps in enumerate(group):
            columns = slice(slot * width, (slot + 1) * width)
            start = pl.multiple_of(source_of(steps) * width, 128)
            total = keep_ref[:, columns] + got_ref[:, columns].astype(jnp.float32)
            out_ref[:, pl.ds(start, width)] = total.astype(out_ref.dtype)


def join(groups, keeps, gots):
    rows = keeps[0].shape[0]
    columns = sum(keep.shape[1] for keep in keeps)
    return pl.pallas_call(
        functools.partial(join_kernel, groups),
        out_shape=jax.ShapeDtypeStruct((rows, columns), jnp.bfloat16),
        in_specs=[VMEM] * (2 * len(keeps)),
        out_specs=VMEM,
        compiler_params=pltpu.CompilerParams(vmem_limit_bytes=VMEM_LIMIT),
        cost_estimate=pl.CostEstimate(
            flops=rows * columns, bytes_accessed=8 * rows * columns, transcendentals=0
        ),
    )(*keeps, *gots)


def broadcast_from(value, root):
    me = lax.axis_index("ctx")
    for bit in range(int(math.log2(lax.axis_size("ctx")))):
        other = swap(value, "ctx", 1 << bit)
        same = ((me >> bit) & 1) == ((root >> bit) & 1)
        value = jnp.where(same, value, other)
    return value


def local(
    activations,
    norm_gain,
    query_weight,
    kv_weight,
    out_weight,
    tile_mask,
    anchor_mask,
    anchor_index,
):
    tokens, depth = activations.shape
    head = kv_weight.shape[2]
    ctx_size, zero_size = lax.axis_size("ctx"), lax.axis_size("zero")
    ctx_rank, zero_rank = lax.axis_index("ctx"), lax.axis_index("zero")
    core = zero_rank % 2
    groups = zero_size // 2
    size = tokens // zero_size

    by_core = activations.reshape(groups, 2, size, depth)
    mine = lax.dynamic_index_in_dim(by_core, core, 1, keepdims=False).reshape(-1, depth)
    theirs = lax.dynamic_index_in_dim(by_core, 1 - core, 1, keepdims=False).reshape(-1, depth)
    x_pieces = [mine] + [
        swap(theirs if m % 2 else mine, "zero", m) for m in range(1, zero_size)
    ]

    shard_rows = kv_weight.shape[0]
    gain = lax.dynamic_slice_in_dim(norm_gain, ctx_rank * shard_rows, shard_rows)
    gain = gain.astype(jnp.float32)[:, None]

    def of_chip(own, axis):
        other = swap(own, "zero", 1)
        return jnp.where(
            core == 0,
            jnp.concatenate([own, other], axis),
            jnp.concatenate([other, own], axis),
        )

    kv_pair = (of_chip(kv_weight[:, 0, :], 1).astype(jnp.float32) * gain).astype(jnp.bfloat16)
    query_pair = (of_chip(query_weight, 1).astype(jnp.float32) * gain).astype(jnp.bfloat16)
    out_pair = of_chip(out_weight, 0)
    kv_held = ring_gather(kv_pair, core)
    query_held = ring_gather(query_pair, core)
    out_held = ring_gather(out_pair, core)

    half = head // 2
    frequency = jnp.power(
        jnp.float32(ROPE_BASE), -(jnp.arange(half, dtype=jnp.float32) * 2.0 / head)
    )
    local_token = jnp.arange(tokens // 2, dtype=jnp.int32)
    offsets = (2 * (local_token // size) + core) * size + local_token % size
    positions = ctx_rank * tokens + offsets
    angles = positions.astype(jnp.float32)[:, None] * frequency[None, :]
    cos_half, sin_half = jnp.cos(angles), jnp.sin(angles)
    cos = jnp.concatenate([cos_half, cos_half], -1)
    sin = jnp.concatenate([-sin_half, sin_half], -1)
    shrink = head ** (-0.5)

    near, scale = project(cos, cos, sin, x_pieces, kv_held, True)
    anchor = anchor_index[0]
    far = broadcast_from(near, anchor)
    near_other = swap(near, "zero", 1)
    far_other = swap(far, "zero", 1)
    (queries,) = project(scale, cos * shrink, sin * shrink, x_pieces, query_held, False)
    far_mask = jnp.where(ctx_rank != anchor, anchor_mask[0], 0)
    attended = attend(groups, tile_mask[0], far_mask, queries, near, near_other, far, far_other)

    slots = []
    for steps, share, piece in out_held:
        if share == 1:
            slots[-1][1].append((share, piece))
        else:
            slots.append((steps, [(share, piece)]))
    per = max(1, ctx_size // CHUNKS)
    step_groups, keeps, gots = [], [], []
    top = zero_size // 2
    for at in range(0, ctx_size, per):
        step_groups.append([steps for steps, _ in slots[at : at + per]])
        keep, send = terms(top, attended, [pieces for _, pieces in slots[at : at + per]])
        got = swap(send, "zero", top)
        stride = top // 2
        while stride > 1:
            both = keep + got.astype(jnp.float32)
            rows = both.shape[0] // 2
            bit = (zero_rank // stride) % 2
            keep = lax.dynamic_slice_in_dim(both, bit * rows, rows, 0)
            send = lax.dynamic_slice_in_dim(both, (1 - bit) * rows, rows, 0)
            got = swap(send.astype(jnp.bfloat16), "zero", stride)
            stride //= 2
        keeps.append(keep)
        gots.append(got)
    return join(step_groups, keeps, gots)


def solution(mesh):
    placed = (
        P("ctx", "zero"),
        P(),
        P("ctx", "zero"),
        P("ctx", "zero", None),
        P("zero", "ctx"),
        P("ctx", None, None),
        P("ctx", None, None),
        P(),
    )
    return jax.shard_map(
        local, mesh=mesh, in_specs=placed, out_specs=P(("ctx", "zero"), None), check_vma=False
    )
```

```python
import functools
import math

import jax
import jax.numpy as jnp
from jax import lax
from jax.experimental import pallas as pl
from jax.experimental.pallas import tpu as pltpu
from jax.sharding import PartitionSpec as P

HBM = pl.BlockSpec(memory_space=pltpu.HBM)
VMEM = pl.BlockSpec(memory_space=pltpu.VMEM)
SMEM = pl.BlockSpec(memory_space=pltpu.SMEM)
VMEM_LIMIT = 48 * 1024 * 1024
ROPE_BASE = 500000.0
CHUNKS = 4


def swap(value, axis, stride):
    pairs = [(source, source ^ stride) for source in range(lax.axis_size(axis))]
    return lax.ppermute(value, axis, pairs)


def cycle(size):
    return list(range(0, size, 2)) + list(range(1, size, 2))[::-1]


def ring_step(value):
    ctx_size, zero_size = lax.axis_size("ctx"), lax.axis_size("zero")
    order = cycle(ctx_size)
    pairs = []
    for at in range(ctx_size):
        for zero in range(zero_size):
            to = order[(at + (1 if zero % 2 == 0 else -1)) % ctx_size]
            pairs.append((order[at] * zero_size + zero, to * zero_size + zero))
    return lax.ppermute(value, ("ctx", "zero"), pairs)


class Ring:
    def __init__(self, shard, core):
        self.held = [(0, None, shard)]
        self.moving, self.core, self.at = shard, core, 0
        self.length = lax.axis_size("ctx") // 2

    def step(self, *after):
        self.at += 1
        last = self.at == self.length
        if last:
            half = self.moving.shape[0] // 2
            self.moving = lax.dynamic_slice_in_dim(self.moving, self.core * half, half, 0)
        self.moving = ring_step(tied(self.moving, *after))
        self.held.append((-self.at, 0 if last else None, self.moving))
        self.held.append((self.at, 1 if last else None, swap(self.moving, "zero", 1)))
        return self.moving

    def advance(self, part, parts, *after):
        while self.at < self.length * (part + 1) // parts:
            self.step(*after)
        return self.moving


def tied(value, *others):
    return lax.optimization_barrier((value, *others))[0] if others else value


def source_of(steps):
    size = lax.axis_size("ctx")
    ctx, core = lax.axis_index("ctx"), lax.axis_index("zero") % 2
    place = jnp.where(ctx % 2 == 0, ctx // 2, size - 1 - ctx // 2)
    place = lax.rem(place + steps * (1 - 2 * core) + size, size)
    return jnp.where(place < size // 2, 2 * place, 2 * (size - 1 - place) + 1)


def share_of(share):
    core = lax.axis_index("zero") % 2
    return core if share == 0 else 1 - core


def token_rows(group, other, size):
    core = lax.axis_index("zero") % 2
    if other:
        core = 1 - core
    return pl.ds(pl.multiple_of((2 * group + core) * size, 16), size)


def deal_kernel(count, *refs):
    x_refs, outs, sem = refs[:count], refs[count:-1], refs[-1]
    groups = lax.axis_size("zero") // 2
    size = x_refs[0].shape[0] // (2 * groups)
    copies = []
    for x_ref, out_ref in zip(x_refs, outs):
        for group in range(groups):
            copies.append(
                pltpu.make_async_copy(
                    x_ref.at[token_rows(group, True, size)],
                    out_ref.at[pl.ds(group * size, size)],
                    sem.at[len(copies)],
                )
            )
    for copy in copies:
        copy.start()
    for copy in copies:
        copy.wait()


def deal(arrays):
    tokens, depth = arrays[0].shape
    part = jax.ShapeDtypeStruct((tokens // 2, depth), arrays[0].dtype)
    copies = len(arrays) * lax.axis_size("zero") // 2
    return pl.pallas_call(
        functools.partial(deal_kernel, len(arrays)),
        out_shape=[part] * len(arrays),
        in_specs=[HBM] * len(arrays),
        out_specs=[HBM] * len(arrays),
        scratch_shapes=[pltpu.SemaphoreType.DMA((copies,))],
        compiler_params=pltpu.CompilerParams(vmem_limit_bytes=VMEM_LIMIT),
    )(*arrays)


def project_kernel(layout, first_call, *refs):
    (x_buf, w_buf, x_sem, w_sem) = refs[-4:]
    pieces, tokens, depth = x_buf.shape
    scale_ref, cos_ref, sin_ref = refs[:3]
    x_refs = refs[3 : 3 + pieces]
    w_refs = refs[3 + pieces : 3 + pieces + len(layout)]
    out_ref = refs[3 + pieces + len(layout)]
    zero = lax.axis_index("zero")
    shard_rows = w_refs[0].shape[0]
    x_copies, w_copies = [], []
    for m, ref in enumerate(x_refs):
        target = x_buf.at[jnp.bitwise_xor(zero, m)]
        if m % 2:
            x_copies.append(pltpu.make_async_copy(ref, target, x_sem.at[len(x_copies)]))
            continue
        size = 2 * tokens // pieces
        for group in range(pieces // 2):
            x_copies.append(
                pltpu.make_async_copy(
                    ref.at[token_rows(group, False, size)],
                    target.at[pl.ds(group * size, size)],
                    x_sem.at[len(x_copies)],
                )
            )
    for at, (ref, (steps, share)) in enumerate(zip(w_refs, layout)):
        start = source_of(steps) * shard_rows
        if share is not None:
            start = start + share_of(share) * ref.shape[0]
        rows = pl.ds(pl.multiple_of(start, 16), ref.shape[0])
        w_copies.append(pltpu.make_async_copy(ref, w_buf.at[rows], w_sem.at[at]))
    for copy in x_copies + w_copies:
        copy.start()
    for copy in x_copies:
        copy.wait()
    if first_call:
        squares = jnp.zeros((x_buf.shape[1], 128), jnp.float32)
        for at in range(pieces):
            for first in range(0, depth, 128):
                x_float = x_buf[at, :, first : first + 128].astype(jnp.float32)
                squares += x_float * x_float
        mean = jnp.sum(squares, axis=1, keepdims=True) / (depth * pieces)
        scale = jnp.broadcast_to(lax.rsqrt(mean + 1e-05), squares.shape)
        scale_out = refs[4 + pieces + len(layout)]
        scale_out[...] = scale
    else:
        scale = scale_ref[...]
    for copy in w_copies:
        copy.wait()
    total = jnp.zeros(out_ref.shape, jnp.float32)
    for at in range(pieces):
        total += jnp.dot(
            x_buf[at], w_buf[at * depth : (at + 1) * depth, :], preferred_element_type=jnp.float32
        )
    head = cos_ref.shape[1]
    for first in range(0, out_ref.shape[1], head):
        part = total[:, first : first + head] * scale
        if not first_call or first == 0:
            part = part * cos_ref[...] + pltpu.roll(part, head // 2, 1) * sin_ref[...]
        out_ref[:, first : first + head] = part.astype(out_ref.dtype)


def project(scale, cos, sin, x_pieces, held, first_call):
    layout = [(steps, share) for steps, share, _ in held]
    shards = [piece for _, _, piece in held]
    tokens, depth = x_pieces[1].shape
    pieces = len(x_pieces)
    width = shards[0].shape[1]
    full = depth * pieces
    out = [jax.ShapeDtypeStruct((tokens, width), jnp.bfloat16)]
    if first_call:
        out.append(jax.ShapeDtypeStruct((tokens, 128), jnp.float32))
    return pl.pallas_call(
        functools.partial(project_kernel, layout, first_call),
        out_shape=out,
        in_specs=[VMEM] * 3 + [HBM] * (pieces + len(shards)),
        out_specs=[VMEM] * len(out),
        scratch_shapes=[
            pltpu.VMEM((pieces, tokens, depth), jnp.bfloat16),
            pltpu.VMEM((full, width), jnp.bfloat16),
            pltpu.SemaphoreType.DMA((pieces // 2 * (1 + pieces // 2),)),
            pltpu.SemaphoreType.DMA((len(shards),)),
        ],
        compiler_params=pltpu.CompilerParams(vmem_limit_bytes=VMEM_LIMIT),
        cost_estimate=pl.CostEstimate(
            flops=2 * tokens * full * width,
            bytes_accessed=2 * full * (tokens + width),
            transcendentals=0,
        ),
    )(scale, cos, sin, *x_pieces, *shards)


def attend_kernel(groups, own_ref, far_ref, q_ref, near0, near1, far0, far1, out_ref):
    tokens, pair = near0.shape
    head = pair // 2
    size = tokens // groups
    tiles = own_ref.shape[0]
    tile = 2 * tokens // tiles
    heads = q_ref.shape[1] // head
    rows = heads * size
    core = lax.axis_index("zero") % 2
    column = lax.broadcasted_iota(jnp.int32, (1, tokens), 1)
    column_group = column // size
    within = lax.rem(lax.broadcasted_iota(jnp.int32, (rows, 1), 0), size)
    hidden = jnp.float32(-1e30)
    nt = (((1,), (1,)), ((), ()))
    for h in range(groups):
        across = slice(h * size, (h + 1) * size)
        q = jnp.concatenate(
            [q_ref[across, g * head : (g + 1) * head] for g in range(heads)], axis=0
        )
        first = (2 * h + core) * size
        own_tile = first // tile
        seen = min(tokens, -(-(h + 1) * size // 128) * 128)
        parts, blocks = [], []
        for ref, mask_ref, width, parity, causal in (
            (far0, far_ref, tokens, core, False),
            (far1, far_ref, tokens, 1 - core, False),
            (near0, own_ref, seen, core, True),
            (near1, own_ref, seen, 1 - core, True),
        ):
            visible = jnp.zeros((1, width), jnp.int32)
            for g in range(-(-width // size)):
                at = mask_ref[own_tile, (2 * g + parity) * size // tile]
                visible = jnp.where(column_group[:, :width] == g, at, visible)
            visible = visible == 1
            if causal:
                group = column_group[:, :width]
                offset = (2 * group + parity) * size + column[:, :width] - group * size
                visible = visible & (offset <= first + within)
            scores = lax.dot_general(
                q, ref[:width, :head], nt, preferred_element_type=jnp.float32
            )
            parts.append(jnp.where(visible, scores, hidden))
            blocks.append((ref, width))
        scores = jnp.concatenate(parts, axis=1)
        largest = jnp.max(scores, axis=1, keepdims=True)
        weights = jnp.exp(scores - largest)
        total = jnp.sum(weights, axis=1, keepdims=True)
        rounded = weights.astype(jnp.bfloat16)
        mixed = jnp.zeros((rows, head), jnp.float32)
        start = 0
        for ref, width in blocks:
            mixed += jnp.dot(
                rounded[:, start : start + width],
                ref[:width, head:],
                preferred_element_type=jnp.float32,
            )
            start += width
        mixed = (mixed / total).astype(out_ref.dtype)
        for g in range(heads):
            out_ref[across, g * head : (g + 1) * head] = mixed[g * size : (g + 1) * size, :]


def attend(groups, own_mask, far_mask, queries, near, near_other, far, far_other):
    tokens, width = queries.shape
    return pl.pallas_call(
        functools.partial(attend_kernel, groups),
        out_shape=jax.ShapeDtypeStruct(queries.shape, jnp.bfloat16),
        in_specs=[SMEM, SMEM] + [VMEM] * 5,
        out_specs=VMEM,
        compiler_params=pltpu.CompilerParams(vmem_limit_bytes=VMEM_LIMIT),
        cost_estimate=pl.CostEstimate(
            flops=16 * tokens * tokens * width,
            bytes_accessed=8 * tokens * width,
            transcendentals=16 * tokens * tokens,
        ),
    )(own_mask, far_mask, queries, near, near_other, far, far_other)


def terms_kernel(layout, split, a_ref, *refs):
    keep_ref, send_ref, w_buf, sem = refs[-4:]
    half = keep_ref.shape[0]
    width = w_buf.shape[2]
    copies = []
    for at, (ref, (slot, share)) in enumerate(zip(refs[:-4], layout)):
        target = w_buf.at[slot]
        if share is not None:
            rows = ref.shape[0]
            target = w_buf.at[slot, pl.ds(pl.multiple_of(share_of(share) * rows, 16), rows)]
        copies.append(pltpu.make_async_copy(ref, target, sem.at[at]))
    for copy in copies:
        copy.start()
    pick = lax.axis_index("zero") // split % 2
    mine = a_ref[pl.ds(pl.multiple_of(pick * half, 16), half), :]
    other = a_ref[pl.ds(pl.multiple_of((1 - pick) * half, 16), half), :]
    both = jnp.concatenate([other, mine], axis=0)
    for copy in copies:
        copy.wait()
    for slot in range(w_buf.shape[0]):
        out = jnp.dot(both, w_buf[slot], preferred_element_type=jnp.float32)
        columns = slice(slot * width, (slot + 1) * width)
        send_ref[:, columns] = out[:half].astype(send_ref.dtype)
        keep_ref[:, columns] = out[half:]


def terms(split, attended, slots):
    layout = [(slot, share) for slot, pieces in enumerate(slots) for share, _ in pieces]
    shards = [piece for pieces in slots for _, piece in pieces]
    width = shards[0].shape[1]
    rows, depth = attended.shape
    columns = width * len(slots)
    return pl.pallas_call(
        functools.partial(terms_kernel, layout, split),
        out_shape=(
            jax.ShapeDtypeStruct((rows // 2, columns), jnp.float32),
            jax.ShapeDtypeStruct((rows // 2, columns), jnp.bfloat16),
        ),
        in_specs=[VMEM] + [HBM] * len(shards),
        out_specs=(VMEM, VMEM),
        scratch_shapes=[
            pltpu.VMEM((len(slots), depth, width), jnp.bfloat16),
            pltpu.SemaphoreType.DMA((len(shards),)),
        ],
        compiler_params=pltpu.CompilerParams(vmem_limit_bytes=VMEM_LIMIT),
        cost_estimate=pl.CostEstimate(
            flops=2 * rows * depth * columns,
            bytes_accessed=2 * (rows + columns) * depth + 3 * rows * columns,
            transcendentals=0,
        ),
    )(attended, *shards)


def join_kernel(groups, *refs):
    out_ref = refs[-1]
    count = len(groups)
    width = out_ref.shape[1] // sum(len(group) for group in groups)
    for group, keep_ref, got_ref in zip(groups, refs[:count], refs[count:-1]):
        for slot, steps in enumerate(group):
            columns = slice(slot * width, (slot + 1) * width)
            start = pl.multiple_of(source_of(steps) * width, 128)
            total = keep_ref[:, columns] + got_ref[:, columns].astype(jnp.float32)
            out_ref[:, pl.ds(start, width)] = total.astype(out_ref.dtype)


def join(groups, keeps, gots):
    rows = keeps[0].shape[0]
    columns = sum(keep.shape[1] for keep in keeps)
    return pl.pallas_call(
        functools.partial(join_kernel, groups),
        out_shape=jax.ShapeDtypeStruct((rows, columns), jnp.bfloat16),
        in_specs=[VMEM] * (2 * len(keeps)),
        out_specs=VMEM,
        compiler_params=pltpu.CompilerParams(vmem_limit_bytes=VMEM_LIMIT),
        cost_estimate=pl.CostEstimate(
            flops=rows * columns, bytes_accessed=8 * rows * columns, transcendentals=0
        ),
    )(*keeps, *gots)


def exchange_from(value, root, bit):
    other = swap(value, "ctx", 1 << bit)
    same = ((lax.axis_index("ctx") >> bit) & 1) == ((root >> bit) & 1)
    return jnp.where(same, value, other)


def local(
    activations,
    norm_gain,
    query_weight,
    kv_weight,
    out_weight,
    tile_mask,
    anchor_mask,
    anchor_index,
):
    tokens, depth = activations.shape
    head = kv_weight.shape[2]
    ctx_size, zero_size = lax.axis_size("ctx"), lax.axis_size("zero")
    ctx_rank, zero_rank = lax.axis_index("ctx"), lax.axis_index("zero")
    core = zero_rank % 2
    groups = zero_size // 2
    size = tokens // zero_size

    blocks = {0: activations}
    stride = groups
    while stride > 1:
        for known in range(0, zero_size, 2 * stride):
            blocks[known + stride] = swap(blocks[known], "zero", stride)
        stride //= 2

    shard_rows = kv_weight.shape[0]
    gain = lax.dynamic_slice_in_dim(norm_gain, ctx_rank * shard_rows, shard_rows)
    gain = gain.astype(jnp.float32)[:, None]

    def of_chip(own, axis):
        other = swap(own, "zero", 1)
        return jnp.where(
            core == 0,
            jnp.concatenate([own, other], axis),
            jnp.concatenate([other, own], axis),
        )

    kv_pair = (of_chip(kv_weight[:, 0, :], 1).astype(jnp.float32) * gain).astype(jnp.bfloat16)
    query_pair = (of_chip(query_weight, 1).astype(jnp.float32) * gain).astype(jnp.bfloat16)
    out_pair = of_chip(out_weight, 0)
    kv_ring = Ring(kv_pair, core)
    query_ring = Ring(query_pair, core)
    out_ring = Ring(out_pair, core)
    kv_ring.advance(0, 4)
    query_ring.advance(0, 4)
    kv_ring.advance(1, 4)
    third = kv_ring.advance(2, 4)
    second = query_ring.advance(1, 4, third)
    done = kv_ring.advance(3, 4)
    query_ring.advance(2, 4, done)
    query_ring.advance(3, 4)
    out_ring.advance(0, 4, query_ring.moving)

    for known in range(2, zero_size, 2):
        blocks[known] = tied(blocks[known], third)
    own = deal([blocks[0]]) + (deal([blocks[m] for m in range(2, zero_size, 2)]))
    x_pieces = []
    for m, theirs in zip(range(0, zero_size, 2), own):
        x_pieces += [blocks[m], swap(theirs, "zero", 1)]

    half = head // 2
    frequency = jnp.power(
        jnp.float32(ROPE_BASE), -(jnp.arange(half, dtype=jnp.float32) * 2.0 / head)
    )
    local_token = jnp.arange(tokens // 2, dtype=jnp.int32)
    offsets = (2 * (local_token // size) + core) * size + local_token % size
    positions = ctx_rank * tokens + offsets
    angles = positions.astype(jnp.float32)[:, None] * frequency[None, :]
    cos_half, sin_half = jnp.cos(angles), jnp.sin(angles)
    cos = jnp.concatenate([cos_half, cos_half], -1)
    sin = jnp.concatenate([-sin_half, sin_half], -1)
    shrink = head ** (-0.5)

    near, scale = project(cos, cos, sin, x_pieces, kv_ring.held, True)
    (queries,) = project(
        scale, cos * shrink, sin * shrink, x_pieces, query_ring.held, False
    )
    anchor = anchor_index[0]
    far = near
    bits = int(math.log2(ctx_size))
    for bit in range(bits):
        far = exchange_from(tied(far, queries) if bit == bits - 1 else far, anchor, bit)
        if bit == bits - 2:
            out_ring.advance(1, 4, far)
    near_other = swap(near, "zero", 1)
    far_other = swap(far, "zero", 1)
    out_ring.advance(2, 4, far)
    out_ring.advance(3, 4)
    far_mask = jnp.where(ctx_rank != anchor, anchor_mask[0], 0)
    attended = attend(groups, tile_mask[0], far_mask, queries, near, near_other, far, far_other)

    slots = []
    for steps, share, piece in out_ring.held:
        if share == 1:
            slots[-1][1].append((share, piece))
        else:
            slots.append((steps, [(share, piece)]))
    per = max(1, ctx_size // CHUNKS)
    cuts = [0] + list(range(per + 1, ctx_size, per)) + [ctx_size]
    step_groups, keeps, gots = [], [], []
    top = zero_size // 2
    for first, end in zip(cuts, cuts[1:]):
        step_groups.append([steps for steps, _ in slots[first:end]])
        keep, send = terms(top, attended, [pieces for _, pieces in slots[first:end]])
        got = swap(send, "zero", top)
        stride = top // 2
        while stride > 1:
            both = keep + got.astype(jnp.float32)
            rows = both.shape[0] // 2
            bit = (zero_rank // stride) % 2
            keep = lax.dynamic_slice_in_dim(both, bit * rows, rows, 0)
            send = lax.dynamic_slice_in_dim(both, (1 - bit) * rows, rows, 0)
            got = swap(send.astype(jnp.bfloat16), "zero", stride)
            stride //= 2
        keeps.append(keep)
        gots.append(got)
    return join(step_groups, keeps, gots)


def solution(mesh):
    placed = (
        P("ctx", "zero"),
        P(),
        P("ctx", "zero"),
        P("ctx", "zero", None),
        P("zero", "ctx"),
        P("ctx", None, None),
        P("ctx", None, None),
        P(),
    )
    return jax.shard_map(
        local, mesh=mesh, in_specs=placed, out_specs=P(("ctx", "zero"), None), check_vma=False
    )
```

```python
import functools
import math

import jax
import jax.numpy as jnp
from jax import lax
from jax.experimental import pallas as pl
from jax.experimental.pallas import tpu as pltpu
from jax.sharding import PartitionSpec as P

HBM = pl.BlockSpec(memory_space=pltpu.HBM)
VMEM = pl.BlockSpec(memory_space=pltpu.VMEM)
SMEM = pl.BlockSpec(memory_space=pltpu.SMEM)
VMEM_LIMIT = 48 * 1024 * 1024
ROPE_BASE = 500000.0


def swap(value, axis, stride):
    pairs = [(source, source ^ stride) for source in range(lax.axis_size(axis))]
    return lax.ppermute(value, axis, pairs)


def cycle(size):
    return list(range(0, size, 2)) + list(range(1, size, 2))[::-1]


def ring_step(value):
    ctx_size, zero_size = lax.axis_size("ctx"), lax.axis_size("zero")
    order = cycle(ctx_size)
    pairs = []
    for at in range(ctx_size):
        for zero in range(zero_size):
            to = order[(at + (1 if zero % 2 == 0 else -1)) % ctx_size]
            pairs.append((order[at] * zero_size + zero, to * zero_size + zero))
    return lax.ppermute(value, ("ctx", "zero"), pairs)


class Ring:
    def __init__(self, shard, core):
        self.held = [(0, None, shard)]
        self.moving, self.core, self.at = shard, core, 0
        self.length = lax.axis_size("ctx") // 2

    def step(self, *after):
        self.at += 1
        last = self.at == self.length
        if last:
            half = self.moving.shape[0] // 2
            self.moving = lax.dynamic_slice_in_dim(self.moving, self.core * half, half, 0)
        self.moving = ring_step(tied(self.moving, *after))
        self.held.append((-self.at, 0 if last else None, self.moving))
        self.held.append((self.at, 1 if last else None, swap(self.moving, "zero", 1)))
        return self.moving

    def advance(self, part, parts, *after):
        while self.at < self.length * (part + 1) // parts:
            self.step(*after)
        return self.moving


def tied(value, *others):
    return lax.optimization_barrier((value, *others))[0] if others else value


def source_of(steps):
    size = lax.axis_size("ctx")
    ctx, core = lax.axis_index("ctx"), lax.axis_index("zero") % 2
    place = jnp.where(ctx % 2 == 0, ctx // 2, size - 1 - ctx // 2)
    place = lax.rem(place + steps * (1 - 2 * core) + size, size)
    return jnp.where(place < size // 2, 2 * place, 2 * (size - 1 - place) + 1)


def share_of(share):
    core = lax.axis_index("zero") % 2
    return core if share == 0 else 1 - core


def token_rows(group, other, size):
    core = lax.axis_index("zero") % 2
    if other:
        core = 1 - core
    return pl.ds(pl.multiple_of((2 * group + core) * size, 16), size)


def deal_kernel(count, *refs):
    x_refs, outs, sem = refs[:count], refs[count:-1], refs[-1]
    groups = lax.axis_size("zero") // 4
    size = x_refs[0].shape[0] // (2 * groups)
    copies = []
    for x_ref, out_ref in zip(x_refs, outs):
        for group in range(groups):
            copies.append(
                pltpu.make_async_copy(
                    x_ref.at[token_rows(group, True, size)],
                    out_ref.at[pl.ds(group * size, size)],
                    sem.at[len(copies)],
                )
            )
    for copy in copies:
        copy.start()
    for copy in copies:
        copy.wait()


def deal(arrays):
    tokens, depth = arrays[0].shape
    part = jax.ShapeDtypeStruct((tokens // 2, depth), arrays[0].dtype)
    copies = len(arrays) * lax.axis_size("zero") // 4
    return pl.pallas_call(
        functools.partial(deal_kernel, len(arrays)),
        out_shape=[part] * len(arrays),
        in_specs=[HBM] * len(arrays),
        out_specs=[HBM] * len(arrays),
        scratch_shapes=[pltpu.SemaphoreType.DMA((copies,))],
        compiler_params=pltpu.CompilerParams(vmem_limit_bytes=VMEM_LIMIT),
    )(*arrays)


def project_kernel(layout, columns, first_call, *refs):
    (x_buf, w_buf, x_sem, w_sem) = refs[-4:]
    pieces, tokens, depth = x_buf.shape
    scale_ref, cos_ref, sin_ref = refs[:3]
    x_refs = refs[3 : 3 + 2 * pieces]
    w_refs = refs[3 + 2 * pieces : 3 + 2 * pieces + len(layout)]
    outs = refs[3 + 2 * pieces + len(layout) : -4]
    out_ref = outs[0]
    zero = lax.axis_index("zero")
    shard_rows = w_refs[0].shape[0]
    x_copies, w_copies = [], []
    for at, ref in enumerate(x_refs):
        m, part = divmod(at, 2)
        target = x_buf.at[jnp.bitwise_xor(zero, m), pl.ds(part * tokens // 2, tokens // 2)]
        if m % 2:
            x_copies.append(pltpu.make_async_copy(ref, target, x_sem.at[len(x_copies)]))
            continue
        size = 2 * tokens // pieces
        for group in range(pieces // 4):
            x_copies.append(
                pltpu.make_async_copy(
                    ref.at[token_rows(group, False, size)],
                    target.at[pl.ds(group * size, size)],
                    x_sem.at[len(x_copies)],
                )
            )
    for at, (ref, (steps, share)) in enumerate(zip(w_refs, layout)):
        start = source_of(steps) * shard_rows
        if share is not None:
            start = start + share_of(share) * ref.shape[0]
        rows = pl.ds(pl.multiple_of(start, 16), ref.shape[0])
        source = ref.at[:, pl.ds(columns, w_buf.shape[1])]
        w_copies.append(pltpu.make_async_copy(source, w_buf.at[rows], w_sem.at[at]))
    for copy in x_copies + w_copies:
        copy.start()
    for copy in x_copies:
        copy.wait()
    if first_call:
        squares = jnp.zeros((x_buf.shape[1], 128), jnp.float32)
        for at in range(pieces):
            for first in range(0, depth, 128):
                x_float = x_buf[at, :, first : first + 128].astype(jnp.float32)
                squares += x_float * x_float
        mean = jnp.sum(squares, axis=1, keepdims=True) / (depth * pieces)
        scale = jnp.broadcast_to(lax.rsqrt(mean + 1e-05), squares.shape)
        outs[1][...] = scale
    else:
        scale = scale_ref[...]
    for copy in w_copies:
        copy.wait()
    total = jnp.zeros(out_ref.shape, jnp.float32)
    for at in range(pieces):
        total += jnp.dot(
            x_buf[at], w_buf[at * depth : (at + 1) * depth, :], preferred_element_type=jnp.float32
        )
    head = cos_ref.shape[1]
    for first in range(0, out_ref.shape[1], head):
        part = total[:, first : first + head] * scale
        if not first_call or first == 0:
            part = part * cos_ref[...] + pltpu.roll(part, head // 2, 1) * sin_ref[...]
        out_ref[:, first : first + head] = part.astype(out_ref.dtype)


def project(scale, cos, sin, x_parts, held, columns, width, first_call):
    layout = [(steps, share) for steps, share, _ in held]
    shards = [piece for _, _, piece in held]
    tokens, depth = 2 * x_parts[2].shape[0], x_parts[2].shape[1]
    pieces = len(x_parts) // 2
    full = depth * pieces
    out = [jax.ShapeDtypeStruct((tokens, width), jnp.bfloat16)]
    if first_call:
        out.append(jax.ShapeDtypeStruct((tokens, 128), jnp.float32))
    return pl.pallas_call(
        functools.partial(project_kernel, layout, columns, first_call),
        out_shape=out,
        in_specs=[VMEM] * 3 + [HBM] * (2 * pieces + len(shards)),
        out_specs=[VMEM] * len(out),
        scratch_shapes=[
            pltpu.VMEM((pieces, tokens, depth), jnp.bfloat16),
            pltpu.VMEM((full, width), jnp.bfloat16),
            pltpu.SemaphoreType.DMA((pieces + pieces * pieces // 4,)),
            pltpu.SemaphoreType.DMA((len(shards),)),
        ],
        compiler_params=pltpu.CompilerParams(vmem_limit_bytes=VMEM_LIMIT),
        cost_estimate=pl.CostEstimate(
            flops=2 * tokens * full * width,
            bytes_accessed=2 * full * (tokens + width),
            transcendentals=0,
        ),
    )(scale, cos, sin, *x_parts, *shards)


def attend_kernel(groups, own_ref, far_ref, q_ref, near0, near1, far0, far1, keep, send):
    tokens, pair = near0.shape
    head = pair // 2
    size = tokens // groups
    tiles = own_ref.shape[0]
    tile = 2 * tokens // tiles
    heads = q_ref.shape[1] // head
    rows = heads * size
    core = lax.axis_index("zero") % 2
    column = lax.broadcasted_iota(jnp.int32, (1, tokens), 1)
    column_group = column // size
    within = lax.rem(lax.broadcasted_iota(jnp.int32, (rows, 1), 0), size)
    hidden = jnp.float32(-1e30)
    nt = (((1,), (1,)), ((), ()))
    for h in range(groups):
        across = slice(h * size, (h + 1) * size)
        q = jnp.concatenate(
            [q_ref[across, g * head : (g + 1) * head] for g in range(heads)], axis=0
        )
        first = (2 * h + core) * size
        own_tile = first // tile
        seen = min(tokens, -(-(h + 1) * size // 128) * 128)
        parts, blocks = [], []
        for ref, mask_ref, width, parity, causal in (
            (far0, far_ref, tokens, core, False),
            (far1, far_ref, tokens, 1 - core, False),
            (near0, own_ref, seen, core, True),
            (near1, own_ref, seen, 1 - core, True),
        ):
            visible = jnp.zeros((1, width), jnp.int32)
            for g in range(-(-width // size)):
                at = mask_ref[own_tile, (2 * g + parity) * size // tile]
                visible = jnp.where(column_group[:, :width] == g, at, visible)
            visible = visible == 1
            if causal:
                group = column_group[:, :width]
                offset = (2 * group + parity) * size + column[:, :width] - group * size
                visible = visible & (offset <= first + within)
            scores = lax.dot_general(
                q, ref[:width, :head], nt, preferred_element_type=jnp.float32
            )
            parts.append(jnp.where(visible, scores, hidden))
            blocks.append((ref, width))
        scores = jnp.concatenate(parts, axis=1)
        largest = jnp.max(scores, axis=1, keepdims=True)
        weights = jnp.exp(scores - largest)
        total = jnp.sum(weights, axis=1, keepdims=True)
        rounded = weights.astype(jnp.bfloat16)
        mixed = jnp.zeros((rows, head), jnp.float32)
        start = 0
        for ref, width in blocks:
            mixed += jnp.dot(
                rounded[:, start : start + width],
                ref[:width, head:],
                preferred_element_type=jnp.float32,
            )
            start += width
        mixed = (mixed / total).astype(keep.dtype)
        stays = lax.axis_index("zero") // 2 % 2 == h % 2
        rows_out = slice(h // 2 * size, (h // 2 + 1) * size)

        def store(out_ref, rows_out=rows_out, mixed=mixed):
            for g in range(heads):
                out_ref[rows_out, g * head : (g + 1) * head] = mixed[g * size : (g + 1) * size, :]

        pl.when(stays)(functools.partial(store, keep))
        pl.when(jnp.logical_not(stays))(functools.partial(store, send))


def attend(groups, own_mask, far_mask, queries, near, near_other, far, far_other):
    tokens, width = queries.shape
    return pl.pallas_call(
        functools.partial(attend_kernel, groups),
        out_shape=[jax.ShapeDtypeStruct((tokens // 2, width), jnp.bfloat16)] * 2,
        in_specs=[SMEM, SMEM] + [VMEM] * 5,
        out_specs=[VMEM] * 2,
        compiler_params=pltpu.CompilerParams(vmem_limit_bytes=VMEM_LIMIT),
        cost_estimate=pl.CostEstimate(
            flops=16 * tokens * tokens * width,
            bytes_accessed=8 * tokens * width,
            transcendentals=16 * tokens * tokens,
        ),
    )(own_mask, far_mask, queries, near, near_other, far, far_other)


def mix_kernel(layout, steps, *refs):
    a_refs, w_refs = refs[:2], refs[2 : 2 + len(layout)]
    out_ref, w_buf, sem = refs[2 + len(layout) :]
    width = w_buf.shape[2]
    half = a_refs[0].shape[1]
    copies = []
    for at, (ref, (slot, side, share)) in enumerate(zip(w_refs, layout)):
        rows = ref.shape[0]
        start = side * half
        if share is not None:
            start = pl.multiple_of(start + share_of(share) * rows, 16)
        copies.append(pltpu.make_async_copy(ref, w_buf.at[slot, pl.ds(start, rows)], sem.at[at]))
    for copy in copies:
        copy.start()
    both = jnp.concatenate([a_refs[0][...], a_refs[1][...]], axis=1)
    for slot, along in enumerate(steps):
        for copy, (its_slot, _, _) in zip(copies, layout):
            if its_slot == slot:
                copy.wait()
        total = jnp.dot(both, w_buf[slot], preferred_element_type=jnp.float32)
        start = pl.multiple_of(source_of(along) * width, 128)
        out_ref[:, pl.ds(start, width)] = total.astype(out_ref.dtype)


def mix(keep, got, slots, dtype):
    layout, shards = [], []
    for slot, (_, pieces) in enumerate(slots):
        for side, share, piece in pieces:
            layout.append((slot, side, share))
            shards.append(piece)
    rows, half = keep.shape
    width = shards[0].shape[1]
    columns = width * len(slots)
    return pl.pallas_call(
        functools.partial(mix_kernel, layout, [steps for steps, _ in slots]),
        out_shape=jax.ShapeDtypeStruct((rows, columns), dtype),
        in_specs=[VMEM, VMEM] + [HBM] * len(shards),
        out_specs=VMEM,
        scratch_shapes=[
            pltpu.VMEM((len(slots), 2 * half, width), jnp.bfloat16),
            pltpu.SemaphoreType.DMA((len(shards),)),
        ],
        compiler_params=pltpu.CompilerParams(vmem_limit_bytes=VMEM_LIMIT),
        cost_estimate=pl.CostEstimate(
            flops=4 * rows * half * columns,
            bytes_accessed=4 * half * (rows + columns) + 4 * rows * columns,
            transcendentals=0,
        ),
    )(keep, got, *shards)


def exchange_from(value, root, bit):
    other = swap(value, "ctx", 1 << bit)
    same = ((lax.axis_index("ctx") >> bit) & 1) == ((root >> bit) & 1)
    return jnp.where(same, value, other)


def local(
    activations,
    norm_gain,
    query_weight,
    kv_weight,
    out_weight,
    tile_mask,
    anchor_mask,
    anchor_index,
):
    tokens, depth = activations.shape
    head = kv_weight.shape[2]
    ctx_size, zero_size = lax.axis_size("ctx"), lax.axis_size("zero")
    ctx_rank, zero_rank = lax.axis_index("ctx"), lax.axis_index("zero")
    core = zero_rank % 2
    groups = zero_size // 2
    size = tokens // zero_size

    halves = [{0: activations[: tokens // 2]}, {0: activations[tokens // 2 :]}]
    for blocks in halves:
        stride = groups
        while stride > 1:
            for known in range(0, zero_size, 2 * stride):
                blocks[known + stride] = swap(blocks[known], "zero", stride)
            stride //= 2
    far_halves = [[blocks[m] for m in range(2, zero_size, 2)] for blocks in halves]

    shard_rows = kv_weight.shape[0]
    gain = lax.dynamic_slice_in_dim(norm_gain, ctx_rank * shard_rows, shard_rows)
    gain = gain.astype(jnp.float32)[:, None]
    kv_own = kv_weight[:, 0, :]
    kv_other, query_other = swap(kv_own, "zero", 1), swap(query_weight, "zero", 1)
    pair = jnp.where(
        core == 0,
        jnp.concatenate([kv_own, kv_other, query_weight, query_other], 1),
        jnp.concatenate([kv_other, kv_own, query_other, query_weight], 1),
    )
    pair = (pair.astype(jnp.float32) * gain).astype(jnp.bfloat16)
    out_other = swap(out_weight, "zero", 1)
    out_pair = jnp.where(
        core == 0,
        jnp.concatenate([out_weight, out_other], 0),
        jnp.concatenate([out_other, out_weight], 0),
    )
    ring = Ring(pair, core)
    out_ring = Ring(out_pair, core)
    ring.advance(0, 4)
    ring.advance(1, 4, *far_halves[0])
    out_ring.advance(0, 4)
    ring.advance(2, 4, *far_halves[1], out_ring.moving)
    out_ring.advance(1, 4)
    ring.advance(3, 4)
    out_ring.advance(2, 4, ring.moving)

    x_parts = []
    dealt = [deal([half[0]]) + deal(far) for half, far in zip(halves, far_halves)]
    for at in range(zero_size // 2):
        x_parts += [halves[0][2 * at], halves[1][2 * at]]
        x_parts += [swap(dealt[0][at], "zero", 1), swap(dealt[1][at], "zero", 1)]

    half = head // 2
    frequency = jnp.power(
        jnp.float32(ROPE_BASE), -(jnp.arange(half, dtype=jnp.float32) * 2.0 / head)
    )
    local_token = jnp.arange(tokens // 2, dtype=jnp.int32)
    offsets = (2 * (local_token // size) + core) * size + local_token % size
    positions = ctx_rank * tokens + offsets
    angles = positions.astype(jnp.float32)[:, None] * frequency[None, :]
    cos_half, sin_half = jnp.cos(angles), jnp.sin(angles)
    cos = jnp.concatenate([cos_half, cos_half], -1)
    sin = jnp.concatenate([-sin_half, sin_half], -1)
    shrink = head ** (-0.5)

    near, scale = project(cos, cos, sin, x_parts, ring.held, 0, 2 * head, True)
    (queries,) = project(
        scale, cos * shrink, sin * shrink, x_parts, ring.held, 2 * head, 4 * head, False
    )
    anchor = anchor_index[0]
    far = near
    bits = int(math.log2(ctx_size))
    for bit in range(bits):
        far = exchange_from(tied(far, queries) if bit == bits - 1 else far, anchor, bit)
        if bit == 0:
            out_ring.advance(3, 4, far)
    near_other = swap(near, "zero", 1)
    far_other = swap(far, "zero", 1)
    far_mask = jnp.where(ctx_rank != anchor, anchor_mask[0], 0)
    keep, send = attend(
        groups, tile_mask[0], far_mask, queries, near, near_other, far, far_other
    )

    slots = []
    for steps, share, piece in out_ring.held:
        if share != 1:
            slots.append((steps, []))
        if steps <= 0:
            beyond = swap(out_weight if steps == 0 else piece, "zero", 2)
            across = swap(beyond, "zero", 1)
        if steps == 0:
            pieces = [(0, None, piece), (1, 0, beyond), (1, 1, across)]
        else:
            pieces = [(0, share, piece), (1, share, beyond if steps < 0 else across)]
        slots[-1][1].extend(pieces)
    got = swap(send, "zero", 2)
    if zero_size == 4:
        return mix(keep, got, slots, jnp.bfloat16)
    total = mix(keep, got, slots, jnp.float32)
    stride = zero_size // 2
    while stride > 2:
        rows = total.shape[0] // 2
        bit = (zero_rank // stride) % 2
        stay = lax.dynamic_slice_in_dim(total, bit * rows, rows, 0)
        go = lax.dynamic_slice_in_dim(total, (1 - bit) * rows, rows, 0)
        total = stay + swap(go.astype(jnp.bfloat16), "zero", stride).astype(jnp.float32)
        stride //= 2
    return total.astype(jnp.bfloat16)


def solution(mesh):
    placed = (
        P("ctx", "zero"),
        P(),
        P("ctx", "zero"),
        P("ctx", "zero", None),
        P("zero", "ctx"),
        P("ctx", None, None),
        P("ctx", None, None),
        P(),
    )
    return jax.shard_map(
        local, mesh=mesh, in_specs=placed, out_specs=P(("ctx", "zero"), None), check_vma=False
    )
```

```python
import functools
import math

import jax
import jax.numpy as jnp
from jax import lax
from jax.experimental import pallas as pl
from jax.experimental.pallas import tpu as pltpu
from jax.sharding import PartitionSpec as P

HBM = pl.BlockSpec(memory_space=pltpu.HBM)
VMEM = pl.BlockSpec(memory_space=pltpu.VMEM)
SMEM = pl.BlockSpec(memory_space=pltpu.SMEM)
VMEM_LIMIT = 48 * 1024 * 1024
ROPE_BASE = 500000.0
CHUNKS = 4


def swap(value, axis, stride):
    pairs = [(source, source ^ stride) for source in range(lax.axis_size(axis))]
    return lax.ppermute(value, axis, pairs)


def cycle(size):
    return list(range(0, size, 2)) + list(range(1, size, 2))[::-1]


def ring_step(value):
    ctx_size, zero_size = lax.axis_size("ctx"), lax.axis_size("zero")
    order = cycle(ctx_size)
    pairs = []
    for at in range(ctx_size):
        for zero in range(zero_size):
            to = order[(at + (1 if zero % 2 == 0 else -1)) % ctx_size]
            pairs.append((order[at] * zero_size + zero, to * zero_size + zero))
    return lax.ppermute(value, ("ctx", "zero"), pairs)


class Ring:
    def __init__(self, shard, core):
        self.held = [(0, None, shard)]
        self.moving, self.core, self.at = shard, core, 0
        self.length = lax.axis_size("ctx") // 2

    def step(self, *after):
        self.at += 1
        last = self.at == self.length
        if last:
            half = self.moving.shape[0] // 2
            self.moving = lax.dynamic_slice_in_dim(self.moving, self.core * half, half, 0)
        self.moving = ring_step(tied(self.moving, *after))
        self.held.append((-self.at, 0 if last else None, self.moving))
        self.held.append((self.at, 1 if last else None, swap(self.moving, "zero", 1)))
        return self.moving

    def advance(self, part, parts, *after):
        while self.at < self.length * (part + 1) // parts:
            self.step(*after)
        return self.moving


def tied(value, *others):
    return lax.optimization_barrier((value, *others))[0] if others else value


def source_of(steps):
    size = lax.axis_size("ctx")
    ctx, core = lax.axis_index("ctx"), lax.axis_index("zero") % 2
    place = jnp.where(ctx % 2 == 0, ctx // 2, size - 1 - ctx // 2)
    place = lax.rem(place + steps * (1 - 2 * core) + size, size)
    return jnp.where(place < size // 2, 2 * place, 2 * (size - 1 - place) + 1)


def share_of(share):
    core = lax.axis_index("zero") % 2
    return core if share == 0 else 1 - core


def token_rows(group, other, size):
    core = lax.axis_index("zero") % 2
    if other:
        core = 1 - core
    return pl.ds(pl.multiple_of((2 * group + core) * size, 16), size)


def deal_kernel(x_ref, mine_ref, theirs_ref, sem):
    groups = lax.axis_size("zero") // 2
    size = x_ref.shape[0] // (2 * groups)
    copies = []
    for other, out_ref in ((True, theirs_ref), (False, mine_ref)):
        for group in range(groups):
            copies.append(
                pltpu.make_async_copy(
                    x_ref.at[token_rows(group, other, size)],
                    out_ref.at[pl.ds(group * size, size)],
                    sem.at[len(copies)],
                )
            )
    for copy in copies:
        copy.start()
    for copy in copies:
        copy.wait()


def deal(x):
    tokens, depth = x.shape
    part = jax.ShapeDtypeStruct((tokens // 2, depth), x.dtype)
    return pl.pallas_call(
        deal_kernel,
        out_shape=[part] * 2,
        in_specs=[HBM],
        out_specs=[HBM] * 2,
        scratch_shapes=[pltpu.SemaphoreType.DMA((lax.axis_size("zero"),))],
        compiler_params=pltpu.CompilerParams(vmem_limit_bytes=VMEM_LIMIT),
    )(x)


def project_kernel(layout, first_call, *refs):
    (x_buf, w_buf, x_sem, w_sem) = refs[-4:]
    pieces, tokens, depth = x_buf.shape
    scale_ref, cos_ref, sin_ref = refs[:3]
    x_refs = refs[3 : 3 + pieces]
    w_refs = refs[3 + pieces : 3 + pieces + len(layout)]
    outs = refs[3 + pieces + len(layout) : -4]
    out_ref = outs[0]
    zero = lax.axis_index("zero")
    shard_rows = w_refs[0].shape[0]
    x_copies, w_copies = [], []
    for m, ref in enumerate(x_refs):
        place = jnp.bitwise_xor(zero, m)
        x_copies.append(pltpu.make_async_copy(ref, x_buf.at[place], x_sem.at[m]))
    for at, (ref, (steps, share)) in enumerate(zip(w_refs, layout)):
        start = source_of(steps) * shard_rows
        if share is not None:
            start = start + share_of(share) * ref.shape[0]
        rows = pl.ds(pl.multiple_of(start, 16), ref.shape[0])
        w_copies.append(pltpu.make_async_copy(ref, w_buf.at[rows], w_sem.at[at]))
    for copy in x_copies + w_copies:
        copy.start()
    for copy in x_copies:
        copy.wait()
    if first_call:
        squares = jnp.zeros((x_buf.shape[1], 128), jnp.float32)
        for at in range(pieces):
            for first in range(0, depth, 128):
                x_float = x_buf[at, :, first : first + 128].astype(jnp.float32)
                squares += x_float * x_float
        mean = jnp.sum(squares, axis=1, keepdims=True) / (depth * pieces)
        scale = jnp.broadcast_to(lax.rsqrt(mean + 1e-05), squares.shape)
        outs[1][...] = scale
    else:
        scale = scale_ref[...]
    for copy in w_copies:
        copy.wait()
    total = jnp.zeros(out_ref.shape, jnp.float32)
    for at in range(pieces):
        total += jnp.dot(
            x_buf[at], w_buf[at * depth : (at + 1) * depth, :], preferred_element_type=jnp.float32
        )
    head = cos_ref.shape[1]
    for first in range(0, out_ref.shape[1], head):
        part = total[:, first : first + head] * scale
        if not first_call or first == 0:
            part = part * cos_ref[...] + pltpu.roll(part, head // 2, 1) * sin_ref[...]
        out_ref[:, first : first + head] = part.astype(out_ref.dtype)


def project(scale, cos, sin, x_pieces, held, first_call):
    layout = [(steps, share) for steps, share, _ in held]
    shards = [piece for _, _, piece in held]
    tokens, depth = x_pieces[0].shape
    pieces = len(x_pieces)
    width = shards[0].shape[1]
    full = depth * pieces
    out = [jax.ShapeDtypeStruct((tokens, width), jnp.bfloat16)]
    if first_call:
        out.append(jax.ShapeDtypeStruct((tokens, 128), jnp.float32))
    return pl.pallas_call(
        functools.partial(project_kernel, layout, first_call),
        out_shape=out,
        in_specs=[VMEM] * 3 + [HBM] * (pieces + len(shards)),
        out_specs=[VMEM] * len(out),
        scratch_shapes=[
            pltpu.VMEM((pieces, tokens, depth), jnp.bfloat16),
            pltpu.VMEM((full, width), jnp.bfloat16),
            pltpu.SemaphoreType.DMA((pieces,)),
            pltpu.SemaphoreType.DMA((len(shards),)),
        ],
        compiler_params=pltpu.CompilerParams(vmem_limit_bytes=VMEM_LIMIT),
        cost_estimate=pl.CostEstimate(
            flops=2 * tokens * full * width,
            bytes_accessed=2 * full * (tokens + width),
            transcendentals=0,
        ),
    )(scale, cos, sin, *x_pieces, *shards)


def attend_kernel(groups, own_ref, far_ref, q_ref, near0, near1, far0, far1, out_ref):
    tokens, pair = near0.shape
    head = pair // 2
    size = tokens // groups
    tiles = own_ref.shape[0]
    tile = 2 * tokens // tiles
    heads = q_ref.shape[1] // head
    rows = heads * size
    core = lax.axis_index("zero") % 2
    column = lax.broadcasted_iota(jnp.int32, (1, tokens), 1)
    column_group = column // size
    within = lax.rem(lax.broadcasted_iota(jnp.int32, (rows, 1), 0), size)
    hidden = jnp.float32(-1e30)
    nt = (((1,), (1,)), ((), ()))
    for h in range(groups):
        across = slice(h * size, (h + 1) * size)
        q = jnp.concatenate(
            [q_ref[across, g * head : (g + 1) * head] for g in range(heads)], axis=0
        )
        first = (2 * h + core) * size
        own_tile = first // tile
        seen = min(tokens, -(-(h + 1) * size // 128) * 128)
        parts, blocks = [], []
        for ref, mask_ref, width, parity, causal in (
            (far0, far_ref, tokens, core, False),
            (far1, far_ref, tokens, 1 - core, False),
            (near0, own_ref, seen, core, True),
            (near1, own_ref, seen, 1 - core, True),
        ):
            visible = jnp.zeros((1, width), jnp.int32)
            for g in range(-(-width // size)):
                at = mask_ref[own_tile, (2 * g + parity) * size // tile]
                visible = jnp.where(column_group[:, :width] == g, at, visible)
            visible = visible == 1
            if causal:
                group = column_group[:, :width]
                offset = (2 * group + parity) * size + column[:, :width] - group * size
                visible = visible & (offset <= first + within)
            scores = lax.dot_general(
                q, ref[:width, :head], nt, preferred_element_type=jnp.float32
            )
            parts.append(jnp.where(visible, scores, hidden))
            blocks.append((ref, width))
        scores = jnp.concatenate(parts, axis=1)
        largest = jnp.max(scores, axis=1, keepdims=True)
        weights = jnp.exp(scores - largest)
        total = jnp.sum(weights, axis=1, keepdims=True)
        rounded = weights.astype(jnp.bfloat16)
        mixed = jnp.zeros((rows, head), jnp.float32)
        start = 0
        for ref, width in blocks:
            mixed += jnp.dot(
                rounded[:, start : start + width],
                ref[:width, head:],
                preferred_element_type=jnp.float32,
            )
            start += width
        mixed = (mixed / total).astype(out_ref.dtype)
        for g in range(heads):
            out_ref[across, g * head : (g + 1) * head] = mixed[g * size : (g + 1) * size, :]


def attend(groups, own_mask, far_mask, queries, near, near_other, far, far_other):
    tokens, width = queries.shape
    return pl.pallas_call(
        functools.partial(attend_kernel, groups),
        out_shape=jax.ShapeDtypeStruct(queries.shape, jnp.bfloat16),
        in_specs=[SMEM, SMEM] + [VMEM] * 5,
        out_specs=VMEM,
        compiler_params=pltpu.CompilerParams(vmem_limit_bytes=VMEM_LIMIT),
        cost_estimate=pl.CostEstimate(
            flops=16 * tokens * tokens * width,
            bytes_accessed=8 * tokens * width,
            transcendentals=16 * tokens * tokens,
        ),
    )(own_mask, far_mask, queries, near, near_other, far, far_other)


def terms_kernel(split, first, a_ref, w0_ref, w1_ref, keep_ref, send_ref, w_buf, sem):
    half, width = keep_ref.shape
    depth = w0_ref.shape[0]
    core = lax.axis_index("zero") % 2
    copies = []
    for at, (ref, side) in enumerate(((w0_ref, core), (w1_ref, 1 - core))):
        copies.append(
            pltpu.make_async_copy(ref.at[:, pl.ds(first, width)], w_buf.at[side], sem.at[at])
        )
    for copy in copies:
        copy.start()
    pick = lax.axis_index("zero") // split % 2
    mine = a_ref[pl.ds(pl.multiple_of(pick * half, 16), half), :]
    other = a_ref[pl.ds(pl.multiple_of((1 - pick) * half, 16), half), :]
    both = jnp.concatenate([other, mine], axis=0)
    for copy in copies:
        copy.wait()
    total = jnp.dot(both[:, :depth], w_buf[0], preferred_element_type=jnp.float32)
    total += jnp.dot(both[:, depth:], w_buf[1], preferred_element_type=jnp.float32)
    send_ref[...] = total[:half].astype(send_ref.dtype)
    keep_ref[...] = total[half:]


def terms(split, attended, own, partner, first, width):
    rows, depth = attended.shape
    return pl.pallas_call(
        functools.partial(terms_kernel, split, first),
        out_shape=(
            jax.ShapeDtypeStruct((rows // 2, width), jnp.float32),
            jax.ShapeDtypeStruct((rows // 2, width), jnp.bfloat16),
        ),
        in_specs=[VMEM, HBM, HBM],
        out_specs=(VMEM, VMEM),
        scratch_shapes=[
            pltpu.VMEM((2, depth // 2, width), jnp.bfloat16),
            pltpu.SemaphoreType.DMA((2,)),
        ],
        compiler_params=pltpu.CompilerParams(vmem_limit_bytes=VMEM_LIMIT),
        cost_estimate=pl.CostEstimate(
            flops=2 * rows * depth * width,
            bytes_accessed=2 * (rows + width) * depth + 3 * rows * width,
            transcendentals=0,
        ),
    )(attended, own, partner)


def join_kernel(*refs):
    out_ref = refs[-1]
    count = (len(refs) - 1) // 2
    width = out_ref.shape[1] // count
    for at in range(count):
        total = refs[at][...] + refs[count + at][...].astype(jnp.float32)
        out_ref[:, at * width : (at + 1) * width] = total.astype(out_ref.dtype)


def join(keeps, gots):
    rows, width = keeps[0].shape
    columns = width * len(keeps)
    return pl.pallas_call(
        join_kernel,
        out_shape=jax.ShapeDtypeStruct((rows, columns), jnp.bfloat16),
        in_specs=[VMEM] * (2 * len(keeps)),
        out_specs=VMEM,
        compiler_params=pltpu.CompilerParams(vmem_limit_bytes=VMEM_LIMIT),
        cost_estimate=pl.CostEstimate(
            flops=rows * columns, bytes_accessed=8 * rows * columns, transcendentals=0
        ),
    )(*keeps, *gots)


def exchange_from(value, root, bit):
    other = swap(value, "ctx", 1 << bit)
    same = ((lax.axis_index("ctx") >> bit) & 1) == ((root >> bit) & 1)
    return jnp.where(same, value, other)


def local(
    activations,
    norm_gain,
    query_weight,
    kv_weight,
    out_weight,
    tile_mask,
    anchor_mask,
    anchor_index,
):
    tokens, depth = activations.shape
    head = kv_weight.shape[2]
    ctx_size, zero_size = lax.axis_size("ctx"), lax.axis_size("zero")
    ctx_rank, zero_rank = lax.axis_index("ctx"), lax.axis_index("zero")
    core = zero_rank % 2
    groups = zero_size // 2
    size = tokens // zero_size

    out_own = lax.all_gather(out_weight, "ctx", axis=1, tiled=True)

    mine, theirs = deal(activations)
    x_pieces = [mine, swap(theirs, "zero", 1)]
    for m in range(2, zero_size):
        piece = theirs if m % 2 else mine
        x_pieces.append(swap(tied(piece, *x_pieces[2:][-1:]), "zero", m))

    shard_rows = kv_weight.shape[0]
    gain = lax.dynamic_slice_in_dim(norm_gain, ctx_rank * shard_rows, shard_rows)
    gain = gain.astype(jnp.float32)[:, None]

    def of_chip(own):
        other = swap(own, "zero", 1)
        pair = jnp.where(
            core == 0,
            jnp.concatenate([own, other], 1),
            jnp.concatenate([other, own], 1),
        )
        return (pair.astype(jnp.float32) * gain).astype(jnp.bfloat16)

    kv_ring = Ring(of_chip(kv_weight[:, 0, :]), core)
    query_ring = Ring(of_chip(query_weight), core)
    kv_ring.advance(0, 4)
    second = kv_ring.advance(1, 4)
    query_ring.advance(0, 4, second)
    third = kv_ring.advance(2, 4)
    query_ring.advance(1, 4, third)
    last = kv_ring.advance(3, 4)
    query_ring.advance(2, 4, last)

    half = head // 2
    frequency = jnp.power(
        jnp.float32(ROPE_BASE), -(jnp.arange(half, dtype=jnp.float32) * 2.0 / head)
    )
    local_token = jnp.arange(tokens // 2, dtype=jnp.int32)
    offsets = (2 * (local_token // size) + core) * size + local_token % size
    positions = ctx_rank * tokens + offsets
    angles = positions.astype(jnp.float32)[:, None] * frequency[None, :]
    cos_half, sin_half = jnp.cos(angles), jnp.sin(angles)
    cos = jnp.concatenate([cos_half, cos_half], -1)
    sin = jnp.concatenate([-sin_half, sin_half], -1)
    shrink = head ** (-0.5)

    near, scale = project(cos, cos, sin, x_pieces, kv_ring.held, True)
    query_ring.advance(3, 4, near)
    (queries,) = project(
        scale, cos * shrink, sin * shrink, x_pieces, query_ring.held, False
    )
    anchor = anchor_index[0]
    far = near
    bits = int(math.log2(ctx_size))
    for bit in range(bits):
        far = exchange_from(tied(far, queries) if bit == bits - 1 else far, anchor, bit)
    near_other = swap(near, "zero", 1)
    far_other = swap(far, "zero", 1)
    far_mask = jnp.where(ctx_rank != anchor, anchor_mask[0], 0)
    attended = attend(groups, tile_mask[0], far_mask, queries, near, near_other, far, far_other)

    out_partner = swap(tied(out_own, far), "zero", 1)
    width = out_own.shape[1] // CHUNKS
    keeps, gots = [], []
    top = zero_size // 2
    for at in range(CHUNKS):
        keep, send = terms(top, attended, out_own, out_partner, at * width, width)
        got = swap(send, "zero", top)
        stride = top // 2
        while stride > 1:
            both = keep + got.astype(jnp.float32)
            rows = both.shape[0] // 2
            bit = (zero_rank // stride) % 2
            keep = lax.dynamic_slice_in_dim(both, bit * rows, rows, 0)
            send = lax.dynamic_slice_in_dim(both, (1 - bit) * rows, rows, 0)
            got = swap(send.astype(jnp.bfloat16), "zero", stride)
            stride //= 2
        keeps.append(keep)
        gots.append(got)
    return join(keeps, gots)


def solution(mesh):
    placed = (
        P("ctx", "zero"),
        P(),
        P("ctx", "zero"),
        P("ctx", "zero", None),
        P("zero", "ctx"),
        P("ctx", None, None),
        P("ctx", None, None),
        P(),
    )
    return jax.shard_map(
        local, mesh=mesh, in_specs=placed, out_specs=P(("ctx", "zero"), None), check_vma=False
    )
```

```python
import functools
import math

import jax
import jax.numpy as jnp
from jax import lax
from jax.experimental import pallas as pl
from jax.experimental.pallas import tpu as pltpu
from jax.sharding import PartitionSpec as P

HBM = pl.BlockSpec(memory_space=pltpu.HBM)
VMEM = pl.BlockSpec(memory_space=pltpu.VMEM)
SMEM = pl.BlockSpec(memory_space=pltpu.SMEM)
VMEM_LIMIT = 48 * 1024 * 1024
ROPE_BASE = 500000.0
CHUNKS = 4


def swap(value, axis, stride):
    pairs = [(source, source ^ stride) for source in range(lax.axis_size(axis))]
    return lax.ppermute(value, axis, pairs)


def cycle(size):
    return list(range(0, size, 2)) + list(range(1, size, 2))[::-1]


def ring_step(value):
    ctx_size, zero_size = lax.axis_size("ctx"), lax.axis_size("zero")
    order = cycle(ctx_size)
    pairs = []
    for at in range(ctx_size):
        for zero in range(zero_size):
            to = order[(at + (1 if zero % 2 == 0 else -1)) % ctx_size]
            pairs.append((order[at] * zero_size + zero, to * zero_size + zero))
    return lax.ppermute(value, ("ctx", "zero"), pairs)


class Ring:
    def __init__(self, shard, core):
        self.held = [(0, None, shard)]
        self.moving, self.core, self.at = shard, core, 0
        self.length = lax.axis_size("ctx") // 2

    def step(self, *after):
        self.at += 1
        last = self.at == self.length
        if last:
            half = self.moving.shape[0] // 2
            self.moving = lax.dynamic_slice_in_dim(self.moving, self.core * half, half, 0)
        self.moving = ring_step(tied(self.moving, *after))
        self.held.append((-self.at, 0 if last else None, self.moving))
        self.held.append((self.at, 1 if last else None, swap(self.moving, "zero", 1)))
        return self.moving

    def advance(self, part, parts, *after):
        while self.at < self.length * (part + 1) // parts:
            self.step(*after)
        return self.moving


def tied(value, *others):
    return lax.optimization_barrier((value, *others))[0] if others else value


def source_of(steps):
    size = lax.axis_size("ctx")
    ctx, core = lax.axis_index("ctx"), lax.axis_index("zero") % 2
    place = jnp.where(ctx % 2 == 0, ctx // 2, size - 1 - ctx // 2)
    place = lax.rem(place + steps * (1 - 2 * core) + size, size)
    return jnp.where(place < size // 2, 2 * place, 2 * (size - 1 - place) + 1)


def share_of(share):
    core = lax.axis_index("zero") % 2
    return core if share == 0 else 1 - core


def token_rows(group, other, size):
    core = lax.axis_index("zero") % 2
    if other:
        core = 1 - core
    return pl.ds(pl.multiple_of((2 * group + core) * size, 16), size)


def deal_kernel(count, *refs):
    x_refs, outs, sem = refs[:count], refs[count:-1], refs[-1]
    groups = lax.axis_size("zero") // 2
    size = x_refs[0].shape[0] // (2 * groups)
    copies = []
    for x_ref, out_ref in zip(x_refs, outs):
        for group in range(groups):
            copies.append(
                pltpu.make_async_copy(
                    x_ref.at[token_rows(group, True, size)],
                    out_ref.at[pl.ds(group * size, size)],
                    sem.at[len(copies)],
                )
            )
    for copy in copies:
        copy.start()
    for copy in copies:
        copy.wait()


def deal(arrays):
    tokens, depth = arrays[0].shape
    part = jax.ShapeDtypeStruct((tokens // 2, depth), arrays[0].dtype)
    copies = len(arrays) * lax.axis_size("zero") // 2
    return pl.pallas_call(
        functools.partial(deal_kernel, len(arrays)),
        out_shape=[part] * len(arrays),
        in_specs=[HBM] * len(arrays),
        out_specs=[HBM] * len(arrays),
        scratch_shapes=[pltpu.SemaphoreType.DMA((copies,))],
        compiler_params=pltpu.CompilerParams(vmem_limit_bytes=VMEM_LIMIT),
    )(*arrays)


def project_kernel(layout, first_call, *refs):
    (x_buf, w_buf, x_sem, w_sem) = refs[-4:]
    pieces, tokens, depth = x_buf.shape
    scale_ref, cos_ref, sin_ref = refs[:3]
    x_refs = refs[3 : 3 + pieces]
    w_refs = refs[3 + pieces : 3 + pieces + len(layout)]
    out_ref = refs[3 + pieces + len(layout)]
    zero = lax.axis_index("zero")
    shard_rows = w_refs[0].shape[0]
    x_copies, w_copies = [], []
    for m, ref in enumerate(x_refs):
        target = x_buf.at[jnp.bitwise_xor(zero, m)]
        if m % 2:
            x_copies.append(pltpu.make_async_copy(ref, target, x_sem.at[len(x_copies)]))
            continue
        size = 2 * tokens // pieces
        for group in range(pieces // 2):
            x_copies.append(
                pltpu.make_async_copy(
                    ref.at[token_rows(group, False, size)],
                    target.at[pl.ds(group * size, size)],
                    x_sem.at[len(x_copies)],
                )
            )
    for at, (ref, (steps, share)) in enumerate(zip(w_refs, layout)):
        start = source_of(steps) * shard_rows
        if share is not None:
            start = start + share_of(share) * ref.shape[0]
        rows = pl.ds(pl.multiple_of(start, 16), ref.shape[0])
        w_copies.append(pltpu.make_async_copy(ref, w_buf.at[rows], w_sem.at[at]))
    for copy in x_copies + w_copies:
        copy.start()
    for copy in x_copies:
        copy.wait()
    if first_call:
        squares = jnp.zeros((x_buf.shape[1], 128), jnp.float32)
        for at in range(pieces):
            for first in range(0, depth, 128):
                x_float = x_buf[at, :, first : first + 128].astype(jnp.float32)
                squares += x_float * x_float
        mean = jnp.sum(squares, axis=1, keepdims=True) / (depth * pieces)
        scale = jnp.broadcast_to(lax.rsqrt(mean + 1e-05), squares.shape)
        scale_out = refs[4 + pieces + len(layout)]
        scale_out[...] = scale
    else:
        scale = scale_ref[...]
    for copy in w_copies:
        copy.wait()
    total = jnp.zeros(out_ref.shape, jnp.float32)
    for at in range(pieces):
        total += jnp.dot(
            x_buf[at], w_buf[at * depth : (at + 1) * depth, :], preferred_element_type=jnp.float32
        )
    head = cos_ref.shape[1]
    for first in range(0, out_ref.shape[1], head):
        part = total[:, first : first + head] * scale
        if not first_call or first == 0:
            part = part * cos_ref[...] + pltpu.roll(part, head // 2, 1) * sin_ref[...]
        out_ref[:, first : first + head] = part.astype(out_ref.dtype)


def project(scale, cos, sin, x_pieces, held, first_call):
    layout = [(steps, share) for steps, share, _ in held]
    shards = [piece for _, _, piece in held]
    tokens, depth = x_pieces[1].shape
    pieces = len(x_pieces)
    width = shards[0].shape[1]
    full = depth * pieces
    out = [jax.ShapeDtypeStruct((tokens, width), jnp.bfloat16)]
    if first_call:
        out.append(jax.ShapeDtypeStruct((tokens, 128), jnp.float32))
    return pl.pallas_call(
        functools.partial(project_kernel, layout, first_call),
        out_shape=out,
        in_specs=[VMEM] * 3 + [HBM] * (pieces + len(shards)),
        out_specs=[VMEM] * len(out),
        scratch_shapes=[
            pltpu.VMEM((pieces, tokens, depth), jnp.bfloat16),
            pltpu.VMEM((full, width), jnp.bfloat16),
            pltpu.SemaphoreType.DMA((pieces // 2 * (1 + pieces // 2),)),
            pltpu.SemaphoreType.DMA((len(shards),)),
        ],
        compiler_params=pltpu.CompilerParams(vmem_limit_bytes=VMEM_LIMIT),
        cost_estimate=pl.CostEstimate(
            flops=2 * tokens * full * width,
            bytes_accessed=2 * full * (tokens + width),
            transcendentals=0,
        ),
    )(scale, cos, sin, *x_pieces, *shards)


def attend_kernel(groups, own_ref, far_ref, q_ref, near0, near1, far0, far1, out_ref):
    tokens, pair = near0.shape
    head = pair // 2
    size = tokens // groups
    tiles = own_ref.shape[0]
    tile = 2 * tokens // tiles
    heads = q_ref.shape[1] // head
    rows = heads * size
    core = lax.axis_index("zero") % 2
    column = lax.broadcasted_iota(jnp.int32, (1, tokens), 1)
    column_group = column // size
    within = lax.rem(lax.broadcasted_iota(jnp.int32, (rows, 1), 0), size)
    hidden = jnp.float32(-1e30)
    nt = (((1,), (1,)), ((), ()))
    for h in range(groups):
        across = slice(h * size, (h + 1) * size)
        q = jnp.concatenate(
            [q_ref[across, g * head : (g + 1) * head] for g in range(heads)], axis=0
        )
        first = (2 * h + core) * size
        own_tile = first // tile
        seen = min(tokens, -(-(h + 1) * size // 128) * 128)
        parts, blocks = [], []
        for ref, mask_ref, width, parity, causal in (
            (far0, far_ref, tokens, core, False),
            (far1, far_ref, tokens, 1 - core, False),
            (near0, own_ref, seen, core, True),
            (near1, own_ref, seen, 1 - core, True),
        ):
            visible = jnp.zeros((1, width), jnp.int32)
            for g in range(-(-width // size)):
                at = mask_ref[own_tile, (2 * g + parity) * size // tile]
                visible = jnp.where(column_group[:, :width] == g, at, visible)
            visible = visible == 1
            if causal:
                group = column_group[:, :width]
                offset = (2 * group + parity) * size + column[:, :width] - group * size
                visible = visible & (offset <= first + within)
            scores = lax.dot_general(
                q, ref[:width, :head], nt, preferred_element_type=jnp.float32
            )
            parts.append(jnp.where(visible, scores, hidden))
            blocks.append((ref, width))
        scores = jnp.concatenate(parts, axis=1)
        largest = jnp.max(scores, axis=1, keepdims=True)
        weights = jnp.exp(scores - largest)
        total = jnp.sum(weights, axis=1, keepdims=True)
        rounded = weights.astype(jnp.bfloat16)
        mixed = jnp.zeros((rows, head), jnp.float32)
        start = 0
        for ref, width in blocks:
            mixed += jnp.dot(
                rounded[:, start : start + width],
                ref[:width, head:],
                preferred_element_type=jnp.float32,
            )
            start += width
        mixed = (mixed / total).astype(out_ref.dtype)
        for g in range(heads):
            out_ref[across, g * head : (g + 1) * head] = mixed[g * size : (g + 1) * size, :]


def attend(groups, own_mask, far_mask, queries, near, near_other, far, far_other):
    tokens, width = queries.shape
    return pl.pallas_call(
        functools.partial(attend_kernel, groups),
        out_shape=jax.ShapeDtypeStruct(queries.shape, jnp.bfloat16),
        in_specs=[SMEM, SMEM] + [VMEM] * 5,
        out_specs=VMEM,
        compiler_params=pltpu.CompilerParams(vmem_limit_bytes=VMEM_LIMIT),
        cost_estimate=pl.CostEstimate(
            flops=16 * tokens * tokens * width,
            bytes_accessed=8 * tokens * width,
            transcendentals=16 * tokens * tokens,
        ),
    )(own_mask, far_mask, queries, near, near_other, far, far_other)


def terms_kernel(layout, split, a_ref, *refs):
    keep_ref, send_ref, w_buf, sem = refs[-4:]
    half = keep_ref.shape[0]
    width = w_buf.shape[2]
    copies = []
    for at, (ref, (slot, share)) in enumerate(zip(refs[:-4], layout)):
        target = w_buf.at[slot]
        if share is not None:
            rows = ref.shape[0]
            target = w_buf.at[slot, pl.ds(pl.multiple_of(share_of(share) * rows, 16), rows)]
        copies.append(pltpu.make_async_copy(ref, target, sem.at[at]))
    for copy in copies:
        copy.start()
    pick = lax.axis_index("zero") // split % 2
    mine = a_ref[pl.ds(pl.multiple_of(pick * half, 16), half), :]
    other = a_ref[pl.ds(pl.multiple_of((1 - pick) * half, 16), half), :]
    both = jnp.concatenate([other, mine], axis=0)
    for copy in copies:
        copy.wait()
    for slot in range(w_buf.shape[0]):
        out = jnp.dot(both, w_buf[slot], preferred_element_type=jnp.float32)
        columns = slice(slot * width, (slot + 1) * width)
        send_ref[:, columns] = out[:half].astype(send_ref.dtype)
        keep_ref[:, columns] = out[half:]


def terms(split, attended, slots):
    layout = [(slot, share) for slot, pieces in enumerate(slots) for share, _ in pieces]
    shards = [piece for pieces in slots for _, piece in pieces]
    width = shards[0].shape[1]
    rows, depth = attended.shape
    columns = width * len(slots)
    return pl.pallas_call(
        functools.partial(terms_kernel, layout, split),
        out_shape=(
            jax.ShapeDtypeStruct((rows // 2, columns), jnp.float32),
            jax.ShapeDtypeStruct((rows // 2, columns), jnp.bfloat16),
        ),
        in_specs=[VMEM] + [HBM] * len(shards),
        out_specs=(VMEM, VMEM),
        scratch_shapes=[
            pltpu.VMEM((len(slots), depth, width), jnp.bfloat16),
            pltpu.SemaphoreType.DMA((len(shards),)),
        ],
        compiler_params=pltpu.CompilerParams(vmem_limit_bytes=VMEM_LIMIT),
        cost_estimate=pl.CostEstimate(
            flops=2 * rows * depth * columns,
            bytes_accessed=2 * (rows + columns) * depth + 3 * rows * columns,
            transcendentals=0,
        ),
    )(attended, *shards)


def join_kernel(groups, *refs):
    out_ref = refs[-1]
    count = len(groups)
    width = out_ref.shape[1] // sum(len(group) for group in groups)
    for group, keep_ref, got_ref in zip(groups, refs[:count], refs[count:-1]):
        for slot, steps in enumerate(group):
            columns = slice(slot * width, (slot + 1) * width)
            start = pl.multiple_of(source_of(steps) * width, 128)
            total = keep_ref[:, columns] + got_ref[:, columns].astype(jnp.float32)
            out_ref[:, pl.ds(start, width)] = total.astype(out_ref.dtype)


def join(groups, keeps, gots):
    rows = keeps[0].shape[0]
    columns = sum(keep.shape[1] for keep in keeps)
    return pl.pallas_call(
        functools.partial(join_kernel, groups),
        out_shape=jax.ShapeDtypeStruct((rows, columns), jnp.bfloat16),
        in_specs=[VMEM] * (2 * len(keeps)),
        out_specs=VMEM,
        compiler_params=pltpu.CompilerParams(vmem_limit_bytes=VMEM_LIMIT),
        cost_estimate=pl.CostEstimate(
            flops=rows * columns, bytes_accessed=8 * rows * columns, transcendentals=0
        ),
    )(*keeps, *gots)


def exchange_from(value, root, bit):
    other = swap(value, "ctx", 1 << bit)
    same = ((lax.axis_index("ctx") >> bit) & 1) == ((root >> bit) & 1)
    return jnp.where(same, value, other)


def local(
    activations,
    norm_gain,
    query_weight,
    kv_weight,
    out_weight,
    tile_mask,
    anchor_mask,
    anchor_index,
):
    tokens, depth = activations.shape
    head = kv_weight.shape[2]
    ctx_size, zero_size = lax.axis_size("ctx"), lax.axis_size("zero")
    ctx_rank, zero_rank = lax.axis_index("ctx"), lax.axis_index("zero")
    core = zero_rank % 2
    groups = zero_size // 2
    size = tokens // zero_size

    blocks = {0: activations}
    stride = groups
    while stride > 1:
        for known in range(0, zero_size, 2 * stride):
            blocks[known + stride] = swap(blocks[known], "zero", stride)
        stride //= 2

    shard_rows = kv_weight.shape[0]
    gain = lax.dynamic_slice_in_dim(norm_gain, ctx_rank * shard_rows, shard_rows)
    gain = gain.astype(jnp.float32)[:, None]

    def of_chip(own, axis):
        other = swap(own, "zero", 1)
        return jnp.where(
            core == 0,
            jnp.concatenate([own, other], axis),
            jnp.concatenate([other, own], axis),
        )

    kv_pair = (of_chip(kv_weight[:, 0, :], 1).astype(jnp.float32) * gain).astype(jnp.bfloat16)
    query_pair = (of_chip(query_weight, 1).astype(jnp.float32) * gain).astype(jnp.bfloat16)
    out_pair = of_chip(out_weight, 0)
    kv_ring = Ring(kv_pair, core)
    query_ring = Ring(query_pair, core)
    out_ring = Ring(out_pair, core)
    a1 = kv_ring.advance(0, 4)
    b1 = query_ring.advance(0, 4)
    a2 = kv_ring.advance(1, 4)
    b2 = query_ring.advance(1, 4, a1)
    a3 = kv_ring.advance(2, 4, b1)
    b3 = query_ring.advance(2, 4, a2)
    far_blocks = [blocks[m] for m in range(2, zero_size, 2)]
    a4 = kv_ring.advance(3, 4, b2, *far_blocks)
    b4 = query_ring.advance(3, 4, a3)
    b5 = out_ring.advance(0, 4, a4, b4)

    own = deal([blocks[0]]) + (deal([blocks[m] for m in range(2, zero_size, 2)]))
    x_pieces = []
    for m, theirs in zip(range(0, zero_size, 2), own):
        x_pieces += [blocks[m], swap(theirs, "zero", 1)]

    half = head // 2
    frequency = jnp.power(
        jnp.float32(ROPE_BASE), -(jnp.arange(half, dtype=jnp.float32) * 2.0 / head)
    )
    local_token = jnp.arange(tokens // 2, dtype=jnp.int32)
    offsets = (2 * (local_token // size) + core) * size + local_token % size
    positions = ctx_rank * tokens + offsets
    angles = positions.astype(jnp.float32)[:, None] * frequency[None, :]
    cos_half, sin_half = jnp.cos(angles), jnp.sin(angles)
    cos = jnp.concatenate([cos_half, cos_half], -1)
    sin = jnp.concatenate([-sin_half, sin_half], -1)
    shrink = head ** (-0.5)

    near, scale = project(cos, cos, sin, x_pieces, kv_ring.held, True)
    (queries,) = project(
        scale, cos * shrink, sin * shrink, x_pieces, query_ring.held, False
    )
    anchor = anchor_index[0]
    b6 = out_ring.advance(1, 4, near)
    far = near
    bits = int(math.log2(ctx_size))
    for bit in range(bits):
        if bit == 0:
            far = exchange_from(far, anchor, bit)
            out_ring.advance(2, 4, far)
        elif bit < bits - 1:
            far = exchange_from(tied(far, b5), anchor, bit)
        else:
            out_ring.advance(3, 4, far)
            far = exchange_from(tied(far, queries, b6), anchor, bit)
    near_other = swap(near, "zero", 1)
    far_other = swap(far, "zero", 1)
    far_mask = jnp.where(ctx_rank != anchor, anchor_mask[0], 0)
    attended = attend(groups, tile_mask[0], far_mask, queries, near, near_other, far, far_other)

    slots = []
    for steps, share, piece in out_ring.held:
        if share == 1:
            slots[-1][1].append((share, piece))
        else:
            slots.append((steps, [(share, piece)]))
    per = max(1, ctx_size // CHUNKS)
    cuts = [0] + list(range(per + 1, ctx_size, per)) + [ctx_size]
    step_groups, keeps, gots = [], [], []
    top = zero_size // 2
    for first, end in zip(cuts, cuts[1:]):
        step_groups.append([steps for steps, _ in slots[first:end]])
        keep, send = terms(top, attended, [pieces for _, pieces in slots[first:end]])
        got = swap(send, "zero", top)
        stride = top // 2
        while stride > 1:
            both = keep + got.astype(jnp.float32)
            rows = both.shape[0] // 2
            bit = (zero_rank // stride) % 2
            keep = lax.dynamic_slice_in_dim(both, bit * rows, rows, 0)
            send = lax.dynamic_slice_in_dim(both, (1 - bit) * rows, rows, 0)
            got = swap(send.astype(jnp.bfloat16), "zero", stride)
            stride //= 2
        keeps.append(keep)
        gots.append(got)
    return join(step_groups, keeps, gots)


def solution(mesh):
    placed = (
        P("ctx", "zero"),
        P(),
        P("ctx", "zero"),
        P("ctx", "zero", None),
        P("zero", "ctx"),
        P("ctx", None, None),
        P("ctx", None, None),
        P(),
    )
    return jax.shard_map(
        local, mesh=mesh, in_specs=placed, out_specs=P(("ctx", "zero"), None), check_vma=False
    )
```

```python
import functools
import math

import jax
import jax.numpy as jnp
from jax import lax
from jax.experimental import pallas as pl
from jax.experimental.pallas import tpu as pltpu
from jax.sharding import PartitionSpec as P

HBM = pl.BlockSpec(memory_space=pltpu.HBM)
VMEM = pl.BlockSpec(memory_space=pltpu.VMEM)
SMEM = pl.BlockSpec(memory_space=pltpu.SMEM)
VMEM_LIMIT = 24 * 1024 * 1024
ROPE_BASE = 500000.0


def swap(value, axis, stride):
    pairs = [(source, source ^ stride) for source in range(lax.axis_size(axis))]
    return lax.ppermute(value, axis, pairs)


def cycle(size):
    return list(range(0, size, 2)) + list(range(1, size, 2))[::-1]


def ring_step(value):
    ctx_size, zero_size = lax.axis_size("ctx"), lax.axis_size("zero")
    order = cycle(ctx_size)
    pairs = []
    for at in range(ctx_size):
        for zero in range(zero_size):
            to = order[(at + (1 if zero % 2 == 0 else -1)) % ctx_size]
            pairs.append((order[at] * zero_size + zero, to * zero_size + zero))
    return lax.ppermute(value, ("ctx", "zero"), pairs)


class Ring:
    def __init__(self, shard, core):
        self.held = [(0, None, shard)]
        self.moving, self.core, self.at = shard, core, 0
        self.length = lax.axis_size("ctx") // 2

    def step(self, *after):
        self.at += 1
        last = self.at == self.length
        if last:
            half = self.moving.shape[0] // 2
            self.moving = lax.dynamic_slice_in_dim(self.moving, self.core * half, half, 0)
        self.moving = ring_step(tied(self.moving, *after))
        self.held.append((-self.at, 0 if last else None, self.moving))
        self.held.append((self.at, 1 if last else None, swap(self.moving, "zero", 1)))
        return self.moving

    def advance(self, part, parts, *after):
        while self.at < self.length * (part + 1) // parts:
            self.step(*after)
        return self.moving


def tied(value, *others):
    return lax.optimization_barrier((value, *others))[0] if others else value


def source_of(steps):
    size = lax.axis_size("ctx")
    ctx, core = lax.axis_index("ctx"), lax.axis_index("zero") % 2
    place = jnp.where(ctx % 2 == 0, ctx // 2, size - 1 - ctx // 2)
    place = lax.rem(place + steps * (1 - 2 * core) + size, size)
    return jnp.where(place < size // 2, 2 * place, 2 * (size - 1 - place) + 1)


def share_of(share):
    core = lax.axis_index("zero") % 2
    return core if share == 0 else 1 - core


def token_rows(group, other, size):
    core = lax.axis_index("zero") % 2
    if other:
        core = 1 - core
    return pl.ds(pl.multiple_of((2 * group + core) * size, 16), size)


def deal_kernel(count, *refs):
    x_refs, outs, sem = refs[:count], refs[count:-1], refs[-1]
    groups = lax.axis_size("zero") // 2
    size = x_refs[0].shape[0] // (2 * groups)
    copies = []
    for x_ref, out_ref in zip(x_refs, outs):
        for group in range(groups):
            copies.append(
                pltpu.make_async_copy(
                    x_ref.at[token_rows(group, True, size)],
                    out_ref.at[pl.ds(group * size, size)],
                    sem.at[len(copies)],
                )
            )
    for copy in copies:
        copy.start()
    for copy in copies:
        copy.wait()


def deal(arrays):
    tokens, depth = arrays[0].shape
    part = jax.ShapeDtypeStruct((tokens // 2, depth), arrays[0].dtype)
    copies = len(arrays) * lax.axis_size("zero") // 2
    return pl.pallas_call(
        functools.partial(deal_kernel, len(arrays)),
        out_shape=[part] * len(arrays),
        in_specs=[HBM] * len(arrays),
        out_specs=[HBM] * len(arrays),
        scratch_shapes=[pltpu.SemaphoreType.DMA((copies,))],
        compiler_params=pltpu.CompilerParams(vmem_limit_bytes=VMEM_LIMIT),
    )(*arrays)


def project_kernel(layout, columns, first_call, *refs):
    (x_buf, w_buf, x_sem, w_sem) = refs[-4:]
    pieces, tokens, depth = x_buf.shape
    scale_ref, cos_ref, sin_ref = refs[:3]
    x_refs = refs[3 : 3 + pieces]
    w_refs = refs[3 + pieces : 3 + pieces + len(layout)]
    outs = refs[3 + pieces + len(layout) : -4]
    out_ref = outs[0]
    zero = lax.axis_index("zero")
    shard_rows = w_refs[0].shape[0]
    x_copies, w_copies = [], []
    for m, ref in enumerate(x_refs):
        target = x_buf.at[jnp.bitwise_xor(zero, m)]
        if m % 2:
            x_copies.append(pltpu.make_async_copy(ref, target, x_sem.at[len(x_copies)]))
            continue
        size = 2 * tokens // pieces
        for group in range(pieces // 2):
            x_copies.append(
                pltpu.make_async_copy(
                    ref.at[token_rows(group, False, size)],
                    target.at[pl.ds(group * size, size)],
                    x_sem.at[len(x_copies)],
                )
            )
    for at, (ref, (steps, share)) in enumerate(zip(w_refs, layout)):
        start = source_of(steps) * shard_rows
        if share is not None:
            start = start + share_of(share) * ref.shape[0]
        rows = pl.ds(pl.multiple_of(start, 16), ref.shape[0])
        source = ref.at[:, pl.ds(columns, w_buf.shape[1])]
        w_copies.append(pltpu.make_async_copy(source, w_buf.at[rows], w_sem.at[at]))
    for copy in x_copies + w_copies:
        copy.start()
    for copy in x_copies:
        copy.wait()
    if first_call:
        squares = jnp.zeros((x_buf.shape[1], 128), jnp.float32)
        for at in range(pieces):
            for first in range(0, depth, 128):
                x_float = x_buf[at, :, first : first + 128].astype(jnp.float32)
                squares += x_float * x_float
        mean = jnp.sum(squares, axis=1, keepdims=True) / (depth * pieces)
        scale = jnp.broadcast_to(lax.rsqrt(mean + 1e-05), squares.shape)
        outs[1][...] = scale
    else:
        scale = scale_ref[...]
    for copy in w_copies:
        copy.wait()
    total = jnp.zeros(out_ref.shape, jnp.float32)
    for at in range(pieces):
        total += jnp.dot(
            x_buf[at], w_buf[at * depth : (at + 1) * depth, :], preferred_element_type=jnp.float32
        )
    head = cos_ref.shape[1]
    for first in range(0, out_ref.shape[1], head):
        part = total[:, first : first + head] * scale
        if not first_call or first == 0:
            part = part * cos_ref[...] + pltpu.roll(part, head // 2, 1) * sin_ref[...]
        out_ref[:, first : first + head] = part.astype(out_ref.dtype)


def project(scale, cos, sin, x_pieces, held, columns, width, first_call):
    layout = [(steps, share) for steps, share, _ in held]
    shards = [piece for _, _, piece in held]
    tokens, depth = x_pieces[1].shape
    pieces = len(x_pieces)
    full = depth * pieces
    out = [jax.ShapeDtypeStruct((tokens, width), jnp.bfloat16)]
    if first_call:
        out.append(jax.ShapeDtypeStruct((tokens, 128), jnp.float32))
    return pl.pallas_call(
        functools.partial(project_kernel, layout, columns, first_call),
        out_shape=out,
        in_specs=[VMEM] * 3 + [HBM] * (pieces + len(shards)),
        out_specs=[VMEM] * len(out),
        scratch_shapes=[
            pltpu.VMEM((pieces, tokens, depth), jnp.bfloat16),
            pltpu.VMEM((full, width), jnp.bfloat16),
            pltpu.SemaphoreType.DMA((pieces // 2 * (1 + pieces // 2),)),
            pltpu.SemaphoreType.DMA((len(shards),)),
        ],
        compiler_params=pltpu.CompilerParams(vmem_limit_bytes=VMEM_LIMIT),
        cost_estimate=pl.CostEstimate(
            flops=2 * tokens * full * width,
            bytes_accessed=2 * full * (tokens + width),
            transcendentals=0,
        ),
    )(scale, cos, sin, *x_pieces, *shards)


def attend_kernel(groups, own_ref, far_ref, q_ref, near0, near1, far0, far1, keep, send):
    tokens, pair = near0.shape
    head = pair // 2
    size = tokens // groups
    tiles = own_ref.shape[0]
    tile = 2 * tokens // tiles
    heads = q_ref.shape[1] // head
    rows = heads * size
    core = lax.axis_index("zero") % 2
    column = lax.broadcasted_iota(jnp.int32, (1, tokens), 1)
    column_group = column // size
    within = lax.rem(lax.broadcasted_iota(jnp.int32, (rows, 1), 0), size)
    hidden = jnp.float32(-1e30)
    nt = (((1,), (1,)), ((), ()))
    for h in range(groups):
        across = slice(h * size, (h + 1) * size)
        q = jnp.concatenate(
            [q_ref[across, g * head : (g + 1) * head] for g in range(heads)], axis=0
        )
        first = (2 * h + core) * size
        own_tile = first // tile
        seen = min(tokens, -(-(h + 1) * size // 128) * 128)
        parts, blocks = [], []
        for ref, mask_ref, width, parity, causal in (
            (far0, far_ref, tokens, core, False),
            (far1, far_ref, tokens, 1 - core, False),
            (near0, own_ref, seen, core, True),
            (near1, own_ref, seen, 1 - core, True),
        ):
            visible = jnp.zeros((1, width), jnp.int32)
            for g in range(-(-width // size)):
                at = mask_ref[own_tile, (2 * g + parity) * size // tile]
                visible = jnp.where(column_group[:, :width] == g, at, visible)
            visible = visible == 1
            if causal:
                group = column_group[:, :width]
                offset = (2 * group + parity) * size + column[:, :width] - group * size
                visible = visible & (offset <= first + within)
            scores = lax.dot_general(
                q, ref[:width, :head], nt, preferred_element_type=jnp.float32
            )
            parts.append(jnp.where(visible, scores, hidden))
            blocks.append((ref, width))
        scores = jnp.concatenate(parts, axis=1)
        largest = jnp.max(scores, axis=1, keepdims=True)
        weights = jnp.exp(scores - largest)
        total = jnp.sum(weights, axis=1, keepdims=True)
        rounded = weights.astype(jnp.bfloat16)
        mixed = jnp.zeros((rows, head), jnp.float32)
        start = 0
        for ref, width in blocks:
            mixed += jnp.dot(
                rounded[:, start : start + width],
                ref[:width, head:],
                preferred_element_type=jnp.float32,
            )
            start += width
        mixed = (mixed / total).astype(keep.dtype)
        stays = lax.axis_index("zero") // 2 % 2 == h % 2
        rows_out = slice(h // 2 * size, (h // 2 + 1) * size)

        def store(out_ref, rows_out=rows_out, mixed=mixed):
            for g in range(heads):
                out_ref[rows_out, g * head : (g + 1) * head] = mixed[g * size : (g + 1) * size, :]

        pl.when(stays)(functools.partial(store, keep))
        pl.when(jnp.logical_not(stays))(functools.partial(store, send))


def attend(groups, own_mask, far_mask, queries, near, near_other, far, far_other):
    tokens, width = queries.shape
    return pl.pallas_call(
        functools.partial(attend_kernel, groups),
        out_shape=[jax.ShapeDtypeStruct((tokens // 2, width), jnp.bfloat16)] * 2,
        in_specs=[SMEM, SMEM] + [VMEM] * 5,
        out_specs=[VMEM] * 2,
        compiler_params=pltpu.CompilerParams(vmem_limit_bytes=VMEM_LIMIT),
        cost_estimate=pl.CostEstimate(
            flops=16 * tokens * tokens * width,
            bytes_accessed=8 * tokens * width,
            transcendentals=16 * tokens * tokens,
        ),
    )(own_mask, far_mask, queries, near, near_other, far, far_other)


def mix_kernel(layout, steps, *refs):
    a_refs, w_refs = refs[:2], refs[2 : 2 + len(layout)]
    out_ref, w_buf, sem = refs[2 + len(layout) :]
    width = w_buf.shape[2]
    half = a_refs[0].shape[1]
    copies = []
    for at, (ref, (slot, side, share)) in enumerate(zip(w_refs, layout)):
        rows = ref.shape[0]
        start = side * half
        if share is not None:
            start = pl.multiple_of(start + share_of(share) * rows, 16)
        copies.append(pltpu.make_async_copy(ref, w_buf.at[slot, pl.ds(start, rows)], sem.at[at]))
    for copy in copies:
        copy.start()
    both = jnp.concatenate([a_refs[0][...], a_refs[1][...]], axis=1)
    for slot, along in enumerate(steps):
        for copy, (its_slot, _, _) in zip(copies, layout):
            if its_slot == slot:
                copy.wait()
        total = jnp.dot(both, w_buf[slot], preferred_element_type=jnp.float32)
        start = pl.multiple_of(source_of(along) * width, 128)
        out_ref[:, pl.ds(start, width)] = total.astype(out_ref.dtype)


def mix(keep, got, slots, dtype):
    layout, shards = [], []
    for slot, (_, pieces) in enumerate(slots):
        for side, share, piece in pieces:
            layout.append((slot, side, share))
            shards.append(piece)
    rows, half = keep.shape
    width = shards[0].shape[1]
    columns = width * len(slots)
    return pl.pallas_call(
        functools.partial(mix_kernel, layout, [steps for steps, _ in slots]),
        out_shape=jax.ShapeDtypeStruct((rows, columns), dtype),
        in_specs=[VMEM, VMEM] + [HBM] * len(shards),
        out_specs=VMEM,
        scratch_shapes=[
            pltpu.VMEM((len(slots), 2 * half, width), jnp.bfloat16),
            pltpu.SemaphoreType.DMA((len(shards),)),
        ],
        compiler_params=pltpu.CompilerParams(vmem_limit_bytes=VMEM_LIMIT),
        cost_estimate=pl.CostEstimate(
            flops=4 * rows * half * columns,
            bytes_accessed=4 * half * (rows + columns) + 4 * rows * columns,
            transcendentals=0,
        ),
    )(keep, got, *shards)


def exchange_from(value, root, bit):
    other = swap(value, "ctx", 1 << bit)
    same = ((lax.axis_index("ctx") >> bit) & 1) == ((root >> bit) & 1)
    return jnp.where(same, value, other)


def local(
    activations,
    norm_gain,
    query_weight,
    kv_weight,
    out_weight,
    tile_mask,
    anchor_mask,
    anchor_index,
):
    tokens, depth = activations.shape
    head = kv_weight.shape[2]
    ctx_size, zero_size = lax.axis_size("ctx"), lax.axis_size("zero")
    ctx_rank, zero_rank = lax.axis_index("ctx"), lax.axis_index("zero")
    core = zero_rank % 2
    groups = zero_size // 2
    size = tokens // zero_size

    blocks = {0: activations}
    stride = groups
    while stride > 1:
        for known in range(0, zero_size, 2 * stride):
            blocks[known + stride] = swap(blocks[known], "zero", stride)
        stride //= 2

    shard_rows = kv_weight.shape[0]
    gain = lax.dynamic_slice_in_dim(norm_gain, ctx_rank * shard_rows, shard_rows)
    gain = gain.astype(jnp.float32)[:, None]
    kv_own = kv_weight[:, 0, :]
    kv_other, query_other = swap(kv_own, "zero", 1), swap(query_weight, "zero", 1)
    pair = jnp.where(
        core == 0,
        jnp.concatenate([kv_own, kv_other, query_weight, query_other], 1),
        jnp.concatenate([kv_other, kv_own, query_other, query_weight], 1),
    )
    pair = (pair.astype(jnp.float32) * gain).astype(jnp.bfloat16)
    out_other = swap(out_weight, "zero", 1)
    out_pair = jnp.where(
        core == 0,
        jnp.concatenate([out_weight, out_other], 0),
        jnp.concatenate([out_other, out_weight], 0),
    )
    ring = Ring(pair, core)
    out_ring = Ring(out_pair, core)
    first = ring.advance(0, 4)
    out_ring.advance(0, 4, first)
    second = ring.advance(1, 4)
    third = ring.advance(2, 4)
    out_ring.advance(1, 4, third)
    last = ring.advance(3, 4)
    out_ring.advance(2, 4, last)

    far_blocks = [tied(blocks[m], second) for m in range(2, zero_size, 2)]
    x_pieces = []
    for at, theirs in enumerate(deal([blocks[0]]) + deal(far_blocks)):
        x_pieces += [([blocks[0]] + far_blocks)[at], swap(theirs, "zero", 1)]

    half = head // 2
    frequency = jnp.power(
        jnp.float32(ROPE_BASE), -(jnp.arange(half, dtype=jnp.float32) * 2.0 / head)
    )
    local_token = jnp.arange(tokens // 2, dtype=jnp.int32)
    offsets = (2 * (local_token // size) + core) * size + local_token % size
    positions = ctx_rank * tokens + offsets
    angles = positions.astype(jnp.float32)[:, None] * frequency[None, :]
    cos_half, sin_half = jnp.cos(angles), jnp.sin(angles)
    cos = jnp.concatenate([cos_half, cos_half], -1)
    sin = jnp.concatenate([-sin_half, sin_half], -1)
    shrink = head ** (-0.5)

    near, scale = project(cos, cos, sin, x_pieces, ring.held, 0, 2 * head, True)
    (queries,) = project(
        scale, cos * shrink, sin * shrink, x_pieces, ring.held, 2 * head, 4 * head, False
    )
    anchor = anchor_index[0]
    far = near
    bits = int(math.log2(ctx_size))
    for bit in range(bits):
        far = exchange_from(tied(far, queries) if bit == bits - 1 else far, anchor, bit)
        if bit == 0:
            out_ring.advance(3, 4, far)
    near_other = swap(near, "zero", 1)
    far_other = swap(far, "zero", 1)
    far_mask = jnp.where(ctx_rank != anchor, anchor_mask[0], 0)
    keep, send = attend(
        groups, tile_mask[0], far_mask, queries, near, near_other, far, far_other
    )

    slots = []
    for steps, share, piece in out_ring.held:
        if share != 1:
            slots.append((steps, []))
        if steps <= 0:
            beyond = swap(out_weight if steps == 0 else piece, "zero", 2)
            across = swap(beyond, "zero", 1)
        if steps == 0:
            pieces = [(0, None, piece), (1, 0, beyond), (1, 1, across)]
        else:
            pieces = [(0, share, piece), (1, share, beyond if steps < 0 else across)]
        slots[-1][1].extend(pieces)
    got = swap(send, "zero", 2)
    if zero_size == 4:
        return mix(keep, got, slots, jnp.bfloat16)
    total = mix(keep, got, slots, jnp.float32)
    stride = zero_size // 2
    while stride > 2:
        rows = total.shape[0] // 2
        bit = (zero_rank // stride) % 2
        stay = lax.dynamic_slice_in_dim(total, bit * rows, rows, 0)
        go = lax.dynamic_slice_in_dim(total, (1 - bit) * rows, rows, 0)
        total = stay + swap(go.astype(jnp.bfloat16), "zero", stride).astype(jnp.float32)
        stride //= 2
    return total.astype(jnp.bfloat16)


def solution(mesh):
    placed = (
        P("ctx", "zero"),
        P(),
        P("ctx", "zero"),
        P("ctx", "zero", None),
        P("zero", "ctx"),
        P("ctx", None, None),
        P("ctx", None, None),
        P(),
    )
    return jax.shard_map(
        local, mesh=mesh, in_specs=placed, out_specs=P(("ctx", "zero"), None), check_vma=False
    )
```

```python
import functools
import math

import jax
import jax.numpy as jnp
from jax import lax
from jax.experimental import pallas as pl
from jax.experimental.pallas import tpu as pltpu
from jax.sharding import PartitionSpec as P

HBM = pl.BlockSpec(memory_space=pltpu.HBM)
VMEM = pl.BlockSpec(memory_space=pltpu.VMEM)
SMEM = pl.BlockSpec(memory_space=pltpu.SMEM)
VMEM_LIMIT = 40 * 1024 * 1024
ROPE_BASE = 500000.0


def swap(value, axis, stride):
    pairs = [(source, source ^ stride) for source in range(lax.axis_size(axis))]
    return lax.ppermute(value, axis, pairs)


def cycle(size):
    return list(range(0, size, 2)) + list(range(1, size, 2))[::-1]


def ring_step(value):
    ctx_size, zero_size = lax.axis_size("ctx"), lax.axis_size("zero")
    order = cycle(ctx_size)
    pairs = []
    for at in range(ctx_size):
        for zero in range(zero_size):
            to = order[(at + (1 if zero % 2 == 0 else -1)) % ctx_size]
            pairs.append((order[at] * zero_size + zero, to * zero_size + zero))
    return lax.ppermute(value, ("ctx", "zero"), pairs)


class Ring:
    def __init__(self, shard, core, whole=None, base=0):
        self.held = [(0, None, 0, shard if whole is None else whole)] if base == 0 else []
        self.base = base
        self.moving, self.core, self.at = shard, core, 0
        self.length = lax.axis_size("ctx") // 2

    def step(self, *after):
        self.at += 1
        last = self.at == self.length
        if last:
            half = self.moving.shape[0] // 2
            self.moving = lax.dynamic_slice_in_dim(self.moving, self.core * half, half, 0)
        self.moving = ring_step(tied(self.moving, *after))
        self.held.append((-self.at, 0 if last else None, self.base, self.moving))
        self.held.append(
            (self.at, 1 if last else None, self.base, swap(self.moving, "zero", 1))
        )
        return self.moving

    def advance(self, part, parts, *after):
        while self.at < self.length * (part + 1) // parts:
            self.step(*after)
        return self.moving


def tied(value, *others):
    return lax.optimization_barrier((value, *others))[0] if others else value


def source_of(steps):
    size = lax.axis_size("ctx")
    ctx, core = lax.axis_index("ctx"), lax.axis_index("zero") % 2
    place = jnp.where(ctx % 2 == 0, ctx // 2, size - 1 - ctx // 2)
    place = lax.rem(place + steps * (1 - 2 * core) + size, size)
    return jnp.where(place < size // 2, 2 * place, 2 * (size - 1 - place) + 1)


def share_of(share):
    core = lax.axis_index("zero") % 2
    return core if share == 0 else 1 - core


def token_rows(group, other, size):
    core = lax.axis_index("zero") % 2
    if other:
        core = 1 - core
    return pl.ds(pl.multiple_of((2 * group + core) * size, 16), size)


def deal_kernel(count, *refs):
    x_refs, outs, sem = refs[:count], refs[count:-1], refs[-1]
    groups = lax.axis_size("zero") // 2
    size = x_refs[0].shape[0] // (2 * groups)
    copies = []
    for x_ref, out_ref in zip(x_refs, outs):
        for group in range(groups):
            copies.append(
                pltpu.make_async_copy(
                    x_ref.at[token_rows(group, True, size)],
                    out_ref.at[pl.ds(group * size, size)],
                    sem.at[len(copies)],
                )
            )
    for copy in copies:
        copy.start()
    for copy in copies:
        copy.wait()


def deal(arrays):
    tokens, depth = arrays[0].shape
    part = jax.ShapeDtypeStruct((tokens // 2, depth), arrays[0].dtype)
    copies = len(arrays) * lax.axis_size("zero") // 2
    return pl.pallas_call(
        functools.partial(deal_kernel, len(arrays)),
        out_shape=[part] * len(arrays),
        in_specs=[HBM] * len(arrays),
        out_specs=[HBM] * len(arrays),
        scratch_shapes=[pltpu.SemaphoreType.DMA((copies,))],
        compiler_params=pltpu.CompilerParams(vmem_limit_bytes=VMEM_LIMIT),
    )(*arrays)


def project_kernel(layout, columns, first_call, *refs):
    (x_buf, w_buf, x_sem, w_sem) = refs[-4:]
    pieces, tokens, depth = x_buf.shape
    scale_ref, cos_ref, sin_ref = refs[:3]
    x_refs = refs[3 : 3 + pieces]
    w_refs = refs[3 + pieces : 3 + pieces + len(layout)]
    outs = refs[3 + pieces + len(layout) : -4]
    out_ref = outs[0]
    zero = lax.axis_index("zero")
    shard_rows = w_refs[0].shape[0]
    x_copies, w_copies = [], []
    for m, ref in enumerate(x_refs):
        target = x_buf.at[jnp.bitwise_xor(zero, m)]
        if m % 2:
            x_copies.append(pltpu.make_async_copy(ref, target, x_sem.at[len(x_copies)]))
            continue
        size = 2 * tokens // pieces
        for group in range(pieces // 2):
            x_copies.append(
                pltpu.make_async_copy(
                    ref.at[token_rows(group, False, size)],
                    target.at[pl.ds(group * size, size)],
                    x_sem.at[len(x_copies)],
                )
            )
    for at, (ref, (steps, share, base)) in enumerate(zip(w_refs, layout)):
        start = source_of(steps) * shard_rows + base
        if share is not None:
            start = start + share_of(share) * ref.shape[0]
        rows = pl.ds(pl.multiple_of(start, 16), ref.shape[0])
        source = ref.at[:, pl.ds(columns, w_buf.shape[1])]
        w_copies.append(pltpu.make_async_copy(source, w_buf.at[rows], w_sem.at[at]))
    for copy in x_copies + w_copies:
        copy.start()
    for copy in x_copies:
        copy.wait()
    if first_call:
        squares = jnp.zeros((x_buf.shape[1], 128), jnp.float32)
        for at in range(pieces):
            for first in range(0, depth, 128):
                x_float = x_buf[at, :, first : first + 128].astype(jnp.float32)
                squares += x_float * x_float
        mean = jnp.sum(squares, axis=1, keepdims=True) / (depth * pieces)
        scale = jnp.broadcast_to(lax.rsqrt(mean + 1e-05), squares.shape)
        outs[1][...] = scale
    else:
        scale = scale_ref[...]
    for copy in w_copies:
        copy.wait()
    total = jnp.zeros(out_ref.shape, jnp.float32)
    for at in range(pieces):
        total += jnp.dot(
            x_buf[at], w_buf[at * depth : (at + 1) * depth, :], preferred_element_type=jnp.float32
        )
    head = cos_ref.shape[1]
    for first in range(0, out_ref.shape[1], head):
        part = total[:, first : first + head] * scale
        if not first_call or first == 0:
            part = part * cos_ref[...] + pltpu.roll(part, head // 2, 1) * sin_ref[...]
        out_ref[:, first : first + head] = part.astype(out_ref.dtype)


def project(scale, cos, sin, x_pieces, held, columns, width, first_call):
    layout = [(steps, share, base) for steps, share, base, _ in held]
    shards = [piece for _, _, _, piece in held]
    tokens, depth = x_pieces[1].shape
    pieces = len(x_pieces)
    full = depth * pieces
    out = [jax.ShapeDtypeStruct((tokens, width), jnp.bfloat16)]
    if first_call:
        out.append(jax.ShapeDtypeStruct((tokens, 128), jnp.float32))
    return pl.pallas_call(
        functools.partial(project_kernel, layout, columns, first_call),
        out_shape=out,
        in_specs=[VMEM] * 3 + [HBM] * (pieces + len(shards)),
        out_specs=[VMEM] * len(out),
        scratch_shapes=[
            pltpu.VMEM((pieces, tokens, depth), jnp.bfloat16),
            pltpu.VMEM((full, width), jnp.bfloat16),
            pltpu.SemaphoreType.DMA((pieces // 2 * (1 + pieces // 2),)),
            pltpu.SemaphoreType.DMA((len(shards),)),
        ],
        compiler_params=pltpu.CompilerParams(vmem_limit_bytes=VMEM_LIMIT),
        cost_estimate=pl.CostEstimate(
            flops=2 * tokens * full * width,
            bytes_accessed=2 * full * (tokens + width),
            transcendentals=0,
        ),
    )(scale, cos, sin, *x_pieces, *shards)


def attend_kernel(groups, own_ref, far_ref, q_ref, near0, near1, far0, far1, keep, send):
    tokens, pair = near0.shape
    head = pair // 2
    size = tokens // groups
    tiles = own_ref.shape[0]
    tile = 2 * tokens // tiles
    heads = q_ref.shape[1] // head
    rows = heads * size
    core = lax.axis_index("zero") % 2
    column = lax.broadcasted_iota(jnp.int32, (1, tokens), 1)
    column_group = column // size
    within = lax.rem(lax.broadcasted_iota(jnp.int32, (rows, 1), 0), size)
    hidden = jnp.float32(-1e30)
    nt = (((1,), (1,)), ((), ()))
    for h in range(groups):
        across = slice(h * size, (h + 1) * size)
        q = jnp.concatenate(
            [q_ref[across, g * head : (g + 1) * head] for g in range(heads)], axis=0
        )
        first = (2 * h + core) * size
        own_tile = first // tile
        seen = min(tokens, -(-(h + 1) * size // 128) * 128)
        parts, blocks = [], []
        for ref, mask_ref, width, parity, causal in (
            (far0, far_ref, tokens, core, False),
            (far1, far_ref, tokens, 1 - core, False),
            (near0, own_ref, seen, core, True),
            (near1, own_ref, seen, 1 - core, True),
        ):
            visible = jnp.zeros((1, width), jnp.int32)
            for g in range(-(-width // size)):
                at = mask_ref[own_tile, (2 * g + parity) * size // tile]
                visible = jnp.where(column_group[:, :width] == g, at, visible)
            visible = visible == 1
            if causal:
                group = column_group[:, :width]
                offset = (2 * group + parity) * size + column[:, :width] - group * size
                visible = visible & (offset <= first + within)
            scores = lax.dot_general(
                q, ref[:width, :head], nt, preferred_element_type=jnp.float32
            )
            parts.append(jnp.where(visible, scores, hidden))
            blocks.append((ref, width))
        scores = jnp.concatenate(parts, axis=1)
        largest = jnp.max(scores, axis=1, keepdims=True)
        weights = jnp.exp(scores - largest)
        total = jnp.sum(weights, axis=1, keepdims=True)
        rounded = weights.astype(jnp.bfloat16)
        mixed = jnp.zeros((rows, head), jnp.float32)
        start = 0
        for ref, width in blocks:
            mixed += jnp.dot(
                rounded[:, start : start + width],
                ref[:width, head:],
                preferred_element_type=jnp.float32,
            )
            start += width
        mixed = (mixed / total).astype(keep.dtype)
        stays = lax.axis_index("zero") // 2 % 2 == h % 2
        rows_out = slice(h // 2 * size, (h // 2 + 1) * size)

        def store(out_ref, rows_out=rows_out, mixed=mixed):
            for g in range(heads):
                out_ref[rows_out, g * head : (g + 1) * head] = mixed[g * size : (g + 1) * size, :]

        pl.when(stays)(functools.partial(store, keep))
        pl.when(jnp.logical_not(stays))(functools.partial(store, send))


def attend(groups, own_mask, far_mask, queries, near, near_other, far, far_other):
    tokens, width = queries.shape
    return pl.pallas_call(
        functools.partial(attend_kernel, groups),
        out_shape=[jax.ShapeDtypeStruct((tokens // 2, width), jnp.bfloat16)] * 2,
        in_specs=[SMEM, SMEM] + [VMEM] * 5,
        out_specs=[VMEM] * 2,
        compiler_params=pltpu.CompilerParams(vmem_limit_bytes=VMEM_LIMIT),
        cost_estimate=pl.CostEstimate(
            flops=16 * tokens * tokens * width,
            bytes_accessed=8 * tokens * width,
            transcendentals=16 * tokens * tokens,
        ),
    )(own_mask, far_mask, queries, near, near_other, far, far_other)


def mix_kernel(layout, steps, *refs):
    a_refs, w_refs = refs[:2], refs[2 : 2 + len(layout)]
    out_ref, w_buf, sem = refs[2 + len(layout) :]
    width = w_buf.shape[2]
    half = a_refs[0].shape[1]
    copies = []
    for at, (ref, (slot, side, share)) in enumerate(zip(w_refs, layout)):
        rows = ref.shape[0]
        start = side * half
        if share is not None:
            start = pl.multiple_of(start + share_of(share) * rows, 16)
        copies.append(pltpu.make_async_copy(ref, w_buf.at[slot, pl.ds(start, rows)], sem.at[at]))
    for copy in copies:
        copy.start()
    both = jnp.concatenate([a_refs[0][...], a_refs[1][...]], axis=1)
    for slot, along in enumerate(steps):
        for copy, (its_slot, _, _) in zip(copies, layout):
            if its_slot == slot:
                copy.wait()
        total = jnp.dot(both, w_buf[slot], preferred_element_type=jnp.float32)
        start = pl.multiple_of(source_of(along) * width, 128)
        out_ref[:, pl.ds(start, width)] = total.astype(out_ref.dtype)


def mix(keep, got, slots, dtype):
    layout, shards = [], []
    for slot, (_, pieces) in enumerate(slots):
        for side, share, piece in pieces:
            layout.append((slot, side, share))
            shards.append(piece)
    rows, half = keep.shape
    width = shards[0].shape[1]
    columns = width * len(slots)
    return pl.pallas_call(
        functools.partial(mix_kernel, layout, [steps for steps, _ in slots]),
        out_shape=jax.ShapeDtypeStruct((rows, columns), dtype),
        in_specs=[VMEM, VMEM] + [HBM] * len(shards),
        out_specs=VMEM,
        scratch_shapes=[
            pltpu.VMEM((len(slots), 2 * half, width), jnp.bfloat16),
            pltpu.SemaphoreType.DMA((len(shards),)),
        ],
        compiler_params=pltpu.CompilerParams(vmem_limit_bytes=VMEM_LIMIT),
        cost_estimate=pl.CostEstimate(
            flops=4 * rows * half * columns,
            bytes_accessed=4 * half * (rows + columns) + 4 * rows * columns,
            transcendentals=0,
        ),
    )(keep, got, *shards)


def exchange_from(value, root, bit):
    other = swap(value, "ctx", 1 << bit)
    same = ((lax.axis_index("ctx") >> bit) & 1) == ((root >> bit) & 1)
    return jnp.where(same, value, other)


def local(
    activations,
    norm_gain,
    query_weight,
    kv_weight,
    out_weight,
    tile_mask,
    anchor_mask,
    anchor_index,
):
    tokens, depth = activations.shape
    head = kv_weight.shape[2]
    ctx_size, zero_size = lax.axis_size("ctx"), lax.axis_size("zero")
    ctx_rank, zero_rank = lax.axis_index("ctx"), lax.axis_index("zero")
    core = zero_rank % 2
    groups = zero_size // 2
    size = tokens // zero_size

    blocks = {0: activations}
    stride = groups
    while stride > 1:
        for known in range(0, zero_size, 2 * stride):
            blocks[known + stride] = swap(blocks[known], "zero", stride)
        stride //= 2

    shard_rows = kv_weight.shape[0]
    gain = lax.dynamic_slice_in_dim(norm_gain, ctx_rank * shard_rows, shard_rows)
    gain = gain.astype(jnp.float32)[:, None]
    kv_own = kv_weight[:, 0, :]
    kv_other, query_other = swap(kv_own, "zero", 1), swap(query_weight, "zero", 1)
    pair = jnp.where(
        core == 0,
        jnp.concatenate([kv_own, kv_other, query_weight, query_other], 1),
        jnp.concatenate([kv_other, kv_own, query_other, query_weight], 1),
    )
    pair = (pair.astype(jnp.float32) * gain).astype(jnp.bfloat16)
    out_other = swap(out_weight, "zero", 1)
    out_pair = jnp.where(
        core == 0,
        jnp.concatenate([out_weight, out_other], 0),
        jnp.concatenate([out_other, out_weight], 0),
    )
    ring_rows = shard_rows // 2
    rings = [
        Ring(pair[:ring_rows], core, pair),
        Ring(pair[ring_rows:], core, None, ring_rows),
    ]
    out_ring = Ring(out_pair, core)
    for part in range(4):
        for ring in rings:
            ring.advance(part, 4)
    held = rings[0].held + rings[1].held
    out_ring.advance(0, 4, rings[0].moving)

    far_blocks = [blocks[m] for m in range(2, zero_size, 2)]
    x_pieces = []
    for at, theirs in enumerate(deal([blocks[0]]) + deal(far_blocks)):
        x_pieces += [([blocks[0]] + far_blocks)[at], swap(theirs, "zero", 1)]

    half = head // 2
    frequency = jnp.power(
        jnp.float32(ROPE_BASE), -(jnp.arange(half, dtype=jnp.float32) * 2.0 / head)
    )
    local_token = jnp.arange(tokens // 2, dtype=jnp.int32)
    offsets = (2 * (local_token // size) + core) * size + local_token % size
    positions = ctx_rank * tokens + offsets
    angles = positions.astype(jnp.float32)[:, None] * frequency[None, :]
    cos_half, sin_half = jnp.cos(angles), jnp.sin(angles)
    cos = jnp.concatenate([cos_half, cos_half], -1)
    sin = jnp.concatenate([-sin_half, sin_half], -1)
    shrink = head ** (-0.5)

    near, scale = project(cos, cos, sin, x_pieces, held, 0, 2 * head, True)
    (queries,) = project(
        scale, cos * shrink, sin * shrink, x_pieces, held, 2 * head, 4 * head, False
    )
    beyond = [swap(out_weight, "zero", 2)]

    def share(part):
        while out_ring.at < out_ring.length * (part + 1) // 4:
            beyond.append(swap(out_ring.step(), "zero", 2))
        return beyond[-1]

    anchor = anchor_index[0]
    far = tied(near, beyond[0])
    for at in range(1, out_ring.at + 1):
        beyond.append(swap(out_ring.held[2 * at - 1][3], "zero", 2))
    bits = int(math.log2(ctx_size))
    for bit in range(bits):
        far = exchange_from(tied(far, queries, beyond[1]) if bit == bits - 1 else far, anchor, bit)
        if bit == 0:
            shared = share(1)
    share(2)
    queries = tied(queries, shared)
    share(3)
    near_other = swap(near, "zero", 1)
    far_other = swap(far, "zero", 1)
    far_mask = jnp.where(ctx_rank != anchor, anchor_mask[0], 0)
    keep, send = attend(
        groups, tile_mask[0], far_mask, queries, near, near_other, far, far_other
    )

    slots = []
    for steps, half_of, _, piece in out_ring.held:
        if half_of != 1:
            slots.append((steps, []))
        if steps <= 0:
            across = swap(beyond[-steps], "zero", 1)
        if steps == 0:
            pieces = [(0, None, piece), (1, 0, beyond[0]), (1, 1, across)]
        else:
            pieces = [(0, half_of, piece), (1, half_of, beyond[-steps] if steps < 0 else across)]
        slots[-1][1].extend(pieces)
    got = swap(send, "zero", 2)
    if zero_size == 4:
        return mix(keep, got, slots, jnp.bfloat16)
    total = mix(keep, got, slots, jnp.float32)
    stride = zero_size // 2
    while stride > 2:
        rows = total.shape[0] // 2
        bit = (zero_rank // stride) % 2
        stay = lax.dynamic_slice_in_dim(total, bit * rows, rows, 0)
        go = lax.dynamic_slice_in_dim(total, (1 - bit) * rows, rows, 0)
        total = stay + swap(go.astype(jnp.bfloat16), "zero", stride).astype(jnp.float32)
        stride //= 2
    return total.astype(jnp.bfloat16)


def solution(mesh):
    placed = (
        P("ctx", "zero"),
        P(),
        P("ctx", "zero"),
        P("ctx", "zero", None),
        P("zero", "ctx"),
        P("ctx", None, None),
        P("ctx", None, None),
        P(),
    )
    return jax.shard_map(
        local, mesh=mesh, in_specs=placed, out_specs=P(("ctx", "zero"), None), check_vma=False
    )
```

```python
import functools
import math

import jax
import jax.numpy as jnp
from jax import lax
from jax.experimental import pallas as pl
from jax.experimental.pallas import tpu as pltpu
from jax.sharding import PartitionSpec as P

HBM = pl.BlockSpec(memory_space=pltpu.HBM)
VMEM = pl.BlockSpec(memory_space=pltpu.VMEM)
SMEM = pl.BlockSpec(memory_space=pltpu.SMEM)
VMEM_LIMIT = 32 * 1024 * 1024
ROPE_BASE = 500000.0


def swap(value, axis, stride):
    pairs = [(source, source ^ stride) for source in range(lax.axis_size(axis))]
    return lax.ppermute(value, axis, pairs)


def cycle(size):
    return list(range(0, size, 2)) + list(range(1, size, 2))[::-1]


def ring_step(value):
    ctx_size, zero_size = lax.axis_size("ctx"), lax.axis_size("zero")
    order = cycle(ctx_size)
    pairs = []
    for at in range(ctx_size):
        for zero in range(zero_size):
            to = order[(at + (1 if zero % 2 == 0 else -1)) % ctx_size]
            pairs.append((order[at] * zero_size + zero, to * zero_size + zero))
    return lax.ppermute(value, ("ctx", "zero"), pairs)


class Ring:
    def __init__(self, shard, core, whole=None, base=0):
        self.held = [(0, None, 0, shard if whole is None else whole)] if base == 0 else []
        self.base = base
        self.moving, self.core, self.at = shard, core, 0
        self.length = lax.axis_size("ctx") // 2

    def step(self, *after):
        self.at += 1
        last = self.at == self.length
        if last:
            half = self.moving.shape[0] // 2
            self.moving = lax.dynamic_slice_in_dim(self.moving, self.core * half, half, 0)
        self.moving = ring_step(tied(self.moving, *after))
        self.held.append((-self.at, 0 if last else None, self.base, self.moving))
        self.held.append(
            (self.at, 1 if last else None, self.base, swap(self.moving, "zero", 1))
        )
        return self.moving

    def advance(self, part, parts, *after):
        while self.at < self.length * (part + 1) // parts:
            self.step(*after)
        return self.moving


def tied(value, *others):
    return lax.optimization_barrier((value, *others))[0] if others else value


def source_of(steps):
    size = lax.axis_size("ctx")
    ctx, core = lax.axis_index("ctx"), lax.axis_index("zero") % 2
    place = jnp.where(ctx % 2 == 0, ctx // 2, size - 1 - ctx // 2)
    place = lax.rem(place + steps * (1 - 2 * core) + size, size)
    return jnp.where(place < size // 2, 2 * place, 2 * (size - 1 - place) + 1)


def share_of(share):
    core = lax.axis_index("zero") % 2
    return core if share == 0 else 1 - core


def token_rows(group, other, size):
    core = lax.axis_index("zero") % 2
    if other:
        core = 1 - core
    return pl.ds(pl.multiple_of((2 * group + core) * size, 16), size)


def deal_kernel(count, *refs):
    x_refs, outs, sem = refs[:count], refs[count:-1], refs[-1]
    groups = lax.axis_size("zero") // 2
    size = x_refs[0].shape[0] // (2 * groups)
    copies = []
    for x_ref, out_ref in zip(x_refs, outs):
        for group in range(groups):
            copies.append(
                pltpu.make_async_copy(
                    x_ref.at[token_rows(group, True, size)],
                    out_ref.at[pl.ds(group * size, size)],
                    sem.at[len(copies)],
                )
            )
    for copy in copies:
        copy.start()
    for copy in copies:
        copy.wait()


def deal(arrays):
    tokens, depth = arrays[0].shape
    part = jax.ShapeDtypeStruct((tokens // 2, depth), arrays[0].dtype)
    copies = len(arrays) * lax.axis_size("zero") // 2
    return pl.pallas_call(
        functools.partial(deal_kernel, len(arrays)),
        out_shape=[part] * len(arrays),
        in_specs=[HBM] * len(arrays),
        out_specs=[HBM] * len(arrays),
        scratch_shapes=[pltpu.SemaphoreType.DMA((copies,))],
        compiler_params=pltpu.CompilerParams(vmem_limit_bytes=VMEM_LIMIT),
    )(*arrays)


def project_kernel(layout, *refs):
    (kv_ref, q_ref, x_buf, w_buf, x_sem, w_sem) = refs[-6:]
    pieces, tokens, depth = x_buf.shape
    cos_ref, sin_ref = refs[:2]
    x_refs = refs[2 : 2 + pieces]
    w_refs = refs[2 + pieces : -6]
    zero = lax.axis_index("zero")
    shard_rows = w_refs[0].shape[0]
    x_copies, w_copies = [], []
    for m, ref in enumerate(x_refs):
        target = x_buf.at[jnp.bitwise_xor(zero, m)]
        if m % 2:
            x_copies.append(pltpu.make_async_copy(ref, target, x_sem.at[len(x_copies)]))
            continue
        size = 2 * tokens // pieces
        for group in range(pieces // 2):
            x_copies.append(
                pltpu.make_async_copy(
                    ref.at[token_rows(group, False, size)],
                    target.at[pl.ds(group * size, size)],
                    x_sem.at[len(x_copies)],
                )
            )
    for at, (ref, (steps, share, base)) in enumerate(zip(w_refs, layout)):
        start = source_of(steps) * shard_rows + base
        if share is not None:
            start = start + share_of(share) * ref.shape[0]
        rows = pl.ds(pl.multiple_of(start, 16), ref.shape[0])
        w_copies.append(pltpu.make_async_copy(ref, w_buf.at[rows], w_sem.at[at]))
    for copy in x_copies + w_copies:
        copy.start()
    for copy in x_copies:
        copy.wait()
    squares = jnp.zeros((tokens, 128), jnp.float32)
    for at in range(pieces):
        for first in range(0, depth, 128):
            x_float = x_buf[at, :, first : first + 128].astype(jnp.float32)
            squares += x_float * x_float
    mean = jnp.sum(squares, axis=1, keepdims=True) / (depth * pieces)
    scale = jnp.broadcast_to(lax.rsqrt(mean + 1e-05), squares.shape)
    for copy in w_copies:
        copy.wait()
    head = cos_ref.shape[1]
    shrink = jnp.float32(head ** (-0.5))
    for out_ref, columns in ((kv_ref, 0), (q_ref, 2 * head)):
        for first in range(0, out_ref.shape[1], 2 * head):
            both = slice(columns + first, columns + first + 2 * head)
            total = jnp.zeros((tokens, 2 * head), jnp.float32)
            for at in range(pieces):
                total += jnp.dot(
                    x_buf[at],
                    w_buf[at * depth : (at + 1) * depth, both],
                    preferred_element_type=jnp.float32,
                )
            for at in range(2):
                part = total[:, at * head : (at + 1) * head] * scale
                if columns or not at:
                    part = part * cos_ref[...] + pltpu.roll(part, head // 2, 1) * sin_ref[...]
                if columns:
                    part = part * shrink
                out_ref[:, first + at * head : first + (at + 1) * head] = part.astype(
                    out_ref.dtype
                )


def project(cos, sin, x_pieces, held):
    layout = [(steps, share, base) for steps, share, base, _ in held]
    shards = [piece for _, _, _, piece in held]
    tokens, depth = x_pieces[1].shape
    pieces, head = len(x_pieces), cos.shape[1]
    width = shards[0].shape[1]
    full = depth * pieces
    return pl.pallas_call(
        functools.partial(project_kernel, layout),
        out_shape=[
            jax.ShapeDtypeStruct((tokens, 2 * head), jnp.bfloat16),
            jax.ShapeDtypeStruct((tokens, width - 2 * head), jnp.bfloat16),
        ],
        in_specs=[VMEM] * 2 + [HBM] * (pieces + len(shards)),
        out_specs=[VMEM] * 2,
        scratch_shapes=[
            pltpu.VMEM((pieces, tokens, depth), jnp.bfloat16),
            pltpu.VMEM((full, width), jnp.bfloat16),
            pltpu.SemaphoreType.DMA((pieces // 2 * (1 + pieces // 2),)),
            pltpu.SemaphoreType.DMA((len(shards),)),
        ],
        compiler_params=pltpu.CompilerParams(vmem_limit_bytes=VMEM_LIMIT),
        cost_estimate=pl.CostEstimate(
            flops=2 * tokens * full * width,
            bytes_accessed=2 * full * (tokens + width),
            transcendentals=0,
        ),
    )(cos, sin, *x_pieces, *shards)


def attend_kernel(groups, own_ref, far_ref, q_ref, near0, near1, far0, far1, keep, send):
    tokens, pair = near0.shape
    head = pair // 2
    size = tokens // groups
    tiles = own_ref.shape[0]
    tile = 2 * tokens // tiles
    heads = q_ref.shape[1] // head
    rows = heads * size
    core = lax.axis_index("zero") % 2
    column = lax.broadcasted_iota(jnp.int32, (1, tokens), 1)
    column_group = column // size
    within = lax.rem(lax.broadcasted_iota(jnp.int32, (rows, 1), 0), size)
    hidden = jnp.float32(-1e30)
    nt = (((1,), (1,)), ((), ()))
    for h in range(groups):
        across = slice(h * size, (h + 1) * size)
        q = jnp.concatenate(
            [q_ref[across, g * head : (g + 1) * head] for g in range(heads)], axis=0
        )
        first = (2 * h + core) * size
        own_tile = first // tile
        seen = min(tokens, -(-(h + 1) * size // 128) * 128)
        parts, blocks = [], []
        for ref, mask_ref, width, parity, causal in (
            (far0, far_ref, tokens, core, False),
            (far1, far_ref, tokens, 1 - core, False),
            (near0, own_ref, seen, core, True),
            (near1, own_ref, seen, 1 - core, True),
        ):
            visible = jnp.zeros((1, width), jnp.int32)
            for g in range(-(-width // size)):
                at = mask_ref[own_tile, (2 * g + parity) * size // tile]
                visible = jnp.where(column_group[:, :width] == g, at, visible)
            visible = visible == 1
            if causal:
                group = column_group[:, :width]
                offset = (2 * group + parity) * size + column[:, :width] - group * size
                visible = visible & (offset <= first + within)
            scores = lax.dot_general(
                q, ref[:width, :head], nt, preferred_element_type=jnp.float32
            )
            parts.append(jnp.where(visible, scores, hidden))
            blocks.append((ref, width))
        scores = jnp.concatenate(parts, axis=1)
        largest = jnp.max(scores, axis=1, keepdims=True)
        weights = jnp.exp(scores - largest)
        total = jnp.sum(weights, axis=1, keepdims=True)
        rounded = weights.astype(jnp.bfloat16)
        mixed = jnp.zeros((rows, head), jnp.float32)
        start = 0
        for ref, width in blocks:
            mixed += jnp.dot(
                rounded[:, start : start + width],
                ref[:width, head:],
                preferred_element_type=jnp.float32,
            )
            start += width
        mixed = (mixed / total).astype(keep.dtype)
        stays = lax.axis_index("zero") // 2 % 2 == h % 2
        rows_out = slice(h // 2 * size, (h // 2 + 1) * size)

        def store(out_ref, rows_out=rows_out, mixed=mixed):
            for g in range(heads):
                out_ref[rows_out, g * head : (g + 1) * head] = mixed[g * size : (g + 1) * size, :]

        pl.when(stays)(functools.partial(store, keep))
        pl.when(jnp.logical_not(stays))(functools.partial(store, send))


def attend(groups, own_mask, far_mask, queries, near, near_other, far, far_other):
    tokens, width = queries.shape
    return pl.pallas_call(
        functools.partial(attend_kernel, groups),
        out_shape=[jax.ShapeDtypeStruct((tokens // 2, width), jnp.bfloat16)] * 2,
        in_specs=[SMEM, SMEM] + [VMEM] * 5,
        out_specs=[VMEM] * 2,
        compiler_params=pltpu.CompilerParams(vmem_limit_bytes=VMEM_LIMIT),
        cost_estimate=pl.CostEstimate(
            flops=16 * tokens * tokens * width,
            bytes_accessed=8 * tokens * width,
            transcendentals=16 * tokens * tokens,
        ),
    )(own_mask, far_mask, queries, near, near_other, far, far_other)


def mix_kernel(layout, steps, *refs):
    a_refs, w_refs = refs[:2], refs[2 : 2 + len(layout)]
    out_ref, w_buf, sem = refs[2 + len(layout) :]
    width = w_buf.shape[2]
    half = a_refs[0].shape[1]
    copies = []
    for at, (ref, (slot, side, share)) in enumerate(zip(w_refs, layout)):
        rows = ref.shape[0]
        start = side * half
        if share is not None:
            start = pl.multiple_of(start + share_of(share) * rows, 16)
        copies.append(pltpu.make_async_copy(ref, w_buf.at[slot, pl.ds(start, rows)], sem.at[at]))
    for copy in copies:
        copy.start()
    both = jnp.concatenate([a_refs[0][...], a_refs[1][...]], axis=1)
    for slot, along in enumerate(steps):
        for copy, (its_slot, _, _) in zip(copies, layout):
            if its_slot == slot:
                copy.wait()
        total = jnp.dot(both, w_buf[slot], preferred_element_type=jnp.float32)
        start = pl.multiple_of(source_of(along) * width, 128)
        out_ref[:, pl.ds(start, width)] = total.astype(out_ref.dtype)


def mix(keep, got, slots, dtype):
    layout, shards = [], []
    for slot, (_, pieces) in enumerate(slots):
        for side, share, piece in pieces:
            layout.append((slot, side, share))
            shards.append(piece)
    rows, half = keep.shape
    width = shards[0].shape[1]
    columns = width * len(slots)
    return pl.pallas_call(
        functools.partial(mix_kernel, layout, [steps for steps, _ in slots]),
        out_shape=jax.ShapeDtypeStruct((rows, columns), dtype),
        in_specs=[VMEM, VMEM] + [HBM] * len(shards),
        out_specs=VMEM,
        scratch_shapes=[
            pltpu.VMEM((len(slots), 2 * half, width), jnp.bfloat16),
            pltpu.SemaphoreType.DMA((len(shards),)),
        ],
        compiler_params=pltpu.CompilerParams(vmem_limit_bytes=VMEM_LIMIT),
        cost_estimate=pl.CostEstimate(
            flops=4 * rows * half * columns,
            bytes_accessed=4 * half * (rows + columns) + 4 * rows * columns,
            transcendentals=0,
        ),
    )(keep, got, *shards)


def exchange_from(value, root, bit):
    other = swap(value, "ctx", 1 << bit)
    same = ((lax.axis_index("ctx") >> bit) & 1) == ((root >> bit) & 1)
    return jnp.where(same, value, other)


def local(
    activations,
    norm_gain,
    query_weight,
    kv_weight,
    out_weight,
    tile_mask,
    anchor_mask,
    anchor_index,
):
    tokens, depth = activations.shape
    head = kv_weight.shape[2]
    ctx_size, zero_size = lax.axis_size("ctx"), lax.axis_size("zero")
    ctx_rank, zero_rank = lax.axis_index("ctx"), lax.axis_index("zero")
    core = zero_rank % 2
    groups = zero_size // 2
    size = tokens // zero_size

    blocks = {0: activations}
    stride = groups
    while stride > 1:
        for known in range(0, zero_size, 2 * stride):
            blocks[known + stride] = swap(blocks[known], "zero", stride)
        stride //= 2

    shard_rows = kv_weight.shape[0]
    gain = lax.dynamic_slice_in_dim(norm_gain, ctx_rank * shard_rows, shard_rows)
    gain = gain.astype(jnp.float32)[:, None]
    kv_own = kv_weight[:, 0, :]
    kv_other, query_other = swap(kv_own, "zero", 1), swap(query_weight, "zero", 1)
    pair = jnp.where(
        core == 0,
        jnp.concatenate([kv_own, kv_other, query_weight, query_other], 1),
        jnp.concatenate([kv_other, kv_own, query_other, query_weight], 1),
    )
    pair = (pair.astype(jnp.float32) * gain).astype(jnp.bfloat16)
    out_other = swap(out_weight, "zero", 1)
    out_pair = jnp.where(
        core == 0,
        jnp.concatenate([out_weight, out_other], 0),
        jnp.concatenate([out_other, out_weight], 0),
    )
    ring_rows = shard_rows // 2
    rings = [
        Ring(pair[:ring_rows], core, pair),
        Ring(pair[ring_rows:], core, None, ring_rows),
    ]
    out_ring = Ring(out_pair, core)
    for part in range(4):
        for ring in rings:
            ring.advance(part, 4)
    held = rings[0].held + rings[1].held
    out_ring.advance(0, 4, *[ring.moving for ring in rings])

    far_blocks = [blocks[m] for m in range(2, zero_size, 2)]
    x_pieces = []
    for at, theirs in enumerate(deal([blocks[0]]) + deal(far_blocks)):
        x_pieces += [([blocks[0]] + far_blocks)[at], swap(theirs, "zero", 1)]

    half = head // 2
    frequency = jnp.power(
        jnp.float32(ROPE_BASE), -(jnp.arange(half, dtype=jnp.float32) * 2.0 / head)
    )
    local_token = jnp.arange(tokens // 2, dtype=jnp.int32)
    offsets = (2 * (local_token // size) + core) * size + local_token % size
    positions = ctx_rank * tokens + offsets
    angles = positions.astype(jnp.float32)[:, None] * frequency[None, :]
    cos_half, sin_half = jnp.cos(angles), jnp.sin(angles)
    cos = jnp.concatenate([cos_half, cos_half], -1)
    sin = jnp.concatenate([-sin_half, sin_half], -1)

    near, queries = project(cos, sin, x_pieces, held)
    beyond = [swap(out_weight, "zero", 2)]

    def share(part, *after):
        while out_ring.at < out_ring.length * (part + 1) // 4:
            beyond.append(swap(out_ring.step(*after), "zero", 2))
        return beyond[-1]

    anchor = anchor_index[0]
    far = tied(near, beyond[0])
    for at in range(1, out_ring.at + 1):
        beyond.append(swap(out_ring.held[2 * at - 1][3], "zero", 2))
    bits = int(math.log2(ctx_size))
    for bit in range(bits):
        far = exchange_from(tied(far, beyond[1]) if bit == bits - 1 else far, anchor, bit)
        if bit == 0:
            shared = share(1, near)
    share(2)
    queries = tied(queries, shared)
    share(3)
    near_other = swap(near, "zero", 1)
    far_other = swap(far, "zero", 1)
    far_mask = jnp.where(ctx_rank != anchor, anchor_mask[0], 0)
    keep, send = attend(
        groups, tile_mask[0], far_mask, queries, near, near_other, far, far_other
    )

    slots = []
    for steps, half_of, _, piece in out_ring.held:
        if half_of != 1:
            slots.append((steps, []))
        if steps <= 0:
            across = swap(beyond[-steps], "zero", 1)
        if steps == 0:
            pieces = [(0, None, piece), (1, 0, beyond[0]), (1, 1, across)]
        else:
            pieces = [(0, half_of, piece), (1, half_of, beyond[-steps] if steps < 0 else across)]
        slots[-1][1].extend(pieces)
    got = swap(send, "zero", 2)
    if zero_size == 4:
        return mix(keep, got, slots, jnp.bfloat16)
    total = mix(keep, got, slots, jnp.float32)
    stride = zero_size // 2
    while stride > 2:
        rows = total.shape[0] // 2
        bit = (zero_rank // stride) % 2
        stay = lax.dynamic_slice_in_dim(total, bit * rows, rows, 0)
        go = lax.dynamic_slice_in_dim(total, (1 - bit) * rows, rows, 0)
        total = stay + swap(go.astype(jnp.bfloat16), "zero", stride).astype(jnp.float32)
        stride //= 2
    return total.astype(jnp.bfloat16)


def solution(mesh):
    placed = (
        P("ctx", "zero"),
        P(),
        P("ctx", "zero"),
        P("ctx", "zero", None),
        P("zero", "ctx"),
        P("ctx", None, None),
        P("ctx", None, None),
        P(),
    )
    return jax.shard_map(
        local, mesh=mesh, in_specs=placed, out_specs=P(("ctx", "zero"), None), check_vma=False
    )
```

```python
import functools
import math

import jax
import jax.numpy as jnp
from jax import lax
from jax.experimental import pallas as pl
from jax.experimental.pallas import tpu as pltpu
from jax.sharding import PartitionSpec as P

HBM = pl.BlockSpec(memory_space=pltpu.HBM)
VMEM = pl.BlockSpec(memory_space=pltpu.VMEM)
SMEM = pl.BlockSpec(memory_space=pltpu.SMEM)
VMEM_LIMIT = 32 * 1024 * 1024
ROPE_BASE = 500000.0


def swap(value, axis, stride):
    pairs = [(source, source ^ stride) for source in range(lax.axis_size(axis))]
    return lax.ppermute(value, axis, pairs)


def cycle(size):
    return list(range(0, size, 2)) + list(range(1, size, 2))[::-1]


def ring_step(value):
    ctx_size, zero_size = lax.axis_size("ctx"), lax.axis_size("zero")
    order = cycle(ctx_size)
    pairs = []
    for at in range(ctx_size):
        for zero in range(zero_size):
            to = order[(at + (1 if zero % 2 == 0 else -1)) % ctx_size]
            pairs.append((order[at] * zero_size + zero, to * zero_size + zero))
    return lax.ppermute(value, ("ctx", "zero"), pairs)


class Ring:
    def __init__(self, shard, core, whole=None, base=0):
        self.held = [(0, None, 0, shard if whole is None else whole)] if base == 0 else []
        self.base = base
        self.moving, self.core, self.at = shard, core, 0
        self.length = lax.axis_size("ctx") // 2

    def step(self, *after):
        self.at += 1
        last = self.at == self.length
        if last:
            half = self.moving.shape[0] // 2
            self.moving = lax.dynamic_slice_in_dim(self.moving, self.core * half, half, 0)
        behind = self.held[-3][3:] if len(self.held) > 3 else []
        self.moving = ring_step(tied(self.moving, *behind, *after))
        self.held.append((-self.at, 0 if last else None, self.base, self.moving))
        self.held.append(
            (self.at, 1 if last else None, self.base, swap(self.moving, "zero", 1))
        )
        return self.moving

    def advance(self, part, parts, *after):
        while self.at < self.length * (part + 1) // parts:
            self.step(*after)
        return self.moving


def tied(value, *others):
    return lax.optimization_barrier((value, *others))[0] if others else value


def source_of(steps):
    size = lax.axis_size("ctx")
    ctx, core = lax.axis_index("ctx"), lax.axis_index("zero") % 2
    place = jnp.where(ctx % 2 == 0, ctx // 2, size - 1 - ctx // 2)
    place = lax.rem(place + steps * (1 - 2 * core) + size, size)
    return jnp.where(place < size // 2, 2 * place, 2 * (size - 1 - place) + 1)


def share_of(share):
    core = lax.axis_index("zero") % 2
    return core if share == 0 else 1 - core


def token_rows(group, other, size):
    core = lax.axis_index("zero") % 2
    if other:
        core = 1 - core
    return pl.ds(pl.multiple_of((2 * group + core) * size, 16), size)


def deal_kernel(count, *refs):
    x_refs, outs, sem = refs[:count], refs[count:-1], refs[-1]
    groups = lax.axis_size("zero") // 2
    size = x_refs[0].shape[0] // (2 * groups)
    copies = []
    for x_ref, out_ref in zip(x_refs, outs):
        for group in range(groups):
            copies.append(
                pltpu.make_async_copy(
                    x_ref.at[token_rows(group, True, size)],
                    out_ref.at[pl.ds(group * size, size)],
                    sem.at[len(copies)],
                )
            )
    for copy in copies:
        copy.start()
    for copy in copies:
        copy.wait()


def deal(arrays):
    tokens, depth = arrays[0].shape
    part = jax.ShapeDtypeStruct((tokens // 2, depth), arrays[0].dtype)
    copies = len(arrays) * lax.axis_size("zero") // 2
    return pl.pallas_call(
        functools.partial(deal_kernel, len(arrays)),
        out_shape=[part] * len(arrays),
        in_specs=[HBM] * len(arrays),
        out_specs=[HBM] * len(arrays),
        scratch_shapes=[pltpu.SemaphoreType.DMA((copies,))],
        compiler_params=pltpu.CompilerParams(vmem_limit_bytes=VMEM_LIMIT),
    )(*arrays)


def project_kernel(layout, *refs):
    (kv_ref, q_ref, x_buf, w_buf, x_sem, w_sem) = refs[-6:]
    pieces, tokens, depth = x_buf.shape
    cos_ref, sin_ref = refs[:2]
    x_refs = refs[2 : 2 + pieces]
    w_refs = refs[2 + pieces : -6]
    zero = lax.axis_index("zero")
    shard_rows = w_refs[0].shape[0]
    x_copies, w_copies = [], []
    for m, ref in enumerate(x_refs):
        target = x_buf.at[jnp.bitwise_xor(zero, m)]
        if m % 2:
            x_copies.append(pltpu.make_async_copy(ref, target, x_sem.at[len(x_copies)]))
            continue
        size = 2 * tokens // pieces
        for group in range(pieces // 2):
            x_copies.append(
                pltpu.make_async_copy(
                    ref.at[token_rows(group, False, size)],
                    target.at[pl.ds(group * size, size)],
                    x_sem.at[len(x_copies)],
                )
            )
    for at, (ref, (steps, share, base)) in enumerate(zip(w_refs, layout)):
        start = source_of(steps) * shard_rows + base
        if share is not None:
            start = start + share_of(share) * ref.shape[0]
        rows = pl.ds(pl.multiple_of(start, 16), ref.shape[0])
        w_copies.append(pltpu.make_async_copy(ref, w_buf.at[rows], w_sem.at[at]))
    for copy in x_copies + w_copies:
        copy.start()
    for copy in x_copies:
        copy.wait()
    squares = jnp.zeros((tokens, 128), jnp.float32)
    for at in range(pieces):
        for first in range(0, depth, 128):
            x_float = x_buf[at, :, first : first + 128].astype(jnp.float32)
            squares += x_float * x_float
    mean = jnp.sum(squares, axis=1, keepdims=True) / (depth * pieces)
    scale = jnp.broadcast_to(lax.rsqrt(mean + 1e-05), squares.shape)
    for copy in w_copies:
        copy.wait()
    head = cos_ref.shape[1]
    shrink = jnp.float32(head ** (-0.5))
    for out_ref, columns in ((kv_ref, 0), (q_ref, 2 * head)):
        for first in range(0, out_ref.shape[1], 2 * head):
            both = slice(columns + first, columns + first + 2 * head)
            total = jnp.zeros((tokens, 2 * head), jnp.float32)
            for at in range(pieces):
                total += jnp.dot(
                    x_buf[at],
                    w_buf[at * depth : (at + 1) * depth, both],
                    preferred_element_type=jnp.float32,
                )
            for at in range(2):
                part = total[:, at * head : (at + 1) * head] * scale
                if columns or not at:
                    part = part * cos_ref[...] + pltpu.roll(part, head // 2, 1) * sin_ref[...]
                if columns:
                    part = part * shrink
                out_ref[:, first + at * head : first + (at + 1) * head] = part.astype(
                    out_ref.dtype
                )


def project(cos, sin, x_pieces, held):
    layout = [(steps, share, base) for steps, share, base, _ in held]
    shards = [piece for _, _, _, piece in held]
    tokens, depth = x_pieces[1].shape
    pieces, head = len(x_pieces), cos.shape[1]
    width = shards[0].shape[1]
    full = depth * pieces
    return pl.pallas_call(
        functools.partial(project_kernel, layout),
        out_shape=[
            jax.ShapeDtypeStruct((tokens, 2 * head), jnp.bfloat16),
            jax.ShapeDtypeStruct((tokens, width - 2 * head), jnp.bfloat16),
        ],
        in_specs=[VMEM] * 2 + [HBM] * (pieces + len(shards)),
        out_specs=[VMEM] * 2,
        scratch_shapes=[
            pltpu.VMEM((pieces, tokens, depth), jnp.bfloat16),
            pltpu.VMEM((full, width), jnp.bfloat16),
            pltpu.SemaphoreType.DMA((pieces // 2 * (1 + pieces // 2),)),
            pltpu.SemaphoreType.DMA((len(shards),)),
        ],
        compiler_params=pltpu.CompilerParams(vmem_limit_bytes=VMEM_LIMIT),
        cost_estimate=pl.CostEstimate(
            flops=2 * tokens * full * width,
            bytes_accessed=2 * full * (tokens + width),
            transcendentals=0,
        ),
    )(cos, sin, *x_pieces, *shards)


def attend_kernel(groups, own_ref, far_ref, *refs):
    keep, send, q_ref, near0, near1, far0, far1, sem = refs[5:]
    copies = [
        pltpu.make_async_copy(source, target, sem.at[at])
        for at, (source, target) in enumerate(zip(refs[:5], refs[7:12]))
    ]
    for copy in copies:
        copy.start()
    for copy in copies:
        copy.wait()
    tokens, pair = near0.shape
    head = pair // 2
    size = tokens // groups
    tiles = own_ref.shape[0]
    tile = 2 * tokens // tiles
    heads = q_ref.shape[1] // head
    rows = heads * size
    core = lax.axis_index("zero") % 2
    column = lax.broadcasted_iota(jnp.int32, (1, tokens), 1)
    column_group = column // size
    within = lax.rem(lax.broadcasted_iota(jnp.int32, (rows, 1), 0), size)
    hidden = jnp.float32(-1e30)
    nt = (((1,), (1,)), ((), ()))
    for h in range(groups):
        across = slice(h * size, (h + 1) * size)
        q = jnp.concatenate(
            [q_ref[across, g * head : (g + 1) * head] for g in range(heads)], axis=0
        )
        first = (2 * h + core) * size
        own_tile = first // tile
        seen = min(tokens, -(-(h + 1) * size // 128) * 128)
        parts, blocks = [], []
        for ref, mask_ref, width, parity, causal in (
            (far0, far_ref, tokens, core, False),
            (far1, far_ref, tokens, 1 - core, False),
            (near0, own_ref, seen, core, True),
            (near1, own_ref, seen, 1 - core, True),
        ):
            visible = jnp.zeros((1, width), jnp.int32)
            for g in range(-(-width // size)):
                at = mask_ref[own_tile, (2 * g + parity) * size // tile]
                visible = jnp.where(column_group[:, :width] == g, at, visible)
            visible = visible == 1
            if causal:
                group = column_group[:, :width]
                offset = (2 * group + parity) * size + column[:, :width] - group * size
                visible = visible & (offset <= first + within)
            scores = lax.dot_general(
                q, ref[:width, :head], nt, preferred_element_type=jnp.float32
            )
            parts.append(jnp.where(visible, scores, hidden))
            blocks.append((ref, width))
        scores = jnp.concatenate(parts, axis=1)
        largest = jnp.max(scores, axis=1, keepdims=True)
        weights = jnp.exp(scores - largest)
        total = jnp.sum(weights, axis=1, keepdims=True)
        rounded = weights.astype(jnp.bfloat16)
        mixed = jnp.zeros((rows, head), jnp.float32)
        start = 0
        for ref, width in blocks:
            mixed += jnp.dot(
                rounded[:, start : start + width],
                ref[:width, head:],
                preferred_element_type=jnp.float32,
            )
            start += width
        mixed = (mixed / total).astype(keep.dtype)
        stays = lax.axis_index("zero") // 2 % 2 == h % 2
        rows_out = slice(h // 2 * size, (h // 2 + 1) * size)

        def store(out_ref, rows_out=rows_out, mixed=mixed):
            for g in range(heads):
                out_ref[rows_out, g * head : (g + 1) * head] = mixed[g * size : (g + 1) * size, :]

        pl.when(stays)(functools.partial(store, keep))
        pl.when(jnp.logical_not(stays))(functools.partial(store, send))


def attend(groups, own_mask, far_mask, queries, near, near_other, far, far_other):
    tokens, width = queries.shape
    return pl.pallas_call(
        functools.partial(attend_kernel, groups),
        out_shape=[jax.ShapeDtypeStruct((tokens // 2, width), jnp.bfloat16)] * 2,
        in_specs=[SMEM, SMEM] + [HBM] * 5,
        out_specs=[VMEM] * 2,
        scratch_shapes=[pltpu.VMEM(queries.shape, jnp.bfloat16)]
        + [pltpu.VMEM(near.shape, jnp.bfloat16)] * 4
        + [pltpu.SemaphoreType.DMA((5,))],
        compiler_params=pltpu.CompilerParams(vmem_limit_bytes=VMEM_LIMIT),
        cost_estimate=pl.CostEstimate(
            flops=16 * tokens * tokens * width,
            bytes_accessed=8 * tokens * width,
            transcendentals=16 * tokens * tokens,
        ),
    )(own_mask, far_mask, queries, near, near_other, far, far_other)


def mix_kernel(layout, slots, out_refs, *refs):
    count = len(refs) - len(layout) - out_refs - 2
    a_refs, w_refs = refs[:count], refs[count : count + len(layout)]
    outs = refs[count + len(layout) : -2]
    w_buf, sem = refs[-2:]
    width = w_buf.shape[2]
    half = a_refs[0].shape[1]
    copies = []
    for at, (ref, (slot, side, share)) in enumerate(zip(w_refs, layout)):
        rows = ref.shape[0]
        start = side * half
        if share is not None:
            start = pl.multiple_of(start + share_of(share) * rows, 16)
        copies.append(pltpu.make_async_copy(ref, w_buf.at[slot, pl.ds(start, rows)], sem.at[at]))
    for copy in copies:
        copy.start()
    slot = 0
    for out_ref, sides, number in zip(outs, *slots):
        rows = jnp.concatenate([ref[...] for ref in a_refs[:sides]], axis=1)
        for place in range(number):
            for copy, (its_slot, _, _) in zip(copies, layout):
                if its_slot == slot:
                    copy.wait()
            total = jnp.dot(
                rows, w_buf[slot, : sides * half], preferred_element_type=jnp.float32
            )
            out_ref[:, place * width : (place + 1) * width] = total.astype(out_ref.dtype)
            slot += 1


def mix(rows, blocks, dtypes):
    layout, shards = [], []
    sides = [1 + max(side for side, _, _ in block[0]) for block in blocks]
    slots = [slot for block in blocks for slot in block]
    for at, slot in enumerate(slots):
        for side, share, piece in slot:
            layout.append((at, side, share))
            shards.append(piece)
    tokens, half = rows[0].shape
    width = shards[0].shape[1]
    return pl.pallas_call(
        functools.partial(
            mix_kernel, layout, (sides, [len(block) for block in blocks]), len(blocks)
        ),
        out_shape=[
            jax.ShapeDtypeStruct((tokens, width * len(block)), dtype)
            for block, dtype in zip(blocks, dtypes)
        ],
        in_specs=[VMEM] * len(rows) + [HBM] * len(shards),
        out_specs=[VMEM] * len(blocks),
        scratch_shapes=[
            pltpu.VMEM((len(slots), max(sides) * half, width), jnp.bfloat16),
            pltpu.SemaphoreType.DMA((len(shards),)),
        ],
        compiler_params=pltpu.CompilerParams(vmem_limit_bytes=VMEM_LIMIT),
        cost_estimate=pl.CostEstimate(
            flops=2 * tokens * half * width * len(shards),
            bytes_accessed=6 * half * width * len(shards) + 4 * tokens * width * len(slots),
            transcendentals=0,
        ),
    )(*rows, *shards)


def join_kernel(steps, full_ref, keep_ref, got_ref, out_ref):
    width = out_ref.shape[1] // len(steps)
    whole = full_ref.shape[1] // width
    for slot, along in enumerate(steps):
        start = pl.multiple_of(source_of(along) * width, 128)
        if slot < whole:
            block = full_ref[:, slot * width : (slot + 1) * width]
        else:
            columns = slice((slot - whole) * width, (slot - whole + 1) * width)
            block = keep_ref[:, columns] + got_ref[:, columns].astype(jnp.float32)
        out_ref[:, pl.ds(start, width)] = block.astype(out_ref.dtype)


def join(steps, full, keep, got, dtype):
    rows = full.shape[0]
    columns = full.shape[1] + keep.shape[1]
    return pl.pallas_call(
        functools.partial(join_kernel, steps),
        out_shape=jax.ShapeDtypeStruct((rows, columns), dtype),
        in_specs=[VMEM] * 3,
        out_specs=VMEM,
        compiler_params=pltpu.CompilerParams(vmem_limit_bytes=VMEM_LIMIT),
        cost_estimate=pl.CostEstimate(
            flops=rows * columns, bytes_accessed=8 * rows * columns, transcendentals=0
        ),
    )(full, keep, got)


def exchange_from(value, root, bit):
    other = swap(value, "ctx", 1 << bit)
    same = ((lax.axis_index("ctx") >> bit) & 1) == ((root >> bit) & 1)
    return jnp.where(same, value, other)


def local(
    activations,
    norm_gain,
    query_weight,
    kv_weight,
    out_weight,
    tile_mask,
    anchor_mask,
    anchor_index,
):
    tokens, depth = activations.shape
    head = kv_weight.shape[2]
    ctx_size, zero_size = lax.axis_size("ctx"), lax.axis_size("zero")
    ctx_rank, zero_rank = lax.axis_index("ctx"), lax.axis_index("zero")
    core = zero_rank % 2
    groups = zero_size // 2
    size = tokens // zero_size

    blocks = {0: activations}
    stride = groups
    while stride > 1:
        for known in range(0, zero_size, 2 * stride):
            blocks[known + stride] = swap(blocks[known], "zero", stride)
        stride //= 2

    shard_rows = kv_weight.shape[0]
    gain = lax.dynamic_slice_in_dim(norm_gain, ctx_rank * shard_rows, shard_rows)
    gain = gain.astype(jnp.float32)[:, None]
    kv_own = kv_weight[:, 0, :]
    kv_other, query_other = swap(kv_own, "zero", 1), swap(query_weight, "zero", 1)
    pair = jnp.where(
        core == 0,
        jnp.concatenate([kv_own, kv_other, query_weight, query_other], 1),
        jnp.concatenate([kv_other, kv_own, query_other, query_weight], 1),
    )
    pair = (pair.astype(jnp.float32) * gain).astype(jnp.bfloat16)
    out_other = swap(out_weight, "zero", 1)
    out_pair = jnp.where(
        core == 0,
        jnp.concatenate([out_weight, out_other], 0),
        jnp.concatenate([out_other, out_weight], 0),
    )
    ring_rows = shard_rows // 2
    rings = [
        Ring(pair[:ring_rows], core, pair),
        Ring(pair[ring_rows:], core, None, ring_rows),
    ]
    out_ring = Ring(out_pair, core)
    for part in range(4):
        for ring in rings:
            ring.advance(part, 4)
    held = rings[0].held + rings[1].held
    beyond = [swap(out_weight, "zero", 2)]
    out_ring.advance(0, 4, *[ring.moving for ring in rings], *beyond)

    far_blocks = [tied(blocks[m], rings[0].moving) for m in range(2, zero_size, 2)]
    x_pieces = []
    for at, theirs in enumerate(deal([blocks[0]]) + deal(far_blocks)):
        x_pieces += [([blocks[0]] + far_blocks)[at], swap(theirs, "zero", 1)]

    half = head // 2
    frequency = jnp.power(
        jnp.float32(ROPE_BASE), -(jnp.arange(half, dtype=jnp.float32) * 2.0 / head)
    )
    local_token = jnp.arange(tokens // 2, dtype=jnp.int32)
    offsets = (2 * (local_token // size) + core) * size + local_token % size
    positions = ctx_rank * tokens + offsets
    angles = positions.astype(jnp.float32)[:, None] * frequency[None, :]
    cos_half, sin_half = jnp.cos(angles), jnp.sin(angles)
    cos = jnp.concatenate([cos_half, cos_half], -1)
    sin = jnp.concatenate([-sin_half, sin_half], -1)

    near, queries = project(cos, sin, x_pieces, held)

    def share():
        for at in range(len(beyond), out_ring.at + 1):
            beyond.append(swap(out_ring.held[2 * at - 1][3], "zero", 2))

    share()
    anchor = anchor_index[0]
    far = tied(near, out_ring.moving)
    for bit in range(int(math.log2(ctx_size))):
        far = exchange_from(far, anchor, bit)
        if bit < 2:
            out_ring.advance(1 + bit, 4, far)
        if bit == 0:
            share()
    out_ring.advance(3, 4)
    queries = tied(queries, beyond[-1])
    near_other = swap(near, "zero", 1)
    far_other = swap(far, "zero", 1)
    far_mask = jnp.where(ctx_rank != anchor, anchor_mask[0], 0)
    keep, send = attend(
        groups, tile_mask[0], far_mask, queries, near, near_other, far, far_other
    )

    steps_of, both_chips, one_chip = [], [], []
    for steps, half_of, _, piece in out_ring.held:
        slots = both_chips if abs(steps) < len(beyond) else one_chip
        if half_of != 1:
            steps_of.append(steps)
            slots.append([])
        slots[-1].append((0, half_of, piece))
        if slots is both_chips:
            if steps <= 0:
                across = swap(beyond[-steps], "zero", 1)
            if steps == 0:
                slots[-1] += [(1, 0, beyond[0]), (1, 1, across)]
            else:
                slots[-1].append((1, half_of, beyond[-steps] if steps < 0 else across))
    got = swap(send, "zero", 2)
    (terms,) = mix([send], [one_chip], [jnp.bfloat16])
    got_terms = swap(tied(terms, got), "zero", 2)
    full, kept = mix([keep, got], [both_chips, one_chip], [jnp.float32, jnp.float32])
    if zero_size == 4:
        return join(steps_of, full, kept, got_terms, jnp.bfloat16)
    total = join(steps_of, full, kept, got_terms, jnp.float32)
    stride = zero_size // 2
    while stride > 2:
        rows = total.shape[0] // 2
        bit = (zero_rank // stride) % 2
        stay = lax.dynamic_slice_in_dim(total, bit * rows, rows, 0)
        go = lax.dynamic_slice_in_dim(total, (1 - bit) * rows, rows, 0)
        total = stay + swap(go.astype(jnp.bfloat16), "zero", stride).astype(jnp.float32)
        stride //= 2
    return total.astype(jnp.bfloat16)


def solution(mesh):
    placed = (
        P("ctx", "zero"),
        P(),
        P("ctx", "zero"),
        P("ctx", "zero", None),
        P("zero", "ctx"),
        P("ctx", None, None),
        P("ctx", None, None),
        P(),
    )
    return jax.shard_map(
        local, mesh=mesh, in_specs=placed, out_specs=P(("ctx", "zero"), None), check_vma=False
    )
```

```python
import functools
import math

import jax
import jax.numpy as jnp
from jax import lax
from jax.experimental import pallas as pl
from jax.experimental.pallas import tpu as pltpu
from jax.sharding import PartitionSpec as P

HBM = pl.BlockSpec(memory_space=pltpu.HBM)
VMEM = pl.BlockSpec(memory_space=pltpu.VMEM)
SMEM = pl.BlockSpec(memory_space=pltpu.SMEM)
VMEM_LIMIT = 32 * 1024 * 1024
ROPE_BASE = 500000.0


def swap(value, axis, stride):
    pairs = [(source, source ^ stride) for source in range(lax.axis_size(axis))]
    return lax.ppermute(value, axis, pairs)


def cycle(size):
    return list(range(0, size, 2)) + list(range(1, size, 2))[::-1]


def ring_step(value):
    ctx_size, zero_size = lax.axis_size("ctx"), lax.axis_size("zero")
    order = cycle(ctx_size)
    pairs = []
    for at in range(ctx_size):
        for zero in range(zero_size):
            to = order[(at + (1 if zero % 2 == 0 else -1)) % ctx_size]
            pairs.append((order[at] * zero_size + zero, to * zero_size + zero))
    return lax.ppermute(value, ("ctx", "zero"), pairs)


class Ring:
    def __init__(self, shard, core, whole=None, base=0):
        self.held = [(0, None, 0, shard if whole is None else whole)] if base == 0 else []
        self.base = base
        self.moving, self.core, self.at = shard, core, 0
        self.length = lax.axis_size("ctx") // 2

    def step(self, *after):
        self.at += 1
        last = self.at == self.length
        if last:
            half = self.moving.shape[0] // 2
            self.moving = lax.dynamic_slice_in_dim(self.moving, self.core * half, half, 0)
        behind = self.held[-3][3:] if len(self.held) > 3 else []
        self.moving = ring_step(tied(self.moving, *behind, *after))
        self.held.append((-self.at, 0 if last else None, self.base, self.moving))
        self.held.append(
            (self.at, 1 if last else None, self.base, swap(self.moving, "zero", 1))
        )
        return self.moving

    def advance(self, part, parts, *after):
        while self.at < self.length * (part + 1) // parts:
            self.step(*after)
        return self.moving


def tied(value, *others):
    return lax.optimization_barrier((value, *others))[0] if others else value


def source_of(steps):
    size = lax.axis_size("ctx")
    ctx, core = lax.axis_index("ctx"), lax.axis_index("zero") % 2
    place = jnp.where(ctx % 2 == 0, ctx // 2, size - 1 - ctx // 2)
    place = lax.rem(place + steps * (1 - 2 * core) + size, size)
    return jnp.where(place < size // 2, 2 * place, 2 * (size - 1 - place) + 1)


def share_of(share):
    core = lax.axis_index("zero") % 2
    return core if share == 0 else 1 - core


def token_rows(group, other, size):
    core = lax.axis_index("zero") % 2
    if other:
        core = 1 - core
    return pl.ds(pl.multiple_of((2 * group + core) * size, 16), size)


def deal_kernel(count, *refs):
    x_refs, outs, sem = refs[:count], refs[count:-1], refs[-1]
    groups = lax.axis_size("zero") // 2
    size = x_refs[0].shape[0] // (2 * groups)
    copies = []
    for x_ref, out_ref in zip(x_refs, outs):
        for group in range(groups):
            copies.append(
                pltpu.make_async_copy(
                    x_ref.at[token_rows(group, True, size)],
                    out_ref.at[pl.ds(group * size, size)],
                    sem.at[len(copies)],
                )
            )
    for copy in copies:
        copy.start()
    for copy in copies:
        copy.wait()


def deal(arrays):
    tokens, depth = arrays[0].shape
    part = jax.ShapeDtypeStruct((tokens // 2, depth), arrays[0].dtype)
    copies = len(arrays) * lax.axis_size("zero") // 2
    return pl.pallas_call(
        functools.partial(deal_kernel, len(arrays)),
        out_shape=[part] * len(arrays),
        in_specs=[HBM] * len(arrays),
        out_specs=[HBM] * len(arrays),
        scratch_shapes=[pltpu.SemaphoreType.DMA((copies,))],
        compiler_params=pltpu.CompilerParams(vmem_limit_bytes=VMEM_LIMIT),
    )(*arrays)


def project_kernel(layout, *refs):
    (kv_ref, q_ref, x_buf, w_buf, x_sem, w_sem) = refs[-6:]
    pieces, tokens, depth = x_buf.shape
    cos_ref, sin_ref = refs[:2]
    x_refs = refs[2 : 2 + pieces]
    w_refs = refs[2 + pieces : -6]
    zero = lax.axis_index("zero")
    shard_rows = w_refs[0].shape[0]
    x_copies, w_copies = [], []
    for m, ref in enumerate(x_refs):
        target = x_buf.at[jnp.bitwise_xor(zero, m)]
        if m % 2:
            x_copies.append(pltpu.make_async_copy(ref, target, x_sem.at[len(x_copies)]))
            continue
        size = 2 * tokens // pieces
        for group in range(pieces // 2):
            x_copies.append(
                pltpu.make_async_copy(
                    ref.at[token_rows(group, False, size)],
                    target.at[pl.ds(group * size, size)],
                    x_sem.at[len(x_copies)],
                )
            )
    for at, (ref, (steps, share, base)) in enumerate(zip(w_refs, layout)):
        start = source_of(steps) * shard_rows + base
        if share is not None:
            start = start + share_of(share) * ref.shape[0]
        rows = pl.ds(pl.multiple_of(start, 16), ref.shape[0])
        w_copies.append(pltpu.make_async_copy(ref, w_buf.at[rows], w_sem.at[at]))
    for copy in x_copies + w_copies:
        copy.start()
    for copy in x_copies:
        copy.wait()
    squares = jnp.zeros((tokens, 128), jnp.float32)
    for at in range(pieces):
        for first in range(0, depth, 128):
            x_float = x_buf[at, :, first : first + 128].astype(jnp.float32)
            squares += x_float * x_float
    mean = jnp.sum(squares, axis=1, keepdims=True) / (depth * pieces)
    scale = jnp.broadcast_to(lax.rsqrt(mean + 1e-05), squares.shape)
    for copy in w_copies:
        copy.wait()
    head = cos_ref.shape[1]
    shrink = jnp.float32(head ** (-0.5))
    for out_ref, columns in ((kv_ref, 0), (q_ref, 2 * head)):
        for first in range(0, out_ref.shape[1], 2 * head):
            both = slice(columns + first, columns + first + 2 * head)
            total = jnp.zeros((tokens, 2 * head), jnp.float32)
            for at in range(pieces):
                total += jnp.dot(
                    x_buf[at],
                    w_buf[at * depth : (at + 1) * depth, both],
                    preferred_element_type=jnp.float32,
                )
            for at in range(2):
                part = total[:, at * head : (at + 1) * head] * scale
                if columns or not at:
                    part = part * cos_ref[...] + pltpu.roll(part, head // 2, 1) * sin_ref[...]
                if columns:
                    part = part * shrink
                out_ref[:, first + at * head : first + (at + 1) * head] = part.astype(
                    out_ref.dtype
                )


def project(cos, sin, x_pieces, held):
    layout = [(steps, share, base) for steps, share, base, _ in held]
    shards = [piece for _, _, _, piece in held]
    tokens, depth = x_pieces[1].shape
    pieces, head = len(x_pieces), cos.shape[1]
    width = shards[0].shape[1]
    full = depth * pieces
    return pl.pallas_call(
        functools.partial(project_kernel, layout),
        out_shape=[
            jax.ShapeDtypeStruct((tokens, 2 * head), jnp.bfloat16),
            jax.ShapeDtypeStruct((tokens, width - 2 * head), jnp.bfloat16),
        ],
        in_specs=[VMEM] * 2 + [HBM] * (pieces + len(shards)),
        out_specs=[VMEM] * 2,
        scratch_shapes=[
            pltpu.VMEM((pieces, tokens, depth), jnp.bfloat16),
            pltpu.VMEM((full, width), jnp.bfloat16),
            pltpu.SemaphoreType.DMA((pieces // 2 * (1 + pieces // 2),)),
            pltpu.SemaphoreType.DMA((len(shards),)),
        ],
        compiler_params=pltpu.CompilerParams(vmem_limit_bytes=VMEM_LIMIT),
        cost_estimate=pl.CostEstimate(
            flops=2 * tokens * full * width,
            bytes_accessed=2 * full * (tokens + width),
            transcendentals=0,
        ),
    )(cos, sin, *x_pieces, *shards)


def attend_kernel(groups, stays, own_ref, far_ref, *refs):
    out_ref, q_ref, near0, near1, far0, far1, sem = refs[5:]
    copies = [
        pltpu.make_async_copy(source, target, sem.at[at])
        for at, (source, target) in enumerate(zip(refs[:5], refs[6:11]))
    ]
    for copy in copies:
        copy.start()
    for copy in copies:
        copy.wait()
    tokens, pair = near0.shape
    head = pair // 2
    size = tokens // groups
    tiles = own_ref.shape[0]
    tile = 2 * tokens // tiles
    heads = q_ref.shape[1] // head
    rows = heads * size
    core = lax.axis_index("zero") % 2
    column = lax.broadcasted_iota(jnp.int32, (1, tokens), 1)
    column_group = column // size
    within = lax.rem(lax.broadcasted_iota(jnp.int32, (rows, 1), 0), size)
    hidden = jnp.float32(-1e30)
    nt = (((1,), (1,)), ((), ()))
    side = lax.axis_index("zero") // 2 % 2
    for pair_of in range(groups // 2):
        h = 2 * pair_of + (side if stays else 1 - side)
        across = pl.ds(pl.multiple_of(h * size, 16), size)
        q = jnp.concatenate(
            [q_ref[across, g * head : (g + 1) * head] for g in range(heads)], axis=0
        )
        first = (2 * h + core) * size
        own_tile = first // tile
        seen = min(tokens, -(-(2 * pair_of + 2) * size // 128) * 128)
        parts, blocks = [], []
        for ref, mask_ref, width, parity, causal in (
            (far0, far_ref, tokens, core, False),
            (far1, far_ref, tokens, 1 - core, False),
            (near0, own_ref, seen, core, True),
            (near1, own_ref, seen, 1 - core, True),
        ):
            visible = jnp.zeros((1, width), jnp.int32)
            for g in range(-(-width // size)):
                at = mask_ref[own_tile, (2 * g + parity) * size // tile]
                visible = jnp.where(column_group[:, :width] == g, at, visible)
            visible = visible == 1
            if causal:
                group = column_group[:, :width]
                offset = (2 * group + parity) * size + column[:, :width] - group * size
                visible = visible & (offset <= first + within)
            scores = lax.dot_general(
                q, ref[:width, :head], nt, preferred_element_type=jnp.float32
            )
            parts.append(jnp.where(visible, scores, hidden))
            blocks.append((ref, width))
        scores = jnp.concatenate(parts, axis=1)
        largest = jnp.max(scores, axis=1, keepdims=True)
        weights = jnp.exp(scores - largest)
        total = jnp.sum(weights, axis=1, keepdims=True)
        rounded = weights.astype(jnp.bfloat16)
        mixed = jnp.zeros((rows, head), jnp.float32)
        start = 0
        for ref, width in blocks:
            mixed += jnp.dot(
                rounded[:, start : start + width],
                ref[:width, head:],
                preferred_element_type=jnp.float32,
            )
            start += width
        mixed = (mixed / total).astype(out_ref.dtype)
        for g in range(heads):
            out_ref[pair_of * size : (pair_of + 1) * size, g * head : (g + 1) * head] = mixed[
                g * size : (g + 1) * size, :
            ]


def attend(groups, stays, own_mask, far_mask, queries, near, near_other, far, far_other):
    tokens, width = queries.shape
    return pl.pallas_call(
        functools.partial(attend_kernel, groups, stays),
        out_shape=jax.ShapeDtypeStruct((tokens // 2, width), jnp.bfloat16),
        in_specs=[SMEM, SMEM] + [HBM] * 5,
        out_specs=VMEM,
        scratch_shapes=[pltpu.VMEM(queries.shape, jnp.bfloat16)]
        + [pltpu.VMEM(near.shape, jnp.bfloat16)] * 4
        + [pltpu.SemaphoreType.DMA((5,))],
        compiler_params=pltpu.CompilerParams(vmem_limit_bytes=VMEM_LIMIT),
        cost_estimate=pl.CostEstimate(
            flops=8 * tokens * tokens * width,
            bytes_accessed=8 * tokens * width,
            transcendentals=8 * tokens * tokens,
        ),
    )(own_mask, far_mask, queries, near, near_other, far, far_other)


def mix_kernel(layout, slots, out_refs, *refs):
    count = len(refs) - len(layout) - out_refs - 2
    a_refs, w_refs = refs[:count], refs[count : count + len(layout)]
    outs = refs[count + len(layout) : -2]
    w_buf, sem = refs[-2:]
    width = w_buf.shape[2]
    half = a_refs[0].shape[1]
    copies = []
    for at, (ref, (slot, side, share)) in enumerate(zip(w_refs, layout)):
        rows = ref.shape[0]
        start = side * half
        if share is not None:
            start = pl.multiple_of(start + share_of(share) * rows, 16)
        copies.append(pltpu.make_async_copy(ref, w_buf.at[slot, pl.ds(start, rows)], sem.at[at]))
    for copy in copies:
        copy.start()
    slot = 0
    for out_ref, sides, number in zip(outs, *slots):
        rows = jnp.concatenate([ref[...] for ref in a_refs[:sides]], axis=1)
        for place in range(number):
            for copy, (its_slot, _, _) in zip(copies, layout):
                if its_slot == slot:
                    copy.wait()
            total = jnp.dot(
                rows, w_buf[slot, : sides * half], preferred_element_type=jnp.float32
            )
            out_ref[:, place * width : (place + 1) * width] = total.astype(out_ref.dtype)
            slot += 1


def mix(rows, blocks, dtypes):
    layout, shards = [], []
    sides = [1 + max(side for side, _, _ in block[0]) for block in blocks]
    slots = [slot for block in blocks for slot in block]
    for at, slot in enumerate(slots):
        for side, share, piece in slot:
            layout.append((at, side, share))
            shards.append(piece)
    tokens, half = rows[0].shape
    width = shards[0].shape[1]
    return pl.pallas_call(
        functools.partial(
            mix_kernel, layout, (sides, [len(block) for block in blocks]), len(blocks)
        ),
        out_shape=[
            jax.ShapeDtypeStruct((tokens, width * len(block)), dtype)
            for block, dtype in zip(blocks, dtypes)
        ],
        in_specs=[VMEM] * len(rows) + [HBM] * len(shards),
        out_specs=[VMEM] * len(blocks),
        scratch_shapes=[
            pltpu.VMEM((len(slots), max(sides) * half, width), jnp.bfloat16),
            pltpu.SemaphoreType.DMA((len(shards),)),
        ],
        compiler_params=pltpu.CompilerParams(vmem_limit_bytes=VMEM_LIMIT),
        cost_estimate=pl.CostEstimate(
            flops=2 * tokens * half * width * len(shards),
            bytes_accessed=6 * half * width * len(shards) + 4 * tokens * width * len(slots),
            transcendentals=0,
        ),
    )(*rows, *shards)


def join_kernel(steps, full_ref, keep_ref, got_ref, out_ref):
    width = out_ref.shape[1] // len(steps)
    whole = full_ref.shape[1] // width
    for slot, along in enumerate(steps):
        start = pl.multiple_of(source_of(along) * width, 128)
        if slot < whole:
            block = full_ref[:, slot * width : (slot + 1) * width]
        else:
            columns = slice((slot - whole) * width, (slot - whole + 1) * width)
            block = keep_ref[:, columns] + got_ref[:, columns].astype(jnp.float32)
        out_ref[:, pl.ds(start, width)] = block.astype(out_ref.dtype)


def join(steps, full, keep, got, dtype):
    rows = full.shape[0]
    columns = full.shape[1] + keep.shape[1]
    return pl.pallas_call(
        functools.partial(join_kernel, steps),
        out_shape=jax.ShapeDtypeStruct((rows, columns), dtype),
        in_specs=[VMEM] * 3,
        out_specs=VMEM,
        compiler_params=pltpu.CompilerParams(vmem_limit_bytes=VMEM_LIMIT),
        cost_estimate=pl.CostEstimate(
            flops=rows * columns, bytes_accessed=8 * rows * columns, transcendentals=0
        ),
    )(full, keep, got)


def exchange_from(value, root, bit):
    other = swap(value, "ctx", 1 << bit)
    same = ((lax.axis_index("ctx") >> bit) & 1) == ((root >> bit) & 1)
    return jnp.where(same, value, other)


def local(
    activations,
    norm_gain,
    query_weight,
    kv_weight,
    out_weight,
    tile_mask,
    anchor_mask,
    anchor_index,
):
    tokens, depth = activations.shape
    head = kv_weight.shape[2]
    ctx_size, zero_size = lax.axis_size("ctx"), lax.axis_size("zero")
    ctx_rank, zero_rank = lax.axis_index("ctx"), lax.axis_index("zero")
    core = zero_rank % 2
    groups = zero_size // 2
    size = tokens // zero_size

    blocks = {0: activations}
    stride = groups
    while stride > 1:
        for known in range(0, zero_size, 2 * stride):
            blocks[known + stride] = swap(blocks[known], "zero", stride)
        stride //= 2

    shard_rows = kv_weight.shape[0]
    gain = lax.dynamic_slice_in_dim(norm_gain, ctx_rank * shard_rows, shard_rows)
    gain = gain.astype(jnp.float32)[:, None]
    kv_own = kv_weight[:, 0, :]
    kv_other, query_other = swap(kv_own, "zero", 1), swap(query_weight, "zero", 1)
    pair = jnp.where(
        core == 0,
        jnp.concatenate([kv_own, kv_other, query_weight, query_other], 1),
        jnp.concatenate([kv_other, kv_own, query_other, query_weight], 1),
    )
    pair = (pair.astype(jnp.float32) * gain).astype(jnp.bfloat16)
    out_other = swap(out_weight, "zero", 1)
    out_pair = jnp.where(
        core == 0,
        jnp.concatenate([out_weight, out_other], 0),
        jnp.concatenate([out_other, out_weight], 0),
    )
    ring_rows = shard_rows // 2
    rings = [
        Ring(pair[:ring_rows], core, pair),
        Ring(pair[ring_rows:], core, None, ring_rows),
    ]
    out_ring = Ring(out_pair, core)
    for part in range(4):
        for ring in rings:
            ring.advance(part, 4)
    held = rings[0].held + rings[1].held
    beyond = [swap(out_weight, "zero", 2)]
    out_ring.advance(0, 4, *[ring.moving for ring in rings], *beyond)

    far_blocks = [tied(blocks[m], rings[0].moving) for m in range(2, zero_size, 2)]
    x_pieces = []
    for at, theirs in enumerate(deal([blocks[0]]) + deal(far_blocks)):
        x_pieces += [([blocks[0]] + far_blocks)[at], swap(theirs, "zero", 1)]

    half = head // 2
    frequency = jnp.power(
        jnp.float32(ROPE_BASE), -(jnp.arange(half, dtype=jnp.float32) * 2.0 / head)
    )
    local_token = jnp.arange(tokens // 2, dtype=jnp.int32)
    offsets = (2 * (local_token // size) + core) * size + local_token % size
    positions = ctx_rank * tokens + offsets
    angles = positions.astype(jnp.float32)[:, None] * frequency[None, :]
    cos_half, sin_half = jnp.cos(angles), jnp.sin(angles)
    cos = jnp.concatenate([cos_half, cos_half], -1)
    sin = jnp.concatenate([-sin_half, sin_half], -1)

    near, queries = project(cos, sin, x_pieces, held)

    def share():
        for at in range(len(beyond), out_ring.at + 1):
            beyond.append(swap(out_ring.held[2 * at - 1][3], "zero", 2))

    share()
    anchor = anchor_index[0]
    far = tied(near, out_ring.moving)
    bits = int(math.log2(ctx_size))
    for bit in range(bits):
        far = exchange_from(far, anchor, bit)
        if bit == 0:
            first = beyond[-1]
            out_ring.advance(1, 4, far)
            share()
        elif bit == 1:
            out_ring.advance(2, 4, far, first)
    queries = tied(queries, beyond[-1])
    near_other = swap(near, "zero", 1)
    far_other = swap(far, "zero", 1)
    out_ring.advance(3, 4, far_other)
    far_mask = jnp.where(ctx_rank != anchor, anchor_mask[0], 0)
    both_blocks = (near, near_other, far, far_other)
    send = attend(groups, False, tile_mask[0], far_mask, queries, *both_blocks)
    got = swap(send, "zero", 2)
    out_ring.held[-1] = (
        *out_ring.held[-1][:3],
        swap(tied(out_ring.moving, send), "zero", 1),
    )
    keep = attend(groups, True, tile_mask[0], far_mask, queries, *both_blocks)

    steps_of, both_chips, one_chip = [], [], []
    for steps, half_of, _, piece in out_ring.held:
        slots = both_chips if abs(steps) < len(beyond) else one_chip
        if half_of != 1:
            steps_of.append(steps)
            slots.append([])
        slots[-1].append((0, half_of, piece))
        if slots is both_chips:
            if steps <= 0:
                across = swap(beyond[-steps], "zero", 1)
            if steps == 0:
                slots[-1] += [(1, 0, beyond[0]), (1, 1, across)]
            else:
                slots[-1].append((1, half_of, beyond[-steps] if steps < 0 else across))
    (terms,) = mix([send], [one_chip], [jnp.bfloat16])
    got_terms = swap(tied(terms, got), "zero", 2)
    full, kept = mix([keep, got], [both_chips, one_chip], [jnp.float32, jnp.float32])
    if zero_size == 4:
        return join(steps_of, full, kept, got_terms, jnp.bfloat16)
    total = join(steps_of, full, kept, got_terms, jnp.float32)
    stride = zero_size // 2
    while stride > 2:
        rows = total.shape[0] // 2
        bit = (zero_rank // stride) % 2
        stay = lax.dynamic_slice_in_dim(total, bit * rows, rows, 0)
        go = lax.dynamic_slice_in_dim(total, (1 - bit) * rows, rows, 0)
        total = stay + swap(go.astype(jnp.bfloat16), "zero", stride).astype(jnp.float32)
        stride //= 2
    return total.astype(jnp.bfloat16)


def solution(mesh):
    placed = (
        P("ctx", "zero"),
        P(),
        P("ctx", "zero"),
        P("ctx", "zero", None),
        P("zero", "ctx"),
        P("ctx", None, None),
        P("ctx", None, None),
        P(),
    )
    return jax.shard_map(
        local, mesh=mesh, in_specs=placed, out_specs=P(("ctx", "zero"), None), check_vma=False
    )
```

```python
import functools
import math

import jax
import jax.numpy as jnp
from jax import lax
from jax.experimental import pallas as pl
from jax.experimental.pallas import tpu as pltpu
from jax.sharding import PartitionSpec as P

HBM = pl.BlockSpec(memory_space=pltpu.HBM)
VMEM = pl.BlockSpec(memory_space=pltpu.VMEM)
SMEM = pl.BlockSpec(memory_space=pltpu.SMEM)
VMEM_LIMIT = 60 * 1024 * 1024
ROPE_BASE = 500000.0


def swap(value, axis, stride):
    pairs = [(source, source ^ stride) for source in range(lax.axis_size(axis))]
    return lax.ppermute(value, axis, pairs)


def cycle(size):
    return list(range(0, size, 2)) + list(range(1, size, 2))[::-1]


def ring_step(value):
    ctx_size, zero_size = lax.axis_size("ctx"), lax.axis_size("zero")
    order = cycle(ctx_size)
    pairs = []
    for at in range(ctx_size):
        for zero in range(zero_size):
            to = order[(at + (1 if zero % 2 == 0 else -1)) % ctx_size]
            pairs.append((order[at] * zero_size + zero, to * zero_size + zero))
    return lax.ppermute(value, ("ctx", "zero"), pairs)


class Ring:
    def __init__(self, shard, core, whole=None, base=0):
        self.held = [(0, None, 0, shard if whole is None else whole)] if base == 0 else []
        self.base = base
        self.moving, self.core, self.at = shard, core, 0
        self.length = lax.axis_size("ctx") // 2

    def step(self, *after):
        self.at += 1
        last = self.at == self.length
        if last:
            half = self.moving.shape[0] // 2
            self.moving = lax.dynamic_slice_in_dim(self.moving, self.core * half, half, 0)
        behind = self.held[-3][3:] if len(self.held) > 3 else []
        self.moving = ring_step(tied(self.moving, *behind, *after))
        self.held.append((-self.at, 0 if last else None, self.base, self.moving))
        self.held.append(
            (self.at, 1 if last else None, self.base, swap(self.moving, "zero", 1))
        )
        return self.moving

    def advance(self, part, parts, *after):
        while self.at < self.length * (part + 1) // parts:
            self.step(*after)
        return self.moving


def tied(value, *others):
    return lax.optimization_barrier((value, *others))[0] if others else value


def source_of(steps):
    size = lax.axis_size("ctx")
    ctx, core = lax.axis_index("ctx"), lax.axis_index("zero") % 2
    place = jnp.where(ctx % 2 == 0, ctx // 2, size - 1 - ctx // 2)
    place = lax.rem(place + steps * (1 - 2 * core) + size, size)
    return jnp.where(place < size // 2, 2 * place, 2 * (size - 1 - place) + 1)


def share_of(share):
    core = lax.axis_index("zero") % 2
    return core if share == 0 else 1 - core


def token_rows(group, other, size):
    core = lax.axis_index("zero") % 2
    if other:
        core = 1 - core
    return pl.ds(pl.multiple_of((2 * group + core) * size, 16), size)


def deal_kernel(count, *refs):
    x_refs, outs, sem = refs[:count], refs[count:-1], refs[-1]
    groups = lax.axis_size("zero") // 2
    size = x_refs[0].shape[0] // (2 * groups)
    copies = []
    for x_ref, out_ref in zip(x_refs, outs):
        for group in range(groups):
            copies.append(
                pltpu.make_async_copy(
                    x_ref.at[token_rows(group, True, size)],
                    out_ref.at[pl.ds(group * size, size)],
                    sem.at[len(copies)],
                )
            )
    for copy in copies:
        copy.start()
    for copy in copies:
        copy.wait()


def deal(arrays):
    tokens, depth = arrays[0].shape
    part = jax.ShapeDtypeStruct((tokens // 2, depth), arrays[0].dtype)
    copies = len(arrays) * lax.axis_size("zero") // 2
    return pl.pallas_call(
        functools.partial(deal_kernel, len(arrays)),
        out_shape=[part] * len(arrays),
        in_specs=[HBM] * len(arrays),
        out_specs=[HBM] * len(arrays),
        scratch_shapes=[pltpu.SemaphoreType.DMA((copies,))],
        compiler_params=pltpu.CompilerParams(vmem_limit_bytes=VMEM_LIMIT),
    )(*arrays)


def project_kernel(layout, *refs):
    (kv_ref, q_ref, x_buf, w_buf, x_sem, w_sem) = refs[-6:]
    pieces, tokens, depth = x_buf.shape
    cos_ref, sin_ref = refs[:2]
    x_refs = refs[2 : 2 + pieces]
    w_refs = refs[2 + pieces : -6]
    zero = lax.axis_index("zero")
    shard_rows = w_refs[0].shape[0]
    x_copies, w_copies = [], []
    for m, ref in enumerate(x_refs):
        target = x_buf.at[jnp.bitwise_xor(zero, m)]
        if m % 2:
            x_copies.append(pltpu.make_async_copy(ref, target, x_sem.at[len(x_copies)]))
            continue
        size = 2 * tokens // pieces
        for group in range(pieces // 2):
            x_copies.append(
                pltpu.make_async_copy(
                    ref.at[token_rows(group, False, size)],
                    target.at[pl.ds(group * size, size)],
                    x_sem.at[len(x_copies)],
                )
            )
    for at, (ref, (steps, share, base)) in enumerate(zip(w_refs, layout)):
        start = source_of(steps) * shard_rows + base
        if share is not None:
            start = start + share_of(share) * ref.shape[0]
        rows = pl.ds(pl.multiple_of(start, 16), ref.shape[0])
        w_copies.append(pltpu.make_async_copy(ref, w_buf.at[rows], w_sem.at[at]))
    for copy in x_copies + w_copies:
        copy.start()
    for copy in x_copies:
        copy.wait()
    squares = jnp.zeros((tokens, 128), jnp.float32)
    for at in range(pieces):
        for first in range(0, depth, 128):
            x_float = x_buf[at, :, first : first + 128].astype(jnp.float32)
            squares += x_float * x_float
    mean = jnp.sum(squares, axis=1, keepdims=True) / (depth * pieces)
    scale = jnp.broadcast_to(lax.rsqrt(mean + 1e-05), squares.shape)
    for copy in w_copies:
        copy.wait()
    head = cos_ref.shape[1]
    shrink = jnp.float32(head ** (-0.5))
    for out_ref, columns in ((kv_ref, 0), (q_ref, 2 * head)):
        for first in range(0, out_ref.shape[1], 2 * head):
            both = slice(columns + first, columns + first + 2 * head)
            total = jnp.zeros((tokens, 2 * head), jnp.float32)
            for at in range(pieces):
                total += jnp.dot(
                    x_buf[at],
                    w_buf[at * depth : (at + 1) * depth, both],
                    preferred_element_type=jnp.float32,
                )
            for at in range(2):
                part = total[:, at * head : (at + 1) * head] * scale
                if columns or not at:
                    part = part * cos_ref[...] + pltpu.roll(part, head // 2, 1) * sin_ref[...]
                if columns:
                    part = part * shrink
                out_ref[:, first + at * head : first + (at + 1) * head] = part.astype(
                    out_ref.dtype
                )


def project(cos, sin, x_pieces, held):
    layout = [(steps, share, base) for steps, share, base, _ in held]
    shards = [piece for _, _, _, piece in held]
    tokens, depth = x_pieces[1].shape
    pieces, head = len(x_pieces), cos.shape[1]
    width = shards[0].shape[1]
    full = depth * pieces
    return pl.pallas_call(
        functools.partial(project_kernel, layout),
        out_shape=[
            jax.ShapeDtypeStruct((tokens, 2 * head), jnp.bfloat16),
            jax.ShapeDtypeStruct((tokens, width - 2 * head), jnp.bfloat16),
        ],
        in_specs=[VMEM] * 2 + [HBM] * (pieces + len(shards)),
        out_specs=[VMEM] * 2,
        scratch_shapes=[
            pltpu.VMEM((pieces, tokens, depth), jnp.bfloat16),
            pltpu.VMEM((full, width), jnp.bfloat16),
            pltpu.SemaphoreType.DMA((pieces // 2 * (1 + pieces // 2),)),
            pltpu.SemaphoreType.DMA((len(shards),)),
        ],
        compiler_params=pltpu.CompilerParams(vmem_limit_bytes=VMEM_LIMIT),
        cost_estimate=pl.CostEstimate(
            flops=2 * tokens * full * width,
            bytes_accessed=2 * full * (tokens + width),
            transcendentals=0,
        ),
    )(cos, sin, *x_pieces, *shards)


def attend_kernel(groups, stays, own_ref, far_ref, *refs):
    out_ref, q_ref, near0, near1, far0, far1, sem = refs[5:]
    copies = [
        pltpu.make_async_copy(source, target, sem.at[at])
        for at, (source, target) in enumerate(zip(refs[:5], refs[6:11]))
    ]
    for copy in copies:
        copy.start()
    for copy in copies:
        copy.wait()
    tokens, pair = near0.shape
    head = pair // 2
    size = tokens // groups
    tiles = own_ref.shape[0]
    tile = 2 * tokens // tiles
    heads = q_ref.shape[1] // head
    rows = heads * size
    core = lax.axis_index("zero") % 2
    column = lax.broadcasted_iota(jnp.int32, (1, tokens), 1)
    column_group = column // size
    within = lax.rem(lax.broadcasted_iota(jnp.int32, (rows, 1), 0), size)
    hidden = jnp.float32(-1e30)
    nt = (((1,), (1,)), ((), ()))
    side = lax.axis_index("zero") // 2 % 2
    for pair_of in range(groups // 2):
        h = 2 * pair_of + (side if stays else 1 - side)
        across = pl.ds(pl.multiple_of(h * size, 16), size)
        q = jnp.concatenate(
            [q_ref[across, g * head : (g + 1) * head] for g in range(heads)], axis=0
        )
        first = (2 * h + core) * size
        own_tile = first // tile
        seen = min(tokens, -(-(2 * pair_of + 2) * size // 128) * 128)
        parts, blocks = [], []
        for ref, mask_ref, width, parity, causal in (
            (far0, far_ref, tokens, core, False),
            (far1, far_ref, tokens, 1 - core, False),
            (near0, own_ref, seen, core, True),
            (near1, own_ref, seen, 1 - core, True),
        ):
            visible = jnp.zeros((1, width), jnp.int32)
            for g in range(-(-width // size)):
                at = mask_ref[own_tile, (2 * g + parity) * size // tile]
                visible = jnp.where(column_group[:, :width] == g, at, visible)
            visible = visible == 1
            if causal:
                group = column_group[:, :width]
                offset = (2 * group + parity) * size + column[:, :width] - group * size
                visible = visible & (offset <= first + within)
            scores = lax.dot_general(
                q, ref[:width, :head], nt, preferred_element_type=jnp.float32
            )
            parts.append(jnp.where(visible, scores, hidden))
            blocks.append((ref, width))
        scores = jnp.concatenate(parts, axis=1)
        largest = jnp.max(scores, axis=1, keepdims=True)
        weights = jnp.exp(scores - largest)
        total = jnp.sum(weights, axis=1, keepdims=True)
        rounded = weights.astype(jnp.bfloat16)
        mixed = jnp.zeros((rows, head), jnp.float32)
        start = 0
        for ref, width in blocks:
            mixed += jnp.dot(
                rounded[:, start : start + width],
                ref[:width, head:],
                preferred_element_type=jnp.float32,
            )
            start += width
        mixed = (mixed / total).astype(out_ref.dtype)
        for g in range(heads):
            out_ref[pair_of * size : (pair_of + 1) * size, g * head : (g + 1) * head] = mixed[
                g * size : (g + 1) * size, :
            ]


def attend(groups, stays, own_mask, far_mask, queries, near, near_other, far, far_other):
    tokens, width = queries.shape
    return pl.pallas_call(
        functools.partial(attend_kernel, groups, stays),
        out_shape=jax.ShapeDtypeStruct((tokens // 2, width), jnp.bfloat16),
        in_specs=[SMEM, SMEM] + [HBM] * 5,
        out_specs=VMEM,
        scratch_shapes=[pltpu.VMEM(queries.shape, jnp.bfloat16)]
        + [pltpu.VMEM(near.shape, jnp.bfloat16)] * 4
        + [pltpu.SemaphoreType.DMA((5,))],
        compiler_params=pltpu.CompilerParams(vmem_limit_bytes=VMEM_LIMIT),
        cost_estimate=pl.CostEstimate(
            flops=8 * tokens * tokens * width,
            bytes_accessed=8 * tokens * width,
            transcendentals=8 * tokens * tokens,
        ),
    )(own_mask, far_mask, queries, near, near_other, far, far_other)


def mix_kernel(layout, slots, out_refs, *refs):
    count = len(refs) - len(layout) - out_refs - 2
    a_refs, w_refs = refs[:count], refs[count : count + len(layout)]
    outs = refs[count + len(layout) : -2]
    w_buf, sem = refs[-2:]
    width = w_buf.shape[2]
    half = a_refs[0].shape[1]
    copies = []
    for at, (ref, (slot, side, share)) in enumerate(zip(w_refs, layout)):
        rows = ref.shape[0]
        start = side * half
        if share is not None:
            start = pl.multiple_of(start + share_of(share) * rows, 16)
        copies.append(pltpu.make_async_copy(ref, w_buf.at[slot, pl.ds(start, rows)], sem.at[at]))
    for copy in copies:
        copy.start()
    slot = 0
    for out_ref, sides, number in zip(outs, *slots):
        rows = jnp.concatenate([ref[...] for ref in a_refs[:sides]], axis=1)
        for place in range(number):
            for copy, (its_slot, _, _) in zip(copies, layout):
                if its_slot == slot:
                    copy.wait()
            total = jnp.dot(
                rows, w_buf[slot, : sides * half], preferred_element_type=jnp.float32
            )
            out_ref[:, place * width : (place + 1) * width] = total.astype(out_ref.dtype)
            slot += 1


def mix(rows, blocks, dtypes):
    layout, shards = [], []
    sides = [1 + max(side for side, _, _ in block[0]) for block in blocks]
    slots = [slot for block in blocks for slot in block]
    for at, slot in enumerate(slots):
        for side, share, piece in slot:
            layout.append((at, side, share))
            shards.append(piece)
    tokens, half = rows[0].shape
    width = shards[0].shape[1]
    return pl.pallas_call(
        functools.partial(
            mix_kernel, layout, (sides, [len(block) for block in blocks]), len(blocks)
        ),
        out_shape=[
            jax.ShapeDtypeStruct((tokens, width * len(block)), dtype)
            for block, dtype in zip(blocks, dtypes)
        ],
        in_specs=[VMEM] * len(rows) + [HBM] * len(shards),
        out_specs=[VMEM] * len(blocks),
        scratch_shapes=[
            pltpu.VMEM((len(slots), max(sides) * half, width), jnp.bfloat16),
            pltpu.SemaphoreType.DMA((len(shards),)),
        ],
        compiler_params=pltpu.CompilerParams(vmem_limit_bytes=VMEM_LIMIT),
        cost_estimate=pl.CostEstimate(
            flops=2 * tokens * half * width * len(shards),
            bytes_accessed=6 * half * width * len(shards) + 4 * tokens * width * len(slots),
            transcendentals=0,
        ),
    )(*rows, *shards)


def join_kernel(steps, full_ref, keep_ref, got_ref, out_ref):
    width = out_ref.shape[1] // len(steps)
    whole = full_ref.shape[1] // width
    for slot, along in enumerate(steps):
        start = pl.multiple_of(source_of(along) * width, 128)
        if slot < whole:
            block = full_ref[:, slot * width : (slot + 1) * width]
        else:
            columns = slice((slot - whole) * width, (slot - whole + 1) * width)
            block = keep_ref[:, columns] + got_ref[:, columns].astype(jnp.float32)
        out_ref[:, pl.ds(start, width)] = block.astype(out_ref.dtype)


def join(steps, full, keep, got, dtype):
    rows = full.shape[0]
    columns = full.shape[1] + keep.shape[1]
    return pl.pallas_call(
        functools.partial(join_kernel, steps),
        out_shape=jax.ShapeDtypeStruct((rows, columns), dtype),
        in_specs=[VMEM] * 3,
        out_specs=VMEM,
        compiler_params=pltpu.CompilerParams(vmem_limit_bytes=VMEM_LIMIT),
        cost_estimate=pl.CostEstimate(
            flops=rows * columns, bytes_accessed=8 * rows * columns, transcendentals=0
        ),
    )(full, keep, got)


def exchange_from(value, root, bit):
    other = swap(value, "ctx", 1 << bit)
    same = ((lax.axis_index("ctx") >> bit) & 1) == ((root >> bit) & 1)
    return jnp.where(same, value, other)


def local(
    activations,
    norm_gain,
    query_weight,
    kv_weight,
    out_weight,
    tile_mask,
    anchor_mask,
    anchor_index,
):
    tokens, depth = activations.shape
    head = kv_weight.shape[2]
    ctx_size, zero_size = lax.axis_size("ctx"), lax.axis_size("zero")
    ctx_rank, zero_rank = lax.axis_index("ctx"), lax.axis_index("zero")
    core = zero_rank % 2
    groups = zero_size // 2
    size = tokens // zero_size

    blocks = {0: activations}
    stride = groups
    while stride > 1:
        for known in range(0, zero_size, 2 * stride):
            blocks[known + stride] = swap(blocks[known], "zero", stride)
        stride //= 2

    shard_rows = kv_weight.shape[0]
    gain = lax.dynamic_slice_in_dim(norm_gain, ctx_rank * shard_rows, shard_rows)
    gain = gain.astype(jnp.float32)[:, None]
    kv_own = kv_weight[:, 0, :]
    kv_other, query_other = swap(kv_own, "zero", 1), swap(query_weight, "zero", 1)
    pair = jnp.where(
        core == 0,
        jnp.concatenate([kv_own, kv_other, query_weight, query_other], 1),
        jnp.concatenate([kv_other, kv_own, query_other, query_weight], 1),
    )
    pair = (pair.astype(jnp.float32) * gain).astype(jnp.bfloat16)
    out_other = swap(out_weight, "zero", 1)
    out_pair = jnp.where(
        core == 0,
        jnp.concatenate([out_weight, out_other], 0),
        jnp.concatenate([out_other, out_weight], 0),
    )
    ring_rows = shard_rows // 2
    rings = [
        Ring(pair[:ring_rows], core, pair),
        Ring(pair[ring_rows:], core, None, ring_rows),
    ]
    out_ring = Ring(out_pair, core)
    for part in range(4):
        for ring in rings:
            ring.advance(part, 4)
    held = rings[0].held + rings[1].held
    beyond = [swap(out_weight, "zero", 2)]
    out_ring.advance(0, 4, *[ring.moving for ring in rings], *beyond)

    far_blocks = [tied(blocks[m], rings[0].moving) for m in range(2, zero_size, 2)]
    x_pieces = []
    for at, theirs in enumerate(deal([blocks[0]]) + deal(far_blocks)):
        x_pieces += [([blocks[0]] + far_blocks)[at], swap(theirs, "zero", 1)]

    half = head // 2
    frequency = jnp.power(
        jnp.float32(ROPE_BASE), -(jnp.arange(half, dtype=jnp.float32) * 2.0 / head)
    )
    local_token = jnp.arange(tokens // 2, dtype=jnp.int32)
    offsets = (2 * (local_token // size) + core) * size + local_token % size
    positions = ctx_rank * tokens + offsets
    angles = positions.astype(jnp.float32)[:, None] * frequency[None, :]
    cos_half, sin_half = jnp.cos(angles), jnp.sin(angles)
    cos = jnp.concatenate([cos_half, cos_half], -1)
    sin = jnp.concatenate([-sin_half, sin_half], -1)

    near, queries = project(cos, sin, x_pieces, held)

    def share():
        for at in range(len(beyond), out_ring.at + 1):
            beyond.append(swap(out_ring.held[2 * at - 1][3], "zero", 2))

    share()
    anchor = anchor_index[0]
    far = tied(near, out_ring.moving)
    bits = int(math.log2(ctx_size))
    for bit in range(bits):
        far = exchange_from(far, anchor, bit)
        if bit == 0:
            near_other = swap(near, "zero", 1)
            far = tied(far, near_other)
            first = beyond[-1]
            out_ring.advance(1, 4, far)
            share()
        elif bit == 1:
            out_ring.advance(2, 4, far, first)
    queries = tied(queries, beyond[-1])
    out_ring.advance(3, 4, far)
    far_other = swap(far, "zero", 1)
    far_mask = jnp.where(ctx_rank != anchor, anchor_mask[0], 0)
    both_blocks = (near, near_other, far, far_other)
    send = attend(groups, False, tile_mask[0], far_mask, queries, *both_blocks)
    got = swap(send, "zero", 2)
    out_ring.held[-1] = (
        *out_ring.held[-1][:3],
        swap(tied(out_ring.moving, send), "zero", 1),
    )
    keep = attend(groups, True, tile_mask[0], far_mask, queries, *both_blocks)

    steps_of, both_chips, one_chip = [], [], []
    for steps, half_of, _, piece in out_ring.held:
        slots = both_chips if abs(steps) < len(beyond) else one_chip
        if half_of != 1:
            steps_of.append(steps)
            slots.append([])
        slots[-1].append((0, half_of, piece))
        if slots is both_chips:
            if steps <= 0:
                across = swap(beyond[-steps], "zero", 1)
            if steps == 0:
                slots[-1] += [(1, 0, beyond[0]), (1, 1, across)]
            else:
                slots[-1].append((1, half_of, beyond[-steps] if steps < 0 else across))
    (terms,) = mix([send], [one_chip], [jnp.bfloat16])
    got_terms = swap(tied(terms, got), "zero", 2)
    full, kept = mix([keep, got], [both_chips, one_chip], [jnp.float32, jnp.float32])
    if zero_size == 4:
        return join(steps_of, full, kept, got_terms, jnp.bfloat16)
    total = join(steps_of, full, kept, got_terms, jnp.float32)
    stride = zero_size // 2
    while stride > 2:
        rows = total.shape[0] // 2
        bit = (zero_rank // stride) % 2
        stay = lax.dynamic_slice_in_dim(total, bit * rows, rows, 0)
        go = lax.dynamic_slice_in_dim(total, (1 - bit) * rows, rows, 0)
        total = stay + swap(go.astype(jnp.bfloat16), "zero", stride).astype(jnp.float32)
        stride //= 2
    return total.astype(jnp.bfloat16)


def solution(mesh):
    placed = (
        P("ctx", "zero"),
        P(),
        P("ctx", "zero"),
        P("ctx", "zero", None),
        P("zero", "ctx"),
        P("ctx", None, None),
        P("ctx", None, None),
        P(),
    )
    return jax.shard_map(
        local, mesh=mesh, in_specs=placed, out_specs=P(("ctx", "zero"), None), check_vma=False
    )
```

```python
import functools
import math

import jax
import jax.numpy as jnp
from jax import lax
from jax.experimental import pallas as pl
from jax.experimental.pallas import tpu as pltpu
from jax.sharding import PartitionSpec as P

HBM = pl.BlockSpec(memory_space=pltpu.HBM)
VMEM = pl.BlockSpec(memory_space=pltpu.VMEM)
SMEM = pl.BlockSpec(memory_space=pltpu.SMEM)
VMEM_LIMIT = 32 * 1024 * 1024
ROPE_BASE = 500000.0


def swap(value, axis, stride):
    pairs = [(source, source ^ stride) for source in range(lax.axis_size(axis))]
    return lax.ppermute(value, axis, pairs)


def cycle(size):
    return list(range(0, size, 2)) + list(range(1, size, 2))[::-1]


def ring_step(value):
    ctx_size, zero_size = lax.axis_size("ctx"), lax.axis_size("zero")
    order = cycle(ctx_size)
    pairs = []
    for at in range(ctx_size):
        for zero in range(zero_size):
            to = order[(at + (1 if zero % 2 == 0 else -1)) % ctx_size]
            pairs.append((order[at] * zero_size + zero, to * zero_size + zero))
    return lax.ppermute(value, ("ctx", "zero"), pairs)


class Ring:
    def __init__(self, shard, core, whole=None, base=0):
        self.held = [(0, None, 0, shard if whole is None else whole)] if base == 0 else []
        self.base = base
        self.moving, self.core, self.at = shard, core, 0
        self.length = lax.axis_size("ctx") // 2

    def step(self, *after):
        self.at += 1
        last = self.at == self.length
        if last:
            half = self.moving.shape[0] // 2
            self.moving = lax.dynamic_slice_in_dim(self.moving, self.core * half, half, 0)
        behind = self.held[-3][3:] if len(self.held) > 3 else []
        self.moving = ring_step(tied(self.moving, *behind, *after))
        self.held.append((-self.at, 0 if last else None, self.base, self.moving))
        self.held.append(
            (self.at, 1 if last else None, self.base, swap(self.moving, "zero", 1))
        )
        return self.moving

    def advance(self, part, parts, *after):
        while self.at < self.length * (part + 1) // parts:
            self.step(*after)
        return self.moving


def tied(value, *others):
    return lax.optimization_barrier((value, *others))[0] if others else value


def source_of(steps):
    size = lax.axis_size("ctx")
    ctx, core = lax.axis_index("ctx"), lax.axis_index("zero") % 2
    place = jnp.where(ctx % 2 == 0, ctx // 2, size - 1 - ctx // 2)
    place = lax.rem(place + steps * (1 - 2 * core) + size, size)
    return jnp.where(place < size // 2, 2 * place, 2 * (size - 1 - place) + 1)


def share_of(share):
    core = lax.axis_index("zero") % 2
    return core if share == 0 else 1 - core


def token_rows(group, other, size):
    core = lax.axis_index("zero") % 2
    if other:
        core = 1 - core
    return pl.ds(pl.multiple_of((2 * group + core) * size, 16), size)


def deal_kernel(count, *refs):
    x_refs, outs, sem = refs[:count], refs[count:-1], refs[-1]
    groups = lax.axis_size("zero") // 2
    size = x_refs[0].shape[0] // (2 * groups)
    copies = []
    for x_ref, out_ref in zip(x_refs, outs):
        for group in range(groups):
            copies.append(
                pltpu.make_async_copy(
                    x_ref.at[token_rows(group, True, size)],
                    out_ref.at[pl.ds(group * size, size)],
                    sem.at[len(copies)],
                )
            )
    for copy in copies:
        copy.start()
    for copy in copies:
        copy.wait()


def deal(arrays):
    tokens, depth = arrays[0].shape
    part = jax.ShapeDtypeStruct((tokens // 2, depth), arrays[0].dtype)
    copies = len(arrays) * lax.axis_size("zero") // 2
    return pl.pallas_call(
        functools.partial(deal_kernel, len(arrays)),
        out_shape=[part] * len(arrays),
        in_specs=[HBM] * len(arrays),
        out_specs=[HBM] * len(arrays),
        scratch_shapes=[pltpu.SemaphoreType.DMA((copies,))],
        compiler_params=pltpu.CompilerParams(vmem_limit_bytes=VMEM_LIMIT),
    )(*arrays)


def project_kernel(layout, *refs):
    (kv_ref, q_ref, x_buf, w_buf, x_sem, w_sem) = refs[-6:]
    pieces, tokens, depth = x_buf.shape
    cos_ref, sin_ref = refs[:2]
    x_refs = refs[2 : 2 + pieces]
    w_refs = refs[2 + pieces : -6]
    zero = lax.axis_index("zero")
    shard_rows = w_refs[0].shape[0]
    x_copies, w_copies = [], []
    for m, ref in enumerate(x_refs):
        target = x_buf.at[jnp.bitwise_xor(zero, m)]
        if m % 2:
            x_copies.append(pltpu.make_async_copy(ref, target, x_sem.at[len(x_copies)]))
            continue
        size = 2 * tokens // pieces
        for group in range(pieces // 2):
            x_copies.append(
                pltpu.make_async_copy(
                    ref.at[token_rows(group, False, size)],
                    target.at[pl.ds(group * size, size)],
                    x_sem.at[len(x_copies)],
                )
            )
    for at, (ref, (steps, share, base)) in enumerate(zip(w_refs, layout)):
        start = source_of(steps) * shard_rows + base
        if share is not None:
            start = start + share_of(share) * ref.shape[0]
        rows = pl.ds(pl.multiple_of(start, 16), ref.shape[0])
        w_copies.append(pltpu.make_async_copy(ref, w_buf.at[rows], w_sem.at[at]))
    for copy in x_copies + w_copies:
        copy.start()
    for copy in x_copies:
        copy.wait()
    squares = jnp.zeros((tokens, 128), jnp.float32)
    for at in range(pieces):
        for first in range(0, depth, 128):
            x_float = x_buf[at, :, first : first + 128].astype(jnp.float32)
            squares += x_float * x_float
    mean = jnp.sum(squares, axis=1, keepdims=True) / (depth * pieces)
    scale = jnp.broadcast_to(lax.rsqrt(mean + 1e-05), squares.shape)
    for copy in w_copies:
        copy.wait()
    head = cos_ref.shape[1]
    shrink = jnp.float32(head ** (-0.5))
    for out_ref, columns in ((kv_ref, 0), (q_ref, 2 * head)):
        for first in range(0, out_ref.shape[1], 2 * head):
            both = slice(columns + first, columns + first + 2 * head)
            total = jnp.zeros((tokens, 2 * head), jnp.float32)
            for at in range(pieces):
                total += jnp.dot(
                    x_buf[at],
                    w_buf[at * depth : (at + 1) * depth, both],
                    preferred_element_type=jnp.float32,
                )
            for at in range(2):
                part = total[:, at * head : (at + 1) * head] * scale
                if columns or not at:
                    part = part * cos_ref[...] + pltpu.roll(part, head // 2, 1) * sin_ref[...]
                if columns:
                    part = part * shrink
                out_ref[:, first + at * head : first + (at + 1) * head] = part.astype(
                    out_ref.dtype
                )


def project(cos, sin, x_pieces, held):
    layout = [(steps, share, base) for steps, share, base, _ in held]
    shards = [piece for _, _, _, piece in held]
    tokens, depth = x_pieces[1].shape
    pieces, head = len(x_pieces), cos.shape[1]
    width = shards[0].shape[1]
    full = depth * pieces
    return pl.pallas_call(
        functools.partial(project_kernel, layout),
        out_shape=[
            jax.ShapeDtypeStruct((tokens, 2 * head), jnp.bfloat16),
            jax.ShapeDtypeStruct((tokens, width - 2 * head), jnp.bfloat16),
        ],
        in_specs=[VMEM] * 2 + [HBM] * (pieces + len(shards)),
        out_specs=[VMEM] * 2,
        scratch_shapes=[
            pltpu.VMEM((pieces, tokens, depth), jnp.bfloat16),
            pltpu.VMEM((full, width), jnp.bfloat16),
            pltpu.SemaphoreType.DMA((pieces // 2 * (1 + pieces // 2),)),
            pltpu.SemaphoreType.DMA((len(shards),)),
        ],
        compiler_params=pltpu.CompilerParams(vmem_limit_bytes=VMEM_LIMIT),
        cost_estimate=pl.CostEstimate(
            flops=2 * tokens * full * width,
            bytes_accessed=2 * full * (tokens + width),
            transcendentals=0,
        ),
    )(cos, sin, *x_pieces, *shards)


def attend_kernel(groups, stays, own_ref, far_ref, *refs):
    out_ref, q_ref, near0, near1, far0, far1, sem = refs[5:]
    copies = [
        pltpu.make_async_copy(source, target, sem.at[at])
        for at, (source, target) in enumerate(zip(refs[:5], refs[6:11]))
    ]
    for copy in copies:
        copy.start()
    for copy in copies:
        copy.wait()
    tokens, pair = near0.shape
    head = pair // 2
    size = tokens // groups
    tiles = own_ref.shape[0]
    tile = 2 * tokens // tiles
    heads = q_ref.shape[1] // head
    rows = heads * size
    core = lax.axis_index("zero") % 2
    column = lax.broadcasted_iota(jnp.int32, (1, tokens), 1)
    column_group = column // size
    within = lax.rem(lax.broadcasted_iota(jnp.int32, (rows, 1), 0), size)
    hidden = jnp.float32(-1e30)
    nt = (((1,), (1,)), ((), ()))
    side = lax.axis_index("zero") // 2 % 2
    for pair_of in range(groups // 2):
        h = 2 * pair_of + (side if stays else 1 - side)
        across = pl.ds(pl.multiple_of(h * size, 16), size)
        q = jnp.concatenate(
            [q_ref[across, g * head : (g + 1) * head] for g in range(heads)], axis=0
        )
        first = (2 * h + core) * size
        own_tile = first // tile
        seen = min(tokens, -(-(2 * pair_of + 2) * size // 128) * 128)
        parts, blocks = [], []
        for ref, mask_ref, width, parity, causal in (
            (far0, far_ref, tokens, core, False),
            (far1, far_ref, tokens, 1 - core, False),
            (near0, own_ref, seen, core, True),
            (near1, own_ref, seen, 1 - core, True),
        ):
            visible = jnp.zeros((1, width), jnp.int32)
            for g in range(-(-width // size)):
                at = mask_ref[own_tile, (2 * g + parity) * size // tile]
                visible = jnp.where(column_group[:, :width] == g, at, visible)
            visible = visible == 1
            if causal:
                group = column_group[:, :width]
                offset = (2 * group + parity) * size + column[:, :width] - group * size
                visible = visible & (offset <= first + within)
            scores = lax.dot_general(
                q, ref[:width, :head], nt, preferred_element_type=jnp.float32
            )
            parts.append(jnp.where(visible, scores, hidden))
            blocks.append((ref, width))
        scores = jnp.concatenate(parts, axis=1)
        largest = jnp.max(scores, axis=1, keepdims=True)
        weights = jnp.exp(scores - largest)
        total = jnp.sum(weights, axis=1, keepdims=True)
        rounded = weights.astype(jnp.bfloat16)
        mixed = jnp.zeros((rows, head), jnp.float32)
        start = 0
        for ref, width in blocks:
            mixed += jnp.dot(
                rounded[:, start : start + width],
                ref[:width, head:],
                preferred_element_type=jnp.float32,
            )
            start += width
        mixed = (mixed / total).astype(out_ref.dtype)
        for g in range(heads):
            out_ref[pair_of * size : (pair_of + 1) * size, g * head : (g + 1) * head] = mixed[
                g * size : (g + 1) * size, :
            ]


def attend(groups, stays, own_mask, far_mask, queries, near, near_other, far, far_other):
    tokens, width = queries.shape
    return pl.pallas_call(
        functools.partial(attend_kernel, groups, stays),
        out_shape=jax.ShapeDtypeStruct((tokens // 2, width), jnp.bfloat16),
        in_specs=[SMEM, SMEM] + [HBM] * 5,
        out_specs=VMEM,
        scratch_shapes=[pltpu.VMEM(queries.shape, jnp.bfloat16)]
        + [pltpu.VMEM(near.shape, jnp.bfloat16)] * 4
        + [pltpu.SemaphoreType.DMA((5,))],
        compiler_params=pltpu.CompilerParams(vmem_limit_bytes=VMEM_LIMIT),
        cost_estimate=pl.CostEstimate(
            flops=8 * tokens * tokens * width,
            bytes_accessed=8 * tokens * width,
            transcendentals=8 * tokens * tokens,
        ),
    )(own_mask, far_mask, queries, near, near_other, far, far_other)


def mix_kernel(layout, slots, out_refs, *refs):
    count = len(refs) - len(layout) - out_refs - 2
    a_refs, w_refs = refs[:count], refs[count : count + len(layout)]
    outs = refs[count + len(layout) : -2]
    w_buf, sem = refs[-2:]
    width = w_buf.shape[2]
    half = a_refs[0].shape[1]
    copies = []
    for at, (ref, (slot, side, share)) in enumerate(zip(w_refs, layout)):
        rows = ref.shape[0]
        start = side * half
        if share is not None:
            start = pl.multiple_of(start + share_of(share) * rows, 16)
        copies.append(pltpu.make_async_copy(ref, w_buf.at[slot, pl.ds(start, rows)], sem.at[at]))
    for copy in copies:
        copy.start()
    slot = 0
    for out_ref, sides, number in zip(outs, *slots):
        rows = jnp.concatenate([ref[...] for ref in a_refs[:sides]], axis=1)
        for place in range(number):
            for copy, (its_slot, _, _) in zip(copies, layout):
                if its_slot == slot:
                    copy.wait()
            total = jnp.dot(
                rows, w_buf[slot, : sides * half], preferred_element_type=jnp.float32
            )
            out_ref[:, place * width : (place + 1) * width] = total.astype(out_ref.dtype)
            slot += 1


def mix(rows, blocks, dtypes):
    layout, shards = [], []
    sides = [1 + max(side for side, _, _ in block[0]) for block in blocks]
    slots = [slot for block in blocks for slot in block]
    for at, slot in enumerate(slots):
        for side, share, piece in slot:
            layout.append((at, side, share))
            shards.append(piece)
    tokens, half = rows[0].shape
    width = shards[0].shape[1]
    return pl.pallas_call(
        functools.partial(
            mix_kernel, layout, (sides, [len(block) for block in blocks]), len(blocks)
        ),
        out_shape=[
            jax.ShapeDtypeStruct((tokens, width * len(block)), dtype)
            for block, dtype in zip(blocks, dtypes)
        ],
        in_specs=[VMEM] * len(rows) + [HBM] * len(shards),
        out_specs=[VMEM] * len(blocks),
        scratch_shapes=[
            pltpu.VMEM((len(slots), max(sides) * half, width), jnp.bfloat16),
            pltpu.SemaphoreType.DMA((len(shards),)),
        ],
        compiler_params=pltpu.CompilerParams(vmem_limit_bytes=VMEM_LIMIT),
        cost_estimate=pl.CostEstimate(
            flops=2 * tokens * half * width * len(shards),
            bytes_accessed=6 * half * width * len(shards) + 4 * tokens * width * len(slots),
            transcendentals=0,
        ),
    )(*rows, *shards)


def join_kernel(steps, full_ref, keep_ref, got_ref, out_ref):
    width = out_ref.shape[1] // len(steps)
    whole = full_ref.shape[1] // width
    for slot, along in enumerate(steps):
        start = pl.multiple_of(source_of(along) * width, 128)
        if slot < whole:
            block = full_ref[:, slot * width : (slot + 1) * width]
        else:
            columns = slice((slot - whole) * width, (slot - whole + 1) * width)
            block = keep_ref[:, columns] + got_ref[:, columns].astype(jnp.float32)
        out_ref[:, pl.ds(start, width)] = block.astype(out_ref.dtype)


def join(steps, full, keep, got, dtype):
    rows = full.shape[0]
    columns = full.shape[1] + keep.shape[1]
    return pl.pallas_call(
        functools.partial(join_kernel, steps),
        out_shape=jax.ShapeDtypeStruct((rows, columns), dtype),
        in_specs=[VMEM] * 3,
        out_specs=VMEM,
        compiler_params=pltpu.CompilerParams(vmem_limit_bytes=VMEM_LIMIT),
        cost_estimate=pl.CostEstimate(
            flops=rows * columns, bytes_accessed=8 * rows * columns, transcendentals=0
        ),
    )(full, keep, got)


def exchange_from(value, root, bit):
    other = swap(value, "ctx", 1 << bit)
    same = ((lax.axis_index("ctx") >> bit) & 1) == ((root >> bit) & 1)
    return jnp.where(same, value, other)


def local(
    activations,
    norm_gain,
    query_weight,
    kv_weight,
    out_weight,
    tile_mask,
    anchor_mask,
    anchor_index,
):
    tokens, depth = activations.shape
    head = kv_weight.shape[2]
    ctx_size, zero_size = lax.axis_size("ctx"), lax.axis_size("zero")
    ctx_rank, zero_rank = lax.axis_index("ctx"), lax.axis_index("zero")
    core = zero_rank % 2
    groups = zero_size // 2
    size = tokens // zero_size

    blocks = {0: activations}
    stride = groups
    while stride > 1:
        for known in range(0, zero_size, 2 * stride):
            blocks[known + stride] = swap(blocks[known], "zero", stride)
        stride //= 2

    shard_rows = kv_weight.shape[0]
    gain = lax.dynamic_slice_in_dim(norm_gain, ctx_rank * shard_rows, shard_rows)
    gain = gain.astype(jnp.float32)[:, None]
    kv_own = kv_weight[:, 0, :]
    kv_other, query_other = swap(kv_own, "zero", 1), swap(query_weight, "zero", 1)
    pair = jnp.where(
        core == 0,
        jnp.concatenate([kv_own, kv_other, query_weight, query_other], 1),
        jnp.concatenate([kv_other, kv_own, query_other, query_weight], 1),
    )
    pair = (pair.astype(jnp.float32) * gain).astype(jnp.bfloat16)
    out_other = swap(out_weight, "zero", 1)
    out_pair = jnp.where(
        core == 0,
        jnp.concatenate([out_weight, out_other], 0),
        jnp.concatenate([out_other, out_weight], 0),
    )
    ring_rows = shard_rows // 2
    rings = [
        Ring(pair[:ring_rows], core, pair),
        Ring(pair[ring_rows:], core, None, ring_rows),
    ]
    out_ring = Ring(out_pair, core)
    for part in range(4):
        for ring in rings:
            ring.advance(part, 4)
    held = rings[0].held + rings[1].held
    beyond = [swap(out_weight, "zero", 2)]
    out_ring.advance(0, 4, *[ring.moving for ring in rings], *beyond)

    far_blocks = [tied(blocks[m], rings[0].moving) for m in range(2, zero_size, 2)]
    x_pieces = []
    for at, theirs in enumerate(deal([blocks[0]]) + deal(far_blocks)):
        x_pieces += [([blocks[0]] + far_blocks)[at], swap(theirs, "zero", 1)]

    half = head // 2
    frequency = jnp.power(
        jnp.float32(ROPE_BASE), -(jnp.arange(half, dtype=jnp.float32) * 2.0 / head)
    )
    local_token = jnp.arange(tokens // 2, dtype=jnp.int32)
    offsets = (2 * (local_token // size) + core) * size + local_token % size
    positions = ctx_rank * tokens + offsets
    angles = positions.astype(jnp.float32)[:, None] * frequency[None, :]
    cos_half, sin_half = jnp.cos(angles), jnp.sin(angles)
    cos = jnp.concatenate([cos_half, cos_half], -1)
    sin = jnp.concatenate([-sin_half, sin_half], -1)

    near, queries = project(cos, sin, x_pieces, held)

    def share():
        for at in range(len(beyond), out_ring.at + 1):
            beyond.append(swap(out_ring.held[2 * at - 1][3], "zero", 2))

    share()
    anchor = anchor_index[0]
    far = tied(near, out_ring.moving)
    bits = int(math.log2(ctx_size))
    for bit in range(bits):
        far = exchange_from(far, anchor, bit)
        if bit == 0:
            near_other = swap(near, "zero", 1)
            far = tied(far, near_other)
            first = beyond[-1]
            out_ring.advance(1, 4, far)
            share()
        elif bit == 1:
            out_ring.advance(2, 4, far, first)
    queries = tied(queries, beyond[-1])
    out_ring.advance(3, 4, far)
    far_other = swap(far, "zero", 1)
    far_mask = jnp.where(ctx_rank != anchor, anchor_mask[0], 0)
    both_blocks = (near, near_other, far, far_other)
    send = attend(groups, False, tile_mask[0], far_mask, queries, *both_blocks)
    got = swap(send, "zero", 2)
    out_ring.held[-1] = (
        *out_ring.held[-1][:3],
        swap(tied(out_ring.moving, send), "zero", 1),
    )
    keep = attend(groups, True, tile_mask[0], far_mask, queries, *both_blocks)

    steps_of, both_chips, one_chip = [], [], []
    for steps, half_of, _, piece in out_ring.held:
        slots = both_chips if abs(steps) < len(beyond) else one_chip
        if half_of != 1:
            steps_of.append(steps)
            slots.append([])
        slots[-1].append((0, half_of, piece))
        if slots is both_chips:
            if steps <= 0:
                across = swap(beyond[-steps], "zero", 1)
            if steps == 0:
                slots[-1] += [(1, 0, beyond[0]), (1, 1, across)]
            else:
                slots[-1].append((1, half_of, beyond[-steps] if steps < 0 else across))
    (terms,) = mix([send], [one_chip], [jnp.bfloat16])
    got_terms = swap(tied(terms, got), "zero", 2)
    full, kept = mix([keep, got], [both_chips, one_chip], [jnp.float32, jnp.float32])
    if zero_size == 4:
        return join(steps_of, full, kept, got_terms, jnp.bfloat16)
    total = join(steps_of, full, kept, got_terms, jnp.float32)
    stride = zero_size // 2
    while stride > 2:
        rows = total.shape[0] // 2
        bit = (zero_rank // stride) % 2
        stay = lax.dynamic_slice_in_dim(total, bit * rows, rows, 0)
        go = lax.dynamic_slice_in_dim(total, (1 - bit) * rows, rows, 0)
        total = stay + swap(go.astype(jnp.bfloat16), "zero", stride).astype(jnp.float32)
        stride //= 2
    return total.astype(jnp.bfloat16)


def solution(mesh):
    placed = (
        P("ctx", "zero"),
        P(),
        P("ctx", "zero"),
        P("ctx", "zero", None),
        P("zero", "ctx"),
        P("ctx", None, None),
        P("ctx", None, None),
        P(),
    )
    return jax.shard_map(
        local, mesh=mesh, in_specs=placed, out_specs=P(("ctx", "zero"), None), check_vma=False
    )
```

```python
import functools
import math

import jax
import jax.numpy as jnp
from jax import lax
from jax.experimental import pallas as pl
from jax.experimental.pallas import tpu as pltpu
from jax.sharding import PartitionSpec as P

HBM = pl.BlockSpec(memory_space=pltpu.HBM)
VMEM = pl.BlockSpec(memory_space=pltpu.VMEM)
SMEM = pl.BlockSpec(memory_space=pltpu.SMEM)
VMEM_LIMIT = 32 * 1024 * 1024
ROPE_BASE = 500000.0


def swap(value, axis, stride):
    pairs = [(source, source ^ stride) for source in range(lax.axis_size(axis))]
    return lax.ppermute(value, axis, pairs)


def cycle(size):
    return list(range(0, size, 2)) + list(range(1, size, 2))[::-1]


def ring_step(value):
    ctx_size, zero_size = lax.axis_size("ctx"), lax.axis_size("zero")
    order = cycle(ctx_size)
    pairs = []
    for at in range(ctx_size):
        for zero in range(zero_size):
            to = order[(at + (1 if zero % 2 == 0 else -1)) % ctx_size]
            pairs.append((order[at] * zero_size + zero, to * zero_size + zero))
    return lax.ppermute(value, ("ctx", "zero"), pairs)


class Ring:
    def __init__(self, shard, core, whole=None, base=0):
        self.held = [(0, None, 0, shard if whole is None else whole)] if base == 0 else []
        self.base = base
        self.moving, self.core, self.at = shard, core, 0
        self.length = lax.axis_size("ctx") // 2

    def step(self, *after):
        self.at += 1
        last = self.at == self.length
        if last:
            half = self.moving.shape[0] // 2
            self.moving = lax.dynamic_slice_in_dim(self.moving, self.core * half, half, 0)
        behind = self.held[-3][3:] if last else []
        self.moving = ring_step(tied(self.moving, *behind, *after))
        self.held.append((-self.at, 0 if last else None, self.base, self.moving))
        self.held.append(
            (self.at, 1 if last else None, self.base, swap(self.moving, "zero", 1))
        )
        return self.moving

    def advance(self, part, parts, *after):
        while self.at < self.length * (part + 1) // parts:
            self.step(*after)
        return self.moving


def tied(value, *others):
    return lax.optimization_barrier((value, *others))[0] if others else value


def source_of(steps):
    size = lax.axis_size("ctx")
    ctx, core = lax.axis_index("ctx"), lax.axis_index("zero") % 2
    place = jnp.where(ctx % 2 == 0, ctx // 2, size - 1 - ctx // 2)
    place = lax.rem(place + steps * (1 - 2 * core) + size, size)
    return jnp.where(place < size // 2, 2 * place, 2 * (size - 1 - place) + 1)


def share_of(share):
    core = lax.axis_index("zero") % 2
    return core if share == 0 else 1 - core


def token_rows(group, other, size):
    core = lax.axis_index("zero") % 2
    if other:
        core = 1 - core
    return pl.ds(pl.multiple_of((2 * group + core) * size, 16), size)


def deal_kernel(count, *refs):
    x_refs, outs, sem = refs[:count], refs[count:-1], refs[-1]
    groups = lax.axis_size("zero") // 2
    size = x_refs[0].shape[0] // (2 * groups)
    copies = []
    for x_ref, out_ref in zip(x_refs, outs):
        for group in range(groups):
            copies.append(
                pltpu.make_async_copy(
                    x_ref.at[token_rows(group, True, size)],
                    out_ref.at[pl.ds(group * size, size)],
                    sem.at[len(copies)],
                )
            )
    for copy in copies:
        copy.start()
    for copy in copies:
        copy.wait()


def deal(arrays):
    tokens, depth = arrays[0].shape
    part = jax.ShapeDtypeStruct((tokens // 2, depth), arrays[0].dtype)
    copies = len(arrays) * lax.axis_size("zero") // 2
    return pl.pallas_call(
        functools.partial(deal_kernel, len(arrays)),
        out_shape=[part] * len(arrays),
        in_specs=[HBM] * len(arrays),
        out_specs=[HBM] * len(arrays),
        scratch_shapes=[pltpu.SemaphoreType.DMA((copies,))],
        compiler_params=pltpu.CompilerParams(vmem_limit_bytes=VMEM_LIMIT),
    )(*arrays)


def project_kernel(layout, *refs):
    (kv_ref, q_ref, x_buf, w_buf, x_sem, w_sem) = refs[-6:]
    pieces, tokens, depth = x_buf.shape
    cos_ref, sin_ref = refs[:2]
    x_refs = refs[2 : 2 + pieces]
    w_refs = refs[2 + pieces : -6]
    zero = lax.axis_index("zero")
    shard_rows = w_refs[0].shape[0]
    x_copies, w_copies = [], []
    for m, ref in enumerate(x_refs):
        target = x_buf.at[jnp.bitwise_xor(zero, m)]
        if m % 2:
            x_copies.append(pltpu.make_async_copy(ref, target, x_sem.at[len(x_copies)]))
            continue
        size = 2 * tokens // pieces
        for group in range(pieces // 2):
            x_copies.append(
                pltpu.make_async_copy(
                    ref.at[token_rows(group, False, size)],
                    target.at[pl.ds(group * size, size)],
                    x_sem.at[len(x_copies)],
                )
            )
    for at, (ref, (steps, share, base)) in enumerate(zip(w_refs, layout)):
        start = source_of(steps) * shard_rows + base
        if share is not None:
            start = start + share_of(share) * ref.shape[0]
        rows = pl.ds(pl.multiple_of(start, 16), ref.shape[0])
        w_copies.append(pltpu.make_async_copy(ref, w_buf.at[rows], w_sem.at[at]))
    for copy in x_copies + w_copies:
        copy.start()
    for copy in x_copies:
        copy.wait()
    squares = jnp.zeros((tokens, 128), jnp.float32)
    for at in range(pieces):
        for first in range(0, depth, 128):
            x_float = x_buf[at, :, first : first + 128].astype(jnp.float32)
            squares += x_float * x_float
    mean = jnp.sum(squares, axis=1, keepdims=True) / (depth * pieces)
    scale = jnp.broadcast_to(lax.rsqrt(mean + 1e-05), squares.shape)
    for copy in w_copies:
        copy.wait()
    head = cos_ref.shape[1]
    shrink = jnp.float32(head ** (-0.5))
    for out_ref, columns in ((kv_ref, 0), (q_ref, 2 * head)):
        for first in range(0, out_ref.shape[1], 2 * head):
            both = slice(columns + first, columns + first + 2 * head)
            total = jnp.zeros((tokens, 2 * head), jnp.float32)
            for at in range(pieces):
                total += jnp.dot(
                    x_buf[at],
                    w_buf[at * depth : (at + 1) * depth, both],
                    preferred_element_type=jnp.float32,
                )
            for at in range(2):
                part = total[:, at * head : (at + 1) * head] * scale
                if columns or not at:
                    part = part * cos_ref[...] + pltpu.roll(part, head // 2, 1) * sin_ref[...]
                if columns:
                    part = part * shrink
                out_ref[:, first + at * head : first + (at + 1) * head] = part.astype(
                    out_ref.dtype
                )


def project(cos, sin, x_pieces, held):
    layout = [(steps, share, base) for steps, share, base, _ in held]
    shards = [piece for _, _, _, piece in held]
    tokens, depth = x_pieces[1].shape
    pieces, head = len(x_pieces), cos.shape[1]
    width = shards[0].shape[1]
    full = depth * pieces
    return pl.pallas_call(
        functools.partial(project_kernel, layout),
        out_shape=[
            jax.ShapeDtypeStruct((tokens, 2 * head), jnp.bfloat16),
            jax.ShapeDtypeStruct((tokens, width - 2 * head), jnp.bfloat16),
        ],
        in_specs=[VMEM] * 2 + [HBM] * (pieces + len(shards)),
        out_specs=[VMEM] * 2,
        scratch_shapes=[
            pltpu.VMEM((pieces, tokens, depth), jnp.bfloat16),
            pltpu.VMEM((full, width), jnp.bfloat16),
            pltpu.SemaphoreType.DMA((pieces // 2 * (1 + pieces // 2),)),
            pltpu.SemaphoreType.DMA((len(shards),)),
        ],
        compiler_params=pltpu.CompilerParams(vmem_limit_bytes=VMEM_LIMIT),
        cost_estimate=pl.CostEstimate(
            flops=2 * tokens * full * width,
            bytes_accessed=2 * full * (tokens + width),
            transcendentals=0,
        ),
    )(cos, sin, *x_pieces, *shards)


def attend_kernel(groups, stays, own_ref, far_ref, *refs):
    out_ref, q_ref, near0, near1, far0, far1, sem = refs[5:]
    copies = [
        pltpu.make_async_copy(source, target, sem.at[at])
        for at, (source, target) in enumerate(zip(refs[:5], refs[6:11]))
    ]
    for copy in copies:
        copy.start()
    for copy in copies:
        copy.wait()
    tokens, pair = near0.shape
    head = pair // 2
    size = tokens // groups
    tiles = own_ref.shape[0]
    tile = 2 * tokens // tiles
    heads = q_ref.shape[1] // head
    rows = heads * size
    core = lax.axis_index("zero") % 2
    column = lax.broadcasted_iota(jnp.int32, (1, tokens), 1)
    column_group = column // size
    within = lax.rem(lax.broadcasted_iota(jnp.int32, (rows, 1), 0), size)
    hidden = jnp.float32(-1e30)
    nt = (((1,), (1,)), ((), ()))
    side = lax.axis_index("zero") // 2 % 2
    for pair_of in range(groups // 2):
        h = 2 * pair_of + (side if stays else 1 - side)
        across = pl.ds(pl.multiple_of(h * size, 16), size)
        q = jnp.concatenate(
            [q_ref[across, g * head : (g + 1) * head] for g in range(heads)], axis=0
        )
        first = (2 * h + core) * size
        own_tile = first // tile
        seen = min(tokens, -(-(2 * pair_of + 2) * size // 128) * 128)
        parts, blocks = [], []
        for ref, mask_ref, width, parity, causal in (
            (far0, far_ref, tokens, core, False),
            (far1, far_ref, tokens, 1 - core, False),
            (near0, own_ref, seen, core, True),
            (near1, own_ref, seen, 1 - core, True),
        ):
            visible = jnp.zeros((1, width), jnp.int32)
            for g in range(-(-width // size)):
                at = mask_ref[own_tile, (2 * g + parity) * size // tile]
                visible = jnp.where(column_group[:, :width] == g, at, visible)
            visible = visible == 1
            if causal:
                group = column_group[:, :width]
                offset = (2 * group + parity) * size + column[:, :width] - group * size
                visible = visible & (offset <= first + within)
            scores = lax.dot_general(
                q, ref[:width, :head], nt, preferred_element_type=jnp.float32
            )
            parts.append(jnp.where(visible, scores, hidden))
            blocks.append((ref, width))
        scores = jnp.concatenate(parts, axis=1)
        largest = jnp.max(scores, axis=1, keepdims=True)
        weights = jnp.exp(scores - largest)
        total = jnp.sum(weights, axis=1, keepdims=True)
        rounded = weights.astype(jnp.bfloat16)
        mixed = jnp.zeros((rows, head), jnp.float32)
        start = 0
        for ref, width in blocks:
            mixed += jnp.dot(
                rounded[:, start : start + width],
                ref[:width, head:],
                preferred_element_type=jnp.float32,
            )
            start += width
        mixed = (mixed / total).astype(out_ref.dtype)
        for g in range(heads):
            out_ref[pair_of * size : (pair_of + 1) * size, g * head : (g + 1) * head] = mixed[
                g * size : (g + 1) * size, :
            ]


def attend(groups, stays, own_mask, far_mask, queries, near, near_other, far, far_other):
    tokens, width = queries.shape
    return pl.pallas_call(
        functools.partial(attend_kernel, groups, stays),
        out_shape=jax.ShapeDtypeStruct((tokens // 2, width), jnp.bfloat16),
        in_specs=[SMEM, SMEM] + [HBM] * 5,
        out_specs=VMEM,
        scratch_shapes=[pltpu.VMEM(queries.shape, jnp.bfloat16)]
        + [pltpu.VMEM(near.shape, jnp.bfloat16)] * 4
        + [pltpu.SemaphoreType.DMA((5,))],
        compiler_params=pltpu.CompilerParams(vmem_limit_bytes=VMEM_LIMIT),
        cost_estimate=pl.CostEstimate(
            flops=8 * tokens * tokens * width,
            bytes_accessed=8 * tokens * width,
            transcendentals=8 * tokens * tokens,
        ),
    )(own_mask, far_mask, queries, near, near_other, far, far_other)


def mix_kernel(layout, slots, out_refs, *refs):
    count = len(refs) - len(layout) - out_refs - 2
    a_refs, w_refs = refs[:count], refs[count : count + len(layout)]
    outs = refs[count + len(layout) : -2]
    w_buf, sem = refs[-2:]
    width = w_buf.shape[2]
    half = a_refs[0].shape[1]
    copies = []
    for at, (ref, (slot, side, share)) in enumerate(zip(w_refs, layout)):
        rows = ref.shape[0]
        start = side * half
        if share is not None:
            start = pl.multiple_of(start + share_of(share) * rows, 16)
        copies.append(pltpu.make_async_copy(ref, w_buf.at[slot, pl.ds(start, rows)], sem.at[at]))
    for copy in copies:
        copy.start()
    slot = 0
    for out_ref, sides, number in zip(outs, *slots):
        rows = jnp.concatenate([ref[...] for ref in a_refs[:sides]], axis=1)
        for place in range(number):
            for copy, (its_slot, _, _) in zip(copies, layout):
                if its_slot == slot:
                    copy.wait()
            total = jnp.dot(
                rows, w_buf[slot, : sides * half], preferred_element_type=jnp.float32
            )
            out_ref[:, place * width : (place + 1) * width] = total.astype(out_ref.dtype)
            slot += 1


def mix(rows, blocks, dtypes):
    layout, shards = [], []
    sides = [1 + max(side for side, _, _ in block[0]) for block in blocks]
    slots = [slot for block in blocks for slot in block]
    for at, slot in enumerate(slots):
        for side, share, piece in slot:
            layout.append((at, side, share))
            shards.append(piece)
    tokens, half = rows[0].shape
    width = shards[0].shape[1]
    return pl.pallas_call(
        functools.partial(
            mix_kernel, layout, (sides, [len(block) for block in blocks]), len(blocks)
        ),
        out_shape=[
            jax.ShapeDtypeStruct((tokens, width * len(block)), dtype)
            for block, dtype in zip(blocks, dtypes)
        ],
        in_specs=[VMEM] * len(rows) + [HBM] * len(shards),
        out_specs=[VMEM] * len(blocks),
        scratch_shapes=[
            pltpu.VMEM((len(slots), max(sides) * half, width), jnp.bfloat16),
            pltpu.SemaphoreType.DMA((len(shards),)),
        ],
        compiler_params=pltpu.CompilerParams(vmem_limit_bytes=VMEM_LIMIT),
        cost_estimate=pl.CostEstimate(
            flops=2 * tokens * half * width * len(shards),
            bytes_accessed=6 * half * width * len(shards) + 4 * tokens * width * len(slots),
            transcendentals=0,
        ),
    )(*rows, *shards)


def join_kernel(steps, full_ref, keep_ref, got_ref, out_ref):
    width = out_ref.shape[1] // len(steps)
    whole = full_ref.shape[1] // width
    for slot, along in enumerate(steps):
        start = pl.multiple_of(source_of(along) * width, 128)
        if slot < whole:
            block = full_ref[:, slot * width : (slot + 1) * width]
        else:
            columns = slice((slot - whole) * width, (slot - whole + 1) * width)
            block = keep_ref[:, columns] + got_ref[:, columns].astype(jnp.float32)
        out_ref[:, pl.ds(start, width)] = block.astype(out_ref.dtype)


def join(steps, full, keep, got, dtype):
    rows = full.shape[0]
    columns = full.shape[1] + keep.shape[1]
    return pl.pallas_call(
        functools.partial(join_kernel, steps),
        out_shape=jax.ShapeDtypeStruct((rows, columns), dtype),
        in_specs=[VMEM] * 3,
        out_specs=VMEM,
        compiler_params=pltpu.CompilerParams(vmem_limit_bytes=VMEM_LIMIT),
        cost_estimate=pl.CostEstimate(
            flops=rows * columns, bytes_accessed=8 * rows * columns, transcendentals=0
        ),
    )(full, keep, got)


def exchange_from(value, root, bit):
    other = swap(value, "ctx", 1 << bit)
    same = ((lax.axis_index("ctx") >> bit) & 1) == ((root >> bit) & 1)
    return jnp.where(same, value, other)


def local(
    activations,
    norm_gain,
    query_weight,
    kv_weight,
    out_weight,
    tile_mask,
    anchor_mask,
    anchor_index,
):
    tokens, depth = activations.shape
    head = kv_weight.shape[2]
    ctx_size, zero_size = lax.axis_size("ctx"), lax.axis_size("zero")
    ctx_rank, zero_rank = lax.axis_index("ctx"), lax.axis_index("zero")
    core = zero_rank % 2
    groups = zero_size // 2
    size = tokens // zero_size

    blocks = {0: activations}
    stride = groups
    while stride > 1:
        for known in range(0, zero_size, 2 * stride):
            blocks[known + stride] = swap(blocks[known], "zero", stride)
        stride //= 2

    shard_rows = kv_weight.shape[0]
    gain = lax.dynamic_slice_in_dim(norm_gain, ctx_rank * shard_rows, shard_rows)
    gain = gain.astype(jnp.float32)[:, None]
    kv_own = kv_weight[:, 0, :]
    kv_other, query_other = swap(kv_own, "zero", 1), swap(query_weight, "zero", 1)
    pair = jnp.where(
        core == 0,
        jnp.concatenate([kv_own, kv_other, query_weight, query_other], 1),
        jnp.concatenate([kv_other, kv_own, query_other, query_weight], 1),
    )
    pair = (pair.astype(jnp.float32) * gain).astype(jnp.bfloat16)
    out_other = swap(out_weight, "zero", 1)
    out_pair = jnp.where(
        core == 0,
        jnp.concatenate([out_weight, out_other], 0),
        jnp.concatenate([out_other, out_weight], 0),
    )
    ring_rows = shard_rows // 2
    rings = [
        Ring(pair[:ring_rows], core, pair),
        Ring(pair[ring_rows:], core, None, ring_rows),
    ]
    out_ring = Ring(out_pair, core)
    for part in range(4):
        for ring in rings:
            ring.advance(part, 4)
    held = rings[0].held + rings[1].held
    beyond = [swap(out_weight, "zero", 2)]
    out_ring.advance(0, 4, *[ring.moving for ring in rings], *beyond)

    far_blocks = [tied(blocks[m], rings[0].moving) for m in range(2, zero_size, 2)]
    x_pieces = []
    for at, theirs in enumerate(deal([blocks[0]]) + deal(far_blocks)):
        x_pieces += [([blocks[0]] + far_blocks)[at], swap(theirs, "zero", 1)]

    half = head // 2
    frequency = jnp.power(
        jnp.float32(ROPE_BASE), -(jnp.arange(half, dtype=jnp.float32) * 2.0 / head)
    )
    local_token = jnp.arange(tokens // 2, dtype=jnp.int32)
    offsets = (2 * (local_token // size) + core) * size + local_token % size
    positions = ctx_rank * tokens + offsets
    angles = positions.astype(jnp.float32)[:, None] * frequency[None, :]
    cos_half, sin_half = jnp.cos(angles), jnp.sin(angles)
    cos = jnp.concatenate([cos_half, cos_half], -1)
    sin = jnp.concatenate([-sin_half, sin_half], -1)

    near, queries = project(cos, sin, x_pieces, held)

    def share():
        for at in range(len(beyond), out_ring.at + 1):
            beyond.append(swap(out_ring.held[2 * at - 1][3], "zero", 2))

    share()
    anchor = anchor_index[0]
    far = tied(near, out_ring.moving)
    bits = int(math.log2(ctx_size))
    for bit in range(bits):
        far = exchange_from(far, anchor, bit)
        if bit == 0:
            near_other = swap(near, "zero", 1)
            far = tied(far, near_other)
            first = beyond[-1]
            out_ring.advance(1, 4, far)
            share()
        elif bit == 1:
            out_ring.advance(2, 4, far, first)
    queries = tied(queries, beyond[-1])
    share()
    out_ring.advance(3, 4, far)
    far_other = swap(far, "zero", 1)
    far_mask = jnp.where(ctx_rank != anchor, anchor_mask[0], 0)
    both_blocks = (near, near_other, far, far_other)
    send = attend(groups, False, tile_mask[0], far_mask, queries, *both_blocks)
    got = swap(send, "zero", 2)
    out_ring.held[-1] = (
        *out_ring.held[-1][:3],
        swap(tied(out_ring.moving, send), "zero", 1),
    )
    keep = attend(groups, True, tile_mask[0], far_mask, queries, *both_blocks)

    steps_of, both_chips, one_chip = [], [], []
    for steps, half_of, _, piece in out_ring.held:
        slots = both_chips if abs(steps) < len(beyond) else one_chip
        if half_of != 1:
            steps_of.append(steps)
            slots.append([])
        slots[-1].append((0, half_of, piece))
        if slots is both_chips:
            if steps <= 0:
                across = swap(beyond[-steps], "zero", 1)
            if steps == 0:
                slots[-1] += [(1, 0, beyond[0]), (1, 1, across)]
            else:
                slots[-1].append((1, half_of, beyond[-steps] if steps < 0 else across))
    (terms,) = mix([tied(send, beyond[-1])], [one_chip], [jnp.bfloat16])
    got_terms = swap(tied(terms, got), "zero", 2)
    full, kept = mix([keep, got], [both_chips, one_chip], [jnp.float32, jnp.float32])
    if zero_size == 4:
        return join(steps_of, full, kept, got_terms, jnp.bfloat16)
    total = join(steps_of, full, kept, got_terms, jnp.float32)
    stride = zero_size // 2
    while stride > 2:
        rows = total.shape[0] // 2
        bit = (zero_rank // stride) % 2
        stay = lax.dynamic_slice_in_dim(total, bit * rows, rows, 0)
        go = lax.dynamic_slice_in_dim(total, (1 - bit) * rows, rows, 0)
        total = stay + swap(go.astype(jnp.bfloat16), "zero", stride).astype(jnp.float32)
        stride //= 2
    return total.astype(jnp.bfloat16)


def solution(mesh):
    placed = (
        P("ctx", "zero"),
        P(),
        P("ctx", "zero"),
        P("ctx", "zero", None),
        P("zero", "ctx"),
        P("ctx", None, None),
        P("ctx", None, None),
        P(),
    )
    return jax.shard_map(
        local, mesh=mesh, in_specs=placed, out_specs=P(("ctx", "zero"), None), check_vma=False
    )
```

```python
import functools
import math

import jax
import jax.numpy as jnp
from jax import lax
from jax.experimental import pallas as pl
from jax.experimental.pallas import tpu as pltpu
from jax.sharding import PartitionSpec as P

HBM = pl.BlockSpec(memory_space=pltpu.HBM)
VMEM = pl.BlockSpec(memory_space=pltpu.VMEM)
SMEM = pl.BlockSpec(memory_space=pltpu.SMEM)
VMEM_LIMIT = 32 * 1024 * 1024
ROPE_BASE = 500000.0


def swap(value, axis, stride):
    pairs = [(source, source ^ stride) for source in range(lax.axis_size(axis))]
    return lax.ppermute(value, axis, pairs)


def cycle(size):
    return list(range(0, size, 2)) + list(range(1, size, 2))[::-1]


def ring_step(value):
    ctx_size, zero_size = lax.axis_size("ctx"), lax.axis_size("zero")
    order = cycle(ctx_size)
    pairs = []
    for at in range(ctx_size):
        for zero in range(zero_size):
            to = order[(at + (1 if zero % 2 == 0 else -1)) % ctx_size]
            pairs.append((order[at] * zero_size + zero, to * zero_size + zero))
    return lax.ppermute(value, ("ctx", "zero"), pairs)


class Ring:
    def __init__(self, shard, core, whole=None, base=0):
        self.held = [(0, None, 0, shard if whole is None else whole)] if base == 0 else []
        self.base = base
        self.moving, self.core, self.at = shard, core, 0
        self.length = lax.axis_size("ctx") // 2

    def step(self, *after):
        self.at += 1
        last = self.at == self.length
        if last:
            half = self.moving.shape[0] // 2
            self.moving = lax.dynamic_slice_in_dim(self.moving, self.core * half, half, 0)
        behind = self.held[-3][3:] if len(self.held) > 3 else []
        self.moving = ring_step(tied(self.moving, *behind, *after))
        self.held.append((-self.at, 0 if last else None, self.base, self.moving))
        self.held.append(
            (self.at, 1 if last else None, self.base, swap(self.moving, "zero", 1))
        )
        return self.moving

    def advance(self, part, parts, *after):
        while self.at < self.length * (part + 1) // parts:
            self.step(*after)
        return self.moving


def tied(value, *others):
    return lax.optimization_barrier((value, *others))[0] if others else value


def source_of(steps):
    size = lax.axis_size("ctx")
    ctx, core = lax.axis_index("ctx"), lax.axis_index("zero") % 2
    place = jnp.where(ctx % 2 == 0, ctx // 2, size - 1 - ctx // 2)
    place = lax.rem(place + steps * (1 - 2 * core) + size, size)
    return jnp.where(place < size // 2, 2 * place, 2 * (size - 1 - place) + 1)


def share_of(share):
    core = lax.axis_index("zero") % 2
    return core if share == 0 else 1 - core


def token_rows(group, other, size):
    core = lax.axis_index("zero") % 2
    if other:
        core = 1 - core
    return pl.ds(pl.multiple_of((2 * group + core) * size, 16), size)


def deal_kernel(count, *refs):
    x_refs, outs, sem = refs[:count], refs[count:-1], refs[-1]
    groups = lax.axis_size("zero") // 2
    size = x_refs[0].shape[0] // (2 * groups)
    copies = []
    for x_ref, out_ref in zip(x_refs, outs):
        for group in range(groups):
            copies.append(
                pltpu.make_async_copy(
                    x_ref.at[token_rows(group, True, size)],
                    out_ref.at[pl.ds(group * size, size)],
                    sem.at[len(copies)],
                )
            )
    for copy in copies:
        copy.start()
    for copy in copies:
        copy.wait()


def deal(arrays):
    tokens, depth = arrays[0].shape
    part = jax.ShapeDtypeStruct((tokens // 2, depth), arrays[0].dtype)
    copies = len(arrays) * lax.axis_size("zero") // 2
    return pl.pallas_call(
        functools.partial(deal_kernel, len(arrays)),
        out_shape=[part] * len(arrays),
        in_specs=[HBM] * len(arrays),
        out_specs=[HBM] * len(arrays),
        scratch_shapes=[pltpu.SemaphoreType.DMA((copies,))],
        compiler_params=pltpu.CompilerParams(vmem_limit_bytes=VMEM_LIMIT),
    )(*arrays)


def project_kernel(layout, *refs):
    (kv_ref, q_ref, x_buf, w_buf, x_sem, w_sem) = refs[-6:]
    pieces, tokens, depth = x_buf.shape
    cos_ref, sin_ref = refs[:2]
    x_refs = refs[2 : 2 + pieces]
    w_refs = refs[2 + pieces : -6]
    zero = lax.axis_index("zero")
    shard_rows = w_refs[0].shape[0]
    x_copies, w_copies = [], []
    for m, ref in enumerate(x_refs):
        target = x_buf.at[jnp.bitwise_xor(zero, m)]
        if m % 2:
            x_copies.append(pltpu.make_async_copy(ref, target, x_sem.at[len(x_copies)]))
            continue
        size = 2 * tokens // pieces
        for group in range(pieces // 2):
            x_copies.append(
                pltpu.make_async_copy(
                    ref.at[token_rows(group, False, size)],
                    target.at[pl.ds(group * size, size)],
                    x_sem.at[len(x_copies)],
                )
            )
    for at, (ref, (steps, share, base)) in enumerate(zip(w_refs, layout)):
        start = source_of(steps) * shard_rows + base
        if share is not None:
            start = start + share_of(share) * ref.shape[0]
        rows = pl.ds(pl.multiple_of(start, 16), ref.shape[0])
        w_copies.append(pltpu.make_async_copy(ref, w_buf.at[rows], w_sem.at[at]))
    for copy in x_copies + w_copies:
        copy.start()
    for copy in x_copies:
        copy.wait()
    squares = jnp.zeros((tokens, 128), jnp.float32)
    for at in range(pieces):
        for first in range(0, depth, 128):
            x_float = x_buf[at, :, first : first + 128].astype(jnp.float32)
            squares += x_float * x_float
    mean = jnp.sum(squares, axis=1, keepdims=True) / (depth * pieces)
    scale = jnp.broadcast_to(lax.rsqrt(mean + 1e-05), squares.shape)
    for copy in w_copies:
        copy.wait()
    head = cos_ref.shape[1]
    shrink = jnp.float32(head ** (-0.5))
    for out_ref, columns in ((kv_ref, 0), (q_ref, 2 * head)):
        for first in range(0, out_ref.shape[1], 2 * head):
            both = slice(columns + first, columns + first + 2 * head)
            total = jnp.zeros((tokens, 2 * head), jnp.float32)
            for at in range(pieces):
                total += jnp.dot(
                    x_buf[at],
                    w_buf[at * depth : (at + 1) * depth, both],
                    preferred_element_type=jnp.float32,
                )
            for at in range(2):
                part = total[:, at * head : (at + 1) * head] * scale
                if columns or not at:
                    part = part * cos_ref[...] + pltpu.roll(part, head // 2, 1) * sin_ref[...]
                if columns:
                    part = part * shrink
                out_ref[:, first + at * head : first + (at + 1) * head] = part.astype(
                    out_ref.dtype
                )


def project(cos, sin, x_pieces, held):
    layout = [(steps, share, base) for steps, share, base, _ in held]
    shards = [piece for _, _, _, piece in held]
    tokens, depth = x_pieces[1].shape
    pieces, head = len(x_pieces), cos.shape[1]
    width = shards[0].shape[1]
    full = depth * pieces
    return pl.pallas_call(
        functools.partial(project_kernel, layout),
        out_shape=[
            jax.ShapeDtypeStruct((tokens, 2 * head), jnp.bfloat16),
            jax.ShapeDtypeStruct((tokens, width - 2 * head), jnp.bfloat16),
        ],
        in_specs=[VMEM] * 2 + [HBM] * (pieces + len(shards)),
        out_specs=[VMEM] * 2,
        scratch_shapes=[
            pltpu.VMEM((pieces, tokens, depth), jnp.bfloat16),
            pltpu.VMEM((full, width), jnp.bfloat16),
            pltpu.SemaphoreType.DMA((pieces // 2 * (1 + pieces // 2),)),
            pltpu.SemaphoreType.DMA((len(shards),)),
        ],
        compiler_params=pltpu.CompilerParams(vmem_limit_bytes=VMEM_LIMIT),
        cost_estimate=pl.CostEstimate(
            flops=2 * tokens * full * width,
            bytes_accessed=2 * full * (tokens + width),
            transcendentals=0,
        ),
    )(cos, sin, *x_pieces, *shards)


def attend_kernel(groups, stays, own_ref, far_ref, *refs):
    out_ref, q_ref, near0, near1, far0, far1, sem = refs[5:]
    copies = [
        pltpu.make_async_copy(source, target, sem.at[at])
        for at, (source, target) in enumerate(zip(refs[:5], refs[6:11]))
    ]
    for copy in copies:
        copy.start()
    for copy in copies:
        copy.wait()
    tokens, pair = near0.shape
    head = pair // 2
    size = tokens // groups
    tiles = own_ref.shape[0]
    tile = 2 * tokens // tiles
    heads = q_ref.shape[1] // head
    rows = heads * size
    core = lax.axis_index("zero") % 2
    column = lax.broadcasted_iota(jnp.int32, (1, tokens), 1)
    column_group = column // size
    within = lax.rem(lax.broadcasted_iota(jnp.int32, (rows, 1), 0), size)
    hidden = jnp.float32(-1e30)
    nt = (((1,), (1,)), ((), ()))
    side = lax.axis_index("zero") // 2 % 2
    for pair_of in range(groups // 2):
        h = 2 * pair_of + (side if stays else 1 - side)
        across = pl.ds(pl.multiple_of(h * size, 16), size)
        q = jnp.concatenate(
            [q_ref[across, g * head : (g + 1) * head] for g in range(heads)], axis=0
        )
        first = (2 * h + core) * size
        own_tile = first // tile
        seen = min(tokens, -(-(2 * pair_of + 2) * size // 128) * 128)
        parts, blocks = [], []
        for ref, mask_ref, width, parity, causal in (
            (far0, far_ref, tokens, core, False),
            (far1, far_ref, tokens, 1 - core, False),
            (near0, own_ref, seen, core, True),
            (near1, own_ref, seen, 1 - core, True),
        ):
            visible = jnp.zeros((1, width), jnp.int32)
            for g in range(-(-width // size)):
                at = mask_ref[own_tile, (2 * g + parity) * size // tile]
                visible = jnp.where(column_group[:, :width] == g, at, visible)
            visible = visible == 1
            if causal:
                group = column_group[:, :width]
                offset = (2 * group + parity) * size + column[:, :width] - group * size
                visible = visible & (offset <= first + within)
            scores = lax.dot_general(
                q, ref[:width, :head], nt, preferred_element_type=jnp.float32
            )
            parts.append(jnp.where(visible, scores, hidden))
            blocks.append((ref, width))
        scores = jnp.concatenate(parts, axis=1)
        largest = jnp.max(scores, axis=1, keepdims=True)
        weights = jnp.exp(scores - largest)
        total = jnp.sum(weights, axis=1, keepdims=True)
        rounded = weights.astype(jnp.bfloat16)
        mixed = jnp.zeros((rows, head), jnp.float32)
        start = 0
        for ref, width in blocks:
            mixed += jnp.dot(
                rounded[:, start : start + width],
                ref[:width, head:],
                preferred_element_type=jnp.float32,
            )
            start += width
        mixed = (mixed / total).astype(out_ref.dtype)
        for g in range(heads):
            out_ref[pair_of * size : (pair_of + 1) * size, g * head : (g + 1) * head] = mixed[
                g * size : (g + 1) * size, :
            ]


def attend(groups, stays, own_mask, far_mask, queries, near, near_other, far, far_other):
    tokens, width = queries.shape
    return pl.pallas_call(
        functools.partial(attend_kernel, groups, stays),
        out_shape=jax.ShapeDtypeStruct((tokens // 2, width), jnp.bfloat16),
        in_specs=[SMEM, SMEM] + [HBM] * 5,
        out_specs=VMEM,
        scratch_shapes=[pltpu.VMEM(queries.shape, jnp.bfloat16)]
        + [pltpu.VMEM(near.shape, jnp.bfloat16)] * 4
        + [pltpu.SemaphoreType.DMA((5,))],
        compiler_params=pltpu.CompilerParams(vmem_limit_bytes=VMEM_LIMIT),
        cost_estimate=pl.CostEstimate(
            flops=8 * tokens * tokens * width,
            bytes_accessed=8 * tokens * width,
            transcendentals=8 * tokens * tokens,
        ),
    )(own_mask, far_mask, queries, near, near_other, far, far_other)


def mix_kernel(layout, slots, out_refs, *refs):
    count = len(refs) - len(layout) - out_refs - 2
    a_refs, w_refs = refs[:count], refs[count : count + len(layout)]
    outs = refs[count + len(layout) : -2]
    w_buf, sem = refs[-2:]
    width = w_buf.shape[2]
    half = a_refs[0].shape[1]
    copies = []
    for at, (ref, (slot, side, share)) in enumerate(zip(w_refs, layout)):
        rows = ref.shape[0]
        start = side * half
        if share is not None:
            start = pl.multiple_of(start + share_of(share) * rows, 16)
        copies.append(pltpu.make_async_copy(ref, w_buf.at[slot, pl.ds(start, rows)], sem.at[at]))
    for copy in copies:
        copy.start()
    slot = 0
    for out_ref, sides, number in zip(outs, *slots):
        rows = jnp.concatenate([ref[...] for ref in a_refs[:sides]], axis=1)
        for place in range(number):
            for copy, (its_slot, _, _) in zip(copies, layout):
                if its_slot == slot:
                    copy.wait()
            total = jnp.dot(
                rows, w_buf[slot, : sides * half], preferred_element_type=jnp.float32
            )
            out_ref[:, place * width : (place + 1) * width] = total.astype(out_ref.dtype)
            slot += 1


def mix(rows, blocks, dtypes):
    layout, shards = [], []
    sides = [1 + max(side for side, _, _ in block[0]) for block in blocks]
    slots = [slot for block in blocks for slot in block]
    for at, slot in enumerate(slots):
        for side, share, piece in slot:
            layout.append((at, side, share))
            shards.append(piece)
    tokens, half = rows[0].shape
    width = shards[0].shape[1]
    return pl.pallas_call(
        functools.partial(
            mix_kernel, layout, (sides, [len(block) for block in blocks]), len(blocks)
        ),
        out_shape=[
            jax.ShapeDtypeStruct((tokens, width * len(block)), dtype)
            for block, dtype in zip(blocks, dtypes)
        ],
        in_specs=[VMEM] * len(rows) + [HBM] * len(shards),
        out_specs=[VMEM] * len(blocks),
        scratch_shapes=[
            pltpu.VMEM((len(slots), max(sides) * half, width), jnp.bfloat16),
            pltpu.SemaphoreType.DMA((len(shards),)),
        ],
        compiler_params=pltpu.CompilerParams(vmem_limit_bytes=VMEM_LIMIT),
        cost_estimate=pl.CostEstimate(
            flops=2 * tokens * half * width * len(shards),
            bytes_accessed=6 * half * width * len(shards) + 4 * tokens * width * len(slots),
            transcendentals=0,
        ),
    )(*rows, *shards)


def join_kernel(steps, full_ref, keep_ref, got_ref, out_ref):
    width = out_ref.shape[1] // len(steps)
    whole = full_ref.shape[1] // width
    for slot, along in enumerate(steps):
        start = pl.multiple_of(source_of(along) * width, 128)
        if slot < whole:
            block = full_ref[:, slot * width : (slot + 1) * width]
        else:
            columns = slice((slot - whole) * width, (slot - whole + 1) * width)
            block = keep_ref[:, columns] + got_ref[:, columns].astype(jnp.float32)
        out_ref[:, pl.ds(start, width)] = block.astype(out_ref.dtype)


def join(steps, full, keep, got, dtype):
    rows = full.shape[0]
    columns = full.shape[1] + keep.shape[1]
    return pl.pallas_call(
        functools.partial(join_kernel, steps),
        out_shape=jax.ShapeDtypeStruct((rows, columns), dtype),
        in_specs=[VMEM] * 3,
        out_specs=VMEM,
        compiler_params=pltpu.CompilerParams(vmem_limit_bytes=VMEM_LIMIT),
        cost_estimate=pl.CostEstimate(
            flops=rows * columns, bytes_accessed=8 * rows * columns, transcendentals=0
        ),
    )(full, keep, got)


def exchange_from(value, root, bit):
    other = swap(value, "ctx", 1 << bit)
    same = ((lax.axis_index("ctx") >> bit) & 1) == ((root >> bit) & 1)
    return jnp.where(same, value, other)


def local(
    activations,
    norm_gain,
    query_weight,
    kv_weight,
    out_weight,
    tile_mask,
    anchor_mask,
    anchor_index,
):
    tokens, depth = activations.shape
    head = kv_weight.shape[2]
    ctx_size, zero_size = lax.axis_size("ctx"), lax.axis_size("zero")
    ctx_rank, zero_rank = lax.axis_index("ctx"), lax.axis_index("zero")
    core = zero_rank % 2
    groups = zero_size // 2
    size = tokens // zero_size

    blocks = {0: activations}
    stride = groups
    while stride > 1:
        for known in range(0, zero_size, 2 * stride):
            blocks[known + stride] = swap(blocks[known], "zero", stride)
        stride //= 2

    shard_rows = kv_weight.shape[0]
    gain = lax.dynamic_slice_in_dim(norm_gain, ctx_rank * shard_rows, shard_rows)
    gain = gain.astype(jnp.float32)[:, None]
    kv_own = kv_weight[:, 0, :]
    kv_other, query_other = swap(kv_own, "zero", 1), swap(query_weight, "zero", 1)
    pair = jnp.where(
        core == 0,
        jnp.concatenate([kv_own, kv_other, query_weight, query_other], 1),
        jnp.concatenate([kv_other, kv_own, query_other, query_weight], 1),
    )
    pair = (pair.astype(jnp.float32) * gain).astype(jnp.bfloat16)
    out_other = swap(out_weight, "zero", 1)
    out_pair = jnp.where(
        core == 0,
        jnp.concatenate([out_weight, out_other], 0),
        jnp.concatenate([out_other, out_weight], 0),
    )
    ring_rows = shard_rows // 2
    rings = [
        Ring(pair[:ring_rows], core, pair),
        Ring(pair[ring_rows:], core, None, ring_rows),
    ]
    out_ring = Ring(out_pair, core)
    for part in range(4):
        for ring in rings:
            ring.advance(part, 4)
    held = rings[0].held + rings[1].held
    beyond = [swap(out_weight, "zero", 2)]
    out_ring.advance(0, 4, *[ring.moving for ring in rings], *beyond)

    far_blocks = [tied(blocks[m], rings[0].moving) for m in range(2, zero_size, 2)]
    x_pieces = []
    for at, theirs in enumerate(deal([blocks[0]]) + deal(far_blocks)):
        x_pieces += [([blocks[0]] + far_blocks)[at], swap(theirs, "zero", 1)]

    half = head // 2
    frequency = jnp.power(
        jnp.float32(ROPE_BASE), -(jnp.arange(half, dtype=jnp.float32) * 2.0 / head)
    )
    local_token = jnp.arange(tokens // 2, dtype=jnp.int32)
    offsets = (2 * (local_token // size) + core) * size + local_token % size
    positions = ctx_rank * tokens + offsets
    angles = positions.astype(jnp.float32)[:, None] * frequency[None, :]
    cos_half, sin_half = jnp.cos(angles), jnp.sin(angles)
    cos = jnp.concatenate([cos_half, cos_half], -1)
    sin = jnp.concatenate([-sin_half, sin_half], -1)

    near, queries = project(cos, sin, x_pieces, held)

    def share():
        for at in range(len(beyond), out_ring.at + 1):
            beyond.append(swap(out_ring.held[2 * at - 1][3], "zero", 2))

    share()
    anchor = anchor_index[0]
    far = tied(near, out_ring.moving)
    bits = int(math.log2(ctx_size))
    for bit in range(bits):
        far = exchange_from(far, anchor, bit)
        if bit == 0:
            near_other = swap(near, "zero", 1)
            far = tied(far, near_other)
            first = beyond[-1]
            out_ring.advance(1, 4, far)
            share()
        elif bit == 1:
            out_ring.advance(2, 4, far, first)
    queries = tied(queries, beyond[-1])
    share()
    far_other = swap(far, "zero", 1)
    out_ring.advance(3, 4, far_other)
    far_mask = jnp.where(ctx_rank != anchor, anchor_mask[0], 0)
    both_blocks = (near, near_other, far, far_other)
    send = attend(groups, False, tile_mask[0], far_mask, queries, *both_blocks)
    got = swap(send, "zero", 2)
    out_ring.held[-1] = (
        *out_ring.held[-1][:3],
        swap(tied(out_ring.moving, send), "zero", 1),
    )
    keep = attend(groups, True, tile_mask[0], far_mask, queries, *both_blocks)

    steps_of, both_chips, one_chip = [], [], []
    for steps, half_of, _, piece in out_ring.held:
        slots = both_chips if abs(steps) < len(beyond) else one_chip
        if half_of != 1:
            steps_of.append(steps)
            slots.append([])
        slots[-1].append((0, half_of, piece))
        if slots is both_chips:
            if steps <= 0:
                across = swap(beyond[-steps], "zero", 1)
            if steps == 0:
                slots[-1] += [(1, 0, beyond[0]), (1, 1, across)]
            else:
                slots[-1].append((1, half_of, beyond[-steps] if steps < 0 else across))
    (terms,) = mix([tied(send, beyond[-1])], [one_chip], [jnp.bfloat16])
    got_terms = swap(tied(terms, got), "zero", 2)
    full, kept = mix([keep, got], [both_chips, one_chip], [jnp.float32, jnp.float32])
    if zero_size == 4:
        return join(steps_of, full, kept, got_terms, jnp.bfloat16)
    total = join(steps_of, full, kept, got_terms, jnp.float32)
    stride = zero_size // 2
    while stride > 2:
        rows = total.shape[0] // 2
        bit = (zero_rank // stride) % 2
        stay = lax.dynamic_slice_in_dim(total, bit * rows, rows, 0)
        go = lax.dynamic_slice_in_dim(total, (1 - bit) * rows, rows, 0)
        total = stay + swap(go.astype(jnp.bfloat16), "zero", stride).astype(jnp.float32)
        stride //= 2
    return total.astype(jnp.bfloat16)


def solution(mesh):
    placed = (
        P("ctx", "zero"),
        P(),
        P("ctx", "zero"),
        P("ctx", "zero", None),
        P("zero", "ctx"),
        P("ctx", None, None),
        P("ctx", None, None),
        P(),
    )
    return jax.shard_map(
        local, mesh=mesh, in_specs=placed, out_specs=P(("ctx", "zero"), None), check_vma=False
    )
```

```python
import functools
import math

import jax
import jax.numpy as jnp
from jax import lax
from jax.experimental import pallas as pl
from jax.experimental.pallas import tpu as pltpu
from jax.sharding import PartitionSpec as P

HBM = pl.BlockSpec(memory_space=pltpu.HBM)
VMEM = pl.BlockSpec(memory_space=pltpu.VMEM)
SMEM = pl.BlockSpec(memory_space=pltpu.SMEM)
VMEM_LIMIT = 32 * 1024 * 1024
ROPE_BASE = 500000.0


def swap(value, axis, stride):
    pairs = [(source, source ^ stride) for source in range(lax.axis_size(axis))]
    return lax.ppermute(value, axis, pairs)


def cycle(size):
    return list(range(0, size, 2)) + list(range(1, size, 2))[::-1]


def ring_step(value):
    ctx_size, zero_size = lax.axis_size("ctx"), lax.axis_size("zero")
    order = cycle(ctx_size)
    pairs = []
    for at in range(ctx_size):
        for zero in range(zero_size):
            to = order[(at + (1 if zero % 2 == 0 else -1)) % ctx_size]
            pairs.append((order[at] * zero_size + zero, to * zero_size + zero))
    return lax.ppermute(value, ("ctx", "zero"), pairs)


class Ring:
    def __init__(self, shard, core, whole=None, base=0):
        self.held = [(0, None, 0, shard if whole is None else whole)] if base == 0 else []
        self.base = base
        self.moving, self.core, self.at = shard, core, 0
        self.length = lax.axis_size("ctx") // 2

    def step(self, *after):
        self.at += 1
        last = self.at == self.length
        if last:
            half = self.moving.shape[0] // 2
            self.moving = lax.dynamic_slice_in_dim(self.moving, self.core * half, half, 0)
        behind = self.held[-3][3:] if len(self.held) > 3 else []
        self.moving = ring_step(tied(self.moving, *behind, *after))
        self.held.append((-self.at, 0 if last else None, self.base, self.moving))
        self.held.append(
            (self.at, 1 if last else None, self.base, swap(self.moving, "zero", 1))
        )
        return self.moving

    def advance(self, part, parts, *after):
        while self.at < self.length * (part + 1) // parts:
            self.step(*after)
        return self.moving


def tied(value, *others):
    return lax.optimization_barrier((value, *others))[0] if others else value


def source_of(steps):
    size = lax.axis_size("ctx")
    ctx, core = lax.axis_index("ctx"), lax.axis_index("zero") % 2
    place = jnp.where(ctx % 2 == 0, ctx // 2, size - 1 - ctx // 2)
    place = lax.rem(place + steps * (1 - 2 * core) + size, size)
    return jnp.where(place < size // 2, 2 * place, 2 * (size - 1 - place) + 1)


def share_of(share):
    core = lax.axis_index("zero") % 2
    return core if share == 0 else 1 - core


def token_rows(group, other, size):
    core = lax.axis_index("zero") % 2
    if other:
        core = 1 - core
    return pl.ds(pl.multiple_of((2 * group + core) * size, 16), size)


def deal_kernel(count, *refs):
    x_refs, outs, sem = refs[:count], refs[count:-1], refs[-1]
    groups = lax.axis_size("zero") // 2
    size = x_refs[0].shape[0] // (2 * groups)
    copies = []
    for x_ref, out_ref in zip(x_refs, outs):
        for group in range(groups):
            copies.append(
                pltpu.make_async_copy(
                    x_ref.at[token_rows(group, True, size)],
                    out_ref.at[pl.ds(group * size, size)],
                    sem.at[len(copies)],
                )
            )
    for copy in copies:
        copy.start()
    for copy in copies:
        copy.wait()


def deal(arrays):
    tokens, depth = arrays[0].shape
    part = jax.ShapeDtypeStruct((tokens // 2, depth), arrays[0].dtype)
    copies = len(arrays) * lax.axis_size("zero") // 2
    return pl.pallas_call(
        functools.partial(deal_kernel, len(arrays)),
        out_shape=[part] * len(arrays),
        in_specs=[HBM] * len(arrays),
        out_specs=[HBM] * len(arrays),
        scratch_shapes=[pltpu.SemaphoreType.DMA((copies,))],
        compiler_params=pltpu.CompilerParams(vmem_limit_bytes=VMEM_LIMIT),
    )(*arrays)


def project_kernel(layout, *refs):
    (kv_ref, q_ref, x_buf, w_buf, x_sem, w_sem) = refs[-6:]
    pieces, tokens, depth = x_buf.shape
    cos_ref, sin_ref = refs[:2]
    x_refs = refs[2 : 2 + pieces]
    w_refs = refs[2 + pieces : -6]
    zero = lax.axis_index("zero")
    shard_rows = w_refs[0].shape[0]
    x_copies, w_copies = [], []
    for m, ref in enumerate(x_refs):
        target = x_buf.at[jnp.bitwise_xor(zero, m)]
        if m % 2:
            x_copies.append(pltpu.make_async_copy(ref, target, x_sem.at[len(x_copies)]))
            continue
        size = 2 * tokens // pieces
        for group in range(pieces // 2):
            x_copies.append(
                pltpu.make_async_copy(
                    ref.at[token_rows(group, False, size)],
                    target.at[pl.ds(group * size, size)],
                    x_sem.at[len(x_copies)],
                )
            )
    for at, (ref, (steps, share, base)) in enumerate(zip(w_refs, layout)):
        start = source_of(steps) * shard_rows + base
        if share is not None:
            start = start + share_of(share) * ref.shape[0]
        rows = pl.ds(pl.multiple_of(start, 16), ref.shape[0])
        w_copies.append(pltpu.make_async_copy(ref, w_buf.at[rows], w_sem.at[at]))
    for copy in x_copies + w_copies:
        copy.start()
    for copy in x_copies:
        copy.wait()
    squares = jnp.zeros((tokens, 128), jnp.float32)
    for at in range(pieces):
        for first in range(0, depth, 128):
            x_float = x_buf[at, :, first : first + 128].astype(jnp.float32)
            squares += x_float * x_float
    mean = jnp.sum(squares, axis=1, keepdims=True) / (depth * pieces)
    scale = jnp.broadcast_to(lax.rsqrt(mean + 1e-05), squares.shape)
    for copy in w_copies:
        copy.wait()
    head = cos_ref.shape[1]
    shrink = jnp.float32(head ** (-0.5))
    for out_ref, columns in ((kv_ref, 0), (q_ref, 2 * head)):
        for first in range(0, out_ref.shape[1], 2 * head):
            both = slice(columns + first, columns + first + 2 * head)
            total = jnp.zeros((tokens, 2 * head), jnp.float32)
            for at in range(pieces):
                total += jnp.dot(
                    x_buf[at],
                    w_buf[at * depth : (at + 1) * depth, both],
                    preferred_element_type=jnp.float32,
                )
            for at in range(2):
                part = total[:, at * head : (at + 1) * head] * scale
                if columns or not at:
                    part = part * cos_ref[...] + pltpu.roll(part, head // 2, 1) * sin_ref[...]
                if columns:
                    part = part * shrink
                out_ref[:, first + at * head : first + (at + 1) * head] = part.astype(
                    out_ref.dtype
                )


def project(cos, sin, x_pieces, held):
    layout = [(steps, share, base) for steps, share, base, _ in held]
    shards = [piece for _, _, _, piece in held]
    tokens, depth = x_pieces[1].shape
    pieces, head = len(x_pieces), cos.shape[1]
    width = shards[0].shape[1]
    full = depth * pieces
    return pl.pallas_call(
        functools.partial(project_kernel, layout),
        out_shape=[
            jax.ShapeDtypeStruct((tokens, 2 * head), jnp.bfloat16),
            jax.ShapeDtypeStruct((tokens, width - 2 * head), jnp.bfloat16),
        ],
        in_specs=[VMEM] * 2 + [HBM] * (pieces + len(shards)),
        out_specs=[VMEM] * 2,
        scratch_shapes=[
            pltpu.VMEM((pieces, tokens, depth), jnp.bfloat16),
            pltpu.VMEM((full, width), jnp.bfloat16),
            pltpu.SemaphoreType.DMA((pieces // 2 * (1 + pieces // 2),)),
            pltpu.SemaphoreType.DMA((len(shards),)),
        ],
        compiler_params=pltpu.CompilerParams(vmem_limit_bytes=VMEM_LIMIT),
        cost_estimate=pl.CostEstimate(
            flops=2 * tokens * full * width,
            bytes_accessed=2 * full * (tokens + width),
            transcendentals=0,
        ),
    )(cos, sin, *x_pieces, *shards)


def attend_kernel(groups, own_ref, far_ref, *refs):
    keep, send, q_ref, near0, near1, far0, far1, sem = refs[5:]
    copies = [
        pltpu.make_async_copy(source, target, sem.at[at])
        for at, (source, target) in enumerate(zip(refs[:5], refs[7:12]))
    ]
    for copy in copies:
        copy.start()
    for copy in copies:
        copy.wait()
    tokens, pair = near0.shape
    head = pair // 2
    size = tokens // groups
    tiles = own_ref.shape[0]
    tile = 2 * tokens // tiles
    heads = q_ref.shape[1] // head
    rows = heads * size
    core = lax.axis_index("zero") % 2
    column = lax.broadcasted_iota(jnp.int32, (1, tokens), 1)
    column_group = column // size
    within = lax.rem(lax.broadcasted_iota(jnp.int32, (rows, 1), 0), size)
    hidden = jnp.float32(-1e30)
    nt = (((1,), (1,)), ((), ()))
    side = lax.axis_index("zero") // 2 % 2
    for h in range(groups):
        across = slice(h * size, (h + 1) * size)
        q = jnp.concatenate(
            [q_ref[across, g * head : (g + 1) * head] for g in range(heads)], axis=0
        )
        first = (2 * h + core) * size
        own_tile = first // tile
        seen = min(tokens, -(-(h + 1) * size // 128) * 128)
        parts, blocks = [], []
        for ref, mask_ref, width, parity, causal in (
            (far0, far_ref, tokens, core, False),
            (far1, far_ref, tokens, 1 - core, False),
            (near0, own_ref, seen, core, True),
            (near1, own_ref, seen, 1 - core, True),
        ):
            visible = jnp.zeros((1, width), jnp.int32)
            for g in range(-(-width // size)):
                at = mask_ref[own_tile, (2 * g + parity) * size // tile]
                visible = jnp.where(column_group[:, :width] == g, at, visible)
            visible = visible == 1
            if causal:
                group = column_group[:, :width]
                offset = (2 * group + parity) * size + column[:, :width] - group * size
                visible = visible & (offset <= first + within)
            scores = lax.dot_general(
                q, ref[:width, :head], nt, preferred_element_type=jnp.float32
            )
            parts.append(jnp.where(visible, scores, hidden))
            blocks.append((ref, width))
        scores = jnp.concatenate(parts, axis=1)
        largest = jnp.max(scores, axis=1, keepdims=True)
        weights = jnp.exp(scores - largest)
        total = jnp.sum(weights, axis=1, keepdims=True)
        rounded = weights.astype(jnp.bfloat16)
        mixed = jnp.zeros((rows, head), jnp.float32)
        start = 0
        for ref, width in blocks:
            mixed += jnp.dot(
                rounded[:, start : start + width],
                ref[:width, head:],
                preferred_element_type=jnp.float32,
            )
            start += width
        mixed = (mixed / total).astype(keep.dtype)
        rows_out = slice(h // 2 * size, (h // 2 + 1) * size)

        def store(out_ref, rows_out=rows_out, mixed=mixed):
            for g in range(heads):
                out_ref[rows_out, g * head : (g + 1) * head] = mixed[g * size : (g + 1) * size, :]

        pl.when(side == h % 2)(functools.partial(store, keep))
        pl.when(side != h % 2)(functools.partial(store, send))


def attend(groups, own_mask, far_mask, queries, near, near_other, far, far_other):
    tokens, width = queries.shape
    return pl.pallas_call(
        functools.partial(attend_kernel, groups),
        out_shape=[jax.ShapeDtypeStruct((tokens // 2, width), jnp.bfloat16)] * 2,
        in_specs=[SMEM, SMEM] + [HBM] * 5,
        out_specs=[VMEM] * 2,
        scratch_shapes=[pltpu.VMEM(queries.shape, jnp.bfloat16)]
        + [pltpu.VMEM(near.shape, jnp.bfloat16)] * 4
        + [pltpu.SemaphoreType.DMA((5,))],
        compiler_params=pltpu.CompilerParams(vmem_limit_bytes=VMEM_LIMIT),
        cost_estimate=pl.CostEstimate(
            flops=8 * tokens * tokens * width,
            bytes_accessed=8 * tokens * width,
            transcendentals=8 * tokens * tokens,
        ),
    )(own_mask, far_mask, queries, near, near_other, far, far_other)


def mix_kernel(layout, slots, out_refs, *refs):
    count = len(refs) - len(layout) - out_refs - 2
    a_refs, w_refs = refs[:count], refs[count : count + len(layout)]
    outs = refs[count + len(layout) : -2]
    w_buf, sem = refs[-2:]
    width = w_buf.shape[2]
    half = a_refs[0].shape[1]
    copies = []
    for at, (ref, (slot, side, share)) in enumerate(zip(w_refs, layout)):
        rows = ref.shape[0]
        start = side * half
        if share is not None:
            start = pl.multiple_of(start + share_of(share) * rows, 16)
        copies.append(pltpu.make_async_copy(ref, w_buf.at[slot, pl.ds(start, rows)], sem.at[at]))
    for copy in copies:
        copy.start()
    slot = 0
    for out_ref, sides, number in zip(outs, *slots):
        rows = jnp.concatenate([ref[...] for ref in a_refs[:sides]], axis=1)
        for place in range(number):
            for copy, (its_slot, _, _) in zip(copies, layout):
                if its_slot == slot:
                    copy.wait()
            total = jnp.dot(
                rows, w_buf[slot, : sides * half], preferred_element_type=jnp.float32
            )
            out_ref[:, place * width : (place + 1) * width] = total.astype(out_ref.dtype)
            slot += 1


def mix(rows, blocks, dtypes):
    layout, shards = [], []
    sides = [1 + max(side for side, _, _ in block[0]) for block in blocks]
    slots = [slot for block in blocks for slot in block]
    for at, slot in enumerate(slots):
        for side, share, piece in slot:
            layout.append((at, side, share))
            shards.append(piece)
    tokens, half = rows[0].shape
    width = shards[0].shape[1]
    return pl.pallas_call(
        functools.partial(
            mix_kernel, layout, (sides, [len(block) for block in blocks]), len(blocks)
        ),
        out_shape=[
            jax.ShapeDtypeStruct((tokens, width * len(block)), dtype)
            for block, dtype in zip(blocks, dtypes)
        ],
        in_specs=[VMEM] * len(rows) + [HBM] * len(shards),
        out_specs=[VMEM] * len(blocks),
        scratch_shapes=[
            pltpu.VMEM((len(slots), max(sides) * half, width), jnp.bfloat16),
            pltpu.SemaphoreType.DMA((len(shards),)),
        ],
        compiler_params=pltpu.CompilerParams(vmem_limit_bytes=VMEM_LIMIT),
        cost_estimate=pl.CostEstimate(
            flops=2 * tokens * half * width * len(shards),
            bytes_accessed=6 * half * width * len(shards) + 4 * tokens * width * len(slots),
            transcendentals=0,
        ),
    )(*rows, *shards)


def join_kernel(steps, full_ref, keep_ref, *refs):
    got_refs, out_ref = refs[:-1], refs[-1]
    width = out_ref.shape[1] // len(steps)
    whole = full_ref.shape[1] // width
    got = [
        (ref, first) for ref in got_refs for first in range(0, ref.shape[1], width)
    ]
    for slot, along in enumerate(steps):
        start = pl.multiple_of(source_of(along) * width, 128)
        if slot < whole:
            block = full_ref[:, slot * width : (slot + 1) * width]
        else:
            columns = slice((slot - whole) * width, (slot - whole + 1) * width)
            got_ref, first = got[slot - whole]
            block = keep_ref[:, columns] + got_ref[:, first : first + width].astype(jnp.float32)
        out_ref[:, pl.ds(start, width)] = block.astype(out_ref.dtype)


def join(steps, full, keep, gots, dtype):
    rows = full.shape[0]
    columns = full.shape[1] + keep.shape[1]
    return pl.pallas_call(
        functools.partial(join_kernel, steps),
        out_shape=jax.ShapeDtypeStruct((rows, columns), dtype),
        in_specs=[VMEM] * (2 + len(gots)),
        out_specs=VMEM,
        compiler_params=pltpu.CompilerParams(vmem_limit_bytes=VMEM_LIMIT),
        cost_estimate=pl.CostEstimate(
            flops=rows * columns, bytes_accessed=8 * rows * columns, transcendentals=0
        ),
    )(full, keep, *gots)


def exchange_from(value, root, bit):
    other = swap(value, "ctx", 1 << bit)
    same = ((lax.axis_index("ctx") >> bit) & 1) == ((root >> bit) & 1)
    return jnp.where(same, value, other)


def local(
    activations,
    norm_gain,
    query_weight,
    kv_weight,
    out_weight,
    tile_mask,
    anchor_mask,
    anchor_index,
):
    tokens, depth = activations.shape
    head = kv_weight.shape[2]
    ctx_size, zero_size = lax.axis_size("ctx"), lax.axis_size("zero")
    ctx_rank, zero_rank = lax.axis_index("ctx"), lax.axis_index("zero")
    core = zero_rank % 2
    groups = zero_size // 2
    size = tokens // zero_size

    blocks = {0: activations}
    stride = groups
    while stride > 1:
        for known in range(0, zero_size, 2 * stride):
            blocks[known + stride] = swap(blocks[known], "zero", stride)
        stride //= 2

    shard_rows = kv_weight.shape[0]
    gain = lax.dynamic_slice_in_dim(norm_gain, ctx_rank * shard_rows, shard_rows)
    gain = gain.astype(jnp.float32)[:, None]
    kv_own = kv_weight[:, 0, :]
    kv_other, query_other = swap(kv_own, "zero", 1), swap(query_weight, "zero", 1)
    pair = jnp.where(
        core == 0,
        jnp.concatenate([kv_own, kv_other, query_weight, query_other], 1),
        jnp.concatenate([kv_other, kv_own, query_other, query_weight], 1),
    )
    pair = (pair.astype(jnp.float32) * gain).astype(jnp.bfloat16)
    out_other = swap(out_weight, "zero", 1)
    out_pair = jnp.where(
        core == 0,
        jnp.concatenate([out_weight, out_other], 0),
        jnp.concatenate([out_other, out_weight], 0),
    )
    ring_rows = shard_rows // 2
    rings = [
        Ring(pair[:ring_rows], core, pair),
        Ring(pair[ring_rows:], core, None, ring_rows),
    ]
    out_ring = Ring(out_pair, core)
    for part in range(4):
        for ring in rings:
            ring.advance(part, 4)
    held = rings[0].held + rings[1].held
    beyond = [swap(out_weight, "zero", 2)]
    out_ring.advance(0, 4, *[ring.moving for ring in rings], *beyond)

    far_blocks = [tied(blocks[m], rings[0].moving) for m in range(2, zero_size, 2)]
    x_pieces = []
    for at, theirs in enumerate(deal([blocks[0]]) + deal(far_blocks)):
        x_pieces += [([blocks[0]] + far_blocks)[at], swap(theirs, "zero", 1)]

    half = head // 2
    frequency = jnp.power(
        jnp.float32(ROPE_BASE), -(jnp.arange(half, dtype=jnp.float32) * 2.0 / head)
    )
    local_token = jnp.arange(tokens // 2, dtype=jnp.int32)
    offsets = (2 * (local_token // size) + core) * size + local_token % size
    positions = ctx_rank * tokens + offsets
    angles = positions.astype(jnp.float32)[:, None] * frequency[None, :]
    cos_half, sin_half = jnp.cos(angles), jnp.sin(angles)
    cos = jnp.concatenate([cos_half, cos_half], -1)
    sin = jnp.concatenate([-sin_half, sin_half], -1)

    near, queries = project(cos, sin, x_pieces, held)

    def share():
        for at in range(len(beyond), out_ring.at + 1):
            beyond.append(swap(out_ring.held[2 * at - 1][3], "zero", 2))

    share()
    anchor = anchor_index[0]
    far = tied(near, out_ring.moving)
    for bit in range(int(math.log2(ctx_size))):
        far = exchange_from(far, anchor, bit)
        if bit == 0:
            near_other = swap(near, "zero", 1)
            far = tied(far, near_other)
            out_ring.advance(1, 4, far)
    far_other = swap(far, "zero", 1)
    out_ring.advance(2, 4, far_other, beyond[-1])
    far_mask = jnp.where(ctx_rank != anchor, anchor_mask[0], 0)
    keep, send = attend(
        groups, tile_mask[0], far_mask, queries, near, near_other, far, far_other
    )
    got = swap(send, "zero", 2)
    out_ring.held[-1] = (
        *out_ring.held[-1][:3],
        swap(tied(out_ring.moving, send), "zero", 1),
    )
    cut = ctx_size // 4
    block = [
        [(0, None, piece)]
        for steps, _, _, piece in out_ring.held
        if len(beyond) <= abs(steps) <= cut
    ]
    (terms,) = mix([send], [block], [jnp.bfloat16])
    got_terms = [swap(terms, "zero", 2)]
    out_ring.advance(3, 4, terms)

    steps_of, both_chips, one_chip = [], [], []
    for steps, half_of, _, piece in out_ring.held:
        slots = both_chips if abs(steps) < len(beyond) else one_chip
        if half_of != 1:
            steps_of.append(steps)
            slots.append([])
        slots[-1].append((0, half_of, piece))
        if slots is both_chips:
            if steps <= 0:
                across = swap(beyond[-steps], "zero", 1)
            if steps == 0:
                slots[-1] += [(1, 0, beyond[0]), (1, 1, across)]
            else:
                slots[-1].append((1, half_of, beyond[-steps] if steps < 0 else across))
    for block, early in ((one_chip[cut : 2 * cut], [got]), (one_chip[2 * cut :], got_terms[:1])):
        (terms,) = mix([tied(send, *early)], [block], [jnp.bfloat16])
        got_terms.append(swap(terms, "zero", 2))
    full, kept = mix([keep, got], [both_chips, one_chip], [jnp.float32, jnp.float32])
    if zero_size == 4:
        return join(steps_of, full, kept, got_terms, jnp.bfloat16)
    total = join(steps_of, full, kept, got_terms, jnp.float32)
    stride = zero_size // 2
    while stride > 2:
        rows = total.shape[0] // 2
        bit = (zero_rank // stride) % 2
        stay = lax.dynamic_slice_in_dim(total, bit * rows, rows, 0)
        go = lax.dynamic_slice_in_dim(total, (1 - bit) * rows, rows, 0)
        total = stay + swap(go.astype(jnp.bfloat16), "zero", stride).astype(jnp.float32)
        stride //= 2
    return total.astype(jnp.bfloat16)


def solution(mesh):
    placed = (
        P("ctx", "zero"),
        P(),
        P("ctx", "zero"),
        P("ctx", "zero", None),
        P("zero", "ctx"),
        P("ctx", None, None),
        P("ctx", None, None),
        P(),
    )
    return jax.shard_map(
        local, mesh=mesh, in_specs=placed, out_specs=P(("ctx", "zero"), None), check_vma=False
    )
```

```python
import functools
import math

import jax
import jax.numpy as jnp
from jax import lax
from jax.experimental import pallas as pl
from jax.experimental.pallas import tpu as pltpu
from jax.sharding import PartitionSpec as P

HBM = pl.BlockSpec(memory_space=pltpu.HBM)
VMEM = pl.BlockSpec(memory_space=pltpu.VMEM)
SMEM = pl.BlockSpec(memory_space=pltpu.SMEM)
VMEM_LIMIT = 32 * 1024 * 1024
ROPE_BASE = 500000.0


def swap(value, axis, stride):
    pairs = [(source, source ^ stride) for source in range(lax.axis_size(axis))]
    return lax.ppermute(value, axis, pairs)


def cycle(size):
    return list(range(0, size, 2)) + list(range(1, size, 2))[::-1]


def ring_step(value):
    ctx_size, zero_size = lax.axis_size("ctx"), lax.axis_size("zero")
    order = cycle(ctx_size)
    pairs = []
    for at in range(ctx_size):
        for zero in range(zero_size):
            to = order[(at + (1 if zero % 2 == 0 else -1)) % ctx_size]
            pairs.append((order[at] * zero_size + zero, to * zero_size + zero))
    return lax.ppermute(value, ("ctx", "zero"), pairs)


class Ring:
    def __init__(self, shard, core, whole=None, base=0):
        self.held = [(0, None, 0, shard if whole is None else whole)] if base == 0 else []
        self.base = base
        self.moving, self.core, self.at = shard, core, 0
        self.length = lax.axis_size("ctx") // 2

    def step(self, *after):
        self.at += 1
        last = self.at == self.length
        if last:
            half = self.moving.shape[0] // 2
            self.moving = lax.dynamic_slice_in_dim(self.moving, self.core * half, half, 0)
            self.sent = self.moving
        behind = self.held[-3][3:] if len(self.held) > 3 else []
        self.moving = ring_step(tied(self.moving, *behind, *after))
        self.held.append((-self.at, 0 if last else None, self.base, self.moving))
        self.held.append(
            (self.at, 1 if last else None, self.base, swap(self.moving, "zero", 1))
        )
        return self.moving

    def advance(self, part, parts, *after):
        while self.at < self.length * (part + 1) // parts:
            self.step(*after)
        return self.moving


def tied(value, *others):
    return lax.optimization_barrier((value, *others))[0] if others else value


def source_of(steps):
    size = lax.axis_size("ctx")
    ctx, core = lax.axis_index("ctx"), lax.axis_index("zero") % 2
    place = jnp.where(ctx % 2 == 0, ctx // 2, size - 1 - ctx // 2)
    place = lax.rem(place + steps * (1 - 2 * core) + size, size)
    return jnp.where(place < size // 2, 2 * place, 2 * (size - 1 - place) + 1)


def share_of(share):
    core = lax.axis_index("zero") % 2
    return core if share == 0 else 1 - core


def token_rows(group, other, size):
    core = lax.axis_index("zero") % 2
    if other:
        core = 1 - core
    return pl.ds(pl.multiple_of((2 * group + core) * size, 16), size)


def deal_kernel(count, *refs):
    x_refs, outs, sem = refs[:count], refs[count:-1], refs[-1]
    groups = lax.axis_size("zero") // 2
    size = x_refs[0].shape[0] // (2 * groups)
    copies = []
    for x_ref, out_ref in zip(x_refs, outs):
        for group in range(groups):
            copies.append(
                pltpu.make_async_copy(
                    x_ref.at[token_rows(group, True, size)],
                    out_ref.at[pl.ds(group * size, size)],
                    sem.at[len(copies)],
                )
            )
    for copy in copies:
        copy.start()
    for copy in copies:
        copy.wait()


def deal(arrays):
    tokens, depth = arrays[0].shape
    part = jax.ShapeDtypeStruct((tokens // 2, depth), arrays[0].dtype)
    copies = len(arrays) * lax.axis_size("zero") // 2
    return pl.pallas_call(
        functools.partial(deal_kernel, len(arrays)),
        out_shape=[part] * len(arrays),
        in_specs=[HBM] * len(arrays),
        out_specs=[HBM] * len(arrays),
        scratch_shapes=[pltpu.SemaphoreType.DMA((copies,))],
        compiler_params=pltpu.CompilerParams(vmem_limit_bytes=VMEM_LIMIT),
    )(*arrays)


def project_kernel(layout, *refs):
    (kv_ref, q_ref, x_buf, w_buf, x_sem, w_sem) = refs[-6:]
    pieces, tokens, depth = x_buf.shape
    cos_ref, sin_ref = refs[:2]
    x_refs = refs[2 : 2 + pieces]
    w_refs = refs[2 + pieces : -6]
    zero = lax.axis_index("zero")
    shard_rows = w_refs[0].shape[0]
    x_copies, w_copies = [], []
    for m, ref in enumerate(x_refs):
        target = x_buf.at[jnp.bitwise_xor(zero, m)]
        if m % 2:
            x_copies.append(pltpu.make_async_copy(ref, target, x_sem.at[len(x_copies)]))
            continue
        size = 2 * tokens // pieces
        for group in range(pieces // 2):
            x_copies.append(
                pltpu.make_async_copy(
                    ref.at[token_rows(group, False, size)],
                    target.at[pl.ds(group * size, size)],
                    x_sem.at[len(x_copies)],
                )
            )
    for at, (ref, (steps, share, base)) in enumerate(zip(w_refs, layout)):
        start = source_of(steps) * shard_rows + base
        if share is not None:
            start = start + share_of(share) * ref.shape[0]
        rows = pl.ds(pl.multiple_of(start, 16), ref.shape[0])
        w_copies.append(pltpu.make_async_copy(ref, w_buf.at[rows], w_sem.at[at]))
    for copy in x_copies + w_copies:
        copy.start()
    for copy in x_copies:
        copy.wait()
    squares = jnp.zeros((tokens, 128), jnp.float32)
    for at in range(pieces):
        for first in range(0, depth, 128):
            x_float = x_buf[at, :, first : first + 128].astype(jnp.float32)
            squares += x_float * x_float
    mean = jnp.sum(squares, axis=1, keepdims=True) / (depth * pieces)
    scale = jnp.broadcast_to(lax.rsqrt(mean + 1e-05), squares.shape)
    for copy in w_copies:
        copy.wait()
    head = cos_ref.shape[1]
    shrink = jnp.float32(head ** (-0.5))
    for out_ref, columns in ((kv_ref, 0), (q_ref, 2 * head)):
        for first in range(0, out_ref.shape[1], 2 * head):
            both = slice(columns + first, columns + first + 2 * head)
            total = jnp.zeros((tokens, 2 * head), jnp.float32)
            for at in range(pieces):
                total += jnp.dot(
                    x_buf[at],
                    w_buf[at * depth : (at + 1) * depth, both],
                    preferred_element_type=jnp.float32,
                )
            for at in range(2):
                part = total[:, at * head : (at + 1) * head] * scale
                if columns or not at:
                    part = part * cos_ref[...] + pltpu.roll(part, head // 2, 1) * sin_ref[...]
                if columns:
                    part = part * shrink
                out_ref[:, first + at * head : first + (at + 1) * head] = part.astype(
                    out_ref.dtype
                )


def project(cos, sin, x_pieces, held):
    layout = [(steps, share, base) for steps, share, base, _ in held]
    shards = [piece for _, _, _, piece in held]
    tokens, depth = x_pieces[1].shape
    pieces, head = len(x_pieces), cos.shape[1]
    width = shards[0].shape[1]
    full = depth * pieces
    return pl.pallas_call(
        functools.partial(project_kernel, layout),
        out_shape=[
            jax.ShapeDtypeStruct((tokens, 2 * head), jnp.bfloat16),
            jax.ShapeDtypeStruct((tokens, width - 2 * head), jnp.bfloat16),
        ],
        in_specs=[VMEM] * 2 + [HBM] * (pieces + len(shards)),
        out_specs=[VMEM] * 2,
        scratch_shapes=[
            pltpu.VMEM((pieces, tokens, depth), jnp.bfloat16),
            pltpu.VMEM((full, width), jnp.bfloat16),
            pltpu.SemaphoreType.DMA((pieces // 2 * (1 + pieces // 2),)),
            pltpu.SemaphoreType.DMA((len(shards),)),
        ],
        compiler_params=pltpu.CompilerParams(vmem_limit_bytes=VMEM_LIMIT),
        cost_estimate=pl.CostEstimate(
            flops=2 * tokens * full * width,
            bytes_accessed=2 * full * (tokens + width),
            transcendentals=0,
        ),
    )(cos, sin, *x_pieces, *shards)


def attend_kernel(groups, own_ref, far_ref, *refs):
    keep, send, q_ref, near0, near1, far0, far1, sem = refs[5:]
    copies = [
        pltpu.make_async_copy(source, target, sem.at[at])
        for at, (source, target) in enumerate(zip(refs[:5], refs[7:12]))
    ]
    for copy in copies:
        copy.start()
    for copy in copies:
        copy.wait()
    tokens, pair = near0.shape
    head = pair // 2
    size = tokens // groups
    tiles = own_ref.shape[0]
    tile = 2 * tokens // tiles
    heads = q_ref.shape[1] // head
    rows = heads * size
    core = lax.axis_index("zero") % 2
    column = lax.broadcasted_iota(jnp.int32, (1, tokens), 1)
    column_group = column // size
    within = lax.rem(lax.broadcasted_iota(jnp.int32, (rows, 1), 0), size)
    hidden = jnp.float32(-1e30)
    nt = (((1,), (1,)), ((), ()))
    side = lax.axis_index("zero") // 2 % 2
    for h in range(groups):
        across = slice(h * size, (h + 1) * size)
        q = jnp.concatenate(
            [q_ref[across, g * head : (g + 1) * head] for g in range(heads)], axis=0
        )
        first = (2 * h + core) * size
        own_tile = first // tile
        seen = min(tokens, -(-(h + 1) * size // 128) * 128)
        parts, blocks = [], []
        for ref, mask_ref, width, parity, causal in (
            (far0, far_ref, tokens, core, False),
            (far1, far_ref, tokens, 1 - core, False),
            (near0, own_ref, seen, core, True),
            (near1, own_ref, seen, 1 - core, True),
        ):
            visible = jnp.zeros((1, width), jnp.int32)
            for g in range(-(-width // size)):
                at = mask_ref[own_tile, (2 * g + parity) * size // tile]
                visible = jnp.where(column_group[:, :width] == g, at, visible)
            visible = visible == 1
            if causal:
                group = column_group[:, :width]
                offset = (2 * group + parity) * size + column[:, :width] - group * size
                visible = visible & (offset <= first + within)
            scores = lax.dot_general(
                q, ref[:width, :head], nt, preferred_element_type=jnp.float32
            )
            parts.append(jnp.where(visible, scores, hidden))
            blocks.append((ref, width))
        scores = jnp.concatenate(parts, axis=1)
        largest = jnp.max(scores, axis=1, keepdims=True)
        weights = jnp.exp(scores - largest)
        total = jnp.sum(weights, axis=1, keepdims=True)
        rounded = weights.astype(jnp.bfloat16)
        mixed = jnp.zeros((rows, head), jnp.float32)
        start = 0
        for ref, width in blocks:
            mixed += jnp.dot(
                rounded[:, start : start + width],
                ref[:width, head:],
                preferred_element_type=jnp.float32,
            )
            start += width
        mixed = (mixed / total).astype(keep.dtype)
        rows_out = slice(h // 2 * size, (h // 2 + 1) * size)

        def store(out_ref, rows_out=rows_out, mixed=mixed):
            for g in range(heads):
                out_ref[rows_out, g * head : (g + 1) * head] = mixed[g * size : (g + 1) * size, :]

        pl.when(side == h % 2)(functools.partial(store, keep))
        pl.when(side != h % 2)(functools.partial(store, send))


def attend(groups, own_mask, far_mask, queries, near, near_other, far, far_other):
    tokens, width = queries.shape
    return pl.pallas_call(
        functools.partial(attend_kernel, groups),
        out_shape=[jax.ShapeDtypeStruct((tokens // 2, width), jnp.bfloat16)] * 2,
        in_specs=[SMEM, SMEM] + [HBM] * 5,
        out_specs=[VMEM] * 2,
        scratch_shapes=[pltpu.VMEM(queries.shape, jnp.bfloat16)]
        + [pltpu.VMEM(near.shape, jnp.bfloat16)] * 4
        + [pltpu.SemaphoreType.DMA((5,))],
        compiler_params=pltpu.CompilerParams(vmem_limit_bytes=VMEM_LIMIT),
        cost_estimate=pl.CostEstimate(
            flops=8 * tokens * tokens * width,
            bytes_accessed=8 * tokens * width,
            transcendentals=8 * tokens * tokens,
        ),
    )(own_mask, far_mask, queries, near, near_other, far, far_other)


def mix_kernel(layout, slots, out_refs, *refs):
    count = len(refs) - len(layout) - out_refs - 2
    a_refs, w_refs = refs[:count], refs[count : count + len(layout)]
    outs = refs[count + len(layout) : -2]
    w_buf, sem = refs[-2:]
    width = w_buf.shape[2]
    half = a_refs[0].shape[1]
    copies = []
    for at, (ref, (slot, side, share)) in enumerate(zip(w_refs, layout)):
        rows = ref.shape[0]
        start = side * half
        if share is not None:
            start = pl.multiple_of(start + share_of(share) * rows, 16)
        copies.append(pltpu.make_async_copy(ref, w_buf.at[slot, pl.ds(start, rows)], sem.at[at]))
    for copy in copies:
        copy.start()
    slot = 0
    for out_ref, sides, number in zip(outs, *slots):
        rows = jnp.concatenate([ref[...] for ref in a_refs[:sides]], axis=1)
        for place in range(number):
            for copy, (its_slot, _, _) in zip(copies, layout):
                if its_slot == slot:
                    copy.wait()
            total = jnp.dot(
                rows, w_buf[slot, : sides * half], preferred_element_type=jnp.float32
            )
            out_ref[:, place * width : (place + 1) * width] = total.astype(out_ref.dtype)
            slot += 1


def mix(rows, blocks, dtypes):
    layout, shards = [], []
    sides = [1 + max(side for side, _, _ in block[0]) for block in blocks]
    slots = [slot for block in blocks for slot in block]
    for at, slot in enumerate(slots):
        for side, share, piece in slot:
            layout.append((at, side, share))
            shards.append(piece)
    tokens, half = rows[0].shape
    width = shards[0].shape[1]
    return pl.pallas_call(
        functools.partial(
            mix_kernel, layout, (sides, [len(block) for block in blocks]), len(blocks)
        ),
        out_shape=[
            jax.ShapeDtypeStruct((tokens, width * len(block)), dtype)
            for block, dtype in zip(blocks, dtypes)
        ],
        in_specs=[VMEM] * len(rows) + [HBM] * len(shards),
        out_specs=[VMEM] * len(blocks),
        scratch_shapes=[
            pltpu.VMEM((len(slots), max(sides) * half, width), jnp.bfloat16),
            pltpu.SemaphoreType.DMA((len(shards),)),
        ],
        compiler_params=pltpu.CompilerParams(vmem_limit_bytes=VMEM_LIMIT),
        cost_estimate=pl.CostEstimate(
            flops=2 * tokens * half * width * len(shards),
            bytes_accessed=6 * half * width * len(shards) + 4 * tokens * width * len(slots),
            transcendentals=0,
        ),
    )(*rows, *shards)


def join_kernel(steps, full_ref, keep_ref, *refs):
    got_refs, out_ref = refs[:-1], refs[-1]
    width = out_ref.shape[1] // len(steps)
    whole = full_ref.shape[1] // width
    got = [
        (ref, first) for ref in got_refs for first in range(0, ref.shape[1], width)
    ]
    for slot, along in enumerate(steps):
        start = pl.multiple_of(source_of(along) * width, 128)
        if slot < whole:
            block = full_ref[:, slot * width : (slot + 1) * width]
        else:
            columns = slice((slot - whole) * width, (slot - whole + 1) * width)
            got_ref, first = got[slot - whole]
            block = keep_ref[:, columns] + got_ref[:, first : first + width].astype(jnp.float32)
        out_ref[:, pl.ds(start, width)] = block.astype(out_ref.dtype)


def join(steps, full, keep, gots, dtype):
    rows = full.shape[0]
    columns = full.shape[1] + keep.shape[1]
    return pl.pallas_call(
        functools.partial(join_kernel, steps),
        out_shape=jax.ShapeDtypeStruct((rows, columns), dtype),
        in_specs=[VMEM] * (2 + len(gots)),
        out_specs=VMEM,
        compiler_params=pltpu.CompilerParams(vmem_limit_bytes=VMEM_LIMIT),
        cost_estimate=pl.CostEstimate(
            flops=rows * columns, bytes_accessed=8 * rows * columns, transcendentals=0
        ),
    )(full, keep, *gots)


def exchange_from(value, root, bit):
    other = swap(value, "ctx", 1 << bit)
    same = ((lax.axis_index("ctx") >> bit) & 1) == ((root >> bit) & 1)
    return jnp.where(same, value, other)


def local(
    activations,
    norm_gain,
    query_weight,
    kv_weight,
    out_weight,
    tile_mask,
    anchor_mask,
    anchor_index,
):
    tokens, depth = activations.shape
    head = kv_weight.shape[2]
    ctx_size, zero_size = lax.axis_size("ctx"), lax.axis_size("zero")
    ctx_rank, zero_rank = lax.axis_index("ctx"), lax.axis_index("zero")
    core = zero_rank % 2
    groups = zero_size // 2
    size = tokens // zero_size

    blocks = {0: activations}
    stride = groups
    while stride > 1:
        for known in range(0, zero_size, 2 * stride):
            blocks[known + stride] = swap(blocks[known], "zero", stride)
        stride //= 2

    shard_rows = kv_weight.shape[0]
    gain = lax.dynamic_slice_in_dim(norm_gain, ctx_rank * shard_rows, shard_rows)
    gain = gain.astype(jnp.float32)[:, None]
    kv_own = kv_weight[:, 0, :]
    kv_other, query_other = swap(kv_own, "zero", 1), swap(query_weight, "zero", 1)
    pair = jnp.where(
        core == 0,
        jnp.concatenate([kv_own, kv_other, query_weight, query_other], 1),
        jnp.concatenate([kv_other, kv_own, query_other, query_weight], 1),
    )
    pair = (pair.astype(jnp.float32) * gain).astype(jnp.bfloat16)
    out_other = swap(out_weight, "zero", 1)
    out_pair = jnp.where(
        core == 0,
        jnp.concatenate([out_weight, out_other], 0),
        jnp.concatenate([out_other, out_weight], 0),
    )
    ring_rows = shard_rows // 2
    rings = [
        Ring(pair[:ring_rows], core, pair),
        Ring(pair[ring_rows:], core, None, ring_rows),
    ]
    out_ring = Ring(out_pair, core)
    for part in range(4):
        for ring in rings:
            ring.advance(part, 4)
    held = rings[0].held + rings[1].held
    beyond = [swap(out_weight, "zero", 2)]

    far_blocks = [tied(blocks[m], rings[0].moving) for m in range(2, zero_size, 2)]
    x_pieces = []
    dealt = deal([blocks[0]]) + deal(far_blocks)
    out_ring.advance(0, 4, rings[1].sent, dealt[-1])
    for at, theirs in enumerate(dealt):
        x_pieces += [([blocks[0]] + far_blocks)[at], swap(theirs, "zero", 1)]

    half = head // 2
    frequency = jnp.power(
        jnp.float32(ROPE_BASE), -(jnp.arange(half, dtype=jnp.float32) * 2.0 / head)
    )
    local_token = jnp.arange(tokens // 2, dtype=jnp.int32)
    offsets = (2 * (local_token // size) + core) * size + local_token % size
    positions = ctx_rank * tokens + offsets
    angles = positions.astype(jnp.float32)[:, None] * frequency[None, :]
    cos_half, sin_half = jnp.cos(angles), jnp.sin(angles)
    cos = jnp.concatenate([cos_half, cos_half], -1)
    sin = jnp.concatenate([-sin_half, sin_half], -1)

    near, queries = project(cos, sin, x_pieces, held)

    def share():
        for at in range(len(beyond), out_ring.at + 1):
            beyond.append(swap(out_ring.held[2 * at - 1][3], "zero", 2))

    share()
    anchor = anchor_index[0]
    far = tied(near, out_ring.moving, beyond[0])
    for bit in range(int(math.log2(ctx_size))):
        far = exchange_from(far, anchor, bit)
        if bit == 0:
            near_other = swap(near, "zero", 1)
            far = tied(far, near_other)
            out_ring.advance(1, 4, far)
    far_other = swap(far, "zero", 1)
    out_ring.advance(2, 4, far_other, beyond[-1])
    far_mask = jnp.where(ctx_rank != anchor, anchor_mask[0], 0)
    keep, send = attend(
        groups, tile_mask[0], far_mask, queries, near, near_other, far, far_other
    )
    got = swap(send, "zero", 2)
    out_ring.held[-1] = (
        *out_ring.held[-1][:3],
        swap(tied(out_ring.moving, send), "zero", 1),
    )
    cut = ctx_size // 4
    block = [
        [(0, None, piece)]
        for steps, _, _, piece in out_ring.held
        if len(beyond) <= abs(steps) <= cut
    ]
    (terms,) = mix([send], [block], [jnp.bfloat16])
    got_terms = [swap(terms, "zero", 2)]
    out_ring.advance(3, 4, terms)

    steps_of, both_chips, one_chip = [], [], []
    for steps, half_of, _, piece in out_ring.held:
        slots = both_chips if abs(steps) < len(beyond) else one_chip
        if half_of != 1:
            steps_of.append(steps)
            slots.append([])
        slots[-1].append((0, half_of, piece))
        if slots is both_chips:
            if steps <= 0:
                across = swap(beyond[-steps], "zero", 1)
            if steps == 0:
                slots[-1] += [(1, 0, beyond[0]), (1, 1, across)]
            else:
                slots[-1].append((1, half_of, beyond[-steps] if steps < 0 else across))
    for block, early in ((one_chip[cut : 2 * cut], [got]), (one_chip[2 * cut :], got_terms[:1])):
        (terms,) = mix([tied(send, *early)], [block], [jnp.bfloat16])
        got_terms.append(swap(terms, "zero", 2))
    full, kept = mix([keep, got], [both_chips, one_chip], [jnp.float32, jnp.float32])
    if zero_size == 4:
        return join(steps_of, full, kept, got_terms, jnp.bfloat16)
    total = join(steps_of, full, kept, got_terms, jnp.float32)
    stride = zero_size // 2
    while stride > 2:
        rows = total.shape[0] // 2
        bit = (zero_rank // stride) % 2
        stay = lax.dynamic_slice_in_dim(total, bit * rows, rows, 0)
        go = lax.dynamic_slice_in_dim(total, (1 - bit) * rows, rows, 0)
        total = stay + swap(go.astype(jnp.bfloat16), "zero", stride).astype(jnp.float32)
        stride //= 2
    return total.astype(jnp.bfloat16)


def solution(mesh):
    placed = (
        P("ctx", "zero"),
        P(),
        P("ctx", "zero"),
        P("ctx", "zero", None),
        P("zero", "ctx"),
        P("ctx", None, None),
        P("ctx", None, None),
        P(),
    )
    return jax.shard_map(
        local, mesh=mesh, in_specs=placed, out_specs=P(("ctx", "zero"), None), check_vma=False
    )
```

```python
import functools
import math

import jax
import jax.numpy as jnp
from jax import lax
from jax.experimental import pallas as pl
from jax.experimental.pallas import tpu as pltpu
from jax.sharding import PartitionSpec as P

HBM = pl.BlockSpec(memory_space=pltpu.HBM)
VMEM = pl.BlockSpec(memory_space=pltpu.VMEM)
SMEM = pl.BlockSpec(memory_space=pltpu.SMEM)
VMEM_LIMIT = 32 * 1024 * 1024
ROPE_BASE = 500000.0


def swap(value, axis, stride):
    pairs = [(source, source ^ stride) for source in range(lax.axis_size(axis))]
    return lax.ppermute(value, axis, pairs)


def cycle(size):
    return list(range(0, size, 2)) + list(range(1, size, 2))[::-1]


def ring_step(value):
    ctx_size, zero_size = lax.axis_size("ctx"), lax.axis_size("zero")
    order = cycle(ctx_size)
    pairs = []
    for at in range(ctx_size):
        for zero in range(zero_size):
            to = order[(at + (1 if zero % 2 == 0 else -1)) % ctx_size]
            pairs.append((order[at] * zero_size + zero, to * zero_size + zero))
    return lax.ppermute(value, ("ctx", "zero"), pairs)


class Ring:
    def __init__(self, shard, core, whole=None, base=0):
        self.held = [(0, None, 0, shard if whole is None else whole)] if base == 0 else []
        self.base = base
        self.moving, self.core, self.at = shard, core, 0
        self.length = lax.axis_size("ctx") // 2

    def step(self, *after):
        self.at += 1
        last = self.at == self.length
        if last:
            half = self.moving.shape[0] // 2
            self.moving = lax.dynamic_slice_in_dim(self.moving, self.core * half, half, 0)
        behind = self.held[-3][3:] if len(self.held) > 3 else []
        self.moving = ring_step(tied(self.moving, *behind, *after))
        self.held.append((-self.at, 0 if last else None, self.base, self.moving))
        self.held.append(
            (self.at, 1 if last else None, self.base, swap(self.moving, "zero", 1))
        )
        return self.moving

    def advance(self, part, parts, *after):
        while self.at < self.length * (part + 1) // parts:
            self.step(*after)
        return self.moving


def tied(value, *others):
    return lax.optimization_barrier((value, *others))[0] if others else value


def source_of(steps):
    size = lax.axis_size("ctx")
    ctx, core = lax.axis_index("ctx"), lax.axis_index("zero") % 2
    place = jnp.where(ctx % 2 == 0, ctx // 2, size - 1 - ctx // 2)
    place = lax.rem(place + steps * (1 - 2 * core) + size, size)
    return jnp.where(place < size // 2, 2 * place, 2 * (size - 1 - place) + 1)


def share_of(share):
    core = lax.axis_index("zero") % 2
    return core if share == 0 else 1 - core


def token_rows(group, other, size):
    core = lax.axis_index("zero") % 2
    if other:
        core = 1 - core
    return pl.ds(pl.multiple_of((2 * group + core) * size, 16), size)


def deal_kernel(count, *refs):
    x_refs, outs, sem = refs[:count], refs[count:-1], refs[-1]
    groups = lax.axis_size("zero") // 2
    size = x_refs[0].shape[0] // (2 * groups)
    copies = []
    for x_ref, out_ref in zip(x_refs, outs):
        for group in range(groups):
            copies.append(
                pltpu.make_async_copy(
                    x_ref.at[token_rows(group, True, size)],
                    out_ref.at[pl.ds(group * size, size)],
                    sem.at[len(copies)],
                )
            )
    for copy in copies:
        copy.start()
    for copy in copies:
        copy.wait()


def deal(arrays):
    tokens, depth = arrays[0].shape
    part = jax.ShapeDtypeStruct((tokens // 2, depth), arrays[0].dtype)
    copies = len(arrays) * lax.axis_size("zero") // 2
    return pl.pallas_call(
        functools.partial(deal_kernel, len(arrays)),
        out_shape=[part] * len(arrays),
        in_specs=[HBM] * len(arrays),
        out_specs=[HBM] * len(arrays),
        scratch_shapes=[pltpu.SemaphoreType.DMA((copies,))],
        compiler_params=pltpu.CompilerParams(vmem_limit_bytes=VMEM_LIMIT),
    )(*arrays)


def project_kernel(layout, *refs):
    (kv_ref, q_ref, x_buf, w_buf, x_sem, w_sem) = refs[-6:]
    pieces, tokens, depth = x_buf.shape
    cos_ref, sin_ref = refs[:2]
    x_refs = refs[2 : 2 + pieces]
    w_refs = refs[2 + pieces : -6]
    zero = lax.axis_index("zero")
    shard_rows = w_refs[0].shape[0]
    x_copies, w_copies = [], []
    for m, ref in enumerate(x_refs):
        target = x_buf.at[jnp.bitwise_xor(zero, m)]
        if m % 2:
            x_copies.append(pltpu.make_async_copy(ref, target, x_sem.at[len(x_copies)]))
            continue
        size = 2 * tokens // pieces
        for group in range(pieces // 2):
            x_copies.append(
                pltpu.make_async_copy(
                    ref.at[token_rows(group, False, size)],
                    target.at[pl.ds(group * size, size)],
                    x_sem.at[len(x_copies)],
                )
            )
    for at, (ref, (steps, share, base)) in enumerate(zip(w_refs, layout)):
        start = source_of(steps) * shard_rows + base
        if share is not None:
            start = start + share_of(share) * ref.shape[0]
        rows = pl.ds(pl.multiple_of(start, 16), ref.shape[0])
        w_copies.append(pltpu.make_async_copy(ref, w_buf.at[rows], w_sem.at[at]))
    for copy in x_copies + w_copies:
        copy.start()
    for copy in x_copies:
        copy.wait()
    squares = jnp.zeros((tokens, 128), jnp.float32)
    for at in range(pieces):
        for first in range(0, depth, 128):
            x_float = x_buf[at, :, first : first + 128].astype(jnp.float32)
            squares += x_float * x_float
    mean = jnp.sum(squares, axis=1, keepdims=True) / (depth * pieces)
    scale = jnp.broadcast_to(lax.rsqrt(mean + 1e-05), squares.shape)
    for copy in w_copies:
        copy.wait()
    head = cos_ref.shape[1]
    shrink = jnp.float32(head ** (-0.5))
    for out_ref, columns in ((kv_ref, 0), (q_ref, 2 * head)):
        for first in range(0, out_ref.shape[1], 2 * head):
            both = slice(columns + first, columns + first + 2 * head)
            total = jnp.zeros((tokens, 2 * head), jnp.float32)
            for at in range(pieces):
                total += jnp.dot(
                    x_buf[at],
                    w_buf[at * depth : (at + 1) * depth, both],
                    preferred_element_type=jnp.float32,
                )
            for at in range(2):
                part = total[:, at * head : (at + 1) * head] * scale
                if columns or not at:
                    part = part * cos_ref[...] + pltpu.roll(part, head // 2, 1) * sin_ref[...]
                if columns:
                    part = part * shrink
                out_ref[:, first + at * head : first + (at + 1) * head] = part.astype(
                    out_ref.dtype
                )


def project(cos, sin, x_pieces, held):
    layout = [(steps, share, base) for steps, share, base, _ in held]
    shards = [piece for _, _, _, piece in held]
    tokens, depth = x_pieces[1].shape
    pieces, head = len(x_pieces), cos.shape[1]
    width = shards[0].shape[1]
    full = depth * pieces
    return pl.pallas_call(
        functools.partial(project_kernel, layout),
        out_shape=[
            jax.ShapeDtypeStruct((tokens, 2 * head), jnp.bfloat16),
            jax.ShapeDtypeStruct((tokens, width - 2 * head), jnp.bfloat16),
        ],
        in_specs=[VMEM] * 2 + [HBM] * (pieces + len(shards)),
        out_specs=[VMEM] * 2,
        scratch_shapes=[
            pltpu.VMEM((pieces, tokens, depth), jnp.bfloat16),
            pltpu.VMEM((full, width), jnp.bfloat16),
            pltpu.SemaphoreType.DMA((pieces // 2 * (1 + pieces // 2),)),
            pltpu.SemaphoreType.DMA((len(shards),)),
        ],
        compiler_params=pltpu.CompilerParams(vmem_limit_bytes=VMEM_LIMIT),
        cost_estimate=pl.CostEstimate(
            flops=2 * tokens * full * width,
            bytes_accessed=2 * full * (tokens + width),
            transcendentals=0,
        ),
    )(cos, sin, *x_pieces, *shards)


def attend_kernel(groups, own_ref, far_ref, *refs):
    keep, send, q_ref, near0, near1, far0, far1, sem = refs[5:]
    copies = [
        pltpu.make_async_copy(source, target, sem.at[at])
        for at, (source, target) in enumerate(zip(refs[:5], refs[7:12]))
    ]
    for copy in copies:
        copy.start()
    for copy in copies:
        copy.wait()
    tokens, pair = near0.shape
    head = pair // 2
    size = tokens // groups
    tiles = own_ref.shape[0]
    tile = 2 * tokens // tiles
    heads = q_ref.shape[1] // head
    rows = heads * size
    core = lax.axis_index("zero") % 2
    column = lax.broadcasted_iota(jnp.int32, (1, tokens), 1)
    column_group = column // size
    within = lax.rem(lax.broadcasted_iota(jnp.int32, (rows, 1), 0), size)
    hidden = jnp.float32(-1e30)
    nt = (((1,), (1,)), ((), ()))
    side = lax.axis_index("zero") // 2 % 2
    for h in range(groups):
        across = slice(h * size, (h + 1) * size)
        q = jnp.concatenate(
            [q_ref[across, g * head : (g + 1) * head] for g in range(heads)], axis=0
        )
        first = (2 * h + core) * size
        own_tile = first // tile
        seen = min(tokens, -(-(h + 1) * size // 128) * 128)
        parts, blocks = [], []
        for ref, mask_ref, width, parity, causal in (
            (far0, far_ref, tokens, core, False),
            (far1, far_ref, tokens, 1 - core, False),
            (near0, own_ref, seen, core, True),
            (near1, own_ref, seen, 1 - core, True),
        ):
            visible = jnp.zeros((1, width), jnp.int32)
            for g in range(-(-width // size)):
                at = mask_ref[own_tile, (2 * g + parity) * size // tile]
                visible = jnp.where(column_group[:, :width] == g, at, visible)
            visible = visible == 1
            if causal:
                group = column_group[:, :width]
                offset = (2 * group + parity) * size + column[:, :width] - group * size
                visible = visible & (offset <= first + within)
            scores = lax.dot_general(
                q, ref[:width, :head], nt, preferred_element_type=jnp.float32
            )
            parts.append(jnp.where(visible, scores, hidden))
            blocks.append((ref, width))
        scores = jnp.concatenate(parts, axis=1)
        largest = jnp.max(scores, axis=1, keepdims=True)
        weights = jnp.exp(scores - largest)
        total = jnp.sum(weights, axis=1, keepdims=True)
        rounded = weights.astype(jnp.bfloat16)
        mixed = jnp.zeros((rows, head), jnp.float32)
        start = 0
        for ref, width in blocks:
            mixed += jnp.dot(
                rounded[:, start : start + width],
                ref[:width, head:],
                preferred_element_type=jnp.float32,
            )
            start += width
        mixed = (mixed / total).astype(keep.dtype)
        rows_out = slice(h // 2 * size, (h // 2 + 1) * size)

        def store(out_ref, rows_out=rows_out, mixed=mixed):
            for g in range(heads):
                out_ref[rows_out, g * head : (g + 1) * head] = mixed[g * size : (g + 1) * size, :]

        pl.when(side == h % 2)(functools.partial(store, keep))
        pl.when(side != h % 2)(functools.partial(store, send))


def attend(groups, own_mask, far_mask, queries, near, near_other, far, far_other):
    tokens, width = queries.shape
    return pl.pallas_call(
        functools.partial(attend_kernel, groups),
        out_shape=[jax.ShapeDtypeStruct((tokens // 2, width), jnp.bfloat16)] * 2,
        in_specs=[SMEM, SMEM] + [HBM] * 5,
        out_specs=[VMEM] * 2,
        scratch_shapes=[pltpu.VMEM(queries.shape, jnp.bfloat16)]
        + [pltpu.VMEM(near.shape, jnp.bfloat16)] * 4
        + [pltpu.SemaphoreType.DMA((5,))],
        compiler_params=pltpu.CompilerParams(vmem_limit_bytes=VMEM_LIMIT),
        cost_estimate=pl.CostEstimate(
            flops=8 * tokens * tokens * width,
            bytes_accessed=8 * tokens * width,
            transcendentals=8 * tokens * tokens,
        ),
    )(own_mask, far_mask, queries, near, near_other, far, far_other)


def mix_kernel(layout, slots, out_refs, carry, *refs):
    count = len(refs) - len(layout) - out_refs - 2
    a_refs, w_refs = refs[:count], refs[count : count + len(layout)]
    outs = refs[count + len(layout) : -2]
    w_buf, sem = refs[-2:]
    width = w_buf.shape[2]
    half = a_refs[0].shape[1]
    copies = []
    for at, (ref, (slot, side, share)) in enumerate(zip(w_refs, layout)):
        rows = ref.shape[0]
        start = side * half
        if share is not None:
            start = pl.multiple_of(start + share_of(share) * rows, 16)
        copies.append(pltpu.make_async_copy(ref, w_buf.at[slot, pl.ds(start, rows)], sem.at[at]))
    for copy in copies:
        copy.start()
    slot = 0
    for out_ref, sides, number in zip(outs, *slots):
        rows = jnp.concatenate([ref[:, :half] for ref in a_refs[:sides]], axis=1)
        if carry:
            out_ref[:, :half] = rows
        for place in range(number):
            for copy, (its_slot, _, _) in zip(copies, layout):
                if its_slot == slot:
                    copy.wait()
            total = jnp.dot(
                rows, w_buf[slot, : sides * half], preferred_element_type=jnp.float32
            )
            start = place * width + (half if carry else 0)
            out_ref[:, start : start + width] = total.astype(out_ref.dtype)
            slot += 1


def mix(rows, blocks, dtypes, carry=False):
    layout, shards = [], []
    sides = [1 + max(side for side, _, _ in block[0]) for block in blocks]
    slots = [slot for block in blocks for slot in block]
    for at, slot in enumerate(slots):
        for side, share, piece in slot:
            layout.append((at, side, share))
            shards.append(piece)
    tokens, half = rows[0].shape
    width = shards[0].shape[1]
    return pl.pallas_call(
        functools.partial(
            mix_kernel, layout, (sides, [len(block) for block in blocks]), len(blocks), carry
        ),
        out_shape=[
            jax.ShapeDtypeStruct((tokens, width * len(block) + (half if carry else 0)), dtype)
            for block, dtype in zip(blocks, dtypes)
        ],
        in_specs=[VMEM] * len(rows) + [HBM] * len(shards),
        out_specs=[VMEM] * len(blocks),
        scratch_shapes=[
            pltpu.VMEM((len(slots), max(sides) * half, width), jnp.bfloat16),
            pltpu.SemaphoreType.DMA((len(shards),)),
        ],
        compiler_params=pltpu.CompilerParams(vmem_limit_bytes=VMEM_LIMIT),
        cost_estimate=pl.CostEstimate(
            flops=2 * tokens * half * width * len(shards),
            bytes_accessed=6 * half * width * len(shards) + 4 * tokens * width * len(slots),
            transcendentals=0,
        ),
    )(*rows, *shards)


def join_kernel(steps, carried, full_ref, keep_ref, *refs):
    got_refs, out_ref = refs[:-1], refs[-1]
    width = out_ref.shape[1] // len(steps)
    whole = full_ref.shape[1] // width
    got = [
        (ref, first)
        for at, ref in enumerate(got_refs)
        for first in range(0 if at else carried, ref.shape[1], width)
    ]
    for slot, along in enumerate(steps):
        start = pl.multiple_of(source_of(along) * width, 128)
        if slot < whole:
            block = full_ref[:, slot * width : (slot + 1) * width]
        else:
            columns = slice((slot - whole) * width, (slot - whole + 1) * width)
            got_ref, first = got[slot - whole]
            block = keep_ref[:, columns] + got_ref[:, first : first + width].astype(jnp.float32)
        out_ref[:, pl.ds(start, width)] = block.astype(out_ref.dtype)


def join(steps, carried, full, keep, gots, dtype):
    rows = full.shape[0]
    columns = full.shape[1] + keep.shape[1]
    return pl.pallas_call(
        functools.partial(join_kernel, steps, carried),
        out_shape=jax.ShapeDtypeStruct((rows, columns), dtype),
        in_specs=[VMEM] * (2 + len(gots)),
        out_specs=VMEM,
        compiler_params=pltpu.CompilerParams(vmem_limit_bytes=VMEM_LIMIT),
        cost_estimate=pl.CostEstimate(
            flops=rows * columns, bytes_accessed=8 * rows * columns, transcendentals=0
        ),
    )(full, keep, *gots)


def exchange_from(value, root, bit):
    other = swap(value, "ctx", 1 << bit)
    same = ((lax.axis_index("ctx") >> bit) & 1) == ((root >> bit) & 1)
    return jnp.where(same, value, other)


def local(
    activations,
    norm_gain,
    query_weight,
    kv_weight,
    out_weight,
    tile_mask,
    anchor_mask,
    anchor_index,
):
    tokens, depth = activations.shape
    head = kv_weight.shape[2]
    ctx_size, zero_size = lax.axis_size("ctx"), lax.axis_size("zero")
    ctx_rank, zero_rank = lax.axis_index("ctx"), lax.axis_index("zero")
    core = zero_rank % 2
    groups = zero_size // 2
    size = tokens // zero_size

    blocks = {0: activations}
    stride = groups
    while stride > 1:
        for known in range(0, zero_size, 2 * stride):
            blocks[known + stride] = swap(blocks[known], "zero", stride)
        stride //= 2

    shard_rows = kv_weight.shape[0]
    gain = lax.dynamic_slice_in_dim(norm_gain, ctx_rank * shard_rows, shard_rows)
    gain = gain.astype(jnp.float32)[:, None]
    kv_own = kv_weight[:, 0, :]
    kv_other, query_other = swap(kv_own, "zero", 1), swap(query_weight, "zero", 1)
    pair = jnp.where(
        core == 0,
        jnp.concatenate([kv_own, kv_other, query_weight, query_other], 1),
        jnp.concatenate([kv_other, kv_own, query_other, query_weight], 1),
    )
    pair = (pair.astype(jnp.float32) * gain).astype(jnp.bfloat16)
    out_other = swap(out_weight, "zero", 1)
    out_pair = jnp.where(
        core == 0,
        jnp.concatenate([out_weight, out_other], 0),
        jnp.concatenate([out_other, out_weight], 0),
    )
    ring_rows = shard_rows // 2
    rings = [
        Ring(pair[:ring_rows], core, pair),
        Ring(pair[ring_rows:], core, None, ring_rows),
    ]
    out_ring = Ring(out_pair, core)
    for part in range(4):
        for ring in rings:
            ring.advance(part, 4)
    held = rings[0].held + rings[1].held
    beyond = [swap(out_weight, "zero", 2)]
    out_ring.advance(0, 4, *[ring.moving for ring in rings], *beyond)

    far_blocks = [tied(blocks[m], rings[0].moving) for m in range(2, zero_size, 2)]
    x_pieces = []
    for at, theirs in enumerate(deal([blocks[0]]) + deal(far_blocks)):
        x_pieces += [([blocks[0]] + far_blocks)[at], swap(theirs, "zero", 1)]

    half = head // 2
    frequency = jnp.power(
        jnp.float32(ROPE_BASE), -(jnp.arange(half, dtype=jnp.float32) * 2.0 / head)
    )
    local_token = jnp.arange(tokens // 2, dtype=jnp.int32)
    offsets = (2 * (local_token // size) + core) * size + local_token % size
    positions = ctx_rank * tokens + offsets
    angles = positions.astype(jnp.float32)[:, None] * frequency[None, :]
    cos_half, sin_half = jnp.cos(angles), jnp.sin(angles)
    cos = jnp.concatenate([cos_half, cos_half], -1)
    sin = jnp.concatenate([-sin_half, sin_half], -1)

    near, queries = project(cos, sin, x_pieces, held)

    def share():
        for at in range(len(beyond), out_ring.at + 1):
            beyond.append(swap(out_ring.held[2 * at - 1][3], "zero", 2))

    share()
    anchor = anchor_index[0]
    far = tied(near, out_ring.moving)
    for bit in range(int(math.log2(ctx_size))):
        far = exchange_from(far, anchor, bit)
        if bit == 0:
            near_other = swap(near, "zero", 1)
            far = tied(far, near_other)
            out_ring.advance(1, 4, far)
    far_other = swap(far, "zero", 1)
    out_ring.advance(2, 4, far_other, beyond[-1])
    far_mask = jnp.where(ctx_rank != anchor, anchor_mask[0], 0)
    keep, send = attend(
        groups, tile_mask[0], far_mask, queries, near, near_other, far, far_other
    )
    cut = ctx_size // 4
    block = [
        [(0, None, piece)]
        for steps, _, _, piece in out_ring.held
        if len(beyond) <= abs(steps) <= cut
    ]
    (terms,) = mix([send], [block], [jnp.bfloat16], carry=True)
    out_ring.held[-1] = (
        *out_ring.held[-1][:3],
        swap(tied(out_ring.moving, terms), "zero", 1),
    )
    got = swap(terms, "zero", 2)
    got_terms = [got]
    out_ring.advance(3, 4, terms)

    steps_of, both_chips, one_chip = [], [], []
    for steps, half_of, _, piece in out_ring.held:
        slots = both_chips if abs(steps) < len(beyond) else one_chip
        if half_of != 1:
            steps_of.append(steps)
            slots.append([])
        slots[-1].append((0, half_of, piece))
        if slots is both_chips:
            if steps <= 0:
                across = swap(beyond[-steps], "zero", 1)
            if steps == 0:
                slots[-1] += [(1, 0, beyond[0]), (1, 1, across)]
            else:
                slots[-1].append((1, half_of, beyond[-steps] if steps < 0 else across))
    for block, early in ((one_chip[cut : 2 * cut], []), (one_chip[2 * cut :], [got])):
        (terms,) = mix([tied(send, *early)], [block], [jnp.bfloat16])
        got_terms.append(swap(terms, "zero", 2))
    full, kept = mix([keep, got], [both_chips, one_chip], [jnp.float32, jnp.float32])
    if zero_size == 4:
        return join(steps_of, send.shape[1], full, kept, got_terms, jnp.bfloat16)
    total = join(steps_of, send.shape[1], full, kept, got_terms, jnp.float32)
    stride = zero_size // 2
    while stride > 2:
        rows = total.shape[0] // 2
        bit = (zero_rank // stride) % 2
        stay = lax.dynamic_slice_in_dim(total, bit * rows, rows, 0)
        go = lax.dynamic_slice_in_dim(total, (1 - bit) * rows, rows, 0)
        total = stay + swap(go.astype(jnp.bfloat16), "zero", stride).astype(jnp.float32)
        stride //= 2
    return total.astype(jnp.bfloat16)


def solution(mesh):
    placed = (
        P("ctx", "zero"),
        P(),
        P("ctx", "zero"),
        P("ctx", "zero", None),
        P("zero", "ctx"),
        P("ctx", None, None),
        P("ctx", None, None),
        P(),
    )
    return jax.shard_map(
        local, mesh=mesh, in_specs=placed, out_specs=P(("ctx", "zero"), None), check_vma=False
    )
```

```python
import functools
import math

import jax
import jax.numpy as jnp
from jax import lax
from jax.experimental import pallas as pl
from jax.experimental.pallas import tpu as pltpu
from jax.sharding import PartitionSpec as P

HBM = pl.BlockSpec(memory_space=pltpu.HBM)
VMEM = pl.BlockSpec(memory_space=pltpu.VMEM)
SMEM = pl.BlockSpec(memory_space=pltpu.SMEM)
VMEM_LIMIT = 24 * 1024 * 1024
ROPE_BASE = 500000.0


def swap(value, axis, stride):
    pairs = [(source, source ^ stride) for source in range(lax.axis_size(axis))]
    return lax.ppermute(value, axis, pairs)


def cycle(size):
    return list(range(0, size, 2)) + list(range(1, size, 2))[::-1]


def ring_step(value):
    ctx_size, zero_size = lax.axis_size("ctx"), lax.axis_size("zero")
    order = cycle(ctx_size)
    pairs = []
    for at in range(ctx_size):
        for zero in range(zero_size):
            to = order[(at + (1 if zero % 2 == 0 else -1)) % ctx_size]
            pairs.append((order[at] * zero_size + zero, to * zero_size + zero))
    return lax.ppermute(value, ("ctx", "zero"), pairs)


class Ring:
    def __init__(self, shard, core, whole=None, base=0):
        self.held = [(0, None, 0, shard if whole is None else whole)] if base == 0 else []
        self.base = base
        self.moving, self.core, self.at = shard, core, 0
        self.length = lax.axis_size("ctx") // 2

    def step(self, *after):
        self.at += 1
        last = self.at == self.length
        if last:
            half = self.moving.shape[0] // 2
            self.moving = lax.dynamic_slice_in_dim(self.moving, self.core * half, half, 0)
        behind = self.held[-3][3:] if len(self.held) > 3 else []
        self.moving = ring_step(tied(self.moving, *behind, *after))
        self.held.append((-self.at, 0 if last else None, self.base, self.moving))
        self.held.append(
            (self.at, 1 if last else None, self.base, swap(self.moving, "zero", 1))
        )
        return self.moving

    def advance(self, part, parts, *after):
        while self.at < self.length * (part + 1) // parts:
            self.step(*after)
        return self.moving


def tied(value, *others):
    return lax.optimization_barrier((value, *others))[0] if others else value


def source_of(steps):
    size = lax.axis_size("ctx")
    ctx, core = lax.axis_index("ctx"), lax.axis_index("zero") % 2
    place = jnp.where(ctx % 2 == 0, ctx // 2, size - 1 - ctx // 2)
    place = lax.rem(place + steps * (1 - 2 * core) + size, size)
    return jnp.where(place < size // 2, 2 * place, 2 * (size - 1 - place) + 1)


def share_of(share):
    core = lax.axis_index("zero") % 2
    return core if share == 0 else 1 - core


def token_rows(group, other, size):
    core = lax.axis_index("zero") % 2
    if other:
        core = 1 - core
    return pl.ds(pl.multiple_of((2 * group + core) * size, 16), size)


def deal_kernel(count, *refs):
    x_refs, outs, sem = refs[:count], refs[count:-1], refs[-1]
    groups = lax.axis_size("zero") // 2
    size = x_refs[0].shape[0] // (2 * groups)
    copies = []
    for x_ref, out_ref in zip(x_refs, outs):
        for group in range(groups):
            copies.append(
                pltpu.make_async_copy(
                    x_ref.at[token_rows(group, True, size)],
                    out_ref.at[pl.ds(group * size, size)],
                    sem.at[len(copies)],
                )
            )
    for copy in copies:
        copy.start()
    for copy in copies:
        copy.wait()


def deal(arrays):
    tokens, depth = arrays[0].shape
    part = jax.ShapeDtypeStruct((tokens // 2, depth), arrays[0].dtype)
    copies = len(arrays) * lax.axis_size("zero") // 2
    return pl.pallas_call(
        functools.partial(deal_kernel, len(arrays)),
        out_shape=[part] * len(arrays),
        in_specs=[HBM] * len(arrays),
        out_specs=[HBM] * len(arrays),
        scratch_shapes=[pltpu.SemaphoreType.DMA((copies,))],
        compiler_params=pltpu.CompilerParams(vmem_limit_bytes=VMEM_LIMIT),
    )(*arrays)


def project_kernel(layout, *refs):
    (kv_ref, q_ref, x_buf, w_buf, x_sem, w_sem) = refs[-6:]
    pieces, tokens, depth = x_buf.shape
    cos_ref, sin_ref = refs[:2]
    x_refs = refs[2 : 2 + pieces]
    w_refs = refs[2 + pieces : -6]
    zero = lax.axis_index("zero")
    shard_rows = w_refs[0].shape[0]
    x_copies, w_copies = [], []
    for m, ref in enumerate(x_refs):
        target = x_buf.at[jnp.bitwise_xor(zero, m)]
        if m % 2:
            x_copies.append(pltpu.make_async_copy(ref, target, x_sem.at[len(x_copies)]))
            continue
        size = 2 * tokens // pieces
        for group in range(pieces // 2):
            x_copies.append(
                pltpu.make_async_copy(
                    ref.at[token_rows(group, False, size)],
                    target.at[pl.ds(group * size, size)],
                    x_sem.at[len(x_copies)],
                )
            )
    for at, (ref, (steps, share, base)) in enumerate(zip(w_refs, layout)):
        start = source_of(steps) * shard_rows + base
        if share is not None:
            start = start + share_of(share) * ref.shape[0]
        rows = pl.ds(pl.multiple_of(start, 16), ref.shape[0])
        w_copies.append(pltpu.make_async_copy(ref, w_buf.at[rows], w_sem.at[at]))
    for copy in x_copies + w_copies:
        copy.start()
    for copy in x_copies:
        copy.wait()
    squares = jnp.zeros((tokens, 128), jnp.float32)
    for at in range(pieces):
        for first in range(0, depth, 128):
            x_float = x_buf[at, :, first : first + 128].astype(jnp.float32)
            squares += x_float * x_float
    mean = jnp.sum(squares, axis=1, keepdims=True) / (depth * pieces)
    scale = jnp.broadcast_to(lax.rsqrt(mean + 1e-05), squares.shape)
    for copy in w_copies:
        copy.wait()
    head = cos_ref.shape[1]
    shrink = jnp.float32(head ** (-0.5))
    for out_ref, columns in ((kv_ref, 0), (q_ref, 2 * head)):
        for first in range(0, out_ref.shape[1], 2 * head):
            both = slice(columns + first, columns + first + 2 * head)
            total = jnp.zeros((tokens, 2 * head), jnp.float32)
            for at in range(pieces):
                total += jnp.dot(
                    x_buf[at],
                    w_buf[at * depth : (at + 1) * depth, both],
                    preferred_element_type=jnp.float32,
                )
            for at in range(2):
                part = total[:, at * head : (at + 1) * head] * scale
                if columns or not at:
                    part = part * cos_ref[...] + pltpu.roll(part, head // 2, 1) * sin_ref[...]
                if columns:
                    part = part * shrink
                out_ref[:, first + at * head : first + (at + 1) * head] = part.astype(
                    out_ref.dtype
                )


def project(cos, sin, x_pieces, held):
    layout = [(steps, share, base) for steps, share, base, _ in held]
    shards = [piece for _, _, _, piece in held]
    tokens, depth = x_pieces[1].shape
    pieces, head = len(x_pieces), cos.shape[1]
    width = shards[0].shape[1]
    full = depth * pieces
    return pl.pallas_call(
        functools.partial(project_kernel, layout),
        out_shape=[
            jax.ShapeDtypeStruct((tokens, 2 * head), jnp.bfloat16),
            jax.ShapeDtypeStruct((tokens, width - 2 * head), jnp.bfloat16),
        ],
        in_specs=[VMEM] * 2 + [HBM] * (pieces + len(shards)),
        out_specs=[VMEM] * 2,
        scratch_shapes=[
            pltpu.VMEM((pieces, tokens, depth), jnp.bfloat16),
            pltpu.VMEM((full, width), jnp.bfloat16),
            pltpu.SemaphoreType.DMA((pieces // 2 * (1 + pieces // 2),)),
            pltpu.SemaphoreType.DMA((len(shards),)),
        ],
        compiler_params=pltpu.CompilerParams(vmem_limit_bytes=VMEM_LIMIT),
        cost_estimate=pl.CostEstimate(
            flops=2 * tokens * full * width,
            bytes_accessed=2 * full * (tokens + width),
            transcendentals=0,
        ),
    )(cos, sin, *x_pieces, *shards)


def attend_kernel(groups, own_ref, far_ref, *refs):
    keep, send, q_ref, near0, near1, far0, far1, sem = refs[5:]
    copies = [
        pltpu.make_async_copy(source, target, sem.at[at])
        for at, (source, target) in enumerate(zip(refs[:5], refs[7:12]))
    ]
    for copy in copies:
        copy.start()
    for copy in copies:
        copy.wait()
    tokens, pair = near0.shape
    head = pair // 2
    size = tokens // groups
    tiles = own_ref.shape[0]
    tile = 2 * tokens // tiles
    heads = q_ref.shape[1] // head
    rows = heads * size
    core = lax.axis_index("zero") % 2
    column = lax.broadcasted_iota(jnp.int32, (1, tokens), 1)
    column_group = column // size
    within = lax.rem(lax.broadcasted_iota(jnp.int32, (rows, 1), 0), size)
    hidden = jnp.float32(-1e30)
    nt = (((1,), (1,)), ((), ()))
    side = lax.axis_index("zero") // 2 % 2
    for h in range(groups):
        across = slice(h * size, (h + 1) * size)
        q = jnp.concatenate(
            [q_ref[across, g * head : (g + 1) * head] for g in range(heads)], axis=0
        )
        first = (2 * h + core) * size
        own_tile = first // tile
        seen = min(tokens, -(-(h + 1) * size // 128) * 128)
        parts, blocks = [], []
        for ref, mask_ref, width, parity, causal in (
            (far0, far_ref, tokens, core, False),
            (far1, far_ref, tokens, 1 - core, False),
            (near0, own_ref, seen, core, True),
            (near1, own_ref, seen, 1 - core, True),
        ):
            visible = jnp.zeros((1, width), jnp.int32)
            for g in range(-(-width // size)):
                at = mask_ref[own_tile, (2 * g + parity) * size // tile]
                visible = jnp.where(column_group[:, :width] == g, at, visible)
            visible = visible == 1
            if causal:
                group = column_group[:, :width]
                offset = (2 * group + parity) * size + column[:, :width] - group * size
                visible = visible & (offset <= first + within)
            scores = lax.dot_general(
                q, ref[:width, :head], nt, preferred_element_type=jnp.float32
            )
            parts.append(jnp.where(visible, scores, hidden))
            blocks.append((ref, width))
        scores = jnp.concatenate(parts, axis=1)
        largest = jnp.max(scores, axis=1, keepdims=True)
        weights = jnp.exp(scores - largest)
        total = jnp.sum(weights, axis=1, keepdims=True)
        rounded = weights.astype(jnp.bfloat16)
        mixed = jnp.zeros((rows, head), jnp.float32)
        start = 0
        for ref, width in blocks:
            mixed += jnp.dot(
                rounded[:, start : start + width],
                ref[:width, head:],
                preferred_element_type=jnp.float32,
            )
            start += width
        mixed = (mixed / total).astype(keep.dtype)
        rows_out = slice(h // 2 * size, (h // 2 + 1) * size)

        def store(out_ref, rows_out=rows_out, mixed=mixed):
            for g in range(heads):
                out_ref[rows_out, g * head : (g + 1) * head] = mixed[g * size : (g + 1) * size, :]

        pl.when(side == h % 2)(functools.partial(store, keep))
        pl.when(side != h % 2)(functools.partial(store, send))


def attend(groups, own_mask, far_mask, queries, near, near_other, far, far_other):
    tokens, width = queries.shape
    return pl.pallas_call(
        functools.partial(attend_kernel, groups),
        out_shape=[jax.ShapeDtypeStruct((tokens // 2, width), jnp.bfloat16)] * 2,
        in_specs=[SMEM, SMEM] + [HBM] * 5,
        out_specs=[VMEM] * 2,
        scratch_shapes=[pltpu.VMEM(queries.shape, jnp.bfloat16)]
        + [pltpu.VMEM(near.shape, jnp.bfloat16)] * 4
        + [pltpu.SemaphoreType.DMA((5,))],
        compiler_params=pltpu.CompilerParams(vmem_limit_bytes=VMEM_LIMIT),
        cost_estimate=pl.CostEstimate(
            flops=8 * tokens * tokens * width,
            bytes_accessed=8 * tokens * width,
            transcendentals=8 * tokens * tokens,
        ),
    )(own_mask, far_mask, queries, near, near_other, far, far_other)


def mix_kernel(layout, slots, out_refs, *refs):
    count = len(refs) - len(layout) - out_refs - 2
    a_refs, w_refs = refs[:count], refs[count : count + len(layout)]
    outs = refs[count + len(layout) : -2]
    w_buf, sem = refs[-2:]
    width = w_buf.shape[2]
    half = a_refs[0].shape[1]
    copies = []
    for at, (ref, (slot, side, share)) in enumerate(zip(w_refs, layout)):
        rows = ref.shape[0]
        start = side * half
        if share is not None:
            start = pl.multiple_of(start + share_of(share) * rows, 16)
        copies.append(pltpu.make_async_copy(ref, w_buf.at[slot, pl.ds(start, rows)], sem.at[at]))
    for copy in copies:
        copy.start()
    slot = 0
    for out_ref, sides, number in zip(outs, *slots):
        rows = jnp.concatenate([ref[...] for ref in a_refs[:sides]], axis=1)
        for place in range(number):
            for copy, (its_slot, _, _) in zip(copies, layout):
                if its_slot == slot:
                    copy.wait()
            total = jnp.dot(
                rows, w_buf[slot, : sides * half], preferred_element_type=jnp.float32
            )
            out_ref[:, place * width : (place + 1) * width] = total.astype(out_ref.dtype)
            slot += 1


def mix(rows, blocks, dtypes):
    layout, shards = [], []
    sides = [1 + max(side for side, _, _ in block[0]) for block in blocks]
    slots = [slot for block in blocks for slot in block]
    for at, slot in enumerate(slots):
        for side, share, piece in slot:
            layout.append((at, side, share))
            shards.append(piece)
    tokens, half = rows[0].shape
    width = shards[0].shape[1]
    return pl.pallas_call(
        functools.partial(
            mix_kernel, layout, (sides, [len(block) for block in blocks]), len(blocks)
        ),
        out_shape=[
            jax.ShapeDtypeStruct((tokens, width * len(block)), dtype)
            for block, dtype in zip(blocks, dtypes)
        ],
        in_specs=[VMEM] * len(rows) + [HBM] * len(shards),
        out_specs=[VMEM] * len(blocks),
        scratch_shapes=[
            pltpu.VMEM((len(slots), max(sides) * half, width), jnp.bfloat16),
            pltpu.SemaphoreType.DMA((len(shards),)),
        ],
        compiler_params=pltpu.CompilerParams(vmem_limit_bytes=VMEM_LIMIT),
        cost_estimate=pl.CostEstimate(
            flops=2 * tokens * half * width * len(shards),
            bytes_accessed=6 * half * width * len(shards) + 4 * tokens * width * len(slots),
            transcendentals=0,
        ),
    )(*rows, *shards)


def join_kernel(steps, full_ref, keep_ref, *refs):
    got_refs, out_ref = refs[:-1], refs[-1]
    width = out_ref.shape[1] // len(steps)
    whole = full_ref.shape[1] // width
    got = [
        (ref, first) for ref in got_refs for first in range(0, ref.shape[1], width)
    ]
    for slot, along in enumerate(steps):
        start = pl.multiple_of(source_of(along) * width, 128)
        if slot < whole:
            block = full_ref[:, slot * width : (slot + 1) * width]
        else:
            columns = slice((slot - whole) * width, (slot - whole + 1) * width)
            got_ref, first = got[slot - whole]
            block = keep_ref[:, columns] + got_ref[:, first : first + width].astype(jnp.float32)
        out_ref[:, pl.ds(start, width)] = block.astype(out_ref.dtype)


def join(steps, full, keep, gots, dtype):
    rows = full.shape[0]
    columns = full.shape[1] + keep.shape[1]
    return pl.pallas_call(
        functools.partial(join_kernel, steps),
        out_shape=jax.ShapeDtypeStruct((rows, columns), dtype),
        in_specs=[VMEM] * (2 + len(gots)),
        out_specs=VMEM,
        compiler_params=pltpu.CompilerParams(vmem_limit_bytes=VMEM_LIMIT),
        cost_estimate=pl.CostEstimate(
            flops=rows * columns, bytes_accessed=8 * rows * columns, transcendentals=0
        ),
    )(full, keep, *gots)


def exchange_from(value, root, bit):
    other = swap(value, "ctx", 1 << bit)
    same = ((lax.axis_index("ctx") >> bit) & 1) == ((root >> bit) & 1)
    return jnp.where(same, value, other)


def local(
    activations,
    norm_gain,
    query_weight,
    kv_weight,
    out_weight,
    tile_mask,
    anchor_mask,
    anchor_index,
):
    tokens, depth = activations.shape
    head = kv_weight.shape[2]
    ctx_size, zero_size = lax.axis_size("ctx"), lax.axis_size("zero")
    ctx_rank, zero_rank = lax.axis_index("ctx"), lax.axis_index("zero")
    core = zero_rank % 2
    groups = zero_size // 2
    size = tokens // zero_size

    blocks = {0: activations}
    stride = groups
    while stride > 1:
        for known in range(0, zero_size, 2 * stride):
            blocks[known + stride] = swap(blocks[known], "zero", stride)
        stride //= 2

    shard_rows = kv_weight.shape[0]
    gain = lax.dynamic_slice_in_dim(norm_gain, ctx_rank * shard_rows, shard_rows)
    gain = gain.astype(jnp.float32)[:, None]
    kv_own = kv_weight[:, 0, :]
    kv_other, query_other = swap(kv_own, "zero", 1), swap(query_weight, "zero", 1)
    pair = jnp.where(
        core == 0,
        jnp.concatenate([kv_own, kv_other, query_weight, query_other], 1),
        jnp.concatenate([kv_other, kv_own, query_other, query_weight], 1),
    )
    pair = (pair.astype(jnp.float32) * gain).astype(jnp.bfloat16)
    out_other = swap(out_weight, "zero", 1)
    out_pair = jnp.where(
        core == 0,
        jnp.concatenate([out_weight, out_other], 0),
        jnp.concatenate([out_other, out_weight], 0),
    )
    ring_rows = shard_rows // 2
    rings = [
        Ring(pair[:ring_rows], core, pair),
        Ring(pair[ring_rows:], core, None, ring_rows),
    ]
    out_ring = Ring(out_pair, core)
    for part in range(4):
        for ring in rings:
            ring.advance(part, 4)
    held = rings[0].held + rings[1].held
    beyond = [swap(out_weight, "zero", 2)]
    out_ring.advance(0, 4, *[ring.moving for ring in rings], *beyond)

    far_blocks = [tied(blocks[m], rings[0].moving) for m in range(2, zero_size, 2)]
    x_pieces = []
    for at, theirs in enumerate(deal([blocks[0]]) + deal(far_blocks)):
        x_pieces += [([blocks[0]] + far_blocks)[at], swap(theirs, "zero", 1)]

    half = head // 2
    frequency = jnp.power(
        jnp.float32(ROPE_BASE), -(jnp.arange(half, dtype=jnp.float32) * 2.0 / head)
    )
    local_token = jnp.arange(tokens // 2, dtype=jnp.int32)
    offsets = (2 * (local_token // size) + core) * size + local_token % size
    positions = ctx_rank * tokens + offsets
    angles = positions.astype(jnp.float32)[:, None] * frequency[None, :]
    cos_half, sin_half = jnp.cos(angles), jnp.sin(angles)
    cos = jnp.concatenate([cos_half, cos_half], -1)
    sin = jnp.concatenate([-sin_half, sin_half], -1)

    near, queries = project(cos, sin, x_pieces, held)

    def share():
        for at in range(len(beyond), out_ring.at + 1):
            beyond.append(swap(out_ring.held[2 * at - 1][3], "zero", 2))

    share()
    anchor = anchor_index[0]
    far = tied(near, out_ring.moving)
    for bit in range(int(math.log2(ctx_size))):
        far = exchange_from(far, anchor, bit)
        if bit == 0:
            near_other = swap(near, "zero", 1)
            far = tied(far, near_other)
            out_ring.advance(1, 4, far)
    far_other = swap(far, "zero", 1)
    out_ring.advance(2, 4, far_other, beyond[-1])
    far_mask = jnp.where(ctx_rank != anchor, anchor_mask[0], 0)
    keep, send = attend(
        groups, tile_mask[0], far_mask, queries, near, near_other, far, far_other
    )
    got = swap(send, "zero", 2)
    out_ring.held[-1] = (
        *out_ring.held[-1][:3],
        swap(tied(out_ring.moving, send), "zero", 1),
    )
    cut = ctx_size // 4
    block = [
        [(0, None, piece)]
        for steps, _, _, piece in out_ring.held
        if len(beyond) <= abs(steps) <= cut
    ]
    (terms,) = mix([send], [block], [jnp.bfloat16])
    got_terms = [swap(terms, "zero", 2)]
    out_ring.advance(3, 4, terms)

    steps_of, both_chips, one_chip = [], [], []
    for steps, half_of, _, piece in out_ring.held:
        slots = both_chips if abs(steps) < len(beyond) else one_chip
        if half_of != 1:
            steps_of.append(steps)
            slots.append([])
        slots[-1].append((0, half_of, piece))
        if slots is both_chips:
            if steps <= 0:
                across = swap(beyond[-steps], "zero", 1)
            if steps == 0:
                slots[-1] += [(1, 0, beyond[0]), (1, 1, across)]
            else:
                slots[-1].append((1, half_of, beyond[-steps] if steps < 0 else across))
    for block, early in ((one_chip[cut : 2 * cut], [got]), (one_chip[2 * cut :], got_terms[:1])):
        (terms,) = mix([tied(send, *early)], [block], [jnp.bfloat16])
        got_terms.append(swap(terms, "zero", 2))
    full, kept = mix([keep, got], [both_chips, one_chip], [jnp.float32, jnp.float32])
    if zero_size == 4:
        return join(steps_of, full, kept, got_terms, jnp.bfloat16)
    total = join(steps_of, full, kept, got_terms, jnp.float32)
    stride = zero_size // 2
    while stride > 2:
        rows = total.shape[0] // 2
        bit = (zero_rank // stride) % 2
        stay = lax.dynamic_slice_in_dim(total, bit * rows, rows, 0)
        go = lax.dynamic_slice_in_dim(total, (1 - bit) * rows, rows, 0)
        total = stay + swap(go.astype(jnp.bfloat16), "zero", stride).astype(jnp.float32)
        stride //= 2
    return total.astype(jnp.bfloat16)


def solution(mesh):
    placed = (
        P("ctx", "zero"),
        P(),
        P("ctx", "zero"),
        P("ctx", "zero", None),
        P("zero", "ctx"),
        P("ctx", None, None),
        P("ctx", None, None),
        P(),
    )
    return jax.shard_map(
        local, mesh=mesh, in_specs=placed, out_specs=P(("ctx", "zero"), None), check_vma=False
    )
```
